32 devices in a mesh: dp: 16 (over z, x, core), tensor: 2 (over y).
Axes of the slice: x: 2, y: 2, z: 4, core: 2. Of those that a mesh axis runs over, the one named last changes fastest.
Arguments:
- stream: bfloat16 [9216, 767], P('dp'), may hold values from -6 to 6
- w_query: bfloat16 [768, 768], P('dp', 'tensor'), may hold values from -0.21875 to 0.21875
- w_key: bfloat16 [768, 768], P('dp', 'tensor'), may hold values from -0.21875 to 0.21875
- w_value: bfloat16 [768, 768], P('dp', 'tensor'), may hold values from -0.21875 to 0.21875
- b_query: bfloat16 [768], P('tensor'), may hold values from -4 to 4
- b_value: bfloat16 [768], P('tensor'), may hold values from -4 to 4
- w_out: bfloat16 [768, 768], P('tensor', 'dp'), may hold values from -1.75 to 1.75
- b_out: bfloat16 [768], replicated, may hold values from -4 to 4
- gain_attn: bfloat16 [768], replicated, may hold values from 0.099609375 to 1.8984375
- w_up: bfloat16 [768, 3072], P('dp', 'tensor'), may hold values from -0.21875 to 0.21875
- b_up: bfloat16 [3072], P('tensor'), may hold values from -4 to 4
- w_down: bfloat16 [3072, 768], P('tensor', 'dp'), may hold values from -0.109375 to 0.109375
- b_down: bfloat16 [768], replicated, may hold values from -4 to 4
- gain_mlp: bfloat16 [768], replicated, may hold values from 0.099609375 to 1.8984375
- cotangent: bfloat16 [9216, 767], P('dp'), may hold values from -6 to 6
- lengths: int32 [16, 4], P('dp'), may hold values from 1 to 512, 576 in all within a row
Outputs:
- out: bfloat16 [9216, 767], P('dp')
- grad_stream: bfloat16 [9216, 767], P('dp')
- grad_w_query: float32 [768, 768], P('dp', 'tensor')
- grad_w_key: float32 [768, 768], P('dp', 'tensor')
- grad_w_value: float32 [768, 768], P('dp', 'tensor')
- grad_b_query: float32 [768], P('tensor')
- grad_b_value: float32 [768], P('tensor')
- grad_w_out: float32 [768, 768], P('tensor', 'dp')
- grad_b_out: float32 [768], replicated
- grad_gain_attn: float32 [768], replicated
- grad_w_up: float32 [768, 3072], P('dp', 'tensor')
- grad_b_up: float32 [3072], P('tensor')
- grad_w_down: float32 [3072, 768], P('tensor', 'dp')
- grad_b_down: float32 [768], replicated
- grad_gain_mlp: float32 [768], replicated
The draws below stay inside these ranges and needn't reach their ends.
Inputs may be any that keep to these rules, and one draw needn't show every extreme that they name: In each row the lengths sum to 576 and one of them is exactly 512.
All inputs are finite; a program needn't handle non-finite values.
Results may differ from the reference program's by a relative error of at most 0.01.
Values may be sent and summed in bfloat16 or wider, within the bound.
No kernel may reach another device: no remote copies, remote signals or barrier semaphores. Data moves between devices by JAX's collectives and lax.ppermute only.
A program may use at most 128 MiB of HBM per device.

```python
import math
import jax
import jax.numpy as jnp
import numpy as np
from jax import lax

D = 768
H = 12
HD = 64
FF = 3072
TOK_DEV = 576
SLOTS = 4
LONGEST = 512
DC = 767
GROUPS = 16
TOKENS = 9216


def block_scale(stream_key, dims, cuts, smallest, largest):
    level, own = 1.0, jax.random.fold_in(stream_key, 6)
    for position, shards_of in cuts:
        steps = jnp.exp(jax.random.uniform(jax.random.fold_in(own, position), (shards_of,), jnp.float32, smallest / len(cuts), largest / len(cuts)))
        level = level * jnp.repeat(steps, dims[position] // shards_of).reshape([-1 if axis == position else 1 for axis in range(len(dims))])
    return level


def length_profile(count, total, reach, lean):
    weights = [(1 << 20) // math.isqrt(standing ** lean) + 1 for standing in range(2, count + 1)]
    surplus, holding = total - reach - (count - 1), [1] * (count - 1)
    while surplus > 0:
        movable = [i for i in range(count - 1) if holding[i] < reach]
        mass, budget = sum([weights[i] for i in movable]), surplus
        for i in movable:
            addition = min(reach - holding[i], max(1, budget * weights[i] // mass), surplus)
            holding[i] = holding[i] + addition
            surplus = surplus - addition
    return np.array([reach] + holding)


def uneven(rng, count, total, limit, lean):
    if count == 2:
        one = jax.random.randint(rng, (), max(1, total - limit), min(limit, total - 1) + 1)
        return jnp.stack([one, total - one])
    sizes = jnp.asarray(length_profile(count, total, limit, lean), jnp.int32)
    pairs = (count - 1) // 2
    giver, receiver = sizes[1:1 + 2 * pairs:2], sizes[2:2 + 2 * pairs:2]
    margin = jnp.minimum(giver - 1, limit - receiver)
    shifted = jax.random.randint(jax.random.fold_in(rng, 1), (pairs,), 0, 1 << 20) % (margin + 1)
    sizes = sizes.at[1:1 + 2 * pairs:2].set(giver - shifted).at[2:2 + 2 * pairs:2].set(receiver + shifted)
    return sizes[jax.random.permutation(jax.random.fold_in(rng, 2), count)]


def centred(key, extent, scale, most, split=(), held_as=jnp.bfloat16):
    array = jax.random.normal(key, extent, jnp.float32) * scale
    if len(split) > 0:
        array = block_scale(key, extent, split, -0.22, 0.18) * array
    return jnp.clip(array, min=-most, max=most).astype(held_as)


def setup_inputs(seed: int = 0) -> dict:
    key_of = jax.random.split(jax.random.key(seed), 17)
    stream = centred(key_of[0], (TOKENS, DC), 1.0, 6.0, ((0, 16),))
    w_query = centred(key_of[1], (D, D), D ** -0.5, 0.21875, ((0, 16), (1, 2)))
    w_key = centred(key_of[2], (D, D), D ** -0.5, 0.21875, ((0, 16), (1, 2)))
    w_value = centred(key_of[3], (D, D), D ** -0.5, 0.21875, ((0, 16), (1, 2)))
    b_query = centred(key_of[4], (D,), 0.3, 4.0, ((0, 2),))
    b_value = centred(key_of[5], (D,), 0.3, 4.0, ((0, 2),))
    w_out = centred(key_of[6], (D, D), (D // 64) ** -0.5, 1.75, ((0, 2), (1, 16)))
    b_out = centred(key_of[7], (D,), 0.3, 4.0)
    gain_attn = jnp.clip(1.0 + 0.18 * jax.random.normal(key_of[8], (D,), jnp.float32), 0.099609375, 1.8984375).astype(jnp.bfloat16)
    w_up = centred(key_of[9], (D, FF), D ** -0.5, 0.21875, ((0, 16), (1, 2)))
    b_up = centred(key_of[10], (FF,), 0.3, 4.0, ((0, 2),))
    w_down = centred(key_of[11], (FF, D), FF ** -0.5, 0.109375, ((0, 2), (1, 16)))
    b_down = centred(key_of[12], (D,), 0.3, 4.0)
    gain_mlp = jnp.clip(1.0 + 0.18 * jax.random.normal(key_of[13], (D,), jnp.float32), 0.099609375, 1.8984375).astype(jnp.bfloat16)
    cotangent = centred(key_of[14], (TOKENS, DC), 1.0, 6.0, ((0, 16),))
    lengths = jax.vmap(lambda own: uneven(own, SLOTS, TOK_DEV, LONGEST, 2))(jax.random.split(key_of[15], GROUPS)).reshape((GROUPS, SLOTS)).astype(jnp.int32)
    return dict(stream=stream, w_query=w_query, w_key=w_key, w_value=w_value, b_query=b_query, b_value=b_value, w_out=w_out, b_out=b_out, gain_attn=gain_attn, w_up=w_up, b_up=b_up, w_down=w_down, b_down=b_down, gain_mlp=gain_mlp, cotangent=cotangent, lengths=lengths)


epsilon = 1e-05

@jax.custom_vjp
def low(v):
    return lax.optimization_barrier(v.astype(jnp.bfloat16)).astype(jnp.float32)

@jax.custom_vjp
def low_back(v):
    return v

def low_keep(v):
    return (low(v), None)

def low_pass(kept, grad):
    return (grad,)

def back_keep(v):
    return (v, None)

def back_low(kept, grad):
    return (low(grad),)
low.defvjp(low_keep, low_pass)
low_back.defvjp(back_keep, back_low)

def matmul(left_arr, right_arr):
    return jnp.dot(left_arr, right_arr, precision=lax.Precision.HIGHEST)

def expand_full(stream):
    return jnp.concatenate([stream, -lax.optimization_barrier(jnp.sum(stream, axis=1, keepdims=True))], axis=1)

def crms_norm(stream, gain_vec):
    full_vec = expand_full(stream)
    return full_vec * lax.rsqrt(lax.optimization_barrier(jnp.mean(full_vec * full_vec, axis=1, keepdims=True)) + epsilon) * gain_vec

def compress_add(stream, branch):
    return stream + (branch - lax.optimization_barrier(jnp.mean(branch, axis=1, keepdims=True)))[:, :-1]

def apply_layer(param_set, stream, lengths):
    w_query, w_key, w_value, b_query, b_value, w_out, b_out, gain_attn, w_up, b_up, w_down, b_down, gain_mlp = param_set
    row_count = stream.shape[0]
    seq_ends = jnp.cumsum(lengths)
    places = jnp.arange(row_count, dtype=jnp.int32)
    segment_of = lax.optimization_barrier(jnp.sum((places[:, None] >= seq_ends[None, :]).astype(jnp.int32), axis=1))
    allowed = (segment_of[:, None] == segment_of[None, :]) & (places[:, None] >= places[None, :])
    acts_a = low(crms_norm(stream, gain_attn))
    queries = low(low_back(matmul(acts_a, w_query) + b_query)).reshape(row_count, H, HD)
    all_keys = low(low_back(matmul(acts_a, w_key))).reshape(row_count, H, HD)
    values = low(low_back(matmul(acts_a, w_value) + b_value)).reshape(row_count, H, HD)
    raw_scores = jnp.einsum('qhd,khd->hqk', queries, all_keys, precision=lax.Precision.HIGHEST)
    scores = jnp.where(allowed[None], low_back(raw_scores) * HD ** (-0.5), -1e+30)
    attn_probs = low(jax.nn.softmax(scores, axis=2))
    mixed_heads = jnp.einsum('hqk,khd->qhd', attn_probs, values, precision=lax.Precision.HIGHEST)
    context = low(low_back(mixed_heads)).reshape(row_count, D)
    middle = compress_add(stream, low_back(matmul(context, w_out)) + b_out)
    acts_m = low(crms_norm(middle, gain_mlp))
    hidden = low_back(matmul(acts_m, w_up) + b_up)
    active = low(jax.nn.gelu(hidden, approximate=True))
    return compress_add(middle, low_back(matmul(active, w_down)) + b_down)

def reference(stream, w_query, w_key, w_value, b_query, b_value, w_out, b_out, gain_attn, w_up, b_up, w_down, b_down, gain_mlp, cotangent, lengths):
    param_set = jax.tree.map(lambda weight_arr: weight_arr.astype(jnp.float32), (w_query, w_key, w_value, b_query, b_value, w_out, b_out, gain_attn, w_up, b_up, w_down, b_down, gain_mlp))
    group_streams = stream.reshape(GROUPS, TOK_DEV, DC)
    group_grads = cotangent.reshape(GROUPS, TOK_DEV, DC)

    def scan_step(running, inputs):
        stream_group, grad_group, lengths_group = inputs
        result, pull_back = jax.vjp(lambda params_in, stream_in: apply_layer(params_in, stream_in, lengths_group), param_set, stream_group.astype(jnp.float32))
        grad_params, grad_input = pull_back(grad_group.astype(jnp.float32))
        running = jax.tree.map(jnp.add, running, grad_params)
        return (running, (result.astype(jnp.bfloat16), grad_input.astype(jnp.bfloat16)))
    initial = jax.tree.map(jnp.zeros_like, param_set)
    totals, (outputs, grad_inputs) = lax.scan(scan_step, initial, (group_streams, group_grads, lengths))
    return (outputs.reshape(TOKENS, DC), grad_inputs.reshape(TOKENS, DC), totals[0], totals[1], totals[2], totals[3], totals[4], totals[5], totals[6], totals[7], totals[8], totals[9], totals[10], totals[11], totals[12])
```

```python
import jax
import jax.numpy as jnp
from jax import lax
from jax.sharding import PartitionSpec as P

HD = 64
epsilon = 1e-05
F32 = jnp.float32
BF16 = jnp.bfloat16


def phases_of(count):
    found, stride = [], 1
    radix = 2
    while stride < count:
        rest = count // stride
        radix = 2 if stride == 1 or (rest.bit_length() - 1) % 2 == 1 else 4
        found.append((stride, radix))
        stride *= radix
    return found


def relative_order(count):
    blocks = [0]
    for stride, radix in reversed(phases_of(count)):
        blocks = [b ^ (k * stride) for k in range(radix) for b in blocks]
    return blocks


def swap(array, flip):
    count = lax.axis_size("dp")
    return lax.ppermute(array, "dp", [(i, i ^ flip) for i in range(count)])


def swap_tensor(array):
    count = lax.axis_size("tensor")
    return lax.ppermute(array, "tensor", [(i, i ^ 1) for i in range(count)])


def dot_nn(left, right):
    return lax.dot_general(left, right, (((1,), (0,)), ((), ())), preferred_element_type=F32)


def dot_nt(left, right):
    return lax.dot_general(left, right, (((1,), (1,)), ((), ())), preferred_element_type=F32)


def dot_tn(left, right):
    return lax.dot_general(left, right, (((0,), (0,)), ((), ())), preferred_element_type=F32)


def gather_outer(shard, count):
    held = shard
    for stride, radix in reversed(phases_of(count)[1:]):
        held = jnp.concatenate([held] + [swap(held, k * stride) for k in range(1, radix)], axis=0)
    return held


def reduce_phase(held, stride, radix):
    rows = held.shape[0] // radix
    total = held[:rows]
    for k in range(1, radix):
        total = total + swap(held[k * rows : (k + 1) * rows].astype(BF16), k * stride).astype(F32)
    return total


def reduce_rows(acts, grads, count):
    half = acts.shape[1] // 2
    sent = dot_tn(acts[:, half:], grads).astype(BF16)
    total = dot_tn(acts[:, :half], grads) + swap(sent, 1).astype(F32)
    for stride, radix in phases_of(count)[1:]:
        total = reduce_phase(total, stride, radix)
    return total


def reduce_all(vector, count):
    for stride, radix in phases_of(count):
        parts = [vector] + [swap(vector, k * stride) for k in range(1, radix)]
        while len(parts) > 1:
            parts = [parts[i] + parts[i + 1] for i in range(0, len(parts), 2)]
        vector = parts[0]
    return vector


def block_mask(segment_of, row_count):
    places = jnp.arange(row_count, dtype=jnp.int32)
    same_doc = segment_of[:, None] == segment_of[None, :]
    return same_doc & (places[:, None] >= places[None, :])


def body(
    stream,
    w_query,
    w_key,
    w_value,
    b_query,
    b_value,
    w_out,
    b_out,
    gain_attn,
    w_up,
    b_up,
    w_down,
    b_down,
    gain_mlp,
    cotangent,
    lengths,
):
    row_count = stream.shape[0]
    count = lax.axis_size("dp")
    me = lax.axis_index("dp")
    rank = lax.axis_index("tensor")
    shard_rows = w_query.shape[0]
    width = shard_rows * count
    half = width // 2
    own_width = w_query.shape[1]
    head_count = own_width // HD

    shard_qkv = jnp.concatenate([w_query, w_key, w_value], axis=1)
    outer_qkv = gather_outer(shard_qkv, count)
    inner_qkv = swap(outer_qkv, 1)
    shard_ou = jnp.concatenate([w_out.T, w_up], axis=1)
    shard_ou, _ = lax.optimization_barrier((shard_ou, outer_qkv))
    outer_ou = gather_outer(shard_ou, count)
    outer_out, outer_up = outer_ou[:, :own_width], outer_ou[:, own_width:]
    other_out = swap_tensor(outer_out)
    outer_out_full = jnp.where(
        rank == 0,
        jnp.concatenate([outer_out, other_out], axis=1),
        jnp.concatenate([other_out, outer_out], axis=1),
    )
    inner_out_full = swap(outer_out_full, 1)
    inner_up = swap(outer_up, 1)
    shard_down = w_down.T
    shard_down, _ = lax.optimization_barrier((shard_down, outer_ou))
    outer_down = gather_outer(shard_down, count)
    inner_down = swap(outer_down, 1)

    def own_out():
        full = jnp.concatenate([outer_out_full, inner_out_full], axis=0)
        return lax.dynamic_slice_in_dim(full, rank * own_width, own_width, 1)

    blocks = jnp.array(relative_order(count), jnp.int32)
    order = ((me ^ blocks)[:, None] * shard_rows + jnp.arange(shard_rows, dtype=jnp.int32)).reshape(-1)
    chooser = (jnp.arange(width, dtype=jnp.int32)[:, None] == order[None, :]).astype(BF16)
    last = (order == width - 1).astype(F32)[None, :]
    inside = 1.0 - last

    def pad_rows(rows):
        return jnp.pad(rows, ((0, 0), (0, width - rows.shape[1])))

    entering = dot_nn(pad_rows(stream), chooser)
    grad_top = dot_nn(pad_rows(cotangent), chooser)
    vectors = dot_nn(jnp.stack([gain_attn, gain_mlp, b_out, b_down]), chooser)
    gain_a, gain_m, bias_out, bias_down = (vectors[i : i + 1] for i in range(4))

    def expand(rows):
        return rows - jnp.sum(rows, axis=1, keepdims=True) * last

    def norm_forward(full, gain):
        inverse = lax.rsqrt(jnp.mean(full * full, axis=1, keepdims=True) + epsilon)
        normed = full * inverse
        return normed, inverse, normed * gain

    def norm_backward(grad, normed, inverse, gain):
        grad_gain = jnp.sum(grad * normed, axis=0)
        scaled = grad * gain
        full = inverse * (scaled - normed * jnp.mean(scaled * normed, axis=1, keepdims=True))
        return (full - jnp.sum(full * last, axis=1, keepdims=True)) * inside, grad_gain

    def center(rows):
        return rows - jnp.mean(rows, axis=1, keepdims=True)

    seq_ends = jnp.cumsum(lengths[0])
    places = jnp.arange(row_count, dtype=jnp.int32)
    segment_of = jnp.sum((places[:, None] >= seq_ends[None, :]).astype(jnp.int32), axis=1)
    mask = block_mask(segment_of, row_count)

    grad_bm = center(grad_top)
    grad_b_down = jnp.sum(grad_bm, axis=0)
    grad_bm_low = grad_bm.astype(BF16)

    normed_a, inverse_a, scaled_a = norm_forward(expand(entering), gain_a)
    acts_a = scaled_a.astype(BF16)
    qkv = dot_nn(acts_a[:, :half], outer_qkv) + dot_nn(acts_a[:, half:], inner_qkv)
    bias_qkv = jnp.concatenate([b_query, jnp.zeros_like(b_query), b_value]).astype(F32)
    qkv = (qkv + bias_qkv[None]).astype(BF16)
    heads = qkv.reshape(row_count, 3, head_count, HD)
    queries, all_keys, values = heads[:, 0], heads[:, 1], heads[:, 2]

    score_scale = HD ** (-0.5)
    scores = jnp.einsum("qhd,khd->hqk", queries, all_keys, preferred_element_type=F32)
    scores = jnp.where(mask[None], scores * score_scale, -1e30)
    peak = jnp.max(scores, axis=2, keepdims=True)
    exponent = jnp.exp(scores - peak)
    total = jnp.sum(exponent, axis=2, keepdims=True)
    probs_full = exponent / total
    probs = probs_full.astype(BF16)
    context = jnp.einsum("hqk,khd->qhd", probs, values, preferred_element_type=F32)
    context = context.astype(BF16).reshape(row_count, own_width)
    other_context = swap_tensor(context)
    context_full = jnp.where(
        rank == 0,
        jnp.concatenate([context, other_context], axis=1),
        jnp.concatenate([other_context, context], axis=1),
    )
    branch_a = jnp.concatenate(
        [dot_nt(context_full, outer_out_full), dot_nt(context_full, inner_out_full)], axis=1
    )
    middle = entering + center(branch_a + bias_out) * inside
    normed_m, inverse_m, scaled_m = norm_forward(expand(middle), gain_m)
    acts_m = scaled_m.astype(BF16)
    hidden = dot_nn(acts_m[:, :half], outer_up) + dot_nn(acts_m[:, half:], inner_up)
    hidden = hidden + b_up.astype(F32)[None]
    active, gelu_back = jax.vjp(lambda pre: jax.nn.gelu(pre, approximate=True), hidden)
    active = active.astype(BF16)

    grad_active = dot_nn(grad_bm_low[:, :half], outer_down) + dot_nn(grad_bm_low[:, half:], inner_down)
    grad_hidden = gelu_back(grad_active)[0].astype(BF16)
    norm_m_partial = jnp.concatenate(
        [dot_nt(grad_hidden, outer_up), dot_nt(grad_hidden, inner_up)], axis=1
    ).astype(BF16)
    grad_norm_m = norm_m_partial.astype(F32) + swap_tensor(norm_m_partial).astype(F32)

    mlp_partial = jnp.concatenate(
        [dot_nn(active, outer_down.T), dot_nn(active, inner_down.T)], axis=1
    ).astype(BF16)
    mlp_partial, _ = lax.optimization_barrier((mlp_partial, grad_norm_m))
    branch_m = mlp_partial.astype(F32) + swap_tensor(mlp_partial).astype(F32) + bias_down
    result = (middle + center(branch_m) * inside).astype(BF16)
    out_rows = dot_nt(result, chooser).astype(BF16)[:, : stream.shape[1]]

    shard_up = reduce_rows(acts_m, grad_hidden, count)
    shard_down_t = reduce_rows(grad_bm_low, active, count)
    grad_b_up = jnp.sum(grad_hidden.astype(F32), axis=0)

    grad_from_m, grad_gain_mlp = norm_backward(grad_norm_m, normed_m, inverse_m, gain_m)
    grad_middle = grad_top + grad_from_m
    grad_ba = center(grad_middle)
    grad_b_out = jnp.sum(grad_ba, axis=0)
    grad_ba_low = grad_ba.astype(BF16)
    grad_context = dot_nn(grad_ba_low, own_out()).astype(BF16).reshape(row_count, head_count, HD)
    shard_out_t = reduce_rows(grad_ba_low, context, count)

    grad_probs = jnp.einsum("qhd,khd->hqk", grad_context, values, preferred_element_type=F32)
    delta = jnp.sum(probs_full * grad_probs, axis=2, keepdims=True)
    grad_scores = (probs_full * (grad_probs - delta) * score_scale).astype(BF16)
    grad_queries = jnp.einsum("hqk,khd->qhd", grad_scores, all_keys, preferred_element_type=F32)
    grad_keys = jnp.einsum("hqk,qhd->khd", grad_scores, queries, preferred_element_type=F32)
    grad_values = jnp.einsum("hqk,qhd->khd", probs, grad_context, preferred_element_type=F32)
    grad_qkv = jnp.concatenate(
        [g.astype(BF16).reshape(row_count, own_width) for g in (grad_queries, grad_keys, grad_values)], axis=1
    )
    partial_a = jnp.concatenate([dot_nt(grad_qkv, outer_qkv), dot_nt(grad_qkv, inner_qkv)], axis=1).astype(BF16)
    grad_norm_a = partial_a.astype(F32) + swap_tensor(partial_a).astype(F32)
    shard_grad_qkv = reduce_rows(acts_a, grad_qkv, count)
    grad_from_a, grad_gain_attn = norm_backward(grad_norm_a, normed_a, inverse_a, gain_a)
    grad_stream = (grad_middle + grad_from_a).astype(BF16)
    grad_stream = dot_nt(grad_stream, chooser).astype(BF16)[:, : stream.shape[1]]

    def to_plain(rows):
        return lax.dot_general(
            rows,
            chooser.astype(F32),
            (((1,), (1,)), ((), ())),
            precision=lax.Precision.HIGHEST,
            preferred_element_type=F32,
        )

    early = to_plain(jnp.stack([grad_b_down, grad_gain_mlp, grad_b_out])).reshape(-1)
    early = reduce_all(jnp.concatenate([early, grad_b_up]), count)
    late_gain = to_plain(grad_gain_attn[None])[0]
    grad_b_qkv = jnp.sum(grad_qkv.astype(F32), axis=0)
    late = reduce_all(jnp.concatenate([late_gain, grad_b_qkv]), count)
    return (
        out_rows,
        grad_stream,
        shard_grad_qkv[:, :own_width],
        shard_grad_qkv[:, own_width : 2 * own_width],
        shard_grad_qkv[:, 2 * own_width :],
        late[width : width + own_width],
        late[width + 2 * own_width :],
        shard_out_t.T,
        early[2 * width : 3 * width],
        late[:width],
        shard_up,
        early[3 * width :],
        shard_down_t.T,
        early[:width],
        early[width : 2 * width],
    )


def solution(mesh):
    return jax.shard_map(
        body,
        mesh=mesh,
        in_specs=(
            P("dp", None),
            P("dp", "tensor"),
            P("dp", "tensor"),
            P("dp", "tensor"),
            P("tensor"),
            P("tensor"),
            P("tensor", "dp"),
            P(),
            P(),
            P("dp", "tensor"),
            P("tensor"),
            P("tensor", "dp"),
            P(),
            P(),
            P("dp", None),
            P("dp", None),
        ),
        out_specs=(
            P("dp", None),
            P("dp", None),
            P("dp", "tensor"),
            P("dp", "tensor"),
            P("dp", "tensor"),
            P("tensor"),
            P("tensor"),
            P("tensor", "dp"),
            P(),
            P(),
            P("dp", "tensor"),
            P("tensor"),
            P("tensor", "dp"),
            P(),
            P(),
        ),
        check_vma=False,
    )
```

```python
import functools

import jax
import jax.numpy as jnp
from jax import lax
from jax.experimental import pallas as pl
from jax.experimental.pallas import tpu as pltpu
from jax.sharding import PartitionSpec as P

HD = 64
PAIR = 2 * HD
STEP = 256
epsilon = 1e-05
F32 = jnp.float32
BF16 = jnp.bfloat16
VMEM = pl.BlockSpec(memory_space=pltpu.VMEM)
SMEM = pl.BlockSpec(memory_space=pltpu.SMEM)


def phases_of(count):
    found, stride = [], 1
    while stride < count:
        rest = count // stride
        radix = 2 if stride == 1 or (rest.bit_length() - 1) % 2 == 1 else 4
        found.append((stride, radix))
        stride *= radix
    return found


def relative_order(count):
    blocks = [0]
    for stride, radix in reversed(phases_of(count)):
        blocks = [b ^ (k * stride) for k in range(radix) for b in blocks]
    return blocks


def swap(array, flip):
    count = lax.axis_size("dp")
    return lax.ppermute(array, "dp", [(i, i ^ flip) for i in range(count)])


def swap_tensor(array):
    count = lax.axis_size("tensor")
    return lax.ppermute(array, "tensor", [(i, i ^ 1) for i in range(count)])


def dot_nn(left, right):
    return lax.dot_general(left, right, (((1,), (0,)), ((), ())), preferred_element_type=F32)


def dot_nt(left, right):
    return lax.dot_general(left, right, (((1,), (1,)), ((), ())), preferred_element_type=F32)


def dot_tn(left, right):
    return lax.dot_general(left, right, (((0,), (0,)), ((), ())), preferred_element_type=F32)


def shape(rows, columns, dtype):
    return jax.ShapeDtypeStruct((rows, columns), dtype)


def call(kernel, outs, args, scalars=0, scratch=(), flops=0):
    moved = sum(a.size * a.dtype.itemsize for a in args) + sum(o.size * o.dtype.itemsize for o in outs)
    return pl.pallas_call(
        kernel,
        out_shape=outs,
        in_specs=[SMEM] * scalars + [VMEM] * (len(args) - scalars),
        out_specs=[VMEM] * len(outs),
        scratch_shapes=list(scratch),
        compiler_params=pltpu.CompilerParams(vmem_limit_bytes=48 * 1024 * 1024),
        cost_estimate=pl.CostEstimate(flops=flops, bytes_accessed=moved, transcendentals=0),
    )(*args)


def chooser_of(order_ref, rows):
    place = lax.broadcasted_iota(jnp.int32, (rows, order_ref.shape[1]), 0)
    return (place == order_ref[...]).astype(F32).astype(BF16)


def last_of(order_ref):
    return (order_ref[...] == order_ref.shape[1] - 1).astype(F32)


def expand(rows, last):
    return rows - jnp.sum(rows, axis=1, keepdims=True) * last


def norm_of(full):
    inverse = lax.rsqrt(jnp.mean(full * full, axis=1, keepdims=True) + epsilon)
    return full * inverse, inverse


def norm_backward(grad, normed, inverse, gain, last):
    scaled = grad * gain
    full = inverse * (scaled - normed * jnp.mean(scaled * normed, axis=1, keepdims=True))
    return (full - jnp.sum(full * last, axis=1, keepdims=True)) * (1.0 - last)


def center(rows):
    return rows - jnp.mean(rows, axis=1, keepdims=True)


def pack_kernel(q_ref, k_ref, v_ref, out_ref):
    width = q_ref.shape[1]
    for i, ref in enumerate((q_ref, k_ref, v_ref)):
        out_ref[:, i * width : (i + 1) * width] = ref[...]


def pack_late_kernel(out_ref, up_ref, down_ref, ou_ref, dn_ref):
    rows = up_ref.shape[0]
    r = lax.broadcasted_iota(jnp.int32, (rows, rows), 0)
    c = lax.broadcasted_iota(jnp.int32, (rows, rows), 1)
    unit = (r == c).astype(F32).astype(BF16)
    own = out_ref.shape[0]
    ou_ref[:, :own] = dot_nt(unit, out_ref[...]).astype(BF16)
    ou_ref[:, own:] = up_ref[...]
    dn_ref[...] = dot_nt(unit, down_ref[...]).astype(BF16)


def first_kernel(order_ref, stream_ref, cot_ref, vec_ref, ent_ref, top_ref, acts_ref, gbm_ref, row_ref):
    chooser = chooser_of(order_ref, order_ref.shape[1])
    last = last_of(order_ref)
    rows = dot_nn(vec_ref[...], chooser)
    inner = stream_ref.shape[1]
    entering = dot_nn(stream_ref[...], chooser[:inner])
    ent_ref[...] = entering.astype(BF16)
    normed, _ = norm_of(expand(entering, last))
    acts_ref[...] = (normed * rows[0:1]).astype(BF16)
    top = dot_nn(cot_ref[...], chooser[:inner])
    top_ref[...] = top.astype(BF16)
    gbm = center(top)
    gbm_ref[...] = gbm.astype(BF16)
    row_ref[:4, :] = rows[:4]
    row_ref[4:5, :] = jnp.sum(gbm, axis=0, keepdims=True)
    row_ref[5:, :] = jnp.zeros((row_ref.shape[0] - 5, row_ref.shape[1]), F32)


def row_blocks(rows):
    return [(i, min(rows, i + STEP)) for i in range(0, rows, STEP)]


def write_mask(len_ref, mask_ref):
    for lo, hi in row_blocks(mask_ref.shape[0]):
        place = lax.broadcasted_iota(jnp.int32, (1, hi - lo), 1) + lo
        first = jnp.zeros_like(place)
        end = jnp.int32(0)
        for j in range(len_ref.shape[1] - 1):
            end = end + len_ref[0, j]
            first = jnp.where(place >= end, end, first)
        key = lax.broadcasted_iota(jnp.int32, (hi, hi - lo), 0)
        mask_ref[:hi, lo:hi] = jnp.where((key >= first) & (key <= place), 0.0, -1e30)


def head_lanes(head, dims):
    lane = lax.broadcasted_iota(jnp.int32, dims, 1)
    return (lane < HD) if head == 0 else (lane >= HD)


def unit_of(size):
    r = lax.broadcasted_iota(jnp.int32, (size, size), 0)
    c = lax.broadcasted_iota(jnp.int32, (size, size), 1)
    return (r == c).astype(F32).astype(BF16)


def attend_kernel(len_ref, acts_ref, w0_ref, w1_ref, bias_ref, qkv_ref, ctx_ref, lse_ref, mask_ref):
    rows, own = ctx_ref.shape
    half = acts_ref.shape[1] // 2
    write_mask(len_ref, mask_ref)
    full = dot_nn(acts_ref[:, :half], w0_ref[...]) + dot_nn(acts_ref[:, half:], w1_ref[...]) + bias_ref[...]
    qkv_ref[...] = full.astype(BF16)
    unit = unit_of(PAIR)
    scale = jnp.asarray(HD**-0.5, BF16)
    for pair in range(own // PAIR):
        at = pair * PAIR
        keys = qkv_ref[:, own + at : own + at + PAIR]
        values_t = dot_nt(unit, qkv_ref[:, 2 * own + at : 2 * own + at + PAIR]).astype(BF16)
        for lo, hi in row_blocks(rows):
            block = qkv_ref[lo:hi, at : at + PAIR] * scale
            parts = []
            for head in range(2):
                own_q = jnp.where(head_lanes(head, block.shape), block, jnp.zeros_like(block))
                scores = dot_nt(keys[:hi], own_q) + mask_ref[:hi, lo:hi]
                peak = jnp.max(scores, axis=0, keepdims=True)
                expo = jnp.exp(scores - peak)
                total = jnp.sum(expo, axis=0, keepdims=True)
                probs = (expo * (1.0 / total)).astype(BF16)
                parts.append(dot_nn(values_t[:, :hi], probs))
                lse_ref[2 * pair + head : 2 * pair + head + 1, lo:hi] = peak + jnp.log(total)
            row = lax.broadcasted_iota(jnp.int32, parts[0].shape, 0)
            ctx_ref[lo:hi, at : at + PAIR] = jnp.where(row < HD, parts[0], parts[1]).T.astype(BF16)


def middle_kernel(
    rank_ref, order_ref, row_ref, bup_ref, own_ref, other_ref, o00, o01, o10, o11, u0, u1, d0, d1, ent_ref, gbm_ref,
    mid_ref, acts_ref, active_ref, ghid_ref, gn_ref, gbup_ref,
):
    zero = rank_ref[0, 0] == 0
    half = u0.shape[0]
    last = last_of(order_ref)

    def ordered(a, b):
        a, b = a[...], b[...]
        return jnp.where(zero, a, b), jnp.where(zero, b, a)

    first, second = ordered(own_ref, other_ref)
    halves = []
    for a, b in ((o00, o01), (o10, o11)):
        wa, wb = ordered(a, b)
        halves.append(dot_nt(first, wa) + dot_nt(second, wb))
    branch = jnp.concatenate(halves, axis=1) + row_ref[2:3]
    middle = ent_ref[...].astype(F32) + center(branch) * (1.0 - last)
    mid_ref[...] = middle
    normed, _ = norm_of(expand(middle, last))
    acts = (normed * row_ref[1:2]).astype(BF16)
    acts_ref[...] = acts
    units = u0.shape[1]
    piece = units // 3
    g0 = g1 = None
    for at in range(0, units, piece):
        cut = slice(at, at + piece)
        hidden = dot_nn(acts[:, :half], u0[:, cut]) + dot_nn(acts[:, half:], u1[:, cut]) + bup_ref[:, cut]
        gact = dot_nn(gbm_ref[:, :half], d0[:, cut]) + dot_nn(gbm_ref[:, half:], d1[:, cut])
        square = hidden * hidden
        bend = jnp.tanh(hidden * (0.7978845608028654 + 0.7978845608028654 * 0.044715 * square))
        up = 0.5 + 0.5 * bend
        active_ref[:, cut] = (hidden * up).astype(BF16)
        slope = up + (0.5 * hidden) * (1.0 - bend * bend) * (
            0.7978845608028654 + 0.7978845608028654 * 3 * 0.044715 * square
        )
        ghid = (gact * slope).astype(BF16)
        ghid_ref[:, cut] = ghid
        gbup_ref[:, cut] = jnp.sum(ghid.astype(F32), axis=0, keepdims=True)
        a0, a1 = dot_nt(ghid, u0[:, cut]), dot_nt(ghid, u1[:, cut])
        g0, g1 = (a0, a1) if g0 is None else (g0 + a0, g1 + a1)
    gn_ref[:, :half] = g0.astype(BF16)
    gn_ref[:, half:] = g1.astype(BF16)


def back_kernel(order_ref, row_ref, own_ref, other_ref, mid_ref, top_ref, o0, o1, gmid_ref, gba_ref, gctx_ref, sum_ref):
    last = last_of(order_ref)
    half = o0.shape[0]
    grad = own_ref[...].astype(F32) + other_ref[...].astype(F32)
    normed, inverse = norm_of(expand(mid_ref[...], last))
    gmid = top_ref[...].astype(F32) + norm_backward(grad, normed, inverse, row_ref[1:2], last)
    gmid_ref[...] = gmid
    gba = center(gmid)
    low = gba.astype(BF16)
    gba_ref[...] = low
    gctx_ref[...] = (dot_nn(low[:, :half], o0[...]) + dot_nn(low[:, half:], o1[...])).astype(BF16)
    sum_ref[0:1, :] = jnp.sum(grad * normed, axis=0, keepdims=True)
    sum_ref[1:2, :] = jnp.sum(gba, axis=0, keepdims=True)
    sum_ref[2:, :] = jnp.zeros((sum_ref.shape[0] - 2, sum_ref.shape[1]), F32)


def attend_back_kernel(
    len_ref, qkv_ref, lse_ref, gctx_ref, w0_ref, w1_ref, ent_ref, order_ref, out_ref, part_ref, sum_ref, bias_ref,
    mask_ref, gk_ref, gv_ref,
):
    rows, own = gctx_ref.shape
    write_mask(len_ref, mask_ref)
    unit = unit_of(PAIR)
    scale = jnp.asarray(HD**-0.5, BF16)
    for pair in range(own // PAIR):
        at = pair * PAIR
        keys = qkv_ref[:, own + at : own + at + PAIR]
        values = qkv_ref[:, 2 * own + at : 2 * own + at + PAIR]
        keys_t = dot_nt(unit, keys * scale).astype(BF16)
        for lo, hi in reversed(row_blocks(rows)):
            block = qkv_ref[lo:hi, at : at + PAIR] * scale
            gblock = gctx_ref[lo:hi, at : at + PAIR]
            parts, gk, gv = [], None, None
            for head in range(2):
                pick = head_lanes(head, block.shape)
                own_q = jnp.where(pick, block, jnp.zeros_like(block))
                own_g = jnp.where(pick, gblock, jnp.zeros_like(block))
                lse = lse_ref[2 * pair + head : 2 * pair + head + 1, lo:hi]
                probs = jnp.exp(dot_nt(keys[:hi], own_q) + mask_ref[:hi, lo:hi] - lse)
                gprobs = dot_nt(values[:hi], own_g)
                delta = jnp.sum(probs * gprobs, axis=0, keepdims=True)
                gscores = (probs * (gprobs - delta)).astype(BF16)
                parts.append(dot_nn(keys_t[:, :hi], gscores))
                k1 = dot_nn(gscores, own_q)
                v1 = dot_nn(probs.astype(BF16), own_g)
                gk = k1 if gk is None else gk + k1
                gv = v1 if gv is None else gv + v1
            row = lax.broadcasted_iota(jnp.int32, parts[0].shape, 0)
            out_ref[lo:hi, at : at + PAIR] = jnp.where(row < HD, parts[0], parts[1]).T.astype(BF16)
            if hi == rows:
                gk_ref[...] = gk
                gv_ref[...] = gv
            else:
                gk_ref[:hi, :] += gk
                gv_ref[:hi, :] += gv
        out_ref[:, own + at : own + at + PAIR] = gk_ref[...].astype(BF16)
        out_ref[:, 2 * own + at : 2 * own + at + PAIR] = gv_ref[...].astype(BF16)
    half = w0_ref.shape[0]
    grads = out_ref[...]
    partial = jnp.concatenate([dot_nt(grads, w0_ref[...]), dot_nt(grads, w1_ref[...])], axis=1)
    low = partial.astype(BF16)
    part_ref[...] = low
    normed, _ = norm_of(expand(ent_ref[...].astype(F32), last_of(order_ref)))
    sum_ref[...] = jnp.broadcast_to(jnp.sum(low.astype(F32) * normed, axis=0, keepdims=True), sum_ref.shape)
    bias_ref[...] = jnp.sum(grads.astype(F32), axis=0, keepdims=True)


def vector_kernel(order_ref, row_ref, sum_ref, gain_ref, gbup_ref, bias_ref, out_ref):
    width = order_ref.shape[1]
    chooser = chooser_of(order_ref, width)
    rows = jnp.concatenate([row_ref[4:5], sum_ref[0:1], sum_ref[1:2], gain_ref[0:1], jnp.zeros((4, width), F32)], axis=0)
    plain = jnp.zeros_like(rows)
    for _ in range(3):
        low = rows.astype(BF16)
        plain = plain + dot_nt(low, chooser)
        rows = rows - low.astype(F32)
    own = width // 2
    out_ref[0:4, :] = plain[0:4]
    out_ref[4:5, :] = gbup_ref[:, :width]
    out_ref[5:6, :] = gbup_ref[:, width:]
    out_ref[6:7, :own] = bias_ref[:, :own]
    out_ref[6:7, own:] = bias_ref[:, 2 * own :]
    out_ref[7:8, :] = jnp.zeros((1, width), F32)


def result_kernel(order_ref, row_ref, mid_ref, own_ref, other_ref, out_ref):
    last = last_of(order_ref)
    branch = own_ref[...].astype(F32) + other_ref[...].astype(F32) + row_ref[3:4]
    result = (mid_ref[...] + center(branch) * (1.0 - last)).astype(BF16)
    plain = dot_nt(result, chooser_of(order_ref, order_ref.shape[1]))
    out_ref[...] = plain[:, : out_ref.shape[1]].astype(BF16)


def final_kernel(order_ref, row_ref, own_ref, other_ref, ent_ref, gmid_ref, out_ref):
    last = last_of(order_ref)
    grad = own_ref[...].astype(F32) + other_ref[...].astype(F32)
    normed, inverse = norm_of(expand(ent_ref[...].astype(F32), last))
    grad = (gmid_ref[...] + norm_backward(grad, normed, inverse, row_ref[0:1], last)).astype(BF16)
    plain = dot_nt(grad, chooser_of(order_ref, order_ref.shape[1]))
    out_ref[...] = plain[:, : out_ref.shape[1]].astype(BF16)


def gather_outer(shard, count):
    held = shard
    for stride, radix in reversed(phases_of(count)[1:]):
        held = jnp.concatenate([held] + [swap(held, k * stride) for k in range(1, radix)], axis=0)
    return held


class Sum:
    def __init__(self, acts, grads, count):
        self.acts, self.grads, self.phases = acts, grads, phases_of(count)
        half = acts.shape[1] // 2
        self.got = swap(dot_tn(acts[:, half:], grads).astype(BF16), 1)
        self.total = None

    def step(self):
        radix = self.phases[1][1] if len(self.phases) > 1 else 1
        stride = self.phases[1][0] if len(self.phases) > 1 else 0
        if self.total is None:
            whole = self.got.shape[0]
            rows = whole // radix
            parts = []
            for k in range(radix):
                part = dot_tn(self.acts[:, k * rows : (k + 1) * rows], self.grads)
                parts.append(part + self.got[k * rows : (k + 1) * rows].astype(F32))
        else:
            whole = self.total
            for piece in self.got:
                whole = whole + piece.astype(F32)
            rows = whole.shape[0] // radix
            parts = [whole[k * rows : (k + 1) * rows] for k in range(radix)]
        self.total = parts[0]
        self.got = [swap(parts[k].astype(BF16), k * stride) for k in range(1, radix)]
        self.phases = self.phases[1:]
        return self

    def end(self):
        while len(self.phases) > 1:
            self.step()
        total = self.total
        for piece in self.got:
            total = total + piece.astype(F32)
        return total


def reduce_all(vector, count):
    for stride, radix in phases_of(count):
        parts = [vector] + [swap(vector, k * stride) for k in range(1, radix)]
        while len(parts) > 1:
            parts = [parts[i] + parts[i + 1] for i in range(0, len(parts), 2)]
        vector = parts[0]
    return vector


def body(
    stream,
    w_query,
    w_key,
    w_value,
    b_query,
    b_value,
    w_out,
    b_out,
    gain_attn,
    w_up,
    b_up,
    w_down,
    b_down,
    gain_mlp,
    cotangent,
    lengths,
):
    rows, inner_width = stream.shape
    count = lax.axis_size("dp")
    me = lax.axis_index("dp")
    rank = lax.axis_index("tensor").astype(jnp.int32).reshape(1, 1)
    shard_rows, own = w_query.shape
    width = shard_rows * count
    units = w_up.shape[1]
    matmul = 2 * rows * width * units

    (shard_qkv,) = call(pack_kernel, [shape(shard_rows, 3 * own, BF16)], [w_query, w_key, w_value])
    qkv0 = gather_outer(shard_qkv, count)
    qkv1 = swap(qkv0, 1)
    w_out, w_up, w_down, _ = lax.optimization_barrier((w_out, w_up, w_down, shard_qkv))
    shard_ou, shard_dn = call(
        pack_late_kernel, [shape(shard_rows, own + units, BF16), shape(shard_rows, units, BF16)], [w_out, w_up, w_down]
    )
    shard_ou, _ = lax.optimization_barrier((shard_ou, qkv0))
    ou0 = gather_outer(shard_ou, count)
    o00, u0 = ou0[:, :own], ou0[:, own:]
    o01 = swap_tensor(o00)
    o10, o11 = swap(o00, 1), swap(o01, 1)
    u1 = swap(u0, 1)
    shard_dn, _ = lax.optimization_barrier((shard_dn, ou0))
    d0 = gather_outer(shard_dn, count)
    d1 = swap(d0, 1)

    blocks = jnp.array(relative_order(count), jnp.int32)
    order = ((me ^ blocks)[:, None] * shard_rows + jnp.arange(shard_rows, dtype=jnp.int32)).reshape(1, -1)
    vectors = jnp.stack([gain_attn, gain_mlp, b_out, b_down] + [jnp.zeros_like(b_out)] * 12)
    ent, top, acts_a, gbm, row = call(
        first_kernel,
        [shape(rows, width, BF16)] * 4 + [shape(8, width, F32)],
        [order, stream, cotangent, vectors],
    )

    bias_qkv = jnp.concatenate([b_query, jnp.zeros_like(b_query), b_value]).astype(F32)[None]
    qkv, context, lse = call(
        attend_kernel,
        [shape(rows, 3 * own, BF16), shape(rows, own, BF16), shape(8, rows, F32)],
        [lengths, acts_a, qkv0, qkv1, bias_qkv],
        scalars=1,
        scratch=[pltpu.VMEM((rows, rows), F32)],
        flops=matmul * 4,
    )
    other_context = swap_tensor(context)
    middle, acts_m, active, ghid, gn, gbup = call(
        middle_kernel,
        [
            shape(rows, width, F32),
            shape(rows, width, BF16),
            shape(rows, units, BF16),
            shape(rows, units, BF16),
            shape(rows, width, BF16),
            shape(1, units, F32),
        ],
        [rank, order, row, b_up.astype(F32)[None], context, other_context, o00, o01, o10, o11, u0, u1, d0, d1, ent, gbm],
        scalars=1,
        flops=matmul * 4,
    )
    gn_other = swap_tensor(gn)

    sum_up = Sum(acts_m, ghid, count)
    sum_dn = Sum(gbm, active, count)
    sum_up.step()
    sum_dn.step()
    mlp = jnp.concatenate([dot_nt(active, d0), dot_nt(active, d1)], axis=1).astype(BF16)
    mlp, _ = lax.optimization_barrier((mlp, gn_other))
    mlp_other = swap_tensor(mlp)

    gmid, gba, gctx, sums = call(
        back_kernel,
        [shape(rows, width, F32), shape(rows, width, BF16), shape(rows, own, BF16), shape(8, width, F32)],
        [order, row, gn, gn_other, middle, top, o00, o10],
        flops=matmul // 4,
    )
    sum_out = Sum(gba, context, count)
    gqkv, part, gain, gbias = call(
        attend_back_kernel,
        [shape(rows, 3 * own, BF16), shape(rows, width, BF16), shape(8, width, F32), shape(1, 3 * own, F32)],
        [lengths, qkv, lse, gctx, qkv0, qkv1, ent, order],
        scalars=1,
        scratch=[pltpu.VMEM((rows, rows), F32), pltpu.VMEM((rows, PAIR), F32), pltpu.VMEM((rows, PAIR), F32)],
        flops=matmul * 4,
    )
    part_other = swap_tensor(part)
    (out_rows,) = call(
        result_kernel, [shape(rows, inner_width, BF16)], [order, row, middle, mlp, mlp_other], flops=matmul // 2
    )
    sum_qkv = Sum(acts_a, gqkv, count)
    (grad_stream,) = call(
        final_kernel, [shape(rows, inner_width, BF16)], [order, row, part, part_other, ent, gmid], flops=matmul // 2
    )
    (plain,) = call(vector_kernel, [shape(8, width, F32)], [order, row, sums, gain, gbup, gbias])
    plain_other = swap_tensor(plain)
    plain = reduce_all(jnp.where(jnp.arange(8)[:, None] == 3, plain + plain_other, plain), count)

    shard_gqkv = sum_qkv.end()
    return (
        out_rows,
        grad_stream,
        shard_gqkv[:, :own],
        shard_gqkv[:, own : 2 * own],
        shard_gqkv[:, 2 * own :],
        plain[6, :own],
        plain[6, own:],
        sum_out.end().T,
        plain[2],
        plain[3],
        sum_up.end(),
        plain[4:6].reshape(-1),
        sum_dn.end().T,
        plain[0],
        plain[1],
    )


def solution(mesh):
    return jax.shard_map(
        body,
        mesh=mesh,
        in_specs=(
            P("dp", None),
            P("dp", "tensor"),
            P("dp", "tensor"),
            P("dp", "tensor"),
            P("tensor"),
            P("tensor"),
            P("tensor", "dp"),
            P(),
            P(),
            P("dp", "tensor"),
            P("tensor"),
            P("tensor", "dp"),
            P(),
            P(),
            P("dp", None),
            P("dp", None),
        ),
        out_specs=(
            P("dp", None),
            P("dp", None),
            P("dp", "tensor"),
            P("dp", "tensor"),
            P("dp", "tensor"),
            P("tensor"),
            P("tensor"),
            P("tensor", "dp"),
            P(),
            P(),
            P("dp", "tensor"),
            P("tensor"),
            P("tensor", "dp"),
            P(),
            P(),
        ),
        check_vma=False,
    )
```

```python
import functools

import jax
import jax.numpy as jnp
from jax import lax
from jax.experimental import pallas as pl
from jax.experimental.pallas import tpu as pltpu
from jax.sharding import PartitionSpec as P

HD = 64
PAIR = 2 * HD
STEP = 256
epsilon = 1e-05
F32 = jnp.float32
BF16 = jnp.bfloat16
VMEM = pl.BlockSpec(memory_space=pltpu.VMEM)
SMEM = pl.BlockSpec(memory_space=pltpu.SMEM)


def phases_of(count):
    found, stride = [], 1
    while stride < count:
        rest = count // stride
        radix = 2 if stride == 1 or (rest.bit_length() - 1) % 2 == 1 else 4
        found.append((stride, radix))
        stride *= radix
    return found


def relative_order(count):
    blocks = [0]
    for stride, radix in reversed(phases_of(count)):
        blocks = [b ^ (k * stride) for k in range(radix) for b in blocks]
    return blocks


def swap(array, flip):
    count = lax.axis_size("dp")
    return lax.ppermute(array, "dp", [(i, i ^ flip) for i in range(count)])


def swap_tensor(array):
    count = lax.axis_size("tensor")
    return lax.ppermute(array, "tensor", [(i, i ^ 1) for i in range(count)])


def dot_nn(left, right):
    return lax.dot_general(left, right, (((1,), (0,)), ((), ())), preferred_element_type=F32)


def dot_nt(left, right):
    return lax.dot_general(left, right, (((1,), (1,)), ((), ())), preferred_element_type=F32)


def dot_tn(left, right):
    return lax.dot_general(left, right, (((0,), (0,)), ((), ())), preferred_element_type=F32)


def shape(rows, columns, dtype):
    return jax.ShapeDtypeStruct((rows, columns), dtype)


def after(array, *others):
    return lax.optimization_barrier((array,) + others)[0]


def call(kernel, outs, args, scalars=0, scratch=(), flops=0, room=16):
    moved = sum(a.size * a.dtype.itemsize for a in args) + sum(o.size * o.dtype.itemsize for o in outs)
    return pl.pallas_call(
        kernel,
        out_shape=outs,
        in_specs=[SMEM] * scalars + [VMEM] * (len(args) - scalars),
        out_specs=[VMEM] * len(outs),
        scratch_shapes=list(scratch),
        compiler_params=pltpu.CompilerParams(vmem_limit_bytes=room * 1024 * 1024),
        cost_estimate=pl.CostEstimate(flops=flops, bytes_accessed=moved, transcendentals=0),
    )(*args)


def chooser_of(order_ref, rows):
    place = lax.broadcasted_iota(jnp.int32, (rows, order_ref.shape[1]), 0)
    return (place == order_ref[...]).astype(F32).astype(BF16)


def last_of(order_ref):
    return (order_ref[...] == order_ref.shape[1] - 1).astype(F32)


def expand(rows, last):
    return rows - jnp.sum(rows, axis=1, keepdims=True) * last


def norm_of(full):
    inverse = lax.rsqrt(jnp.mean(full * full, axis=1, keepdims=True) + epsilon)
    return full * inverse, inverse


def norm_backward(grad, normed, inverse, gain, last):
    scaled = grad * gain
    full = inverse * (scaled - normed * jnp.mean(scaled * normed, axis=1, keepdims=True))
    return (full - jnp.sum(full * last, axis=1, keepdims=True)) * (1.0 - last)


def center(rows):
    return rows - jnp.mean(rows, axis=1, keepdims=True)


def pack_kernel(q_ref, k_ref, v_ref, out_ref):
    width = q_ref.shape[1]
    for i, ref in enumerate((q_ref, k_ref, v_ref)):
        out_ref[:, i * width : (i + 1) * width] = ref[...]


def pack_late_kernel(out_ref, up_ref, down_ref, ou_ref, dn_ref):
    rows = up_ref.shape[0]
    r = lax.broadcasted_iota(jnp.int32, (rows, rows), 0)
    c = lax.broadcasted_iota(jnp.int32, (rows, rows), 1)
    unit = (r == c).astype(F32).astype(BF16)
    own = out_ref.shape[0]
    ou_ref[:, :own] = dot_nt(unit, out_ref[...]).astype(BF16)
    ou_ref[:, own:] = up_ref[...]
    dn_ref[...] = dot_nt(unit, down_ref[...]).astype(BF16)


def first_kernel(order_ref, stream_ref, cot_ref, vec_ref, ent_ref, top_ref, acts_ref, gbm_ref, row_ref):
    chooser = chooser_of(order_ref, order_ref.shape[1])
    last = last_of(order_ref)
    rows = dot_nn(vec_ref[...], chooser)
    inner = stream_ref.shape[1]
    entering = dot_nn(stream_ref[...], chooser[:inner])
    ent_ref[...] = entering.astype(BF16)
    normed, _ = norm_of(expand(entering, last))
    acts_ref[...] = (normed * rows[0:1]).astype(BF16)
    top = dot_nn(cot_ref[...], chooser[:inner])
    top_ref[...] = top.astype(BF16)
    gbm = center(top)
    gbm_ref[...] = gbm.astype(BF16)
    row_ref[:4, :] = rows[:4]
    row_ref[4:5, :] = jnp.sum(gbm, axis=0, keepdims=True)
    row_ref[5:, :] = jnp.zeros((row_ref.shape[0] - 5, row_ref.shape[1]), F32)


def row_blocks(rows):
    return [(i, min(rows, i + STEP)) for i in range(0, rows, STEP)]


def write_mask(len_ref, mask_ref):
    for lo, hi in row_blocks(mask_ref.shape[0]):
        place = lax.broadcasted_iota(jnp.int32, (1, hi - lo), 1) + lo
        first = jnp.zeros_like(place)
        end = jnp.int32(0)
        for j in range(len_ref.shape[1] - 1):
            end = end + len_ref[0, j]
            first = jnp.where(place >= end, end, first)
        key = lax.broadcasted_iota(jnp.int32, (hi, hi - lo), 0)
        mask_ref[:hi, lo:hi] = jnp.where((key >= first) & (key <= place), 0.0, -1e30)


def head_lanes(head, dims):
    lane = lax.broadcasted_iota(jnp.int32, dims, 1)
    return (lane < HD) if head == 0 else (lane >= HD)


def unit_of(size):
    r = lax.broadcasted_iota(jnp.int32, (size, size), 0)
    c = lax.broadcasted_iota(jnp.int32, (size, size), 1)
    return (r == c).astype(F32).astype(BF16)


def attend_kernel(len_ref, acts_ref, w0_ref, w1_ref, bias_ref, qkv_ref, ctx_ref, lse_ref, mask_ref):
    rows, own = ctx_ref.shape
    half = acts_ref.shape[1] // 2
    write_mask(len_ref, mask_ref)
    full = dot_nn(acts_ref[:, :half], w0_ref[...]) + dot_nn(acts_ref[:, half:], w1_ref[...]) + bias_ref[...]
    qkv_ref[...] = full.astype(BF16)
    unit = unit_of(PAIR)
    scale = jnp.asarray(HD**-0.5, BF16)
    for pair in range(own // PAIR):
        at = pair * PAIR
        keys = qkv_ref[:, own + at : own + at + PAIR]
        values_t = dot_nt(unit, qkv_ref[:, 2 * own + at : 2 * own + at + PAIR]).astype(BF16)
        for lo, hi in row_blocks(rows):
            block = qkv_ref[lo:hi, at : at + PAIR] * scale
            parts = []
            for head in range(2):
                own_q = jnp.where(head_lanes(head, block.shape), block, jnp.zeros_like(block))
                scores = dot_nt(keys[:hi], own_q) + mask_ref[:hi, lo:hi]
                peak = jnp.max(scores, axis=0, keepdims=True)
                expo = jnp.exp(scores - peak)
                total = jnp.sum(expo, axis=0, keepdims=True)
                probs = (expo * (1.0 / total)).astype(BF16)
                parts.append(dot_nn(values_t[:, :hi], probs))
                lse_ref[2 * pair + head : 2 * pair + head + 1, lo:hi] = peak + jnp.log(total)
            row = lax.broadcasted_iota(jnp.int32, parts[0].shape, 0)
            ctx_ref[lo:hi, at : at + PAIR] = jnp.where(row < HD, parts[0], parts[1]).T.astype(BF16)


def middle_kernel(
    rank_ref, order_ref, row_ref, bup_ref, own_ref, other_ref, o00, o01, o10, o11, u0, u1, ent_ref,
    mid_ref, acts_ref, active_ref, slope_ref,
):
    zero = rank_ref[0, 0] == 0
    half = u0.shape[0]
    last = last_of(order_ref)

    def ordered(a, b):
        a, b = a[...], b[...]
        return jnp.where(zero, a, b), jnp.where(zero, b, a)

    first, second = ordered(own_ref, other_ref)
    halves = []
    for a, b in ((o00, o01), (o10, o11)):
        wa, wb = ordered(a, b)
        halves.append(dot_nt(first, wa) + dot_nt(second, wb))
    branch = jnp.concatenate(halves, axis=1) + row_ref[2:3]
    middle = ent_ref[...].astype(F32) + center(branch) * (1.0 - last)
    mid_ref[...] = middle
    normed, _ = norm_of(expand(middle, last))
    acts = (normed * row_ref[1:2]).astype(BF16)
    acts_ref[...] = acts
    units = u0.shape[1]
    piece = units // 3
    for at in range(0, units, piece):
        cut = slice(at, at + piece)
        hidden = dot_nn(acts[:, :half], u0[:, cut]) + dot_nn(acts[:, half:], u1[:, cut]) + bup_ref[:, cut]
        square = hidden * hidden
        bend = jnp.tanh(hidden * (0.7978845608028654 + 0.7978845608028654 * 0.044715 * square))
        up = 0.5 + 0.5 * bend
        active_ref[:, cut] = (hidden * up).astype(BF16)
        slope_ref[:, cut] = up + (0.5 * hidden) * (1.0 - bend * bend) * (
            0.7978845608028654 + 0.7978845608028654 * 3 * 0.044715 * square
        )


def turn_kernel(gbm_ref, slope_ref, d0, d1, u0, u1, ghid_ref, gn_ref, gbup_ref):
    half, units = u0.shape
    piece = units // 3
    g0 = g1 = None
    for at in range(0, units, piece):
        cut = slice(at, at + piece)
        gact = dot_nn(gbm_ref[:, :half], d0[:, cut]) + dot_nn(gbm_ref[:, half:], d1[:, cut])
        ghid = (gact * slope_ref[:, cut]).astype(BF16)
        ghid_ref[:, cut] = ghid
        gbup_ref[:, cut] = jnp.sum(ghid.astype(F32), axis=0, keepdims=True)
        a0, a1 = dot_nt(ghid, u0[:, cut]), dot_nt(ghid, u1[:, cut])
        g0, g1 = (a0, a1) if g0 is None else (g0 + a0, g1 + a1)
    gn_ref[:, :half] = g0.astype(BF16)
    gn_ref[:, half:] = g1.astype(BF16)


def back_kernel(order_ref, row_ref, own_ref, other_ref, mid_ref, top_ref, o0, o1, gmid_ref, gba_ref, gctx_ref, sum_ref):
    last = last_of(order_ref)
    half = o0.shape[0]
    grad = own_ref[...].astype(F32) + other_ref[...].astype(F32)
    normed, inverse = norm_of(expand(mid_ref[...], last))
    gmid = top_ref[...].astype(F32) + norm_backward(grad, normed, inverse, row_ref[1:2], last)
    gmid_ref[...] = gmid
    gba = center(gmid)
    low = gba.astype(BF16)
    gba_ref[...] = low
    gctx_ref[...] = (dot_nn(low[:, :half], o0[...]) + dot_nn(low[:, half:], o1[...])).astype(BF16)
    sum_ref[0:1, :] = jnp.sum(grad * normed, axis=0, keepdims=True)
    sum_ref[1:2, :] = jnp.sum(gba, axis=0, keepdims=True)
    sum_ref[2:, :] = jnp.zeros((sum_ref.shape[0] - 2, sum_ref.shape[1]), F32)


def attend_back_kernel(
    len_ref, qkv_ref, lse_ref, gctx_ref, out_ref, mask_ref, gk_ref, gv_ref
):
    rows, own = gctx_ref.shape
    write_mask(len_ref, mask_ref)
    unit = unit_of(PAIR)
    scale = jnp.asarray(HD**-0.5, BF16)
    for pair in range(own // PAIR):
        at = pair * PAIR
        keys = qkv_ref[:, own + at : own + at + PAIR]
        values = qkv_ref[:, 2 * own + at : 2 * own + at + PAIR]
        keys_t = dot_nt(unit, keys * scale).astype(BF16)
        for lo, hi in reversed(row_blocks(rows)):
            block = qkv_ref[lo:hi, at : at + PAIR] * scale
            gblock = gctx_ref[lo:hi, at : at + PAIR]
            parts, gk, gv = [], None, None
            for head in range(2):
                pick = head_lanes(head, block.shape)
                own_q = jnp.where(pick, block, jnp.zeros_like(block))
                own_g = jnp.where(pick, gblock, jnp.zeros_like(block))
                lse = lse_ref[2 * pair + head : 2 * pair + head + 1, lo:hi]
                probs = jnp.exp(dot_nt(keys[:hi], own_q) + mask_ref[:hi, lo:hi] - lse)
                gprobs = dot_nt(values[:hi], own_g)
                delta = jnp.sum(probs * gprobs, axis=0, keepdims=True)
                gscores = (probs * (gprobs - delta)).astype(BF16)
                parts.append(dot_nn(keys_t[:, :hi], gscores))
                k1 = dot_nn(gscores, own_q)
                v1 = dot_nn(probs.astype(BF16), own_g)
                gk = k1 if gk is None else gk + k1
                gv = v1 if gv is None else gv + v1
            row = lax.broadcasted_iota(jnp.int32, parts[0].shape, 0)
            out_ref[lo:hi, at : at + PAIR] = jnp.where(row < HD, parts[0], parts[1]).T.astype(BF16)
            if hi == rows:
                gk_ref[...] = gk
                gv_ref[...] = gv
            else:
                gk_ref[:hi, :] += gk
                gv_ref[:hi, :] += gv
        out_ref[:, own + at : own + at + PAIR] = gk_ref[...].astype(BF16)
        out_ref[:, 2 * own + at : 2 * own + at + PAIR] = gv_ref[...].astype(BF16)


def part_kernel(gqkv_ref, w0_ref, w1_ref, ent_ref, order_ref, part_ref, sum_ref, bias_ref):
    half = w0_ref.shape[0]
    grads = gqkv_ref[...]
    part_ref[:, :half] = dot_nt(grads, w0_ref[...]).astype(BF16)
    part_ref[:, half:] = dot_nt(grads, w1_ref[...]).astype(BF16)
    normed, _ = norm_of(expand(ent_ref[...].astype(F32), last_of(order_ref)))
    total = jnp.sum(part_ref[...].astype(F32) * normed, axis=0, keepdims=True)
    sum_ref[...] = jnp.broadcast_to(total, sum_ref.shape)
    bias_ref[...] = jnp.sum(grads.astype(F32), axis=0, keepdims=True)


def vector_kernel(order_ref, row_ref, sum_ref, gain_ref, gbup_ref, bias_ref, out_ref):
    width = order_ref.shape[1]
    chooser = chooser_of(order_ref, width)
    rows = jnp.concatenate([row_ref[4:5], sum_ref[0:1], sum_ref[1:2], gain_ref[0:1], jnp.zeros((4, width), F32)], axis=0)
    plain = jnp.zeros_like(rows)
    for _ in range(3):
        low = rows.astype(BF16)
        plain = plain + dot_nt(low, chooser)
        rows = rows - low.astype(F32)
    own = width // 2
    out_ref[0:4, :] = plain[0:4]
    out_ref[4:5, :] = gbup_ref[:, :width]
    out_ref[5:6, :] = gbup_ref[:, width:]
    out_ref[6:7, :own] = bias_ref[:, :own]
    out_ref[6:7, own:] = bias_ref[:, 2 * own :]
    out_ref[7:8, :] = jnp.zeros((1, width), F32)


def result_kernel(order_ref, row_ref, mid_ref, own_ref, other_ref, out_ref):
    last = last_of(order_ref)
    branch = own_ref[...].astype(F32) + other_ref[...].astype(F32) + row_ref[3:4]
    result = (mid_ref[...] + center(branch) * (1.0 - last)).astype(BF16)
    plain = dot_nt(result, chooser_of(order_ref, order_ref.shape[1]))
    out_ref[...] = plain[:, : out_ref.shape[1]].astype(BF16)


def final_kernel(order_ref, row_ref, own_ref, other_ref, ent_ref, gmid_ref, out_ref):
    last = last_of(order_ref)
    grad = own_ref[...].astype(F32) + other_ref[...].astype(F32)
    normed, inverse = norm_of(expand(ent_ref[...].astype(F32), last))
    grad = (gmid_ref[...] + norm_backward(grad, normed, inverse, row_ref[0:1], last)).astype(BF16)
    plain = dot_nt(grad, chooser_of(order_ref, order_ref.shape[1]))
    out_ref[...] = plain[:, : out_ref.shape[1]].astype(BF16)


def send_kernel(*refs):
    out_ref, at = refs[-1], 0
    for acts_ref, grads_ref in zip(refs[:-1:2], refs[1:-1:2]):
        half = acts_ref.shape[1] // 2
        columns = grads_ref.shape[1]
        out_ref[:, at : at + columns] = dot_tn(acts_ref[:, half:], grads_ref[...]).astype(BF16)
        at += columns


def keep_kernel(radix, *refs):
    keep_ref, send_refs, got_ref = refs[-radix], refs[len(refs) - radix + 1 :], refs[-radix - 1]
    rows, at = keep_ref.shape[0], 0
    pairs = refs[: -radix - 1]
    for acts_ref, grads_ref in zip(pairs[::2], pairs[1::2]):
        cut = slice(at, at + grads_ref.shape[1])
        half = dot_tn(acts_ref[:, : rows * radix], grads_ref[...]) + got_ref[:, cut].astype(F32)
        keep_ref[:, cut] = half[:rows]
        for k, send_ref in enumerate(send_refs):
            send_ref[:, cut] = half[(k + 1) * rows : (k + 2) * rows].astype(BF16)
        at += grads_ref.shape[1]


def add_kernel(radix, given, *refs):
    total = refs[0][...]
    for ref in refs[1 : 1 + given]:
        total = total + ref[...].astype(F32)
    rows = refs[1 + given].shape[0]
    refs[1 + given][...] = total[:rows]
    for k, ref in enumerate(refs[2 + given :]):
        ref[...] = total[(k + 1) * rows : (k + 2) * rows].astype(BF16)


def gather_far(shard, count):
    early = shard
    for stride, radix in reversed(phases_of(count)[2:]):
        got = [swap(shard, k * stride) for k in range(1, radix)]
        shard, early = jnp.concatenate([shard] + got, axis=0), got[0]
    return shard, early


def gather_near(held, count):
    for stride, radix in phases_of(count)[1:2]:
        held = jnp.concatenate([held] + [swap(held, k * stride) for k in range(1, radix)], axis=0)
    return held


class Sum:
    def __init__(self, pairs, count):
        self.flat = [a for pair in pairs for a in pair]
        self.phases = phases_of(count)
        self.columns = sum(grads.shape[1] for _, grads in pairs)
        self.rows = pairs[0][0].shape[1] // 2
        self.flops = 2 * pairs[0][0].shape[0] * self.rows * self.columns
        (self.sent,) = call(send_kernel, [shape(self.rows, self.columns, BF16)], self.flat, flops=self.flops)
        self.keep = None

    def go(self):
        (stride, _), self.phases = self.phases[0], self.phases[1:]
        sent = [self.sent] if self.keep is None else self.sent
        got = [swap(piece, (k + 1) * stride) for k, piece in enumerate(sent)]
        if not self.phases:
            total = self.keep
            for piece in got:
                total = total + piece.astype(F32)
            self.keep = total
            return self
        radix = self.phases[0][1]
        self.rows //= radix
        outs = [shape(self.rows, self.columns, F32)] + [shape(self.rows, self.columns, BF16)] * (radix - 1)
        if self.keep is None:
            outs = call(functools.partial(keep_kernel, radix), outs, self.flat + got, flops=self.flops)
        elif self.rows % 16 == 0:
            outs = call(functools.partial(add_kernel, radix, len(got)), outs, [self.keep] + got)
        else:
            total = self.keep
            for piece in got:
                total = total + piece.astype(F32)
            parts = [total[k * self.rows : (k + 1) * self.rows] for k in range(radix)]
            outs = [parts[0]] + [part.astype(BF16) for part in parts[1:]]
        self.keep, *self.sent = outs
        return self

    def end(self):
        while self.phases:
            self.go()
        return self.keep


def reduce_all(vector, count):
    for stride, radix in phases_of(count):
        parts = [vector] + [swap(vector, k * stride) for k in range(1, radix)]
        while len(parts) > 1:
            parts = [parts[i] + parts[i + 1] for i in range(0, len(parts), 2)]
        vector = parts[0]
    return vector


def body(
    stream,
    w_query,
    w_key,
    w_value,
    b_query,
    b_value,
    w_out,
    b_out,
    gain_attn,
    w_up,
    b_up,
    w_down,
    b_down,
    gain_mlp,
    cotangent,
    lengths,
):
    rows, inner_width = stream.shape
    count = lax.axis_size("dp")
    me = lax.axis_index("dp")
    rank = lax.axis_index("tensor").astype(jnp.int32).reshape(1, 1)
    shard_rows, own = w_query.shape
    width = shard_rows * count
    units = w_up.shape[1]
    matmul = 2 * rows * width * units

    blocks = jnp.array(relative_order(count), jnp.int32)
    order = ((me ^ blocks)[:, None] * shard_rows + jnp.arange(shard_rows, dtype=jnp.int32)).reshape(1, -1)
    vectors = jnp.stack([gain_attn, gain_mlp, b_out, b_down] + [jnp.zeros_like(b_out)] * 12)

    (shard_qkv,) = call(pack_kernel, [shape(shard_rows, 3 * own, BF16)], [w_query, w_key, w_value])
    qkv_far, early = gather_far(shard_qkv, count)
    w_out, w_up, w_down, order = lax.optimization_barrier((w_out, w_up, w_down, order, shard_qkv))[:4]
    shard_ou, shard_dn = call(
        pack_late_kernel, [shape(shard_rows, own + units, BF16), shape(shard_rows, units, BF16)], [w_out, w_up, w_down]
    )
    ent, top, acts_a, gbm, row = call(
        first_kernel,
        [shape(rows, width, BF16)] * 4 + [shape(8, width, F32)],
        [order, stream, cotangent, vectors],
        flops=matmul,
    )
    qkv_far, acts_a = lax.optimization_barrier((qkv_far, acts_a))
    qkv0 = gather_near(qkv_far, count)
    qkv1 = swap(qkv0, 1)
    shard_ou = after(shard_ou, early, acts_a)
    ou_far, early = gather_far(shard_ou, count)
    shard_dn = after(shard_dn, early)
    o_far, u_far = ou_far[:, :own], ou_far[:, own:]
    o00 = gather_near(o_far, count)
    u0 = gather_near(after(u_far, o_far), count)
    o01 = swap_tensor(o00)
    o10, o11 = swap(o00, 1), swap(o01, 1)
    u1 = swap(u0, 1)
    d_far, _ = gather_far(shard_dn, count)
    acts_a = after(acts_a, o_far, u_far)

    bias_qkv = jnp.concatenate([b_query, jnp.zeros_like(b_query), b_value]).astype(F32)[None]
    qkv, context, lse = call(
        attend_kernel,
        [shape(rows, 3 * own, BF16), shape(rows, own, BF16), shape(8, rows, F32)],
        [lengths, acts_a, qkv0, qkv1, bias_qkv],
        scalars=1,
        scratch=[pltpu.VMEM((rows, rows), F32)],
        flops=matmul * 4,
    )
    other_context = swap_tensor(context)
    d0 = gather_near(after(d_far, lse), count)
    d1 = swap(d0, 1)
    middle, acts_m, active, slope = call(
        middle_kernel,
        [shape(rows, width, F32), shape(rows, width, BF16), shape(rows, units, BF16), shape(rows, units, F32)],
        [rank, order, row, b_up.astype(F32)[None], context, other_context, o00, o01, o10, o11, u0, u1, ent],
        scalars=1,
        flops=matmul * 2,
        room=32,
    )
    sum_dn = Sum([(gbm, active)], count).go()
    d1, slope = lax.optimization_barrier((d1, slope, sum_dn.sent))[:2]
    ghid, gn, gbup = call(
        turn_kernel,
        [shape(rows, units, BF16), shape(rows, width, BF16), shape(1, units, F32)],
        [gbm, slope, d0, d1, u0, u1],
        flops=matmul * 2,
        room=32,
    )
    gn_other = swap_tensor(gn)
    sum_up = Sum([(acts_m, ghid)], count).go()
    sum_dn.go()
    mlp = jnp.concatenate([dot_nt(active, d0), dot_nt(active, d1)], axis=1).astype(BF16)
    gn_other, mlp = lax.optimization_barrier((gn_other, mlp, sum_up.sent, sum_dn.sent))[:2]
    mlp_other = swap_tensor(mlp)

    gmid, gba, gctx, sums = call(
        back_kernel,
        [shape(rows, width, F32), shape(rows, width, BF16), shape(rows, own, BF16), shape(8, width, F32)],
        [order, row, gn, gn_other, middle, top, o00, o10],
        flops=matmul // 4,
    )
    sum_up.go()
    shard_dn_t = sum_dn.end()
    gctx = after(gctx, sum_up.sent, shard_dn_t)
    (gqkv,) = call(
        attend_back_kernel,
        [shape(rows, 3 * own, BF16)],
        [lengths, qkv, lse, gctx],
        scalars=1,
        scratch=[pltpu.VMEM((rows, rows), F32), pltpu.VMEM((rows, PAIR), F32), pltpu.VMEM((rows, PAIR), F32)],
        flops=matmul * 3,
    )
    sum_last = Sum([(gba, context), (acts_a, gqkv)], count)
    shard_up = sum_up.end()
    gqkv_late = after(gqkv, sum_last.sent, shard_up, mlp_other)
    part, gain, gbias = call(
        part_kernel,
        [shape(rows, width, BF16), shape(8, width, F32), shape(1, 3 * own, F32)],
        [gqkv_late, qkv0, qkv1, ent, order],
        flops=matmul,
    )
    part_other = swap_tensor(part)
    sum_last.go().go()
    gain = after(gain, sum_last.sent)
    (out_rows,) = call(
        result_kernel, [shape(rows, inner_width, BF16)], [order, row, middle, mlp, mlp_other], flops=matmul // 2
    )
    (grad_stream,) = call(
        final_kernel, [shape(rows, inner_width, BF16)], [order, row, part, part_other, ent, gmid], flops=matmul // 2
    )
    (plain,) = call(vector_kernel, [shape(8, width, F32)], [order, row, sums, gain, gbup, gbias])
    plain_other = swap_tensor(plain)
    plain = reduce_all(jnp.where(jnp.arange(8)[:, None] == 3, plain + plain_other, plain), count)

    last = sum_last.end()
    return (
        out_rows,
        grad_stream,
        last[:, own : 2 * own],
        last[:, 2 * own : 3 * own],
        last[:, 3 * own :],
        plain[6, :own],
        plain[6, own:],
        last[:, :own].T,
        plain[2],
        plain[3],
        shard_up,
        plain[4:6].reshape(-1),
        shard_dn_t.T,
        plain[0],
        plain[1],
    )


def solution(mesh):
    return jax.shard_map(
        body,
        mesh=mesh,
        in_specs=(
            P("dp", None),
            P("dp", "tensor"),
            P("dp", "tensor"),
            P("dp", "tensor"),
            P("tensor"),
            P("tensor"),
            P("tensor", "dp"),
            P(),
            P(),
            P("dp", "tensor"),
            P("tensor"),
            P("tensor", "dp"),
            P(),
            P(),
            P("dp", None),
            P("dp", None),
        ),
        out_specs=(
            P("dp", None),
            P("dp", None),
            P("dp", "tensor"),
            P("dp", "tensor"),
            P("dp", "tensor"),
            P("tensor"),
            P("tensor"),
            P("tensor", "dp"),
            P(),
            P(),
            P("dp", "tensor"),
            P("tensor"),
            P("tensor", "dp"),
            P(),
            P(),
        ),
        check_vma=False,
    )
```

```python
import functools

import jax
import jax.numpy as jnp
from jax import lax
from jax.experimental import pallas as pl
from jax.experimental.pallas import tpu as pltpu
from jax.sharding import PartitionSpec as P

HD = 64
PAIR = 2 * HD
STEP = 256
epsilon = 1e-05
F32 = jnp.float32
BF16 = jnp.bfloat16
VMEM = pl.BlockSpec(memory_space=pltpu.VMEM)
SMEM = pl.BlockSpec(memory_space=pltpu.SMEM)


def phases_of(count):
    found, stride = [], 1
    while stride < count:
        rest = count // stride
        radix = 2 if stride == 1 or (rest.bit_length() - 1) % 2 == 1 else 4
        found.append((stride, radix))
        stride *= radix
    return found


def relative_order(count):
    blocks = [0]
    for stride, radix in reversed(phases_of(count)):
        blocks = [b ^ (k * stride) for k in range(radix) for b in blocks]
    return blocks


def swap(array, flip):
    count = lax.axis_size("dp")
    return lax.ppermute(array, "dp", [(i, i ^ flip) for i in range(count)])


def swap_tensor(array):
    count = lax.axis_size("tensor")
    return lax.ppermute(array, "tensor", [(i, i ^ 1) for i in range(count)])


def dot_nn(left, right):
    return lax.dot_general(left, right, (((1,), (0,)), ((), ())), preferred_element_type=F32)


def dot_nt(left, right):
    return lax.dot_general(left, right, (((1,), (1,)), ((), ())), preferred_element_type=F32)


def dot_tn(left, right):
    return lax.dot_general(left, right, (((0,), (0,)), ((), ())), preferred_element_type=F32)


def shape(rows, columns, dtype):
    return jax.ShapeDtypeStruct((rows, columns), dtype)


def after(array, *others):
    return lax.optimization_barrier((array,) + others)[0]


def call(kernel, outs, args, scalars=0, scratch=(), room=16):
    return pl.pallas_call(
        kernel,
        out_shape=outs,
        in_specs=[SMEM] * scalars + [VMEM] * (len(args) - scalars),
        out_specs=[VMEM] * len(outs),
        scratch_shapes=list(scratch),
        compiler_params=pltpu.CompilerParams(vmem_limit_bytes=room * 1024 * 1024),
        cost_estimate=pl.CostEstimate(flops=0, bytes_accessed=1024, transcendentals=0),
    )(*args)


def chooser_of(order_ref, rows):
    place = lax.broadcasted_iota(jnp.int32, (rows, order_ref.shape[1]), 0)
    return (place == order_ref[...]).astype(F32).astype(BF16)


def last_of(order_ref):
    return (order_ref[...] == order_ref.shape[1] - 1).astype(F32)


def expand(rows, last):
    return rows - jnp.sum(rows, axis=1, keepdims=True) * last


def norm_of(full):
    inverse = lax.rsqrt(jnp.mean(full * full, axis=1, keepdims=True) + epsilon)
    return full * inverse, inverse


def norm_backward(grad, normed, inverse, gain, last):
    scaled = grad * gain
    full = inverse * (scaled - normed * jnp.mean(scaled * normed, axis=1, keepdims=True))
    return (full - jnp.sum(full * last, axis=1, keepdims=True)) * (1.0 - last)


def center(rows):
    return rows - jnp.mean(rows, axis=1, keepdims=True)


def pack_kernel(*refs):
    at = 0
    for ref in refs[:-1]:
        refs[-1][:, at : at + ref.shape[1]] = ref[...]
        at += ref.shape[1]


def stacked(refs, plan, columns):
    parts = [refs[i][a : a + n, columns] for i, a, n in plan]
    return parts[0] if len(parts) == 1 else jnp.concatenate(parts, axis=0)


def first_kernel(order_ref, stream_ref, cot_ref, vec_ref, ent_ref, top_ref, acts_ref, gbm_ref, row_ref):
    chooser = chooser_of(order_ref, order_ref.shape[1])
    last = last_of(order_ref)
    rows = dot_nn(vec_ref[...], chooser)
    inner = stream_ref.shape[1]
    entering = dot_nn(stream_ref[...], chooser[:inner])
    ent_ref[...] = entering.astype(BF16)
    normed, _ = norm_of(expand(entering, last))
    acts_ref[...] = (normed * rows[0:1]).astype(BF16)
    top = dot_nn(cot_ref[...], chooser[:inner])
    top_ref[...] = top.astype(BF16)
    gbm = center(top)
    gbm_ref[...] = gbm.astype(BF16)
    row_ref[:4, :] = rows[:4]
    row_ref[4:5, :] = jnp.sum(gbm, axis=0, keepdims=True)
    row_ref[5:, :] = jnp.zeros((row_ref.shape[0] - 5, row_ref.shape[1]), F32)


def row_blocks(rows):
    return [(i, min(rows, i + STEP)) for i in range(0, rows, STEP)]


def write_mask(len_ref, mask_ref):
    for lo, hi in row_blocks(mask_ref.shape[0]):
        place = lax.broadcasted_iota(jnp.int32, (1, hi - lo), 1) + lo
        first = jnp.zeros_like(place)
        end = jnp.int32(0)
        for j in range(len_ref.shape[1] - 1):
            end = end + len_ref[0, j]
            first = jnp.where(place >= end, end, first)
        key = lax.broadcasted_iota(jnp.int32, (hi, hi - lo), 0)
        mask_ref[:hi, lo:hi] = jnp.where((key >= first) & (key <= place), 0.0, -1e30)


def head_lanes(head, dims):
    lane = lax.broadcasted_iota(jnp.int32, dims, 1)
    return (lane < HD) if head == 0 else (lane >= HD)


def unit_of(size):
    r = lax.broadcasted_iota(jnp.int32, (size, size), 0)
    c = lax.broadcasted_iota(jnp.int32, (size, size), 1)
    return (r == c).astype(F32).astype(BF16)


def attend_kernel(plan, len_ref, acts_ref, bias_ref, *refs):
    (own, rows), many = (bias_ref.shape[1] // 3, acts_ref.shape[0]), bias_ref.shape[1] // (3 * PAIR)
    weights, (qkv_ref, ctx_ref, lse_ref, *pair_refs, mask_ref) = refs[: -4 - many], refs[-4 - many :]
    write_mask(len_ref, mask_ref)
    for at in range(0, 3 * own, own):
        cut = slice(at, at + own)
        qkv_ref[:, cut] = (dot_nn(acts_ref[...], stacked(weights, plan, cut)) + bias_ref[:, cut]).astype(BF16)
    unit = unit_of(PAIR)
    scale = jnp.asarray(HD**-0.5, BF16)
    for pair in range(own // PAIR):
        at = pair * PAIR
        keys = qkv_ref[:, own + at : own + at + PAIR]
        values_t = dot_nt(unit, qkv_ref[:, 2 * own + at : 2 * own + at + PAIR]).astype(BF16)
        for lo, hi in row_blocks(rows):
            block = qkv_ref[lo:hi, at : at + PAIR] * scale
            parts = []
            for head in range(2):
                own_q = jnp.where(head_lanes(head, block.shape), block, jnp.zeros_like(block))
                scores = dot_nt(keys[:hi], own_q) + mask_ref[:hi, lo:hi]
                peak = jnp.max(scores, axis=0, keepdims=True)
                expo = jnp.exp(scores - peak)
                total = jnp.sum(expo, axis=0, keepdims=True)
                probs = (expo * (1.0 / total)).astype(BF16)
                parts.append(dot_nn(values_t[:, :hi], probs))
                lse_ref[2 * pair + head : 2 * pair + head + 1, lo:hi] = peak + jnp.log(total)
            row = lax.broadcasted_iota(jnp.int32, parts[0].shape, 0)
            mixed = jnp.where(row < HD, parts[0], parts[1]).T.astype(BF16)
            ctx_ref[lo:hi, at : at + PAIR] = mixed
            pair_refs[pair][lo:hi, :] = mixed


def middle_kernel(plan, rank_ref, order_ref, row_ref, bup_ref, own_ref, ent_ref, *refs):
    other, refs = refs[0][...], refs[1:]
    weights, (mid_ref, acts_ref, active_ref, slope_ref) = refs[:-4], refs[-4:]
    zero = rank_ref[0, 0] == 0
    own = own_ref.shape[1]
    last = last_of(order_ref)

    def ordered(a, b):
        return jnp.where(zero, a, b), jnp.where(zero, b, a)

    first, second = ordered(own_ref[...], other)
    w_first, w_second = ordered(stacked(weights, plan, slice(0, own)), stacked(weights, plan, slice(own, 2 * own)))
    branch = dot_nt(first, w_first) + dot_nt(second, w_second) + row_ref[2:3]
    middle = ent_ref[...].astype(F32) + center(branch) * (1.0 - last)
    mid_ref[...] = middle
    normed, _ = norm_of(expand(middle, last))
    acts = (normed * row_ref[1:2]).astype(BF16)
    acts_ref[...] = acts
    units = active_ref.shape[1]
    piece = units // 3
    for at in range(0, units, piece):
        cut = slice(at, at + piece)
        hidden = dot_nn(acts, stacked(weights, plan, slice(2 * own + at, 2 * own + at + piece))) + bup_ref[:, cut]
        square = hidden * hidden
        bend = jnp.tanh(hidden * (0.7978845608028654 + 0.7978845608028654 * 0.044715 * square))
        up = 0.5 + 0.5 * bend
        active_ref[:, cut] = (hidden * up).astype(BF16)
        slope_ref[:, cut] = up + (0.5 * hidden) * (1.0 - bend * bend) * (
            0.7978845608028654 + 0.7978845608028654 * 3 * 0.044715 * square
        )


def turn_kernel(plan_up, plan_dn, many, own, gbm_ref, slope_ref, *refs):
    ups, downs, (ghid_ref, gn_ref, gbup_ref) = refs[:many], refs[many:-3], refs[-3:]
    units = slope_ref.shape[1]
    piece = units // 3
    total = None
    for at in range(0, units, piece):
        cut = slice(at, at + piece)
        gact = dot_nn(gbm_ref[...], stacked(downs, plan_dn, cut))
        ghid = (gact * slope_ref[:, cut]).astype(BF16)
        ghid_ref[:, cut] = ghid
        gbup_ref[:, cut] = jnp.sum(ghid.astype(F32), axis=0, keepdims=True)
        part = dot_nt(ghid, stacked(ups, plan_up, slice(own + at, own + at + piece)))
        total = part if total is None else total + part
    gn_ref[...] = total.astype(BF16)


def mix_kernel(plan, active_ref, *refs):
    refs, outs = refs[:-2], refs[-2:]
    branch = dot_nt(active_ref[...], stacked(refs, plan, slice(None))).astype(BF16)
    rows = outs[0].shape[0]
    for i, out_ref in enumerate(outs):
        out_ref[...] = branch[i * rows : (i + 1) * rows]


def back_kernel(plan, order_ref, row_ref, own_ref, other_ref, mid_ref, top_ref, *refs):
    weights, (gmid_ref, gba_ref, gctx_ref, sum_ref) = refs[:-4], refs[-4:]
    last = last_of(order_ref)
    grad = own_ref[...].astype(F32) + other_ref[...].astype(F32)
    normed, inverse = norm_of(expand(mid_ref[...], last))
    gmid = top_ref[...].astype(F32) + norm_backward(grad, normed, inverse, row_ref[1:2], last)
    gmid_ref[...] = gmid
    gba = center(gmid)
    low = gba.astype(BF16)
    gba_ref[...] = low
    gctx_ref[...] = dot_nn(low, stacked(weights, plan, slice(0, gctx_ref.shape[1]))).astype(BF16)
    sum_ref[0:1, :] = jnp.sum(grad * normed, axis=0, keepdims=True)
    sum_ref[1:2, :] = jnp.sum(gba, axis=0, keepdims=True)
    sum_ref[2:, :] = jnp.zeros((sum_ref.shape[0] - 2, sum_ref.shape[1]), F32)


def attend_back_kernel(
    len_ref, qkv_ref, lse_ref, gctx_ref, out_ref, mask_ref, gk_ref, gv_ref
):
    rows, own = gctx_ref.shape
    write_mask(len_ref, mask_ref)
    unit = unit_of(PAIR)
    scale = jnp.asarray(HD**-0.5, BF16)
    for pair in range(own // PAIR):
        at = pair * PAIR
        keys = qkv_ref[:, own + at : own + at + PAIR]
        values = qkv_ref[:, 2 * own + at : 2 * own + at + PAIR]
        keys_t = dot_nt(unit, keys * scale).astype(BF16)
        for lo, hi in reversed(row_blocks(rows)):
            block = qkv_ref[lo:hi, at : at + PAIR] * scale
            gblock = gctx_ref[lo:hi, at : at + PAIR]
            parts, gk, gv = [], None, None
            for head in range(2):
                pick = head_lanes(head, block.shape)
                own_q = jnp.where(pick, block, jnp.zeros_like(block))
                own_g = jnp.where(pick, gblock, jnp.zeros_like(block))
                lse = lse_ref[2 * pair + head : 2 * pair + head + 1, lo:hi]
                probs = jnp.exp(dot_nt(keys[:hi], own_q) + mask_ref[:hi, lo:hi] - lse)
                gprobs = dot_nt(values[:hi], own_g)
                delta = jnp.sum(probs * gprobs, axis=0, keepdims=True)
                gscores = (probs * (gprobs - delta)).astype(BF16)
                parts.append(dot_nn(keys_t[:, :hi], gscores))
                k1 = dot_nn(gscores, own_q)
                v1 = dot_nn(probs.astype(BF16), own_g)
                gk = k1 if gk is None else gk + k1
                gv = v1 if gv is None else gv + v1
            row = lax.broadcasted_iota(jnp.int32, parts[0].shape, 0)
            out_ref[lo:hi, at : at + PAIR] = jnp.where(row < HD, parts[0], parts[1]).T.astype(BF16)
            if hi == rows:
                gk_ref[...] = gk
                gv_ref[...] = gv
            else:
                gk_ref[:hi, :] += gk
                gv_ref[:hi, :] += gv
        out_ref[:, own + at : own + at + PAIR] = gk_ref[...].astype(BF16)
        out_ref[:, 2 * own + at : 2 * own + at + PAIR] = gv_ref[...].astype(BF16)


def part_kernel(plan, gqkv_ref, ent_ref, order_ref, *refs):
    weights, (part_ref, sum_ref, bias_ref) = refs[:-3], refs[-3:]
    grads = gqkv_ref[...]
    part_ref[...] = dot_nt(grads, stacked(weights, plan, slice(None))).astype(BF16)
    normed, _ = norm_of(expand(ent_ref[...].astype(F32), last_of(order_ref)))
    total = jnp.sum(part_ref[...].astype(F32) * normed, axis=0, keepdims=True)
    sum_ref[...] = jnp.broadcast_to(total, sum_ref.shape)
    bias_ref[...] = jnp.sum(grads.astype(F32), axis=0, keepdims=True)


def vector_kernel(order_ref, row_ref, sum_ref, gain_ref, gbup_ref, bias_ref, out_ref):
    width = order_ref.shape[1]
    chooser = chooser_of(order_ref, width)
    rows = jnp.concatenate([row_ref[4:5], sum_ref[0:1], sum_ref[1:2], gain_ref[0:1], jnp.zeros((4, width), F32)], axis=0)
    plain = jnp.zeros_like(rows)
    for _ in range(3):
        low = rows.astype(BF16)
        plain = plain + dot_nt(low, chooser)
        rows = rows - low.astype(F32)
    own = width // 2
    out_ref[0:4, :] = plain[0:4]
    out_ref[4:5, :] = gbup_ref[:, :width]
    out_ref[5:6, :] = gbup_ref[:, width:]
    out_ref[6:7, :own] = bias_ref[:, :own]
    out_ref[6:7, own:] = bias_ref[:, 2 * own :]
    out_ref[7:8, :] = jnp.zeros((1, width), F32)


def result_kernel(order_ref, row_ref, mid_ref, own0, own1, other0, other1, out_ref):
    last = last_of(order_ref)
    own = jnp.concatenate([own0[...], own1[...]], axis=0).astype(F32)
    other = jnp.concatenate([other0[...], other1[...]], axis=0).astype(F32)
    branch = own + other + row_ref[3:4]
    result = (mid_ref[...] + center(branch) * (1.0 - last)).astype(BF16)
    plain = dot_nt(result, chooser_of(order_ref, order_ref.shape[1]))
    out_ref[...] = plain[:, : out_ref.shape[1]].astype(BF16)


def final_kernel(order_ref, row_ref, own_ref, other_ref, ent_ref, gmid_ref, out_ref):
    last = last_of(order_ref)
    grad = own_ref[...].astype(F32) + other_ref[...].astype(F32)
    normed, inverse = norm_of(expand(ent_ref[...].astype(F32), last))
    grad = (gmid_ref[...] + norm_backward(grad, normed, inverse, row_ref[0:1], last)).astype(BF16)
    plain = dot_nt(grad, chooser_of(order_ref, order_ref.shape[1]))
    out_ref[...] = plain[:, : out_ref.shape[1]].astype(BF16)


def send_kernel(*refs):
    out_ref, at = refs[-1], 0
    for acts_ref, grads_ref in zip(refs[:-1:2], refs[1:-1:2]):
        half = acts_ref.shape[1] // 2
        columns = grads_ref.shape[1]
        out_ref[:, at : at + columns] = dot_tn(acts_ref[:, half:], grads_ref[...]).astype(BF16)
        at += columns


def keep_kernel(radix, *refs):
    keep_ref, send_refs, got_ref = refs[-radix], refs[len(refs) - radix + 1 :], refs[-radix - 1]
    rows, at = keep_ref.shape[0], 0
    pairs = refs[: -radix - 1]
    for acts_ref, grads_ref in zip(pairs[::2], pairs[1::2]):
        cut = slice(at, at + grads_ref.shape[1])
        half = dot_tn(acts_ref[:, : rows * radix], grads_ref[...]) + got_ref[:, cut].astype(F32)
        keep_ref[:, cut] = half[:rows]
        for k, send_ref in enumerate(send_refs):
            send_ref[:, cut] = half[(k + 1) * rows : (k + 2) * rows].astype(BF16)
        at += grads_ref.shape[1]


def add_kernel(radix, given, *refs):
    total = refs[0][...]
    for ref in refs[1 : 1 + given]:
        total = total + ref[...].astype(F32)
    rows = refs[1 + given].shape[0]
    refs[1 + given][...] = total[:rows]
    for k, ref in enumerate(refs[2 + given :]):
        ref[...] = total[(k + 1) * rows : (k + 2) * rows].astype(BF16)


def gather_far(shard, count):
    return jnp.concatenate(gather_far_pieces(shard, count), axis=0)


def gather_far_pieces(shard, count):
    pieces = [shard]
    for stride, radix in reversed(phases_of(count)[2:]):
        held = pieces[0] if len(pieces) == 1 else jnp.concatenate(pieces, axis=0)
        pieces = [held] + [swap(held, k * stride) for k in range(1, radix)]
    return pieces


def gather_near(held, count):
    pieces = [held]
    for stride, radix in phases_of(count)[1:2]:
        pieces += [swap(held, k * stride) for k in range(1, radix)]
    return pieces


def plan_of(pieces):
    return tuple((i, 0, piece.shape[0]) for i, piece in enumerate(pieces))


def near_first(shard, count):
    return jnp.concatenate(gather_near(shard, count), axis=0) if len(phases_of(count)) == 3 else shard


def then_far(held, count):
    phases = phases_of(count)
    if len(phases) != 3:
        pieces = gather_near(gather_far(held, count), count)
        return pieces, plan_of(pieces + pieces)
    (_, near), (stride, far) = phases[1:]
    rows = held.shape[0] // near
    pieces = [held] + [swap(held, k * stride) for k in range(1, far)]
    plan = [(core * far + z, x * rows, rows) for core in range(2) for x in range(near) for z in range(far)]
    return pieces, tuple(plan)


class Sum:
    def __init__(self, pairs, count):
        self.flat = [a for pair in pairs for a in pair]
        self.phases = phases_of(count)
        self.columns = sum(grads.shape[1] for _, grads in pairs)
        self.rows = pairs[0][0].shape[1] // 2
        self.sent = call(send_kernel, [shape(self.rows, self.columns, BF16)], self.flat)
        self.keep = None
        self.got = []

    def go(self):
        (stride, _), self.phases = self.phases[0], self.phases[1:]
        self.got = [swap(piece, (k + 1) * stride) for k, piece in enumerate(self.sent)]
        return self

    def work(self):
        got = self.got
        if not self.phases:
            total = self.keep
            for piece in got:
                total = total + piece.astype(F32)
            self.keep = total
            return self
        radix = self.phases[0][1]
        self.rows //= radix
        outs = [shape(self.rows, self.columns, F32)] + [shape(self.rows, self.columns, BF16)] * (radix - 1)
        if self.keep is None:
            outs = call(functools.partial(keep_kernel, radix), outs, self.flat + got)
        elif self.rows % 16 == 0:
            outs = call(functools.partial(add_kernel, radix, len(got)), outs, [self.keep] + got)
        else:
            total = self.keep
            for piece in got:
                total = total + piece.astype(F32)
            parts = [total[k * self.rows : (k + 1) * self.rows] for k in range(radix)]
            outs = [parts[0]] + [part.astype(BF16) for part in parts[1:]]
        self.keep, *self.sent = outs
        return self

    def end(self):
        while self.phases:
            self.go().work()
        return self.keep


def tie(sums, *arrays):
    flat = list(arrays) + [piece for one in sums for piece in one.got]
    flat = lax.optimization_barrier(tuple(flat))
    at = len(arrays)
    for one in sums:
        one.got = list(flat[at : at + len(one.got)])
        at += len(one.got)
    return flat[: len(arrays)]


def reduce_all(vector, count):
    for stride, radix in phases_of(count):
        parts = [vector] + [swap(vector, k * stride) for k in range(1, radix)]
        while len(parts) > 1:
            parts = [parts[i] + parts[i + 1] for i in range(0, len(parts), 2)]
        vector = parts[0]
    return vector


def body(
    stream,
    w_query,
    w_key,
    w_value,
    b_query,
    b_value,
    w_out,
    b_out,
    gain_attn,
    w_up,
    b_up,
    w_down,
    b_down,
    gain_mlp,
    cotangent,
    lengths,
):
    rows, inner_width = stream.shape
    count = lax.axis_size("dp")
    me = lax.axis_index("dp")
    rank = lax.axis_index("tensor").astype(jnp.int32).reshape(1, 1)
    shard_rows, own = w_query.shape
    width = shard_rows * count
    units = w_up.shape[1]
    blocks = jnp.array(relative_order(count), jnp.int32)
    order = ((me ^ blocks)[:, None] * shard_rows + jnp.arange(shard_rows, dtype=jnp.int32)).reshape(1, -1)

    (shard_qkv,) = call(pack_kernel, [shape(shard_rows, 3 * own, BF16)], [w_query, w_key, w_value])
    qkv_far = gather_far_pieces(shard_qkv, count)
    w_out_t, w_up, shard_dn, order = lax.optimization_barrier((w_out.T, w_up, w_down.T, order, shard_qkv))[:4]
    (shard_ou,) = call(
        pack_kernel, [shape(shard_rows, 2 * own + units, BF16)], [w_out_t, swap_tensor(w_out_t), w_up]
    )
    vectors = jnp.stack([gain_attn, gain_mlp, b_out, b_down] + [jnp.zeros_like(b_out)] * 12)
    ent, top, acts_a, gbm, row = call(
        first_kernel,
        [shape(rows, width, BF16)] * 4 + [shape(8, width, F32)],
        [order, stream, cotangent, vectors],
    )
    dn_near = near_first(shard_dn, count)
    shard_ou, dn_near, acts_a, *qkv_far = lax.optimization_barrier((shard_ou, dn_near, acts_a, *qkv_far))
    middle_at = (len(qkv_far) + 1) // 2
    halves = [jnp.concatenate(part, axis=0) for part in (qkv_far[:middle_at], qkv_far[middle_at:]) if part]
    qkv_w = [piece for group in zip(*(gather_near(half, count) for half in halves)) for piece in group]
    ou_far = gather_far_pieces(shard_ou, count)

    qkv_w = qkv_w + [swap(piece, 1) for piece in qkv_w]
    plan = plan_of(qkv_w)
    bias_qkv = jnp.concatenate([b_query, jnp.zeros_like(b_query), b_value]).astype(F32)[None]
    qkv, context, lse, *pairs = call(
        functools.partial(attend_kernel, plan),
        [shape(rows, 3 * own, BF16), shape(rows, own, BF16), shape(8, rows, F32)]
        + [shape(rows, PAIR, BF16)] * (own // PAIR),
        [lengths, acts_a, bias_qkv] + qkv_w,
        scalars=1,
        scratch=[pltpu.VMEM((rows, rows), F32)],
    )
    dn_near, context, *ou_far = lax.optimization_barrier((dn_near, context, *ou_far))
    ou_far = jnp.concatenate(ou_far, axis=0)
    other_context = [swap_tensor(context)]
    ou_w = gather_near(ou_far, count)
    dn_w, plan_dn = then_far(dn_near, count)
    flat = lax.optimization_barrier((*other_context, *ou_w, *dn_w))
    other_context, ou_w, dn_w = list(flat[:1]), list(flat[1 : 1 + len(ou_w)]), list(flat[1 + len(ou_w) :])
    ou_w = ou_w + [swap(piece, 1) for piece in ou_w]
    plan_ou = plan_of(ou_w)
    dn_w = dn_w + [swap(piece, 1) for piece in dn_w]

    middle, acts_m, active, slope = call(
        functools.partial(middle_kernel, plan_ou),
        [shape(rows, width, F32), shape(rows, width, BF16), shape(rows, units, BF16), shape(rows, units, F32)],
        [rank, order, row, b_up.astype(F32)[None], context, ent] + other_context + ou_w,
        scalars=1,
        room=32,
    )
    active, *dn_w = lax.optimization_barrier((active, *dn_w))
    sum_dn = Sum([(gbm, active)], count)
    slope, *sum_dn.sent = lax.optimization_barrier((slope, *sum_dn.sent))
    sum_dn.go()
    ghid, gn, gbup = call(
        functools.partial(turn_kernel, plan_ou, plan_dn, len(ou_w), 2 * own),
        [shape(rows, units, BF16), shape(rows, width, BF16), shape(1, units, F32)],
        [gbm, slope] + ou_w + dn_w,
        room=32,
    )
    gn_other = swap_tensor(gn)
    (ghid,) = tie([sum_dn], ghid)
    sum_dn.work().go()
    sum_up = Sum([(acts_m, ghid)], count).go()
    mlp = call(
        functools.partial(mix_kernel, plan_dn), [shape(rows // 2, width, BF16)] * 2, [after(active, sum_up.sent)] + dn_w
    )
    sum_up.work().go()
    mlp_other = [swap_tensor(part) for part in mlp]
    sum_dn.work().go()

    gn_other = after(gn_other, sum_dn.sent, sum_up.sent, mlp)
    gmid, gba, gctx, sums = call(
        functools.partial(back_kernel, plan_ou),
        [shape(rows, width, F32), shape(rows, width, BF16), shape(rows, own, BF16), shape(8, width, F32)],
        [order, row, gn, gn_other, middle, top] + ou_w,
    )
    (gqkv,) = call(
        attend_back_kernel,
        [shape(rows, 3 * own, BF16)],
        [lengths, qkv, lse, gctx],
        scalars=1,
        scratch=[pltpu.VMEM((rows, rows), F32), pltpu.VMEM((rows, PAIR), F32), pltpu.VMEM((rows, PAIR), F32)],
    )
    gqkv, mlp_other[0] = tie([sum_dn, sum_up], gqkv, mlp_other[0])
    sum_last = Sum([(gba, context), (acts_a, gqkv)], count).go()
    sum_up.work().go()
    gqkv_late = after(gqkv, sum_last.sent, sum_up.sent)
    part, gain, gbias = call(
        functools.partial(part_kernel, plan),
        [shape(rows, width, BF16), shape(8, width, F32), shape(1, 3 * own, F32)],
        [gqkv_late, ent, order] + qkv_w,
    )
    part_other = swap_tensor(part)
    (plain,) = call(vector_kernel, [shape(8, width, F32)], [order, row, sums, gain, gbup, gbias])
    (plain,) = tie([sum_last], plain)
    sum_last.work().go()
    plain = reduce_all(plain, count)
    plain, mlp_other[1] = tie([sum_last, sum_up], plain, mlp_other[1])
    sum_last.work()
    part_other, mlp_other[1] = lax.optimization_barrier((part_other, mlp_other[1], *sum_last.sent))[:2]
    sum_last.go()
    (out_rows,) = call(
        result_kernel, [shape(rows, inner_width, BF16)], [order, row, middle, *mlp, *mlp_other]
    )
    (grad_stream,) = call(
        final_kernel, [shape(rows, inner_width, BF16)], [order, row, part, part_other, ent, gmid]
    )
    gain_sum = plain[3:4] + swap_tensor(plain[3:4])
    shard_dn_t, shard_up, last = (one.work().end() for one in (sum_dn, sum_up, sum_last))
    return (
        out_rows,
        grad_stream,
        last[:, own : 2 * own],
        last[:, 2 * own : 3 * own],
        last[:, 3 * own :],
        plain[6, :own],
        plain[6, own:],
        last[:, :own].T,
        plain[2],
        gain_sum[0],
        shard_up,
        plain[4:6].reshape(-1),
        shard_dn_t.T,
        plain[0],
        plain[1],
    )


def solution(mesh):
    return jax.shard_map(
        body,
        mesh=mesh,
        in_specs=(
            P("dp", None),
            P("dp", "tensor"),
            P("dp", "tensor"),
            P("dp", "tensor"),
            P("tensor"),
            P("tensor"),
            P("tensor", "dp"),
            P(),
            P(),
            P("dp", "tensor"),
            P("tensor"),
            P("tensor", "dp"),
            P(),
            P(),
            P("dp", None),
            P("dp", None),
        ),
        out_specs=(
            P("dp", None),
            P("dp", None),
            P("dp", "tensor"),
            P("dp", "tensor"),
            P("dp", "tensor"),
            P("tensor"),
            P("tensor"),
            P("tensor", "dp"),
            P(),
            P(),
            P("dp", "tensor"),
            P("tensor"),
            P("tensor", "dp"),
            P(),
            P(),
        ),
        check_vma=False,
    )
```

```python
import functools

import jax
import jax.numpy as jnp
from jax import lax
from jax.experimental import pallas as pl
from jax.experimental.pallas import tpu as pltpu
from jax.sharding import PartitionSpec as P

HD = 64
PAIR = 2 * HD
STEP = 256
epsilon = 1e-05
ROOM = 12 * 1024 * 1024
LONG = 100_000_000_000
F32 = jnp.float32
BF16 = jnp.bfloat16
VMEM = pl.BlockSpec(memory_space=pltpu.VMEM)
SMEM = pl.BlockSpec(memory_space=pltpu.SMEM)


def phases_of(count):
    found, stride = [], 1
    while stride < count:
        rest = count // stride
        radix = 2 if stride == 1 or (rest.bit_length() - 1) % 2 == 1 else 4
        found.append((stride, radix))
        stride *= radix
    return found


def relative_order(count):
    blocks = [0]
    for stride, radix in reversed(phases_of(count)):
        blocks = [b ^ (k * stride) for k in range(radix) for b in blocks]
    return blocks


def swap(array, flip):
    count = lax.axis_size("dp")
    return lax.ppermute(array, "dp", [(i, i ^ flip) for i in range(count)])


def swap_tensor(array):
    count = lax.axis_size("tensor")
    return lax.ppermute(array, "tensor", [(i, i ^ 1) for i in range(count)])


def dot_nn(left, right):
    return lax.dot_general(left, right, (((1,), (0,)), ((), ())), preferred_element_type=F32)


def dot_nt(left, right):
    return lax.dot_general(left, right, (((1,), (1,)), ((), ())), preferred_element_type=F32)


def dot_tn(left, right):
    return lax.dot_general(left, right, (((0,), (0,)), ((), ())), preferred_element_type=F32)


def shape(rows, columns, dtype):
    return jax.ShapeDtypeStruct((rows, columns), dtype)


def after(array, *others):
    return lax.optimization_barrier((array,) + others)[0]


def call(kernel, outs, args, scalars=0, scratch=(), room=ROOM, cost=0):
    return pl.pallas_call(
        kernel,
        out_shape=outs,
        in_specs=[SMEM] * scalars + [VMEM] * (len(args) - scalars),
        out_specs=[VMEM] * len(outs),
        scratch_shapes=list(scratch),
        compiler_params=pltpu.CompilerParams(vmem_limit_bytes=room),
        cost_estimate=pl.CostEstimate(flops=cost, bytes_accessed=1024, transcendentals=0),
    )(*args)


def chooser_of(order_ref, rows):
    place = lax.broadcasted_iota(jnp.int32, (rows, order_ref.shape[1]), 0)
    return (place == order_ref[...]).astype(F32).astype(BF16)


def last_of(order_ref):
    return (order_ref[...] == order_ref.shape[1] - 1).astype(F32)


def expand(rows, last):
    return rows - jnp.sum(rows, axis=1, keepdims=True) * last


def norm_of(full):
    inverse = lax.rsqrt(jnp.mean(full * full, axis=1, keepdims=True) + epsilon)
    return full * inverse, inverse


def norm_backward(grad, normed, inverse, gain, last):
    scaled = grad * gain
    full = inverse * (scaled - normed * jnp.mean(scaled * normed, axis=1, keepdims=True))
    return (full - jnp.sum(full * last, axis=1, keepdims=True)) * (1.0 - last)


def center(rows):
    return rows - jnp.mean(rows, axis=1, keepdims=True)


def pack_kernel(*refs):
    at = 0
    for ref in refs[:-1]:
        refs[-1][:, at : at + ref.shape[1]] = ref[...]
        at += ref.shape[1]


def pack_far_kernel(*refs):
    *parts, out_ref, sems = refs
    copies, at = [], 0
    for i, ref in enumerate(parts):
        copies.append(pltpu.make_async_copy(ref, out_ref.at[:, at : at + ref.shape[1]], sems.at[i]))
        at += ref.shape[1]
    for copy in copies:
        copy.start()
    for copy in copies:
        copy.wait()


def pack(arrays):
    rows, columns = arrays[0].shape[0], sum(a.shape[1] for a in arrays)
    if rows % 16:
        return call(pack_kernel, [shape(rows, columns, BF16)], arrays)[0]
    return pl.pallas_call(
        pack_far_kernel,
        out_shape=shape(rows, columns, BF16),
        in_specs=[pl.BlockSpec(memory_space=pl.ANY)] * len(arrays),
        out_specs=VMEM,
        scratch_shapes=[pltpu.SemaphoreType.DMA((len(arrays),))],
        compiler_params=pltpu.CompilerParams(vmem_limit_bytes=ROOM),
        cost_estimate=pl.CostEstimate(flops=0, bytes_accessed=1024, transcendentals=0),
    )(*arrays)


def joined(refs, columns=slice(None)):
    return refs[0][:, columns] if len(refs) == 1 else jnp.concatenate([ref[:, columns] for ref in refs], axis=0)


def stacked(refs, plan, columns):
    parts = [refs[i][a : a + n, columns] for i, a, n in plan]
    return parts[0] if len(parts) == 1 else jnp.concatenate(parts, axis=0)


def first_kernel(order_ref, stream_ref, cot_ref, vec_ref, ent_ref, top_ref, acts_ref, gbm_ref, row_ref):
    chooser = chooser_of(order_ref, order_ref.shape[1])
    last = last_of(order_ref)
    rows = dot_nn(vec_ref[...], chooser)
    inner = stream_ref.shape[1]
    entering = dot_nn(stream_ref[...], chooser[:inner])
    ent_ref[...] = entering.astype(BF16)
    normed, _ = norm_of(expand(entering, last))
    acts_ref[...] = (normed * rows[0:1]).astype(BF16)
    top = dot_nn(cot_ref[...], chooser[:inner])
    top_ref[...] = top.astype(BF16)
    gbm = center(top)
    gbm_ref[...] = gbm.astype(BF16)
    row_ref[:4, :] = rows[:4]
    row_ref[4:5, :] = jnp.sum(gbm, axis=0, keepdims=True)
    row_ref[5:, :] = jnp.zeros((row_ref.shape[0] - 5, row_ref.shape[1]), F32)


def row_blocks(rows):
    return [(i, min(rows, i + STEP)) for i in range(0, rows, STEP)]


def write_mask(len_ref, mask_ref):
    for lo, hi in row_blocks(mask_ref.shape[0]):
        place = lax.broadcasted_iota(jnp.int32, (1, hi - lo), 1) + lo
        first = jnp.zeros_like(place)
        end = jnp.int32(0)
        for j in range(len_ref.shape[1] - 1):
            end = end + len_ref[0, j]
            first = jnp.where(place >= end, end, first)
        key = lax.broadcasted_iota(jnp.int32, (hi, hi - lo), 0)
        mask_ref[:hi, lo:hi] = jnp.where((key >= first) & (key <= place), 0.0, -1e30)


def head_lanes(head, dims):
    lane = lax.broadcasted_iota(jnp.int32, dims, 1)
    return (lane < HD) if head == 0 else (lane >= HD)


def unit_of(size):
    r = lax.broadcasted_iota(jnp.int32, (size, size), 0)
    c = lax.broadcasted_iota(jnp.int32, (size, size), 1)
    return (r == c).astype(F32).astype(BF16)


def attend_kernel(plan, len_ref, acts_ref, bias_ref, *refs):
    (own, rows), many = (bias_ref.shape[1] // 3, acts_ref.shape[0]), bias_ref.shape[1] // (3 * PAIR)
    weights, (qkv_ref, ctx_ref, lse_ref, *pair_refs, mask_ref) = refs[: -4 - many], refs[-4 - many :]
    write_mask(len_ref, mask_ref)
    for at in range(0, 3 * own, own):
        cut = slice(at, at + own)
        qkv_ref[:, cut] = (dot_nn(acts_ref[...], stacked(weights, plan, cut)) + bias_ref[:, cut]).astype(BF16)
    unit = unit_of(PAIR)
    scale = jnp.asarray(HD**-0.5, BF16)
    for pair in range(own // PAIR):
        at = pair * PAIR
        keys = qkv_ref[:, own + at : own + at + PAIR]
        values_t = dot_nt(unit, qkv_ref[:, 2 * own + at : 2 * own + at + PAIR]).astype(BF16)
        for lo, hi in row_blocks(rows):
            block = qkv_ref[lo:hi, at : at + PAIR] * scale
            parts = []
            for head in range(2):
                own_q = jnp.where(head_lanes(head, block.shape), block, jnp.zeros_like(block))
                scores = dot_nt(keys[:hi], own_q) + mask_ref[:hi, lo:hi]
                peak = jnp.max(scores, axis=0, keepdims=True)
                expo = jnp.exp(scores - peak)
                total = jnp.sum(expo, axis=0, keepdims=True)
                probs = (expo * (1.0 / total)).astype(BF16)
                parts.append(dot_nn(values_t[:, :hi], probs))
                lse_ref[2 * pair + head : 2 * pair + head + 1, lo:hi] = peak + jnp.log(total)
            row = lax.broadcasted_iota(jnp.int32, parts[0].shape, 0)
            mixed = jnp.where(row < HD, parts[0], parts[1]).T.astype(BF16)
            ctx_ref[lo:hi, at : at + PAIR] = mixed
            pair_refs[pair][lo:hi, :] = mixed


def middle_kernel(lo, plan, many, rank_ref, order_ref, row_ref, bup_ref, own_ref, other_ref, ent_ref, gbm_ref, *refs):
    weights, downs, (mid_ref, acts_ref, active_ref, ghid_ref, gn_ref, gbup_ref) = refs[:many], refs[many:-6], refs[-6:]
    plan, plan_dn = plan
    rows = slice(lo, lo + mid_ref.shape[0])
    zero = rank_ref[0, 0] == 0
    own = own_ref.shape[1]
    last = last_of(order_ref)

    def ordered(a, b):
        return jnp.where(zero, a, b), jnp.where(zero, b, a)

    first, second = ordered(own_ref[rows, :], other_ref[rows, :])
    w_first, w_second = ordered(stacked(weights, plan, slice(0, own)), stacked(weights, plan, slice(own, 2 * own)))
    branch = dot_nt(first, w_first) + dot_nt(second, w_second) + row_ref[2:3]
    middle = ent_ref[rows, :].astype(F32) + center(branch) * (1.0 - last)
    mid_ref[...] = middle
    normed, _ = norm_of(expand(middle, last))
    acts = (normed * row_ref[1:2]).astype(BF16)
    acts_ref[...] = acts
    gbm = gbm_ref[rows, :]
    units = active_ref.shape[1]
    piece = units // 3
    total = None
    for at in range(0, units, piece):
        cut, cut_up = slice(at, at + piece), slice(2 * own + at, 2 * own + at + piece)
        up_part = stacked(weights, plan, cut_up)
        hidden = dot_nn(acts, up_part) + bup_ref[:, cut]
        gact = dot_nn(gbm, stacked(downs, plan_dn, cut))
        square = hidden * hidden
        bend = jnp.tanh(hidden * (0.7978845608028654 + 0.7978845608028654 * 0.044715 * square))
        up = 0.5 + 0.5 * bend
        active_ref[:, cut] = (hidden * up).astype(BF16)
        slope = up + (0.5 * hidden) * (1.0 - bend * bend) * (
            0.7978845608028654 + 0.7978845608028654 * 3 * 0.044715 * square
        )
        ghid = (gact * slope).astype(BF16)
        ghid_ref[:, cut] = ghid
        gbup_ref[:, cut] = jnp.sum(ghid.astype(F32), axis=0, keepdims=True)
        part = dot_nt(ghid, up_part)
        total = part if total is None else total + part
    gn_ref[...] = total.astype(BF16)


def mix_kernel(plan, parts, *refs):
    refs[-1][...] = dot_nt(joined(refs[:parts]), stacked(refs[parts:-1], plan, slice(None))).astype(BF16)


def back_kernel(lo, plan, order_ref, row_ref, own_ref, other_ref, mid_ref, top_ref, *refs):
    weights, (gmid_ref, gba_ref, gctx_ref, sum_ref) = refs[:-4], refs[-4:]
    last = last_of(order_ref)
    grad = own_ref[...].astype(F32) + other_ref[...].astype(F32)
    normed, inverse = norm_of(expand(mid_ref[...], last))
    gmid = top_ref[lo : lo + mid_ref.shape[0], :].astype(F32) + norm_backward(grad, normed, inverse, row_ref[1:2], last)
    gmid_ref[...] = gmid
    gba = center(gmid)
    low = gba.astype(BF16)
    gba_ref[...] = low
    gctx_ref[...] = dot_nn(low, stacked(weights, plan, slice(0, gctx_ref.shape[1]))).astype(BF16)
    sum_ref[0:1, :] = jnp.sum(grad * normed, axis=0, keepdims=True)
    sum_ref[1:2, :] = jnp.sum(gba, axis=0, keepdims=True)
    sum_ref[2:, :] = jnp.zeros((sum_ref.shape[0] - 2, sum_ref.shape[1]), F32)


def attend_back_kernel(
    len_ref, qkv_ref, lse_ref, *refs
):
    gctx_refs, (gq_ref, gkv_ref, mask_ref, gk_ref, gv_ref) = refs[:-5], refs[-5:]
    rows, own = gq_ref.shape
    write_mask(len_ref, mask_ref)
    unit = unit_of(PAIR)
    scale = jnp.asarray(HD**-0.5, BF16)
    for pair in range(own // PAIR):
        at = pair * PAIR
        keys = qkv_ref[:, own + at : own + at + PAIR]
        values = qkv_ref[:, 2 * own + at : 2 * own + at + PAIR]
        keys_t = dot_nt(unit, keys * scale).astype(BF16)
        gctx = joined(gctx_refs, slice(at, at + PAIR))
        for lo, hi in reversed(row_blocks(rows)):
            block = qkv_ref[lo:hi, at : at + PAIR] * scale
            gblock = gctx[lo:hi]
            parts, gk, gv = [], None, None
            for head in range(2):
                pick = head_lanes(head, block.shape)
                own_q = jnp.where(pick, block, jnp.zeros_like(block))
                own_g = jnp.where(pick, gblock, jnp.zeros_like(block))
                lse = lse_ref[2 * pair + head : 2 * pair + head + 1, lo:hi]
                probs = jnp.exp(dot_nt(keys[:hi], own_q) + mask_ref[:hi, lo:hi] - lse)
                gprobs = dot_nt(values[:hi], own_g)
                delta = jnp.sum(probs * gprobs, axis=0, keepdims=True)
                gscores = (probs * (gprobs - delta)).astype(BF16)
                parts.append(dot_nn(keys_t[:, :hi], gscores))
                k1 = dot_nn(gscores, own_q)
                v1 = dot_nn(probs.astype(BF16), own_g)
                gk = k1 if gk is None else gk + k1
                gv = v1 if gv is None else gv + v1
            row = lax.broadcasted_iota(jnp.int32, parts[0].shape, 0)
            gq_ref[lo:hi, at : at + PAIR] = jnp.where(row < HD, parts[0], parts[1]).T.astype(BF16)
            if hi == rows:
                gk_ref[...] = gk
                gv_ref[...] = gv
            else:
                gk_ref[:hi, :] += gk
                gv_ref[:hi, :] += gv
        gkv_ref[:, at : at + PAIR] = gk_ref[...].astype(BF16)
        gkv_ref[:, own + at : own + at + PAIR] = gv_ref[...].astype(BF16)


def part_kernel(plan, gq_ref, gkv_ref, ent_ref, order_ref, *refs):
    weights, (part_ref, sum_ref, bias_ref) = refs[:-3], refs[-3:]
    own = gq_ref.shape[1]
    part = dot_nt(gq_ref[...], stacked(weights, plan, slice(0, own)))
    part_ref[...] = (part + dot_nt(gkv_ref[...], stacked(weights, plan, slice(own, 3 * own)))).astype(BF16)
    normed, _ = norm_of(expand(ent_ref[...].astype(F32), last_of(order_ref)))
    total = jnp.sum(part_ref[...].astype(F32) * normed, axis=0, keepdims=True)
    sum_ref[...] = total
    bias_ref[:, :own] = jnp.sum(gq_ref[...].astype(F32), axis=0, keepdims=True)
    bias_ref[:, own:] = jnp.sum(gkv_ref[:, own:].astype(F32), axis=0, keepdims=True)


def vector_kernel(parts, order_ref, row_ref, gain_ref, gain_other, bias_ref, *refs):
    sum_refs, gbup_refs, out_ref = refs[:parts], refs[parts:-1], refs[-1]
    width = order_ref.shape[1]
    chooser = chooser_of(order_ref, width)
    sums = sum(ref[0:2] for ref in sum_refs)
    gbup = sum(ref[...] for ref in gbup_refs)
    gain = gain_ref[...] + gain_other[...]
    rows = jnp.concatenate([row_ref[4:5], sums, gain, jnp.zeros((4, width), F32)], axis=0)
    plain = jnp.zeros_like(rows)
    for _ in range(3):
        low = rows.astype(BF16)
        plain = plain + dot_nt(low, chooser)
        rows = rows - low.astype(F32)
    out_ref[0:4, :] = plain[0:4]
    out_ref[4:5, :] = gbup[:, :width]
    out_ref[5:6, :] = gbup[:, width:]
    out_ref[6:7, :] = bias_ref[...]
    out_ref[7:8, :] = jnp.zeros((1, width), F32)


def result_kernel(parts, order_ref, row_ref, *refs):
    mids, (own_ref, other_ref, out_ref) = refs[:parts], refs[parts:]
    last = last_of(order_ref)
    branch = own_ref[...].astype(F32) + other_ref[...].astype(F32) + row_ref[3:4]
    result = (joined(mids) + center(branch) * (1.0 - last)).astype(BF16)
    plain = dot_nt(result, chooser_of(order_ref, order_ref.shape[1]))
    out_ref[...] = plain[:, : out_ref.shape[1]].astype(BF16)


def final_kernel(order_ref, row_ref, own_ref, other_ref, ent_ref, *refs):
    gmids, out_ref = refs[:-1], refs[-1]
    last = last_of(order_ref)
    grad = own_ref[...].astype(F32) + other_ref[...].astype(F32)
    normed, inverse = norm_of(expand(ent_ref[...].astype(F32), last))
    grad = (joined(gmids) + norm_backward(grad, normed, inverse, row_ref[0:1], last)).astype(BF16)
    plain = dot_nt(grad, chooser_of(order_ref, order_ref.shape[1]))
    out_ref[...] = plain[:, : out_ref.shape[1]].astype(BF16)


def pairs_of(refs, counts):
    found, at = [], 0
    for acts, grads in counts:
        found.append((refs[at : at + acts], refs[at + acts : at + acts + grads]))
        at += acts + grads
    return found


def send_kernel(counts, pieces, *refs):
    outs, at = refs[-pieces:], 0
    rows = outs[0].shape[0]
    for acts, grads in pairs_of(refs, counts):
        half = acts[0].shape[1] // 2
        cut = slice(at, at + grads[0].shape[1])
        made = dot_tn(joined(acts, slice(half, None)), joined(grads)).astype(BF16)
        for i, out_ref in enumerate(outs):
            out_ref[:, cut] = made[i * rows : (i + 1) * rows]
        at += grads[0].shape[1]


def keep_kernel(counts, pieces, radix, each, *refs):
    many = (radix - 1) * each
    keep_ref, send_refs = refs[-many - 1], refs[len(refs) - many :]
    got = joined(refs[-many - 1 - pieces : -many - 1]).astype(F32)
    rows, at = keep_ref.shape[0], 0
    size = rows // each
    for acts, grads in pairs_of(refs, counts):
        cut = slice(at, at + grads[0].shape[1])
        half = dot_tn(joined(acts, slice(0, rows * radix)), joined(grads)) + got[:, cut]
        keep_ref[:, cut] = half[:rows]
        for k, send_ref in enumerate(send_refs):
            send_ref[:, cut] = half[rows + k * size : rows + (k + 1) * size].astype(BF16)
        at += grads[0].shape[1]


def add_kernel(given, each, *refs):
    total = refs[0][...]
    for i in range(1, 1 + given, each):
        total = total + joined(refs[i : i + each]).astype(F32)
    rows = refs[1 + given].shape[0]
    refs[1 + given][...] = total[:rows]
    for k, ref in enumerate(refs[2 + given :]):
        ref[...] = total[(k + 1) * rows : (k + 2) * rows].astype(BF16)


def add_vector_kernel(given, each, *refs):
    vector, refs = refs[0][...].astype(BF16), refs[1:]
    total = refs[0][...]
    for i in range(1, 1 + given, each):
        total = total + joined(refs[i : i + each]).astype(F32)
    rows, columns = refs[1 + given].shape
    refs[1 + given][...] = total[:rows]
    for k, ref in enumerate(refs[2 + given :]):
        ref[:, :columns] = total[(k + 1) * rows : (k + 2) * rows].astype(BF16)
        ref[:, columns:] = vector


def finish_kernel(given, vector_ref, keep_ref, *refs):
    got, (*cuts, sum_ref) = refs[:given], refs[given:]
    columns = keep_ref.shape[1]
    total = keep_ref[...]
    parts = [vector_ref[...].astype(BF16).astype(F32)]
    for ref in got:
        total = total + ref[:, :columns].astype(F32)
        parts.append(ref[:, columns:].astype(F32))
    at = 0
    for ref in cuts:
        ref[...] = total[:, at : at + ref.shape[1]]
        at += ref.shape[1]
    while len(parts) > 1:
        parts = [parts[i] + parts[i + 1] for i in range(0, len(parts), 2)]
    sum_ref[...] = parts[0]


def gather_far(shard, count):
    return jnp.concatenate(gather_far_pieces(shard, count), axis=0)


def gather_far_pieces(shard, count):
    pieces = [shard]
    for stride, radix in reversed(phases_of(count)[2:]):
        held = pieces[0] if len(pieces) == 1 else jnp.concatenate(pieces, axis=0)
        pieces = [held] + [swap(held, k * stride) for k in range(1, radix)]
    return pieces


def gather_near(held, count):
    pieces = [held]
    for stride, radix in phases_of(count)[1:2]:
        pieces += [swap(held, k * stride) for k in range(1, radix)]
    return pieces


def plan_of(pieces):
    return tuple((i, 0, piece.shape[0]) for i, piece in enumerate(pieces))


def near_first(shard, count):
    middle = shard.shape[1] // 2
    halves = [shard[:, :middle], shard[:, middle:]]
    if len(phases_of(count)) != 3:
        return halves
    return [piece for pair in zip(*(gather_near(half, count) for half in halves)) for piece in pair]


def then_far(held, count):
    phases = phases_of(count)
    if len(phases) != 3:
        pieces = gather_near(gather_far(held, count), count)
        return pieces, plan_of(pieces + pieces)
    (_, near), (stride, far) = phases[1:]
    rows = held.shape[0] // near
    pieces = [held] + [swap(held, k * stride) for k in range(1, far)]
    plan = [(core * far + z, x * rows, rows) for core in range(2) for x in range(near) for z in range(far)]
    return pieces, tuple(plan)


class Sum:
    def __init__(self, pairs, count, first=4, second=1):
        self.flat = [a for pair in pairs for parts in pair for a in parts]
        self.counts = tuple((len(acts), len(grads)) for acts, grads in pairs)
        self.phases = phases_of(count)
        self.columns = sum(grads[0].shape[1] for _, grads in pairs)
        self.rows = pairs[0][0][0].shape[1] // 2
        self.each, self.second = first, second
        self.sent = call(
            functools.partial(send_kernel, self.counts, first),
            [shape(self.rows // first, self.columns, BF16)] * first,
            self.flat,
        )
        self.keep = None
        self.got = []

    def go(self):
        (stride, _), self.phases = self.phases[0], self.phases[1:]
        self.got = [swap(piece, (k // self.each + 1) * stride) for k, piece in enumerate(self.sent)]
        return self

    def work(self):
        got = self.got
        if not self.phases:
            total = self.keep
            for piece in got:
                total = total + piece.astype(F32)
            self.keep = total
            return self
        radix = self.phases[0][1]
        self.rows //= radix
        outs = [shape(self.rows, self.columns, F32)]
        if self.keep is None:
            each = self.second if self.rows % (16 * self.second) == 0 else 1
            outs += [shape(self.rows // each, self.columns, BF16)] * ((radix - 1) * each)
            kernel = functools.partial(keep_kernel, self.counts, len(got), radix, each)
            outs = call(kernel, outs, self.flat + got)
        elif self.rows % 16 == 0:
            outs += [shape(self.rows, self.columns, BF16)] * (radix - 1)
            outs = call(functools.partial(add_kernel, len(got), self.each), outs, [self.keep] + got)
            each = 1
        else:
            total = self.keep
            for i in range(0, len(got), self.each):
                total = total + jnp.concatenate(got[i : i + self.each], axis=0).astype(F32)
            parts = [total[k * self.rows : (k + 1) * self.rows] for k in range(radix)]
            outs = [parts[0]] + [part.astype(BF16) for part in parts[1:]]
            each = 1
        self.each = each
        self.keep, *self.sent = outs
        return self

    def end(self):
        while self.phases:
            self.go().work()
        return self.keep


def tie(sums, *arrays):
    flat = list(arrays) + [piece for one in sums for piece in one.got]
    flat = lax.optimization_barrier(tuple(flat))
    at = len(arrays)
    for one in sums:
        one.got = list(flat[at : at + len(one.got)])
        at += len(one.got)
    return flat[: len(arrays)]


def flips_of(phases):
    found = [0]
    for stride, radix in phases:
        found = [k * stride + f for k in range(radix) for f in found]
    return found[1:]


def reduce_all(vector, flips):
    return total_of([vector] + [swap(vector, flip) for flip in flips])


def total_of(parts):
    while len(parts) > 1:
        parts = [parts[i] + parts[i + 1] for i in range(0, len(parts), 2)]
    return parts[0]


def body(
    stream,
    w_query,
    w_key,
    w_value,
    b_query,
    b_value,
    w_out,
    b_out,
    gain_attn,
    w_up,
    b_up,
    w_down,
    b_down,
    gain_mlp,
    cotangent,
    lengths,
):
    rows, inner_width = stream.shape
    count = lax.axis_size("dp")
    me = lax.axis_index("dp")
    rank = lax.axis_index("tensor").astype(jnp.int32).reshape(1, 1)
    shard_rows, own = w_query.shape
    width = shard_rows * count
    units = w_up.shape[1]
    blocks = jnp.array(relative_order(count), jnp.int32)
    order = ((me ^ blocks)[:, None] * shard_rows + jnp.arange(shard_rows, dtype=jnp.int32)).reshape(1, -1)

    shard_qkv = pack([w_query, w_key, w_value])
    qkv_far = gather_far_pieces(shard_qkv, count)
    w_out_t, w_up, shard_dn, order = lax.optimization_barrier((w_out.T, w_up, w_down.T, order, shard_qkv))[:4]
    shard_ou = pack([w_out_t, swap_tensor(w_out_t), w_up])
    vectors = jnp.stack([gain_attn, gain_mlp, b_out, b_down] + [jnp.zeros_like(b_out)] * 12)
    ent, top, acts_a, gbm, row = call(
        first_kernel,
        [shape(rows, width, BF16)] * 4 + [shape(8, width, F32)],
        [order, stream, cotangent, vectors],
    )
    dn_near = near_first(shard_dn, count)
    flat = lax.optimization_barrier((shard_ou, acts_a, *qkv_far, *dn_near))
    shard_ou, acts_a, qkv_far, dn_near = flat[0], flat[1], flat[2 : 2 + len(qkv_far)], flat[2 + len(qkv_far) :]
    middle_at = (len(qkv_far) + 1) // 2
    halves = [jnp.concatenate(part, axis=0) for part in (qkv_far[:middle_at], qkv_far[middle_at:]) if part]
    qkv_w = [piece for group in zip(*(gather_near(half, count) for half in halves)) for piece in group]
    ou_far = gather_far_pieces(shard_ou, count)

    qkv_w = qkv_w + [swap(piece, 1) for piece in qkv_w]
    plan = plan_of(qkv_w)
    bias_qkv = jnp.concatenate([b_query, jnp.zeros_like(b_query), b_value]).astype(F32)[None]
    qkv, context, lse, *pairs = call(
        functools.partial(attend_kernel, plan),
        [shape(rows, 3 * own, BF16), shape(rows, own, BF16), shape(8, rows, F32)]
        + [shape(rows, PAIR, BF16)] * (own // PAIR),
        [lengths, acts_a, bias_qkv] + qkv_w,
        scalars=1,
        scratch=[pltpu.VMEM((rows, rows), F32)],
    )
    context, *ou_far = lax.optimization_barrier((context, *ou_far))
    dn_near = jnp.concatenate([jnp.concatenate(dn_near[i::2], axis=0) for i in range(2)], axis=1)
    ou_far = jnp.concatenate(ou_far, axis=0)
    other_context = [swap_tensor(context)]
    ou_w = gather_near(ou_far, count)
    dn_w, plan_dn = then_far(dn_near, count)
    flat = lax.optimization_barrier((*other_context, *ou_w, *dn_w))
    other_context, ou_w, dn_w = list(flat[:1]), list(flat[1 : 1 + len(ou_w)]), list(flat[1 + len(ou_w) :])
    ou_w = ou_w + [swap(piece, 1) for piece in ou_w]
    plan_ou = plan_of(ou_w)
    dn_w = dn_w + [swap(piece, 1) for piece in dn_w]

    cuts = [(0, rows)]
    bias_up = b_up.astype(F32)[None]
    middle, acts_m, active, ghid, gn, gn_other, gbup = [], [], [], [], [], [], []
    for lo, size in cuts:
        made = call(
            functools.partial(middle_kernel, lo, (plan_ou, plan_dn), len(ou_w)),
            [
                shape(size, width, F32),
                shape(size, width, BF16),
                shape(size, units, BF16),
                shape(size, units, BF16),
                shape(size, width, BF16),
                shape(1, units, F32),
            ],
            [rank, order, row, bias_up, context, *other_context, ent, gbm] + ou_w + dn_w,
            scalars=1,
        )
        for held, new in zip((middle, acts_m, active, ghid, gn, gbup), made):
            held.append(new)
        gn_other.append(swap_tensor(gn[-1]))

    sum_dn = Sum([((gbm,), active)], count).go()
    sum_up = Sum([(acts_m, ghid)], count).go()
    sum_dn.work().go()
    sum_up.work().go()
    (mlp,) = call(
        functools.partial(mix_kernel, plan_dn, len(active)),
        [shape(rows, width, BF16)],
        [after(active[0], sum_up.sent)] + active[1:] + dn_w,
    )
    mlp_other = swap_tensor(mlp)
    sum_dn.work().go()

    gmid, gba, gctx, sums = [], [], [], []
    gn_other[0] = after(gn_other[0], sum_dn.sent, sum_up.sent, mlp)
    for i, (lo, size) in enumerate(cuts):
        made = call(
            functools.partial(back_kernel, lo, plan_ou),
            [shape(size, width, F32), shape(size, width, BF16), shape(size, own, BF16), shape(8, width, F32)],
            [order, row, gn[i], gn_other[i], middle[i], top] + ou_w,
        )
        for held, new in zip((gmid, gba, gctx, sums), made):
            held.append(new)
    gq, gkv = call(
        attend_back_kernel,
        [shape(rows, own, BF16), shape(rows, 2 * own, BF16)],
        [lengths, qkv, lse] + gctx,
        scalars=1,
        scratch=[pltpu.VMEM((rows, rows), F32), pltpu.VMEM((rows, PAIR), F32), pltpu.VMEM((rows, PAIR), F32)],
        cost=LONG,
    )
    gq, gkv = tie([sum_dn, sum_up], gq, gkv)
    sum_last = Sum([(gba, (context,)), ((acts_a,), (gq,)), ((acts_a,), (gkv,))], count).go()
    sum_last.work().go()
    sum_up.work().go()
    gq, gkv, mlp_other = lax.optimization_barrier((gq, gkv, mlp_other, *sum_last.sent, *sum_up.sent))[:3]
    part, gain, gbias = call(
        functools.partial(part_kernel, plan),
        [shape(rows, width, BF16), shape(1, width, F32), shape(1, 2 * own, F32)],
        [gq, gkv, ent, order] + qkv_w,
        cost=LONG,
    )
    gain_other = swap_tensor(gain)
    part_other = swap_tensor(part)
    (plain,) = call(
        functools.partial(vector_kernel, len(cuts)),
        [shape(8, width, F32)],
        [order, row, gain, gain_other, gbias] + sums + gbup,
    )
    phases = phases_of(count)
    parts = [plain] + [swap(plain, flip) for flip in flips_of(phases[:2])]
    plain = total_of(list(tie([sum_last, sum_up], *parts)))
    short = len(phases) == 3
    if short:
        block = plain.reshape(shard_rows, -1)
        given, radix, size = len(sum_last.got), phases[2][1], sum_last.rows // phases[2][1]
        columns = sum_last.columns
        keep, *sent = call(
            functools.partial(add_vector_kernel, given, sum_last.each),
            [shape(size, columns, F32)] + [shape(size, columns + block.shape[1], BF16)] * (radix - 1),
            [block, sum_last.keep] + sum_last.got,
        )
        last_got = [swap(piece, (k + 1) * phases[2][0]) for k, piece in enumerate(sent)]
    else:
        sum_last.work()
        sent = sum_last.sent
        sum_last.go()
        for phase in phases[2:]:
            plain = reduce_all(plain, flips_of([phase]))
    mlp_other = after(mlp_other, sent)
    (out_rows,) = call(
        functools.partial(result_kernel, len(cuts)),
        [shape(rows, inner_width, BF16)],
        [order, row, *middle, mlp, mlp_other],
    )
    part_other, out_rows = lax.optimization_barrier((part_other, out_rows))
    (grad_stream,) = call(
        final_kernel, [shape(rows, inner_width, BF16)], [order, row, part, part_other, ent, *gmid]
    )
    shard_dn_t, shard_up = (one.work().end() for one in (sum_dn, sum_up))
    if short:
        keep, grad_stream = lax.optimization_barrier((keep, grad_stream))
        out_t, grad_q, grad_k, grad_v, block = call(
            functools.partial(finish_kernel, len(last_got)),
            [shape(shard_rows, own, F32)] * 4 + [shape(*block.shape, F32)],
            [block, keep] + last_got,
        )
        plain = block.reshape(plain.shape)
    else:
        last = sum_last.work().end()
        out_t, grad_q, grad_k, grad_v = (last[:, i * own : (i + 1) * own] for i in range(4))
    return (
        out_rows,
        grad_stream,
        grad_q,
        grad_k,
        grad_v,
        plain[6, :own],
        plain[6, own:],
        out_t.T,
        plain[2],
        plain[3],
        shard_up,
        plain[4:6].reshape(-1),
        shard_dn_t.T,
        plain[0],
        plain[1],
    )


def solution(mesh):
    return jax.shard_map(
        body,
        mesh=mesh,
        in_specs=(
            P("dp", None),
            P("dp", "tensor"),
            P("dp", "tensor"),
            P("dp", "tensor"),
            P("tensor"),
            P("tensor"),
            P("tensor", "dp"),
            P(),
            P(),
            P("dp", "tensor"),
            P("tensor"),
            P("tensor", "dp"),
            P(),
            P(),
            P("dp", None),
            P("dp", None),
        ),
        out_specs=(
            P("dp", None),
            P("dp", None),
            P("dp", "tensor"),
            P("dp", "tensor"),
            P("dp", "tensor"),
            P("tensor"),
            P("tensor"),
            P("tensor", "dp"),
            P(),
            P(),
            P("dp", "tensor"),
            P("tensor"),
            P("tensor", "dp"),
            P(),
            P(),
        ),
        check_vma=False,
    )
```

```python
import functools

import jax
import jax.numpy as jnp
from jax import lax
from jax.experimental import pallas as pl
from jax.experimental.pallas import tpu as pltpu
from jax.sharding import PartitionSpec as P

HD = 64
PAIR = 2 * HD
STEP = 384
epsilon = 1e-05
ROOM = 12 * 1024 * 1024
WIDE = 56 * 1024 * 1024
LONG = 100_000_000_000
F32 = jnp.float32
BF16 = jnp.bfloat16
VMEM = pl.BlockSpec(memory_space=pltpu.VMEM)
SMEM = pl.BlockSpec(memory_space=pltpu.SMEM)
FAR = pl.BlockSpec(memory_space=pltpu.HBM)


def phases_of(count):
    found, stride = [], 1
    while stride < count:
        rest = count // stride
        radix = 2 if stride == 1 or (rest.bit_length() - 1) % 2 == 1 else 4
        found.append((stride, radix))
        stride *= radix
    return found


def relative_order(count):
    blocks = [0]
    for stride, radix in reversed(phases_of(count)):
        blocks = [b ^ (k * stride) for k in range(radix) for b in blocks]
    return blocks


def swap(array, flip):
    count = lax.axis_size("dp")
    return lax.ppermute(array, "dp", [(i, i ^ flip) for i in range(count)])


def swap_tensor(array):
    count = lax.axis_size("tensor")
    return lax.ppermute(array, "tensor", [(i, i ^ 1) for i in range(count)])


def dot_nn(left, right):
    return lax.dot_general(left, right, (((1,), (0,)), ((), ())), preferred_element_type=F32)


def dot_nt(left, right):
    return lax.dot_general(left, right, (((1,), (1,)), ((), ())), preferred_element_type=F32)


def dot_tn(left, right):
    return lax.dot_general(left, right, (((0,), (0,)), ((), ())), preferred_element_type=F32)


def shape(rows, columns, dtype):
    return jax.ShapeDtypeStruct((rows, columns), dtype)


def after(array, *others):
    return lax.optimization_barrier((array,) + others)[0]


def call(kernel, outs, args, scalars=0, scratch=(), room=ROOM, cost=0, far=(), far_outs=()):
    return pl.pallas_call(
        kernel,
        out_shape=outs,
        in_specs=[SMEM] * scalars + [FAR if i in far else VMEM for i in range(scalars, len(args))],
        out_specs=[FAR if i in far_outs else VMEM for i in range(len(outs))],
        scratch_shapes=list(scratch),
        compiler_params=pltpu.CompilerParams(vmem_limit_bytes=room),
        cost_estimate=pl.CostEstimate(flops=cost, bytes_accessed=1024, transcendentals=0),
    )(*args)


def chooser_of(order_ref, rows):
    place = lax.broadcasted_iota(jnp.int32, (rows, order_ref.shape[1]), 0)
    return (place == order_ref[...]).astype(F32).astype(BF16)


def last_of(order_ref):
    return (order_ref[...] == order_ref.shape[1] - 1).astype(F32)


def expand(rows, last):
    return rows - jnp.sum(rows, axis=1, keepdims=True) * last


def norm_of(full):
    inverse = lax.rsqrt(jnp.mean(full * full, axis=1, keepdims=True) + epsilon)
    return full * inverse, inverse


def norm_backward(grad, normed, inverse, gain, last):
    scaled = grad * gain
    full = inverse * (scaled - normed * jnp.mean(scaled * normed, axis=1, keepdims=True))
    return (full - jnp.sum(full * last, axis=1, keepdims=True)) * (1.0 - last)


def center(rows):
    return rows - jnp.mean(rows, axis=1, keepdims=True)


def pack_kernel(*refs):
    at = 0
    for ref in refs[:-1]:
        refs[-1][:, at : at + ref.shape[1]] = ref[...]
        at += ref.shape[1]


def move(sems, *pairs):
    copies = [pltpu.make_async_copy(source, target, sems.at[i]) for i, (source, target) in enumerate(pairs)]
    for copy in copies:
        copy.start()
    return copies


def pack_far_kernel(*refs):
    *parts, out_ref, sems = refs
    pairs, at = [], 0
    for ref in parts:
        pairs.append((ref, out_ref.at[:, at : at + ref.shape[1]]))
        at += ref.shape[1]
    for copy in move(sems, *pairs):
        copy.wait()


def pack(arrays):
    rows, columns = arrays[0].shape[0], sum(a.shape[1] for a in arrays)
    if rows % 16:
        return call(pack_kernel, [shape(rows, columns, BF16)], arrays)[0]
    return pl.pallas_call(
        pack_far_kernel,
        out_shape=shape(rows, columns, BF16),
        in_specs=[FAR] * len(arrays),
        out_specs=VMEM,
        scratch_shapes=[pltpu.SemaphoreType.DMA((len(arrays),))],
        compiler_params=pltpu.CompilerParams(vmem_limit_bytes=WIDE),
        cost_estimate=pl.CostEstimate(flops=0, bytes_accessed=1024, transcendentals=0),
    )(*arrays)


def joined(refs, columns=slice(None)):
    return refs[0][:, columns] if len(refs) == 1 else jnp.concatenate([ref[:, columns] for ref in refs], axis=0)


def stacked(refs, plan, columns):
    parts = [refs[i][a : a + n, columns] for i, a, n in plan]
    return parts[0] if len(parts) == 1 else jnp.concatenate(parts, axis=0)


def first_kernel(order_ref, stream_ref, cot_ref, *refs):
    vec_refs, (ent_ref, top_ref, acts_ref, gbm_ref, row_ref) = refs[:-5], refs[-5:]
    chooser = chooser_of(order_ref, order_ref.shape[1])
    last = last_of(order_ref)
    plain = [ref[...].astype(F32).reshape(1, -1) for ref in vec_refs]
    rows = dot_nn(jnp.concatenate(plain + plain, axis=0).astype(BF16), chooser)
    inner = stream_ref.shape[1]
    entering = dot_nn(stream_ref[...], chooser[:inner])
    ent_ref[...] = entering.astype(BF16)
    normed, _ = norm_of(expand(entering, last))
    acts_ref[...] = (normed * rows[0:1]).astype(BF16)
    top = dot_nn(cot_ref[...], chooser[:inner])
    top_ref[...] = top.astype(BF16)
    gbm = center(top)
    gbm_ref[...] = gbm.astype(BF16)
    row_ref[:4, :] = rows[:4]
    row_ref[4:5, :] = jnp.sum(gbm, axis=0, keepdims=True)
    row_ref[5:, :] = jnp.zeros((row_ref.shape[0] - 5, row_ref.shape[1]), F32)


def row_blocks(rows):
    return [(i, min(rows, i + STEP)) for i in range(0, rows, STEP)]


def write_mask(len_ref, mask_ref):
    for lo, hi in row_blocks(mask_ref.shape[0]):
        place = lax.broadcasted_iota(jnp.int32, (1, hi - lo), 1) + lo
        first = jnp.zeros_like(place)
        end = jnp.int32(0)
        for j in range(len_ref.shape[1] - 1):
            end = end + len_ref[0, j]
            first = jnp.where(place >= end, end, first)
        key = lax.broadcasted_iota(jnp.int32, (hi, hi - lo), 0)
        mask_ref[:hi, lo:hi] = jnp.where((key >= first) & (key <= place), 0.0, -1e30)


def both_heads(block):
    zero = jnp.zeros_like(block)
    first = lax.broadcasted_iota(jnp.int32, block.shape, 1) < HD
    return jnp.concatenate([jnp.where(first, block, zero), jnp.where(first, zero, block)], axis=0)


def own_rows(both):
    size = both.shape[1] // 2
    row = lax.broadcasted_iota(jnp.int32, (PAIR, size), 0)
    return jnp.where(row < HD, both[:, :size], both[:, size:])


def unit_of(size):
    r = lax.broadcasted_iota(jnp.int32, (size, size), 0)
    c = lax.broadcasted_iota(jnp.int32, (size, size), 1)
    return (r == c).astype(F32).astype(BF16)


def attend_kernel(plan, len_ref, acts_ref, bias_ref, *refs):
    weights, (qkv_ref, ctx_ref, lse_ref, mask_ref) = refs[:-4], refs[-4:]
    rows, own = ctx_ref.shape
    write_mask(len_ref, mask_ref)
    for at in range(0, 3 * own, own):
        cut = slice(at, at + own)
        qkv_ref[:, cut] = (dot_nn(acts_ref[...], stacked(weights, plan, cut)) + bias_ref[:, cut]).astype(BF16)
    unit = unit_of(PAIR)
    scale = jnp.asarray(HD**-0.5, BF16)
    for pair in range(own // PAIR):
        at = pair * PAIR
        keys = qkv_ref[:, own + at : own + at + PAIR]
        values_t = dot_nt(unit, qkv_ref[:, 2 * own + at : 2 * own + at + PAIR]).astype(BF16)
        for lo, hi in row_blocks(rows):
            size = hi - lo
            both = both_heads(qkv_ref[lo:hi, at : at + PAIR] * scale)
            mask = mask_ref[:hi, lo:hi]
            scores = dot_nt(keys[:hi], both) + jnp.concatenate([mask, mask], axis=1)
            peak = jnp.max(scores, axis=0, keepdims=True)
            expo = jnp.exp(scores - peak)
            total = jnp.sum(expo, axis=0, keepdims=True)
            probs = (expo * (1.0 / total)).astype(BF16)
            lse = peak + jnp.log(total)
            lse_ref[2 * pair : 2 * pair + 1, lo:hi] = lse[:, :size]
            lse_ref[2 * pair + 1 : 2 * pair + 2, lo:hi] = lse[:, size:]
            ctx_ref[lo:hi, at : at + PAIR] = own_rows(dot_nn(values_t[:, :hi], probs)).T.astype(BF16)


def middle_kernel(lo, plan, many, rank_ref, order_ref, row_ref, bup_ref, own_ref, other_ref, ent_ref, gbm_ref, *refs):
    weights, downs, (mid_ref, acts_ref, active_ref, ghid_ref, gn_ref, gbup_ref) = refs[:many], refs[many:-6], refs[-6:]
    plan, plan_dn = plan
    rows = slice(lo, lo + mid_ref.shape[0])
    zero = rank_ref[0, 0] == 0
    own = own_ref.shape[1]
    last = last_of(order_ref)

    def ordered(a, b):
        return jnp.where(zero, a, b), jnp.where(zero, b, a)

    first, second = ordered(own_ref[rows, :], other_ref[rows, :])
    w_first, w_second = ordered(stacked(weights, plan, slice(0, own)), stacked(weights, plan, slice(own, 2 * own)))
    branch = dot_nt(first, w_first) + dot_nt(second, w_second) + row_ref[2:3]
    middle = ent_ref[rows, :].astype(F32) + center(branch) * (1.0 - last)
    mid_ref[...] = middle
    normed, _ = norm_of(expand(middle, last))
    acts = (normed * row_ref[1:2]).astype(BF16)
    acts_ref[...] = acts
    gbm = gbm_ref[rows, :]
    units = active_ref.shape[1]
    piece = units // 3
    total = None
    for at in range(0, units, piece):
        cut, cut_up = slice(at, at + piece), slice(2 * own + at, 2 * own + at + piece)
        up_part = stacked(weights, plan, cut_up)
        hidden = dot_nn(acts, up_part) + bup_ref[:, cut]
        gact = dot_nn(gbm, stacked(downs, plan_dn, cut))
        square = hidden * hidden
        bend = jnp.tanh(hidden * (0.7978845608028654 + 0.7978845608028654 * 0.044715 * square))
        up = 0.5 + 0.5 * bend
        active_ref[:, cut] = (hidden * up).astype(BF16)
        slope = up + (0.5 * hidden) * (1.0 - bend * bend) * (
            0.7978845608028654 + 0.7978845608028654 * 3 * 0.044715 * square
        )
        ghid = (gact * slope).astype(BF16)
        ghid_ref[:, cut] = ghid
        gbup_ref[:, cut] = jnp.sum(ghid.astype(F32), axis=0, keepdims=True)
        part = dot_nt(ghid, up_part)
        total = part if total is None else total + part
    gn_ref[...] = total.astype(BF16)


def mix_kernel(plan, parts, *refs):
    refs[-1][...] = dot_nt(joined(refs[:parts]), stacked(refs[parts:-1], plan, slice(None))).astype(BF16)


def back_kernel(lo, plan, order_ref, row_ref, own_ref, other_ref, mid_ref, top_ref, *refs):
    weights, (gmid_ref, gba_ref, gctx_ref, sum_ref) = refs[:-4], refs[-4:]
    last = last_of(order_ref)
    grad = own_ref[...].astype(F32) + other_ref[...].astype(F32)
    normed, inverse = norm_of(expand(mid_ref[...], last))
    gmid = top_ref[lo : lo + mid_ref.shape[0], :].astype(F32) + norm_backward(grad, normed, inverse, row_ref[1:2], last)
    gmid_ref[...] = gmid
    gba = center(gmid)
    low = gba.astype(BF16)
    gba_ref[...] = low
    gctx_ref[...] = dot_nn(low, stacked(weights, plan, slice(0, gctx_ref.shape[1]))).astype(BF16)
    sum_ref[0:1, :] = jnp.sum(grad * normed, axis=0, keepdims=True)
    sum_ref[1:2, :] = jnp.sum(gba, axis=0, keepdims=True)
    sum_ref[2:, :] = jnp.zeros((sum_ref.shape[0] - 2, sum_ref.shape[1]), F32)


def attend_back_kernel(
    len_ref, qkv_ref, lse_ref, *refs
):
    gctx_refs, (gq_ref, gkv_ref, mask_ref, gk_ref, gv_ref) = refs[:-5], refs[-5:]
    rows, own = gq_ref.shape
    write_mask(len_ref, mask_ref)
    unit = unit_of(PAIR)
    scale = jnp.asarray(HD**-0.5, BF16)
    for pair in range(own // PAIR):
        at = pair * PAIR
        keys = qkv_ref[:, own + at : own + at + PAIR]
        values = qkv_ref[:, 2 * own + at : 2 * own + at + PAIR]
        keys_t = dot_nt(unit, keys * scale).astype(BF16)
        gctx = joined(gctx_refs, slice(at, at + PAIR))
        for lo, hi in reversed(row_blocks(rows)):
            size = hi - lo
            both_q = both_heads(qkv_ref[lo:hi, at : at + PAIR] * scale)
            both_g = both_heads(gctx[lo:hi])
            lse = jnp.concatenate(
                [lse_ref[2 * pair : 2 * pair + 1, lo:hi], lse_ref[2 * pair + 1 : 2 * pair + 2, lo:hi]], axis=1
            )
            mask = mask_ref[:hi, lo:hi]
            probs = jnp.exp(dot_nt(keys[:hi], both_q) + jnp.concatenate([mask, mask], axis=1) - lse)
            gprobs = dot_nt(values[:hi], both_g)
            delta = jnp.sum(probs * gprobs, axis=0, keepdims=True)
            gscores = (probs * (gprobs - delta)).astype(BF16)
            gq_ref[lo:hi, at : at + PAIR] = own_rows(dot_nn(keys_t[:, :hi], gscores)).T.astype(BF16)
            gk = dot_nn(gscores, both_q)
            gv = dot_nn(probs.astype(BF16), both_g)
            if hi == rows:
                gk_ref[...] = gk
                gv_ref[...] = gv
            else:
                gk_ref[:hi, :] += gk
                gv_ref[:hi, :] += gv
        gkv_ref[:, at : at + PAIR] = gk_ref[...].astype(BF16)
        gkv_ref[:, own + at : own + at + PAIR] = gv_ref[...].astype(BF16)


def part_kernel(plan, gq_ref, gkv_ref, ent_ref, order_ref, *refs):
    weights, (part_ref, sum_ref, bias_ref) = refs[:-3], refs[-3:]
    own = gq_ref.shape[1]
    part = dot_nt(gq_ref[...], stacked(weights, plan, slice(0, own)))
    part_ref[...] = (part + dot_nt(gkv_ref[...], stacked(weights, plan, slice(own, 3 * own)))).astype(BF16)
    normed, _ = norm_of(expand(ent_ref[...].astype(F32), last_of(order_ref)))
    total = jnp.sum(part_ref[...].astype(F32) * normed, axis=0, keepdims=True)
    sum_ref[...] = total
    bias_ref[:, :own] = jnp.sum(gq_ref[...].astype(F32), axis=0, keepdims=True)
    bias_ref[:, own:] = jnp.sum(gkv_ref[:, own:].astype(F32), axis=0, keepdims=True)


def vector_kernel(parts, order_ref, row_ref, gain_ref, gain_other, bias_ref, *refs):
    sum_refs, gbup_refs, out_ref = refs[:parts], refs[parts:-1], refs[-1]
    width = order_ref.shape[1]
    chooser = chooser_of(order_ref, width)
    sums = sum(ref[0:2] for ref in sum_refs)
    gbup = sum(ref[...] for ref in gbup_refs)
    gain = gain_ref[...] + gain_other[...]
    rows = jnp.concatenate([row_ref[4:5], sums, gain, jnp.zeros((4, width), F32)], axis=0)
    plain = jnp.zeros_like(rows)
    for _ in range(3):
        low = rows.astype(BF16)
        plain = plain + dot_nt(low, chooser)
        rows = rows - low.astype(F32)
    plain = jnp.concatenate([plain[0:4], gbup[:, :width], gbup[:, width:], bias_ref[...], plain[7:8]], axis=0)
    lanes = out_ref.shape[1]
    for r in range(8):
        for j in range(width // lanes):
            at = r * (width // lanes) + j
            out_ref[at : at + 1, :] = plain[r : r + 1, j * lanes : (j + 1) * lanes]


def result_kernel(parts, order_ref, row_ref, *refs):
    mids, (own_ref, other_ref, out_ref) = refs[:parts], refs[parts:]
    last = last_of(order_ref)
    branch = own_ref[...].astype(F32) + other_ref[...].astype(F32) + row_ref[3:4]
    result = (joined(mids) + center(branch) * (1.0 - last)).astype(BF16)
    plain = dot_nt(result, chooser_of(order_ref, order_ref.shape[1]))
    out_ref[...] = plain[:, : out_ref.shape[1]].astype(BF16)


def final_kernel(order_ref, row_ref, own_ref, other_ref, ent_ref, *refs):
    gmids, out_ref = refs[:-1], refs[-1]
    last = last_of(order_ref)
    grad = own_ref[...].astype(F32) + other_ref[...].astype(F32)
    normed, inverse = norm_of(expand(ent_ref[...].astype(F32), last))
    grad = (joined(gmids) + norm_backward(grad, normed, inverse, row_ref[0:1], last)).astype(BF16)
    plain = dot_nt(grad, chooser_of(order_ref, order_ref.shape[1]))
    out_ref[...] = plain[:, : out_ref.shape[1]].astype(BF16)


def pairs_of(refs, counts):
    found, at = [], 0
    for acts, grads in counts:
        found.append((refs[at : at + acts], refs[at + acts : at + acts + grads]))
        at += acts + grads
    return found


def send_kernel(counts, pieces, *refs):
    outs, at = refs[-pieces:], 0
    rows = outs[0].shape[0]
    for acts, grads in pairs_of(refs, counts):
        half = acts[0].shape[1] // 2
        cut = slice(at, at + grads[0].shape[1])
        made = dot_tn(joined(acts, slice(half, None)), joined(grads)).astype(BF16)
        for i, out_ref in enumerate(outs):
            out_ref[:, cut] = made[i * rows : (i + 1) * rows]
        at += grads[0].shape[1]


def keep_kernel(counts, pieces, radix, each, with_far, *refs):
    many = (radix - 1) * each
    far = ()
    if with_far:
        *refs, keep_ref, sems = refs
        far = [refs[-many - 1]]
    else:
        keep_ref = refs[-many - 1]
    send_refs = refs[len(refs) - many :]
    got = joined(refs[-many - 1 - pieces : -many - 1]).astype(F32)
    rows, at = keep_ref.shape[0], 0
    size = rows // each
    found = []
    for acts, grads in pairs_of(refs, counts):
        acts, grads = joined(acts, slice(0, rows * radix)), joined(grads)
        cut = slice(at, at + grads.shape[1])
        keep_ref[:, cut] = dot_tn(acts[:, :rows], grads) + got[:rows, cut]
        at += grads.shape[1]
        found.append((cut, acts, grads))
    out = move(sems, (keep_ref, far[0])) if with_far else []
    for cut, acts, grads in found:
        half = dot_tn(acts[:, rows:], grads) + got[rows:, cut]
        for k, send_ref in enumerate(send_refs):
            send_ref[:, cut] = half[k * size : (k + 1) * size].astype(BF16)
    for copy in out:
        copy.wait()


def sum_far(given, each, refs):
    near, sems = refs[-2 - given : -1], refs[-1]
    got = move(sems, *zip(refs[: 1 + given], near))
    for copy in got:
        copy.wait()
    total = near[0][...]
    for i in range(1, 1 + given, each):
        total = total + joined(near[i : i + each]).astype(F32)
    return total, refs[: -2 - given]


def far_scratch(arrays):
    return [pltpu.VMEM(a.shape, a.dtype) for a in arrays] + [pltpu.SemaphoreType.DMA((len(arrays),))]


def add_kernel(given, each, *refs):
    total = refs[0][...]
    for i in range(1, 1 + given, each):
        total = total + joined(refs[i : i + each]).astype(F32)
    rows = refs[1 + given].shape[0]
    refs[1 + given][...] = total[:rows]
    for k, ref in enumerate(refs[2 + given :]):
        ref[...] = total[(k + 1) * rows : (k + 2) * rows].astype(BF16)


def add_vector_kernel(given, each, *refs):
    vector, refs = refs[0][...].astype(BF16), refs[1:]
    total, refs = sum_far(given, each, refs)
    rows, columns = refs[1 + given].shape
    refs[1 + given][...] = total[:rows]
    for k, ref in enumerate(refs[2 + given :]):
        ref[:, :columns] = total[(k + 1) * rows : (k + 2) * rows].astype(BF16)
        ref[:, columns:] = vector


def finish_kernel(given, vector_ref, keep_ref, *refs):
    got, (*cuts, sum_ref) = refs[:given], refs[given:]
    columns = keep_ref.shape[1]
    total = keep_ref[...]
    parts = [vector_ref[...].astype(BF16).astype(F32)]
    for ref in got:
        total = total + ref[:, :columns].astype(F32)
        parts.append(ref[:, columns:].astype(F32))
    at = 0
    for ref in cuts:
        ref[...] = total[:, at : at + ref.shape[1]]
        at += ref.shape[1]
    while len(parts) > 1:
        parts = [parts[i] + parts[i + 1] for i in range(0, len(parts), 2)]
    sum_ref[...] = parts[0]


def gather_far(shard, count):
    return jnp.concatenate(gather_far_pieces(shard, count), axis=0)


def gather_far_pieces(shard, count):
    pieces = [shard]
    for stride, radix in reversed(phases_of(count)[2:]):
        held = pieces[0] if len(pieces) == 1 else jnp.concatenate(pieces, axis=0)
        pieces = [held] + [swap(held, k * stride) for k in range(1, radix)]
    return pieces


def gather_near(held, count):
    pieces = [held]
    for stride, radix in phases_of(count)[1:2]:
        pieces += [swap(held, k * stride) for k in range(1, radix)]
    return pieces


def plan_of(pieces):
    return tuple((i, 0, piece.shape[0]) for i, piece in enumerate(pieces))


def near_first(shard, count):
    middle = shard.shape[1] // 2
    halves = [shard[:, :middle], shard[:, middle:]]
    if len(phases_of(count)) != 3:
        return halves
    return [piece for pair in zip(*(gather_near(half, count) for half in halves)) for piece in pair]


def then_far(held, count):
    phases = phases_of(count)
    if len(phases) != 3:
        pieces = gather_near(gather_far(held, count), count)
        return pieces, plan_of(pieces + pieces)
    (_, near), (stride, far) = phases[1:]
    rows = held.shape[0] // near
    pieces = [held] + [swap(held, k * stride) for k in range(1, far)]
    plan = [(core * far + z, x * rows, rows) for core in range(2) for x in range(near) for z in range(far)]
    return pieces, tuple(plan)


class Sum:
    def __init__(self, pairs, count, first=4, second=1, far=False):
        self.flat = [a for pair in pairs for parts in pair for a in parts]
        self.counts = tuple((len(acts), len(grads)) for acts, grads in pairs)
        self.phases = phases_of(count)
        self.columns = sum(grads[0].shape[1] for _, grads in pairs)
        self.rows = pairs[0][0][0].shape[1] // 2
        self.each, self.second, self.far = first, second, far
        self.sent = call(
            functools.partial(send_kernel, self.counts, first),
            [shape(self.rows // first, self.columns, BF16)] * first,
            self.flat,
        )
        self.keep = None
        self.got = []

    def go(self):
        (stride, _), self.phases = self.phases[0], self.phases[1:]
        self.got = [swap(piece, (k // self.each + 1) * stride) for k, piece in enumerate(self.sent)]
        return self

    def work(self):
        got = self.got
        if not self.phases:
            total = self.keep
            for piece in got:
                total = total + piece.astype(F32)
            self.keep = total
            return self
        radix = self.phases[0][1]
        self.rows //= radix
        outs = [shape(self.rows, self.columns, F32)]
        if self.keep is None:
            each = self.second if self.rows % (16 * self.second) == 0 else 1
            outs += [shape(self.rows // each, self.columns, BF16)] * ((radix - 1) * each)
            kernel = functools.partial(keep_kernel, self.counts, len(got), radix, each, self.far)
            scratch = [pltpu.VMEM((self.rows, self.columns), F32), pltpu.SemaphoreType.DMA((1,))]
            outs = call(
                kernel, outs, self.flat + got, far_outs=(0,) if self.far else (), scratch=scratch if self.far else ()
            )
        elif self.rows % 16 == 0:
            outs += [shape(self.rows, self.columns, BF16)] * (radix - 1)
            outs = call(functools.partial(add_kernel, len(got), self.each), outs, [self.keep] + got)
            each = 1
        else:
            total = self.keep
            for i in range(0, len(got), self.each):
                total = total + jnp.concatenate(got[i : i + self.each], axis=0).astype(F32)
            parts = [total[k * self.rows : (k + 1) * self.rows] for k in range(radix)]
            outs = [parts[0]] + [part.astype(BF16) for part in parts[1:]]
            each = 1
        self.each = each
        self.keep, *self.sent = outs
        return self

    def end(self):
        while self.phases:
            self.go().work()
        return self.keep


def tie(sums, *arrays):
    flat = list(arrays) + [piece for one in sums for piece in one.got]
    flat = lax.optimization_barrier(tuple(flat))
    at = len(arrays)
    for one in sums:
        one.got = list(flat[at : at + len(one.got)])
        at += len(one.got)
    return flat[: len(arrays)]


def flips_of(phases):
    found = [0]
    for stride, radix in phases:
        found = [k * stride + f for k in range(radix) for f in found]
    return found[1:]


def reduce_all(vector, flips):
    return total_of([vector] + [swap(vector, flip) for flip in flips])


def total_of(parts):
    while len(parts) > 1:
        parts = [parts[i] + parts[i + 1] for i in range(0, len(parts), 2)]
    return parts[0]


def body(
    stream,
    w_query,
    w_key,
    w_value,
    b_query,
    b_value,
    w_out,
    b_out,
    gain_attn,
    w_up,
    b_up,
    w_down,
    b_down,
    gain_mlp,
    cotangent,
    lengths,
):
    rows, inner_width = stream.shape
    count = lax.axis_size("dp")
    me = lax.axis_index("dp")
    rank = lax.axis_index("tensor").astype(jnp.int32).reshape(1, 1)
    shard_rows, own = w_query.shape
    width = shard_rows * count
    units = w_up.shape[1]
    blocks = jnp.array(relative_order(count), jnp.int32)
    order = ((me ^ blocks)[:, None] * shard_rows + jnp.arange(shard_rows, dtype=jnp.int32)).reshape(1, -1)

    shard_qkv = pack([w_query, w_key, w_value])
    qkv_far = gather_far_pieces(shard_qkv, count)
    w_out_t, w_up, shard_dn, order = lax.optimization_barrier((w_out.T, w_up, w_down.T, order, shard_qkv))[:4]
    shard_ou = pack([w_out_t, swap_tensor(w_out_t), w_up])
    ent, top, acts_a, gbm, row = call(
        first_kernel,
        [shape(rows, width, BF16)] * 4 + [shape(8, width, F32)],
        [order, stream, cotangent, gain_attn, gain_mlp, b_out, b_down],
        room=WIDE,
    )
    dn_near = near_first(shard_dn, count)
    flat = lax.optimization_barrier((shard_ou, acts_a, *qkv_far, *dn_near))
    shard_ou, acts_a, qkv_far, dn_near = flat[0], flat[1], flat[2 : 2 + len(qkv_far)], flat[2 + len(qkv_far) :]
    middle_at = (len(qkv_far) + 1) // 2
    halves = [jnp.concatenate(part, axis=0) for part in (qkv_far[:middle_at], qkv_far[middle_at:]) if part]
    qkv_w = [piece for group in zip(*(gather_near(half, count) for half in halves)) for piece in group]
    ou_far = gather_far_pieces(shard_ou, count)

    qkv_w = qkv_w + [swap(piece, 1) for piece in qkv_w]
    plan = plan_of(qkv_w)
    bias_qkv = jnp.concatenate([b_query, jnp.zeros_like(b_query), b_value]).astype(F32)[None]
    qkv, context, lse = call(
        functools.partial(attend_kernel, plan),
        [shape(rows, 3 * own, BF16), shape(rows, own, BF16), shape(8, rows, F32)],
        [lengths, acts_a, bias_qkv] + qkv_w,
        scalars=1,
        scratch=[pltpu.VMEM((rows, rows), F32)],
    )
    context, *ou_far = lax.optimization_barrier((context, *ou_far))
    dn_near = jnp.concatenate([jnp.concatenate(dn_near[i::2], axis=0) for i in range(2)], axis=1)
    ou_far = jnp.concatenate(ou_far, axis=0)
    other_context = [swap_tensor(context)]
    ou_w = gather_near(ou_far, count)
    dn_w, plan_dn = then_far(dn_near, count)
    flat = lax.optimization_barrier((*other_context, *ou_w, *dn_w))
    other_context, ou_w, dn_w = list(flat[:1]), list(flat[1 : 1 + len(ou_w)]), list(flat[1 + len(ou_w) :])
    ou_w = ou_w + [swap(piece, 1) for piece in ou_w]
    plan_ou = plan_of(ou_w)
    dn_w = dn_w + [swap(piece, 1) for piece in dn_w]

    cuts = [(0, rows)]
    bias_up = b_up.astype(F32)[None]
    middle, acts_m, active, ghid, gn, gn_other, gbup = [], [], [], [], [], [], []
    for lo, size in cuts:
        made = call(
            functools.partial(middle_kernel, lo, (plan_ou, plan_dn), len(ou_w)),
            [
                shape(size, width, F32),
                shape(size, width, BF16),
                shape(size, units, BF16),
                shape(size, units, BF16),
                shape(size, width, BF16),
                shape(1, units, F32),
            ],
            [rank, order, row, bias_up, context, *other_context, ent, gbm] + ou_w + dn_w,
            scalars=1,
        )
        for held, new in zip((middle, acts_m, active, ghid, gn, gbup), made):
            held.append(new)
        gn_other.append(swap_tensor(gn[-1]))

    sum_dn = Sum([((gbm,), active)], count).go()
    sum_up = Sum([(acts_m, ghid)], count).go()
    sum_dn.work().go()
    sum_up.work().go()
    (mlp,) = call(
        functools.partial(mix_kernel, plan_dn, len(active)),
        [shape(rows, width, BF16)],
        [after(active[0], sum_up.sent)] + active[1:] + dn_w,
    )
    mlp_other = swap_tensor(mlp)
    sum_dn.work().go()

    gmid, gba, gctx, sums = [], [], [], []
    gn_other[0] = after(gn_other[0], sum_dn.sent, sum_up.sent, mlp)
    for i, (lo, size) in enumerate(cuts):
        made = call(
            functools.partial(back_kernel, lo, plan_ou),
            [shape(size, width, F32), shape(size, width, BF16), shape(size, own, BF16), shape(8, width, F32)],
            [order, row, gn[i], gn_other[i], middle[i], top] + ou_w,
        )
        for held, new in zip((gmid, gba, gctx, sums), made):
            held.append(new)
    gq, gkv = call(
        attend_back_kernel,
        [shape(rows, own, BF16), shape(rows, 2 * own, BF16)],
        [lengths, qkv, lse] + gctx,
        scalars=1,
        scratch=[pltpu.VMEM((rows, rows), F32), pltpu.VMEM((rows, PAIR), F32), pltpu.VMEM((rows, PAIR), F32)],
        cost=LONG,
    )
    gq, gkv = tie([sum_dn, sum_up], gq, gkv)
    sum_last = Sum([(gba, (context,)), ((acts_a,), (gq,)), ((acts_a,), (gkv,))], count, far=len(phases_of(count)) == 3).go()
    sum_last.work().go()
    sum_up.work().go()
    gq, gkv, mlp_other = lax.optimization_barrier((gq, gkv, mlp_other, *sum_last.sent, *sum_up.sent))[:3]
    part, gain, gbias = call(
        functools.partial(part_kernel, plan),
        [shape(rows, width, BF16), shape(1, width, F32), shape(1, 2 * own, F32)],
        [gq, gkv, ent, order] + qkv_w,
        cost=LONG,
    )
    gain_other = swap_tensor(gain)
    part_other = swap_tensor(part)
    (plain,) = call(
        functools.partial(vector_kernel, len(cuts)),
        [shape(8 * width // 128, 128, F32)],
        [order, row, gain, gain_other, gbias] + sums + gbup,
    )
    phases = phases_of(count)
    parts = [plain] + [swap(plain, flip) for flip in flips_of(phases[:2])]
    plain = total_of(list(tie([sum_last, sum_up], *parts)))
    short = len(phases) == 3
    if short:
        block = plain
        given, radix, size = len(sum_last.got), phases[2][1], sum_last.rows // phases[2][1]
        columns = sum_last.columns
        keep, *sent = call(
            functools.partial(add_vector_kernel, given, sum_last.each),
            [shape(size, columns, F32)] + [shape(size, columns + block.shape[1], BF16)] * (radix - 1),
            [block, sum_last.keep] + sum_last.got,
            far=range(1, 2 + given),
            scratch=far_scratch([sum_last.keep] + sum_last.got),
        )
        last_got = [swap(piece, (k + 1) * phases[2][0]) for k, piece in enumerate(sent)]
    else:
        sum_last.work()
        sent = sum_last.sent
        sum_last.go()
        for phase in phases[2:]:
            plain = reduce_all(plain, flips_of([phase]))
    mlp_other = after(mlp_other, sent)
    (out_rows,) = call(
        functools.partial(result_kernel, len(cuts)),
        [shape(rows, inner_width, BF16)],
        [order, row, *middle, mlp, mlp_other],
    )
    part_other, out_rows = lax.optimization_barrier((part_other, out_rows))
    (grad_stream,) = call(
        final_kernel, [shape(rows, inner_width, BF16)], [order, row, part, part_other, ent, *gmid]
    )
    shard_dn_t, shard_up = (one.work().end() for one in (sum_dn, sum_up))
    if short:
        keep, grad_stream = lax.optimization_barrier((keep, grad_stream))
        out_t, grad_q, grad_k, grad_v, block = call(
            functools.partial(finish_kernel, len(last_got)),
            [shape(shard_rows, own, F32)] * 4 + [shape(*block.shape, F32)],
            [block, keep] + last_got,
        )
        plain = block
    else:
        last = sum_last.work().end()
        out_t, grad_q, grad_k, grad_v = (last[:, i * own : (i + 1) * own] for i in range(4))
    plain = plain.reshape(8, width)
    return (
        out_rows,
        grad_stream,
        grad_q,
        grad_k,
        grad_v,
        plain[6, :own],
        plain[6, own:],
        out_t.T,
        plain[2],
        plain[3],
        shard_up,
        plain[4:6].reshape(-1),
        shard_dn_t.T,
        plain[0],
        plain[1],
    )


def solution(mesh):
    return jax.shard_map(
        body,
        mesh=mesh,
        in_specs=(
            P("dp", None),
            P("dp", "tensor"),
            P("dp", "tensor"),
            P("dp", "tensor"),
            P("tensor"),
            P("tensor"),
            P("tensor", "dp"),
            P(),
            P(),
            P("dp", "tensor"),
            P("tensor"),
            P("tensor", "dp"),
            P(),
            P(),
            P("dp", None),
            P("dp", None),
        ),
        out_specs=(
            P("dp", None),
            P("dp", None),
            P("dp", "tensor"),
            P("dp", "tensor"),
            P("dp", "tensor"),
            P("tensor"),
            P("tensor"),
            P("tensor", "dp"),
            P(),
            P(),
            P("dp", "tensor"),
            P("tensor"),
            P("tensor", "dp"),
            P(),
            P(),
        ),
        check_vma=False,
    )
```

```python
import functools

import jax
import jax.numpy as jnp
from jax import lax
from jax.experimental import pallas as pl
from jax.experimental.pallas import tpu as pltpu
from jax.sharding import PartitionSpec as P

HD = 64
PAIR = 2 * HD
STEP = 384
epsilon = 1e-05
ROOM = 12 * 1024 * 1024
LONG = 100_000_000_000
F32 = jnp.float32
BF16 = jnp.bfloat16
VMEM = pl.BlockSpec(memory_space=pltpu.VMEM)
SMEM = pl.BlockSpec(memory_space=pltpu.SMEM)
FAR = pl.BlockSpec(memory_space=pltpu.HBM)


def phases_of(count):
    found, stride = [], 1
    while stride < count:
        rest = count // stride
        radix = 2 if stride == 1 or (rest.bit_length() - 1) % 2 == 1 else 4
        found.append((stride, radix))
        stride *= radix
    return found


def relative_order(count):
    blocks = [0]
    for stride, radix in reversed(phases_of(count)):
        blocks = [b ^ (k * stride) for k in range(radix) for b in blocks]
    return blocks


def swap(array, flip):
    count = lax.axis_size("dp")
    return lax.ppermute(array, "dp", [(i, i ^ flip) for i in range(count)])


def swap_tensor(array):
    count = lax.axis_size("tensor")
    return lax.ppermute(array, "tensor", [(i, i ^ 1) for i in range(count)])


def dot_nn(left, right):
    return lax.dot_general(left, right, (((1,), (0,)), ((), ())), preferred_element_type=F32)


def dot_nt(left, right):
    return lax.dot_general(left, right, (((1,), (1,)), ((), ())), preferred_element_type=F32)


def dot_tn(left, right):
    return lax.dot_general(left, right, (((0,), (0,)), ((), ())), preferred_element_type=F32)


def shape(rows, columns, dtype):
    return jax.ShapeDtypeStruct((rows, columns), dtype)


def after(array, *others):
    return lax.optimization_barrier((array,) + others)[0]


def call(kernel, outs, args, scalars=0, scratch=(), room=ROOM, cost=0, far=(), far_outs=()):
    return pl.pallas_call(
        kernel,
        out_shape=outs,
        in_specs=[SMEM] * scalars + [FAR if i in far else VMEM for i in range(scalars, len(args))],
        out_specs=[FAR if i in far_outs else VMEM for i in range(len(outs))],
        scratch_shapes=list(scratch),
        compiler_params=pltpu.CompilerParams(vmem_limit_bytes=room),
        cost_estimate=pl.CostEstimate(flops=cost, bytes_accessed=1024, transcendentals=0),
    )(*args)


def chooser_of(order_ref, rows):
    place = lax.broadcasted_iota(jnp.int32, (rows, order_ref.shape[1]), 0)
    return (place == order_ref[...]).astype(F32).astype(BF16)


def last_of(order_ref):
    return (order_ref[...] == order_ref.shape[1] - 1).astype(F32)


def expand(rows, last):
    return rows - jnp.sum(rows, axis=1, keepdims=True) * last


def norm_of(full):
    inverse = lax.rsqrt(jnp.mean(full * full, axis=1, keepdims=True) + epsilon)
    return full * inverse, inverse


def norm_backward(grad, normed, inverse, gain, last):
    scaled = grad * gain
    full = inverse * (scaled - normed * jnp.mean(scaled * normed, axis=1, keepdims=True))
    return (full - jnp.sum(full * last, axis=1, keepdims=True)) * (1.0 - last)


def center(rows):
    return rows - jnp.mean(rows, axis=1, keepdims=True)


def pack_kernel(*refs):
    at = 0
    for ref in refs[:-1]:
        refs[-1][:, at : at + ref.shape[1]] = ref[...]
        at += ref.shape[1]


def move(sems, *pairs):
    copies = [pltpu.make_async_copy(source, target, sems.at[i]) for i, (source, target) in enumerate(pairs)]
    for copy in copies:
        copy.start()
    return copies


def pack_far_kernel(*refs):
    *parts, out_ref, sems = refs
    pairs, at = [], 0
    for ref in parts:
        pairs.append((ref, out_ref.at[:, at : at + ref.shape[1]]))
        at += ref.shape[1]
    for copy in move(sems, *pairs):
        copy.wait()


def pack(arrays):
    rows, columns = arrays[0].shape[0], sum(a.shape[1] for a in arrays)
    if rows % 16:
        return call(pack_kernel, [shape(rows, columns, BF16)], arrays)[0]
    return pl.pallas_call(
        pack_far_kernel,
        out_shape=shape(rows, columns, BF16),
        in_specs=[FAR] * len(arrays),
        out_specs=VMEM,
        scratch_shapes=[pltpu.SemaphoreType.DMA((len(arrays),))],
        compiler_params=pltpu.CompilerParams(vmem_limit_bytes=ROOM),
        cost_estimate=pl.CostEstimate(flops=0, bytes_accessed=1024, transcendentals=0),
    )(*arrays)


def joined(refs, columns=slice(None)):
    return refs[0][:, columns] if len(refs) == 1 else jnp.concatenate([ref[:, columns] for ref in refs], axis=0)


def stacked(refs, plan, columns):
    parts = [refs[i][a : a + n, columns] for i, a, n in plan]
    return parts[0] if len(parts) == 1 else jnp.concatenate(parts, axis=0)


def first_kernel(order_ref, stream_ref, cot_ref, *refs):
    vec_refs, (ent_ref, top_ref, acts_ref, gbm_ref, row_ref) = refs[:-5], refs[-5:]
    chooser = chooser_of(order_ref, order_ref.shape[1])
    last = last_of(order_ref)
    plain = [ref[...].astype(F32).reshape(1, -1) for ref in vec_refs]
    rows = dot_nn(jnp.concatenate(plain + plain, axis=0).astype(BF16), chooser)
    inner = stream_ref.shape[1]
    entering = dot_nn(stream_ref[...], chooser[:inner])
    ent_ref[...] = entering.astype(BF16)
    normed, _ = norm_of(expand(entering, last))
    acts_ref[...] = (normed * rows[0:1]).astype(BF16)
    top = dot_nn(cot_ref[...], chooser[:inner])
    top_ref[...] = top.astype(BF16)
    gbm = center(top)
    gbm_ref[...] = gbm.astype(BF16)
    row_ref[:4, :] = rows[:4]
    row_ref[4:5, :] = jnp.sum(gbm, axis=0, keepdims=True)
    row_ref[5:, :] = jnp.zeros((row_ref.shape[0] - 5, row_ref.shape[1]), F32)


def row_blocks(rows):
    return [(i, min(rows, i + STEP)) for i in range(0, rows, STEP)]


def write_mask(len_ref, mask_ref):
    for lo, hi in row_blocks(mask_ref.shape[0]):
        place = lax.broadcasted_iota(jnp.int32, (1, hi - lo), 1) + lo
        first = jnp.zeros_like(place)
        end = jnp.int32(0)
        for j in range(len_ref.shape[1] - 1):
            end = end + len_ref[0, j]
            first = jnp.where(place >= end, end, first)
        key = lax.broadcasted_iota(jnp.int32, (hi, hi - lo), 0)
        mask_ref[:hi, lo:hi] = jnp.where((key >= first) & (key <= place), 0.0, -1e30)


def both_heads(block):
    zero = jnp.zeros_like(block)
    first = lax.broadcasted_iota(jnp.int32, block.shape, 1) < HD
    return jnp.concatenate([jnp.where(first, block, zero), jnp.where(first, zero, block)], axis=0)


def own_rows(both):
    size = both.shape[1] // 2
    row = lax.broadcasted_iota(jnp.int32, (PAIR, size), 0)
    return jnp.where(row < HD, both[:, :size], both[:, size:])


def unit_of(size):
    r = lax.broadcasted_iota(jnp.int32, (size, size), 0)
    c = lax.broadcasted_iota(jnp.int32, (size, size), 1)
    return (r == c).astype(F32).astype(BF16)


def attend_kernel(plan, len_ref, acts_ref, bias_ref, *refs):
    weights, (qkv_ref, ctx_ref, lse_ref, mask_ref) = refs[:-4], refs[-4:]
    rows, own = ctx_ref.shape
    write_mask(len_ref, mask_ref)
    for at in range(0, 3 * own, own):
        cut = slice(at, at + own)
        qkv_ref[:, cut] = (dot_nn(acts_ref[...], stacked(weights, plan, cut)) + bias_ref[:, cut]).astype(BF16)
    unit = unit_of(PAIR)
    scale = jnp.asarray(HD**-0.5, BF16)
    for pair in range(own // PAIR):
        at = pair * PAIR
        keys = qkv_ref[:, own + at : own + at + PAIR]
        values_t = dot_nt(unit, qkv_ref[:, 2 * own + at : 2 * own + at + PAIR]).astype(BF16)
        for lo, hi in row_blocks(rows):
            size = hi - lo
            both = both_heads(qkv_ref[lo:hi, at : at + PAIR] * scale)
            mask = mask_ref[:hi, lo:hi]
            scores = dot_nt(keys[:hi], both) + jnp.concatenate([mask, mask], axis=1)
            peak = jnp.max(scores, axis=0, keepdims=True)
            expo = jnp.exp(scores - peak)
            total = jnp.sum(expo, axis=0, keepdims=True)
            probs = (expo * (1.0 / total)).astype(BF16)
            lse = peak + jnp.log(total)
            lse_ref[2 * pair : 2 * pair + 1, lo:hi] = lse[:, :size]
            lse_ref[2 * pair + 1 : 2 * pair + 2, lo:hi] = lse[:, size:]
            ctx_ref[lo:hi, at : at + PAIR] = own_rows(dot_nn(values_t[:, :hi], probs)).T.astype(BF16)


def middle_kernel(lo, plan, many, rank_ref, order_ref, row_ref, bup_ref, own_ref, other_ref, ent_ref, gbm_ref, *refs):
    weights, downs, (mid_ref, acts_ref, active_ref, ghid_ref, gn_ref, gbup_ref) = refs[:many], refs[many:-6], refs[-6:]
    plan, plan_dn = plan
    rows = slice(lo, lo + mid_ref.shape[0])
    zero = rank_ref[0, 0] == 0
    own = own_ref.shape[1]
    last = last_of(order_ref)

    def ordered(a, b):
        return jnp.where(zero, a, b), jnp.where(zero, b, a)

    first, second = ordered(own_ref[rows, :], other_ref[rows, :])
    w_first, w_second = ordered(stacked(weights, plan, slice(0, own)), stacked(weights, plan, slice(own, 2 * own)))
    branch = dot_nt(first, w_first) + dot_nt(second, w_second) + row_ref[2:3]
    middle = ent_ref[rows, :].astype(F32) + center(branch) * (1.0 - last)
    mid_ref[...] = middle
    normed, _ = norm_of(expand(middle, last))
    acts = (normed * row_ref[1:2]).astype(BF16)
    acts_ref[...] = acts
    gbm = gbm_ref[rows, :]
    units = active_ref.shape[1]
    piece = units // 3
    total = None
    for at in range(0, units, piece):
        cut, cut_up = slice(at, at + piece), slice(2 * own + at, 2 * own + at + piece)
        up_part = stacked(weights, plan, cut_up)
        hidden = dot_nn(acts, up_part) + bup_ref[:, cut]
        gact = dot_nn(gbm, stacked(downs, plan_dn, cut))
        square = hidden * hidden
        bend = jnp.tanh(hidden * (0.7978845608028654 + 0.7978845608028654 * 0.044715 * square))
        up = 0.5 + 0.5 * bend
        active_ref[:, cut] = (hidden * up).astype(BF16)
        slope = up + (0.5 * hidden) * (1.0 - bend * bend) * (
            0.7978845608028654 + 0.7978845608028654 * 3 * 0.044715 * square
        )
        ghid = (gact * slope).astype(BF16)
        ghid_ref[:, cut] = ghid
        gbup_ref[:, cut] = jnp.sum(ghid.astype(F32), axis=0, keepdims=True)
        part = dot_nt(ghid, up_part)
        total = part if total is None else total + part
    gn_ref[...] = total.astype(BF16)


def mix_kernel(plan, parts, *refs):
    refs[-1][...] = dot_nt(joined(refs[:parts]), stacked(refs[parts:-1], plan, slice(None))).astype(BF16)


def back_kernel(lo, plan, order_ref, row_ref, own_ref, other_ref, mid_ref, top_ref, *refs):
    weights, (gmid_ref, gba_ref, gctx_ref, sum_ref) = refs[:-4], refs[-4:]
    last = last_of(order_ref)
    grad = own_ref[...].astype(F32) + other_ref[...].astype(F32)
    normed, inverse = norm_of(expand(mid_ref[...], last))
    gmid = top_ref[lo : lo + mid_ref.shape[0], :].astype(F32) + norm_backward(grad, normed, inverse, row_ref[1:2], last)
    gmid_ref[...] = gmid
    gba = center(gmid)
    low = gba.astype(BF16)
    gba_ref[...] = low
    gctx_ref[...] = dot_nn(low, stacked(weights, plan, slice(0, gctx_ref.shape[1]))).astype(BF16)
    sum_ref[0:1, :] = jnp.sum(grad * normed, axis=0, keepdims=True)
    sum_ref[1:2, :] = jnp.sum(gba, axis=0, keepdims=True)
    sum_ref[2:, :] = jnp.zeros((sum_ref.shape[0] - 2, sum_ref.shape[1]), F32)


def attend_back_kernel(
    len_ref, qkv_ref, lse_ref, *refs
):
    gctx_refs, (gq_ref, gkv_ref, mask_ref, gk_ref, gv_ref) = refs[:-5], refs[-5:]
    rows, own = gq_ref.shape
    write_mask(len_ref, mask_ref)
    unit = unit_of(PAIR)
    scale = jnp.asarray(HD**-0.5, BF16)
    for pair in range(own // PAIR):
        at = pair * PAIR
        keys = qkv_ref[:, own + at : own + at + PAIR]
        values = qkv_ref[:, 2 * own + at : 2 * own + at + PAIR]
        keys_t = dot_nt(unit, keys * scale).astype(BF16)
        gctx = joined(gctx_refs, slice(at, at + PAIR))
        for lo, hi in reversed(row_blocks(rows)):
            size = hi - lo
            both_q = both_heads(qkv_ref[lo:hi, at : at + PAIR] * scale)
            both_g = both_heads(gctx[lo:hi])
            lse = jnp.concatenate(
                [lse_ref[2 * pair : 2 * pair + 1, lo:hi], lse_ref[2 * pair + 1 : 2 * pair + 2, lo:hi]], axis=1
            )
            mask = mask_ref[:hi, lo:hi]
            probs = jnp.exp(dot_nt(keys[:hi], both_q) + jnp.concatenate([mask, mask], axis=1) - lse)
            gprobs = dot_nt(values[:hi], both_g)
            delta = jnp.sum(probs * gprobs, axis=0, keepdims=True)
            gscores = (probs * (gprobs - delta)).astype(BF16)
            gq_ref[lo:hi, at : at + PAIR] = own_rows(dot_nn(keys_t[:, :hi], gscores)).T.astype(BF16)
            gk = dot_nn(gscores, both_q)
            gv = dot_nn(probs.astype(BF16), both_g)
            if hi == rows:
                gk_ref[...] = gk
                gv_ref[...] = gv
            else:
                gk_ref[:hi, :] += gk
                gv_ref[:hi, :] += gv
        gkv_ref[:, at : at + PAIR] = gk_ref[...].astype(BF16)
        gkv_ref[:, own + at : own + at + PAIR] = gv_ref[...].astype(BF16)


def part_kernel(plan, gq_ref, gkv_ref, ent_ref, order_ref, *refs):
    weights, (part_ref, sum_ref, bias_ref) = refs[:-3], refs[-3:]
    own = gq_ref.shape[1]
    part = dot_nt(gq_ref[...], stacked(weights, plan, slice(0, own)))
    part_ref[...] = (part + dot_nt(gkv_ref[...], stacked(weights, plan, slice(own, 3 * own)))).astype(BF16)
    normed, _ = norm_of(expand(ent_ref[...].astype(F32), last_of(order_ref)))
    total = jnp.sum(part_ref[...].astype(F32) * normed, axis=0, keepdims=True)
    sum_ref[...] = total
    bias_ref[:, :own] = jnp.sum(gq_ref[...].astype(F32), axis=0, keepdims=True)
    bias_ref[:, own:] = jnp.sum(gkv_ref[:, own:].astype(F32), axis=0, keepdims=True)


def vector_kernel(parts, order_ref, row_ref, gain_ref, gain_other, bias_ref, *refs):
    sum_refs, gbup_refs, out_ref = refs[:parts], refs[parts:-1], refs[-1]
    width = order_ref.shape[1]
    chooser = chooser_of(order_ref, width)
    sums = sum(ref[0:2] for ref in sum_refs)
    gbup = sum(ref[...] for ref in gbup_refs)
    gain = gain_ref[...] + gain_other[...]
    rows = jnp.concatenate([row_ref[4:5], sums, gain, jnp.zeros((4, width), F32)], axis=0)
    plain = jnp.zeros_like(rows)
    for _ in range(3):
        low = rows.astype(BF16)
        plain = plain + dot_nt(low, chooser)
        rows = rows - low.astype(F32)
    plain = jnp.concatenate([plain[0:4], gbup[:, :width], gbup[:, width:], bias_ref[...], plain[7:8]], axis=0)
    lanes = out_ref.shape[1]
    for r in range(8):
        for j in range(width // lanes):
            at = r * (width // lanes) + j
            out_ref[at : at + 1, :] = plain[r : r + 1, j * lanes : (j + 1) * lanes]


def result_kernel(parts, order_ref, row_ref, *refs):
    mids, (own_ref, other_ref, out_ref) = refs[:parts], refs[parts:]
    last = last_of(order_ref)
    branch = own_ref[...].astype(F32) + other_ref[...].astype(F32) + row_ref[3:4]
    result = (joined(mids) + center(branch) * (1.0 - last)).astype(BF16)
    plain = dot_nt(result, chooser_of(order_ref, order_ref.shape[1]))
    out_ref[...] = plain[:, : out_ref.shape[1]].astype(BF16)


def final_kernel(order_ref, row_ref, own_ref, other_ref, ent_ref, *refs):
    gmids, out_ref = refs[:-1], refs[-1]
    last = last_of(order_ref)
    grad = own_ref[...].astype(F32) + other_ref[...].astype(F32)
    normed, inverse = norm_of(expand(ent_ref[...].astype(F32), last))
    grad = (joined(gmids) + norm_backward(grad, normed, inverse, row_ref[0:1], last)).astype(BF16)
    plain = dot_nt(grad, chooser_of(order_ref, order_ref.shape[1]))
    out_ref[...] = plain[:, : out_ref.shape[1]].astype(BF16)


def pairs_of(refs, counts):
    found, at = [], 0
    for acts, grads in counts:
        found.append((refs[at : at + acts], refs[at + acts : at + acts + grads]))
        at += acts + grads
    return found


def send_kernel(counts, pieces, *refs):
    outs, at = refs[-pieces:], 0
    rows = outs[0].shape[0]
    for acts, grads in pairs_of(refs, counts):
        half = acts[0].shape[1] // 2
        cut = slice(at, at + grads[0].shape[1])
        made = dot_tn(joined(acts, slice(half, None)), joined(grads)).astype(BF16)
        for i, out_ref in enumerate(outs):
            out_ref[:, cut] = made[i * rows : (i + 1) * rows]
        at += grads[0].shape[1]


def keep_kernel(counts, pieces, radix, each, with_far, *refs):
    many = (radix - 1) * each
    far = ()
    if with_far:
        *refs, keep_ref, sems = refs
        far = [refs[-many - 1]]
    else:
        keep_ref = refs[-many - 1]
    send_refs = refs[len(refs) - many :]
    got = joined(refs[-many - 1 - pieces : -many - 1]).astype(F32)
    rows, at = keep_ref.shape[0], 0
    size = rows // each
    found = []
    for acts, grads in pairs_of(refs, counts):
        acts, grads = joined(acts, slice(0, rows * radix)), joined(grads)
        cut = slice(at, at + grads.shape[1])
        keep_ref[:, cut] = dot_tn(acts[:, :rows], grads) + got[:rows, cut]
        at += grads.shape[1]
        found.append((cut, acts, grads))
    out = move(sems, (keep_ref, far[0])) if with_far else []
    for cut, acts, grads in found:
        half = dot_tn(acts[:, rows:], grads) + got[rows:, cut]
        for k, send_ref in enumerate(send_refs):
            send_ref[:, cut] = half[k * size : (k + 1) * size].astype(BF16)
    for copy in out:
        copy.wait()


def sum_far(given, each, refs):
    near, sems = refs[-2 - given : -1], refs[-1]
    got = move(sems, *zip(refs[: 1 + given], near))
    for copy in got:
        copy.wait()
    total = near[0][...]
    for i in range(1, 1 + given, each):
        total = total + joined(near[i : i + each]).astype(F32)
    return total, refs[: -2 - given]


def far_scratch(arrays):
    return [pltpu.VMEM(a.shape, a.dtype) for a in arrays] + [pltpu.SemaphoreType.DMA((len(arrays),))]


def add_kernel(given, each, *refs):
    total = refs[0][...]
    for i in range(1, 1 + given, each):
        total = total + joined(refs[i : i + each]).astype(F32)
    rows = refs[1 + given].shape[0]
    refs[1 + given][...] = total[:rows]
    for k, ref in enumerate(refs[2 + given :]):
        ref[...] = total[(k + 1) * rows : (k + 2) * rows].astype(BF16)


def add_vector_kernel(given, each, *refs):
    vector, refs = refs[0][...].astype(BF16), refs[1:]
    total, refs = sum_far(given, each, refs)
    rows, columns = refs[1 + given].shape
    refs[1 + given][...] = total[:rows]
    for k, ref in enumerate(refs[2 + given :]):
        ref[:, :columns] = total[(k + 1) * rows : (k + 2) * rows].astype(BF16)
        ref[:, columns:] = vector


def finish_kernel(given, vector_ref, keep_ref, *refs):
    got, (*cuts, sum_ref) = refs[:given], refs[given:]
    columns = keep_ref.shape[1]
    total = keep_ref[...]
    parts = [vector_ref[...].astype(BF16).astype(F32)]
    for ref in got:
        total = total + ref[:, :columns].astype(F32)
        parts.append(ref[:, columns:].astype(F32))
    at = 0
    for ref in cuts:
        ref[...] = total[:, at : at + ref.shape[1]]
        at += ref.shape[1]
    while len(parts) > 1:
        parts = [parts[i] + parts[i + 1] for i in range(0, len(parts), 2)]
    sum_ref[...] = parts[0]


def gather_far(shard, count):
    return jnp.concatenate(gather_far_pieces(shard, count), axis=0)


def gather_far_pieces(shard, count):
    pieces = [shard]
    for stride, radix in reversed(phases_of(count)[2:]):
        held = pieces[0] if len(pieces) == 1 else jnp.concatenate(pieces, axis=0)
        pieces = [held] + [swap(held, k * stride) for k in range(1, radix)]
    return pieces


def gather_near(held, count):
    pieces = [held]
    for stride, radix in phases_of(count)[1:2]:
        pieces += [swap(held, k * stride) for k in range(1, radix)]
    return pieces


def plan_of(pieces):
    return tuple((i, 0, piece.shape[0]) for i, piece in enumerate(pieces))


def near_first(shard, count):
    middle = shard.shape[1] // 2
    halves = [shard[:, :middle], shard[:, middle:]]
    if len(phases_of(count)) != 3:
        return halves
    return [piece for pair in zip(*(gather_near(half, count) for half in halves)) for piece in pair]


def then_far(held, count):
    phases = phases_of(count)
    if len(phases) != 3:
        pieces = gather_near(gather_far(held, count), count)
        return pieces, plan_of(pieces + pieces)
    (_, near), (stride, far) = phases[1:]
    rows = held.shape[0] // near
    pieces = [held] + [swap(held, k * stride) for k in range(1, far)]
    plan = [(core * far + z, x * rows, rows) for core in range(2) for x in range(near) for z in range(far)]
    return pieces, tuple(plan)


class Sum:
    def __init__(self, pairs, count, first=4, second=1, far=False):
        self.flat = [a for pair in pairs for parts in pair for a in parts]
        self.counts = tuple((len(acts), len(grads)) for acts, grads in pairs)
        self.phases = phases_of(count)
        self.columns = sum(grads[0].shape[1] for _, grads in pairs)
        self.rows = pairs[0][0][0].shape[1] // 2
        self.each, self.second, self.far = first, second, far
        self.sent = call(
            functools.partial(send_kernel, self.counts, first),
            [shape(self.rows // first, self.columns, BF16)] * first,
            self.flat,
        )
        self.keep = None
        self.got = []

    def go(self):
        (stride, _), self.phases = self.phases[0], self.phases[1:]
        self.got = [swap(piece, (k // self.each + 1) * stride) for k, piece in enumerate(self.sent)]
        return self

    def work(self):
        got = self.got
        if not self.phases:
            total = self.keep
            for piece in got:
                total = total + piece.astype(F32)
            self.keep = total
            return self
        radix = self.phases[0][1]
        self.rows //= radix
        outs = [shape(self.rows, self.columns, F32)]
        if self.keep is None:
            each = self.second if self.rows % (16 * self.second) == 0 else 1
            outs += [shape(self.rows // each, self.columns, BF16)] * ((radix - 1) * each)
            kernel = functools.partial(keep_kernel, self.counts, len(got), radix, each, self.far)
            scratch = [pltpu.VMEM((self.rows, self.columns), F32), pltpu.SemaphoreType.DMA((1,))]
            outs = call(
                kernel, outs, self.flat + got, far_outs=(0,) if self.far else (), scratch=scratch if self.far else ()
            )
        elif self.rows % 16 == 0:
            outs += [shape(self.rows, self.columns, BF16)] * (radix - 1)
            outs = call(functools.partial(add_kernel, len(got), self.each), outs, [self.keep] + got)
            each = 1
        else:
            total = self.keep
            for i in range(0, len(got), self.each):
                total = total + jnp.concatenate(got[i : i + self.each], axis=0).astype(F32)
            parts = [total[k * self.rows : (k + 1) * self.rows] for k in range(radix)]
            outs = [parts[0]] + [part.astype(BF16) for part in parts[1:]]
            each = 1
        self.each = each
        self.keep, *self.sent = outs
        return self

    def end(self):
        while self.phases:
            self.go().work()
        return self.keep


def tie(sums, *arrays):
    flat = list(arrays) + [piece for one in sums for piece in one.got]
    flat = lax.optimization_barrier(tuple(flat))
    at = len(arrays)
    for one in sums:
        one.got = list(flat[at : at + len(one.got)])
        at += len(one.got)
    return flat[: len(arrays)]


def flips_of(phases):
    found = [0]
    for stride, radix in phases:
        found = [k * stride + f for k in range(radix) for f in found]
    return found[1:]


def reduce_all(vector, flips):
    return total_of([vector] + [swap(vector, flip) for flip in flips])


def total_of(parts):
    while len(parts) > 1:
        parts = [parts[i] + parts[i + 1] for i in range(0, len(parts), 2)]
    return parts[0]


def body(
    stream,
    w_query,
    w_key,
    w_value,
    b_query,
    b_value,
    w_out,
    b_out,
    gain_attn,
    w_up,
    b_up,
    w_down,
    b_down,
    gain_mlp,
    cotangent,
    lengths,
):
    rows, inner_width = stream.shape
    count = lax.axis_size("dp")
    me = lax.axis_index("dp")
    rank = lax.axis_index("tensor").astype(jnp.int32).reshape(1, 1)
    shard_rows, own = w_query.shape
    width = shard_rows * count
    units = w_up.shape[1]
    blocks = jnp.array(relative_order(count), jnp.int32)
    order = ((me ^ blocks)[:, None] * shard_rows + jnp.arange(shard_rows, dtype=jnp.int32)).reshape(1, -1)

    shard_qkv = pack([w_query, w_key, w_value])
    qkv_far = gather_far_pieces(shard_qkv, count)
    w_out_t, w_up, shard_dn, order = lax.optimization_barrier((w_out.T, w_up, w_down.T, order, shard_qkv))[:4]
    shard_ou = pack([w_out_t, swap_tensor(w_out_t), w_up])
    ent, top, acts_a, gbm, row = call(
        first_kernel,
        [shape(rows, width, BF16)] * 4 + [shape(8, width, F32)],
        [order, stream, cotangent, gain_attn, gain_mlp, b_out, b_down],
    )
    dn_near = near_first(shard_dn, count)
    flat = lax.optimization_barrier((shard_ou, acts_a, *qkv_far, *dn_near))
    shard_ou, acts_a, qkv_far, dn_near = flat[0], flat[1], flat[2 : 2 + len(qkv_far)], flat[2 + len(qkv_far) :]
    middle_at = (len(qkv_far) + 1) // 2
    halves = [jnp.concatenate(part, axis=0) for part in (qkv_far[:middle_at], qkv_far[middle_at:]) if part]
    qkv_w = [piece for group in zip(*(gather_near(half, count) for half in halves)) for piece in group]
    ou_far = gather_far_pieces(shard_ou, count)

    qkv_w = qkv_w + [swap(piece, 1) for piece in qkv_w]
    plan = plan_of(qkv_w)
    bias_qkv = jnp.concatenate([b_query, jnp.zeros_like(b_query), b_value]).astype(F32)[None]
    qkv, context, lse = call(
        functools.partial(attend_kernel, plan),
        [shape(rows, 3 * own, BF16), shape(rows, own, BF16), shape(8, rows, F32)],
        [lengths, acts_a, bias_qkv] + qkv_w,
        scalars=1,
        scratch=[pltpu.VMEM((rows, rows), F32)],
    )
    context, *ou_far = lax.optimization_barrier((context, *ou_far))
    dn_near = jnp.concatenate([jnp.concatenate(dn_near[i::2], axis=0) for i in range(2)], axis=1)
    ou_far = jnp.concatenate(ou_far, axis=0)
    other_context = [swap_tensor(context)]
    ou_w = gather_near(ou_far, count)
    dn_w, plan_dn = then_far(dn_near, count)
    flat = lax.optimization_barrier((*other_context, *ou_w, *dn_w))
    other_context, ou_w, dn_w = list(flat[:1]), list(flat[1 : 1 + len(ou_w)]), list(flat[1 + len(ou_w) :])
    ou_w = ou_w + [swap(piece, 1) for piece in ou_w]
    plan_ou = plan_of(ou_w)
    dn_w = dn_w + [swap(piece, 1) for piece in dn_w]

    cuts = [(0, rows)]
    bias_up = b_up.astype(F32)[None]
    middle, acts_m, active, ghid, gn, gn_other, gbup = [], [], [], [], [], [], []
    for lo, size in cuts:
        made = call(
            functools.partial(middle_kernel, lo, (plan_ou, plan_dn), len(ou_w)),
            [
                shape(size, width, F32),
                shape(size, width, BF16),
                shape(size, units, BF16),
                shape(size, units, BF16),
                shape(size, width, BF16),
                shape(1, units, F32),
            ],
            [rank, order, row, bias_up, context, *other_context, ent, gbm] + ou_w + dn_w,
            scalars=1,
        )
        for held, new in zip((middle, acts_m, active, ghid, gn, gbup), made):
            held.append(new)
        gn_other.append(swap_tensor(gn[-1]))

    sum_dn = Sum([((gbm,), active)], count).go()
    sum_up = Sum([(acts_m, ghid)], count).go()
    sum_dn.work().go()
    sum_up.work().go()
    (mlp,) = call(
        functools.partial(mix_kernel, plan_dn, len(active)),
        [shape(rows, width, BF16)],
        [after(active[0], sum_up.sent)] + active[1:] + dn_w,
    )
    mlp_other = swap_tensor(mlp)
    sum_dn.work().go()

    gmid, gba, gctx, sums = [], [], [], []
    gn_other[0] = after(gn_other[0], sum_dn.sent, sum_up.sent, mlp)
    for i, (lo, size) in enumerate(cuts):
        made = call(
            functools.partial(back_kernel, lo, plan_ou),
            [shape(size, width, F32), shape(size, width, BF16), shape(size, own, BF16), shape(8, width, F32)],
            [order, row, gn[i], gn_other[i], middle[i], top] + ou_w,
        )
        for held, new in zip((gmid, gba, gctx, sums), made):
            held.append(new)
    gq, gkv = call(
        attend_back_kernel,
        [shape(rows, own, BF16), shape(rows, 2 * own, BF16)],
        [lengths, qkv, lse] + gctx,
        scalars=1,
        scratch=[pltpu.VMEM((rows, rows), F32), pltpu.VMEM((rows, PAIR), F32), pltpu.VMEM((rows, PAIR), F32)],
        cost=LONG,
    )
    gq, gkv = tie([sum_dn, sum_up], gq, gkv)
    sum_last = Sum([(gba, (context,)), ((acts_a,), (gq,)), ((acts_a,), (gkv,))], count, far=len(phases_of(count)) == 3).go()
    sum_last.work().go()
    sum_up.work().go()
    gq, gkv, mlp_other = lax.optimization_barrier((gq, gkv, mlp_other, *sum_last.sent, *sum_up.sent))[:3]
    part, gain, gbias = call(
        functools.partial(part_kernel, plan),
        [shape(rows, width, BF16), shape(1, width, F32), shape(1, 2 * own, F32)],
        [gq, gkv, ent, order] + qkv_w,
        cost=LONG,
    )
    gain_other = swap_tensor(gain)
    part_other = swap_tensor(part)
    (plain,) = call(
        functools.partial(vector_kernel, len(cuts)),
        [shape(8 * width // 128, 128, F32)],
        [order, row, gain, gain_other, gbias] + sums + gbup,
    )
    phases = phases_of(count)
    parts = [plain] + [swap(plain, flip) for flip in flips_of(phases[:2])]
    plain = total_of(list(tie([sum_last, sum_up], *parts)))
    short = len(phases) == 3
    if short:
        block = plain
        given, radix, size = len(sum_last.got), phases[2][1], sum_last.rows // phases[2][1]
        columns = sum_last.columns
        keep, *sent = call(
            functools.partial(add_vector_kernel, given, sum_last.each),
            [shape(size, columns, F32)] + [shape(size, columns + block.shape[1], BF16)] * (radix - 1),
            [block, sum_last.keep] + sum_last.got,
            far=range(1, 2 + given),
            scratch=far_scratch([sum_last.keep] + sum_last.got),
        )
        last_got = [swap(piece, (k + 1) * phases[2][0]) for k, piece in enumerate(sent)]
    else:
        sum_last.work()
        sent = sum_last.sent
        sum_last.go()
        for phase in phases[2:]:
            plain = reduce_all(plain, flips_of([phase]))
    mlp_other = after(mlp_other, sent)
    (out_rows,) = call(
        functools.partial(result_kernel, len(cuts)),
        [shape(rows, inner_width, BF16)],
        [order, row, *middle, mlp, mlp_other],
    )
    part_other, out_rows = lax.optimization_barrier((part_other, out_rows))
    (grad_stream,) = call(
        final_kernel, [shape(rows, inner_width, BF16)], [order, row, part, part_other, ent, *gmid]
    )
    shard_dn_t, shard_up = (one.work().end() for one in (sum_dn, sum_up))
    if short:
        keep, grad_stream = lax.optimization_barrier((keep, grad_stream))
        out_t, grad_q, grad_k, grad_v, block = call(
            functools.partial(finish_kernel, len(last_got)),
            [shape(shard_rows, own, F32)] * 4 + [shape(*block.shape, F32)],
            [block, keep] + last_got,
        )
        plain = block
    else:
        last = sum_last.work().end()
        out_t, grad_q, grad_k, grad_v = (last[:, i * own : (i + 1) * own] for i in range(4))
    plain = plain.reshape(8, width)
    return (
        out_rows,
        grad_stream,
        grad_q,
        grad_k,
        grad_v,
        plain[6, :own],
        plain[6, own:],
        out_t.T,
        plain[2],
        plain[3],
        shard_up,
        plain[4:6].reshape(-1),
        shard_dn_t.T,
        plain[0],
        plain[1],
    )


def solution(mesh):
    return jax.shard_map(
        body,
        mesh=mesh,
        in_specs=(
            P("dp", None),
            P("dp", "tensor"),
            P("dp", "tensor"),
            P("dp", "tensor"),
            P("tensor"),
            P("tensor"),
            P("tensor", "dp"),
            P(),
            P(),
            P("dp", "tensor"),
            P("tensor"),
            P("tensor", "dp"),
            P(),
            P(),
            P("dp", None),
            P("dp", None),
        ),
        out_specs=(
            P("dp", None),
            P("dp", None),
            P("dp", "tensor"),
            P("dp", "tensor"),
            P("dp", "tensor"),
            P("tensor"),
            P("tensor"),
            P("tensor", "dp"),
            P(),
            P(),
            P("dp", "tensor"),
            P("tensor"),
            P("tensor", "dp"),
            P(),
            P(),
        ),
        check_vma=False,
    )
```

```python
import functools

import jax
import jax.numpy as jnp
from jax import lax
from jax.experimental import pallas as pl
from jax.experimental.pallas import tpu as pltpu
from jax.sharding import PartitionSpec as P

HD = 64
PAIR = 2 * HD
STEP = 384
epsilon = 1e-05
ROOM = 10 * 1024 * 1024
LONG = 100_000_000_000
F32 = jnp.float32
BF16 = jnp.bfloat16
VMEM = pl.BlockSpec(memory_space=pltpu.VMEM)
SMEM = pl.BlockSpec(memory_space=pltpu.SMEM)
FAR = pl.BlockSpec(memory_space=pltpu.HBM)


def phases_of(count):
    found, stride = [], 1
    while stride < count:
        rest = count // stride
        radix = 2 if stride == 1 or (rest.bit_length() - 1) % 2 == 1 else 4
        found.append((stride, radix))
        stride *= radix
    return found


def relative_order(count):
    blocks = [0]
    for stride, radix in reversed(phases_of(count)):
        blocks = [b ^ (k * stride) for k in range(radix) for b in blocks]
    return blocks


def swap(array, flip):
    count = lax.axis_size("dp")
    return lax.ppermute(array, "dp", [(i, i ^ flip) for i in range(count)])


def swap_tensor(array):
    count = lax.axis_size("tensor")
    return lax.ppermute(array, "tensor", [(i, i ^ 1) for i in range(count)])


def dot_nn(left, right):
    return lax.dot_general(left, right, (((1,), (0,)), ((), ())), preferred_element_type=F32)


def dot_nt(left, right):
    return lax.dot_general(left, right, (((1,), (1,)), ((), ())), preferred_element_type=F32)


def dot_tn(left, right):
    return lax.dot_general(left, right, (((0,), (0,)), ((), ())), preferred_element_type=F32)


def shape(rows, columns, dtype):
    return jax.ShapeDtypeStruct((rows, columns), dtype)


def after(array, *others):
    return lax.optimization_barrier((array,) + others)[0]


def call(kernel, outs, args, scalars=0, scratch=(), room=ROOM, cost=0, far=(), far_outs=()):
    return pl.pallas_call(
        kernel,
        out_shape=outs,
        in_specs=[SMEM] * scalars + [FAR if i in far else VMEM for i in range(scalars, len(args))],
        out_specs=[FAR if i in far_outs else VMEM for i in range(len(outs))],
        scratch_shapes=list(scratch),
        compiler_params=pltpu.CompilerParams(vmem_limit_bytes=room),
        cost_estimate=pl.CostEstimate(flops=cost, bytes_accessed=1024, transcendentals=0),
    )(*args)


def chooser_of(order_ref, rows):
    place = lax.broadcasted_iota(jnp.int32, (rows, order_ref.shape[1]), 0)
    return (place == order_ref[...]).astype(F32).astype(BF16)


def last_of(order_ref):
    return (order_ref[...] == order_ref.shape[1] - 1).astype(F32)


def expand(rows, last):
    return rows - jnp.sum(rows, axis=1, keepdims=True) * last


def norm_of(full):
    inverse = lax.rsqrt(jnp.mean(full * full, axis=1, keepdims=True) + epsilon)
    return full * inverse, inverse


def norm_backward(grad, normed, inverse, gain, last):
    scaled = grad * gain
    full = inverse * (scaled - normed * jnp.mean(scaled * normed, axis=1, keepdims=True))
    return (full - jnp.sum(full * last, axis=1, keepdims=True)) * (1.0 - last)


def center(rows):
    return rows - jnp.mean(rows, axis=1, keepdims=True)


def pack_kernel(*refs):
    at = 0
    for ref in refs[:-1]:
        refs[-1][:, at : at + ref.shape[1]] = ref[...]
        at += ref.shape[1]


def move(sems, *pairs):
    copies = [pltpu.make_async_copy(source, target, sems.at[i]) for i, (source, target) in enumerate(pairs)]
    for copy in copies:
        copy.start()
    return copies


def pack_far_kernel(*refs):
    *parts, out_ref, sems = refs
    pairs, at = [], 0
    for ref in parts:
        pairs.append((ref, out_ref.at[:, at : at + ref.shape[1]]))
        at += ref.shape[1]
    for copy in move(sems, *pairs):
        copy.wait()


def pack(arrays):
    rows, columns = arrays[0].shape[0], sum(a.shape[1] for a in arrays)
    if rows % 16:
        return call(pack_kernel, [shape(rows, columns, BF16)], arrays)[0]
    return pl.pallas_call(
        pack_far_kernel,
        out_shape=shape(rows, columns, BF16),
        in_specs=[FAR] * len(arrays),
        out_specs=VMEM,
        scratch_shapes=[pltpu.SemaphoreType.DMA((len(arrays),))],
        compiler_params=pltpu.CompilerParams(vmem_limit_bytes=ROOM),
        cost_estimate=pl.CostEstimate(flops=0, bytes_accessed=1024, transcendentals=0),
    )(*arrays)


def joined(refs, columns=slice(None)):
    return refs[0][:, columns] if len(refs) == 1 else jnp.concatenate([ref[:, columns] for ref in refs], axis=0)


def stacked(refs, plan, columns):
    parts = [refs[i][a : a + n, columns] for i, a, n in plan]
    return parts[0] if len(parts) == 1 else jnp.concatenate(parts, axis=0)


def first_kernel(order_ref, stream_ref, gain_ref, ent_ref, acts_ref):
    chooser = chooser_of(order_ref, order_ref.shape[1])
    gain = gain_ref[...].astype(F32).reshape(1, -1)
    gain = dot_nn(jnp.concatenate([gain] * 8, axis=0).astype(BF16), chooser)[0:1]
    entering = dot_nn(stream_ref[...], chooser[: stream_ref.shape[1]])
    ent_ref[...] = entering.astype(BF16)
    normed, _ = norm_of(expand(entering, last_of(order_ref)))
    acts_ref[...] = (normed * gain).astype(BF16)


def prepare_kernel(rank_ref, order_ref, cot_ref, own_ref, other_ref, ent_in, *refs):
    vec_refs, (ctx_ref, ent_ref, top_ref, gbm_ref, row_ref) = refs[:-5], refs[-5:]
    zero = rank_ref[0, 0] == 0
    width = own_ref.shape[1]
    own, other = own_ref[...], other_ref[...]
    ctx_ref[:, :width] = jnp.where(zero, own, other)
    ctx_ref[:, width:] = jnp.where(zero, other, own)
    ent_ref[...] = ent_in[...]
    chooser = chooser_of(order_ref, order_ref.shape[1])
    plain = [ref[...].astype(F32).reshape(1, -1) for ref in vec_refs]
    rows = dot_nn(jnp.concatenate(plain + plain, axis=0).astype(BF16), chooser)
    top = dot_nn(cot_ref[...], chooser[: cot_ref.shape[1]])
    top_ref[...] = top.astype(BF16)
    gbm = center(top)
    gbm_ref[...] = gbm.astype(BF16)
    row_ref[:4, :] = rows[:4]
    row_ref[4:5, :] = jnp.sum(gbm, axis=0, keepdims=True)
    row_ref[5:, :] = jnp.zeros((row_ref.shape[0] - 5, row_ref.shape[1]), F32)


def row_blocks(rows):
    return [(i, min(rows, i + STEP)) for i in range(0, rows, STEP)]


def write_mask(len_ref, mask_ref):
    for lo, hi in row_blocks(mask_ref.shape[0]):
        place = lax.broadcasted_iota(jnp.int32, (1, hi - lo), 1) + lo
        first = jnp.zeros_like(place)
        end = jnp.int32(0)
        for j in range(len_ref.shape[1] - 1):
            end = end + len_ref[0, j]
            first = jnp.where(place >= end, end, first)
        key = lax.broadcasted_iota(jnp.int32, (hi, hi - lo), 0)
        mask_ref[:hi, lo:hi] = jnp.where((key >= first) & (key <= place), 0.0, -1e30)


def both_heads(block):
    zero = jnp.zeros_like(block)
    first = lax.broadcasted_iota(jnp.int32, block.shape, 1) < HD
    return jnp.concatenate([jnp.where(first, block, zero), jnp.where(first, zero, block)], axis=0)


def own_rows(both):
    size = both.shape[1] // 2
    row = lax.broadcasted_iota(jnp.int32, (PAIR, size), 0)
    return jnp.where(row < HD, both[:, :size], both[:, size:])


def unit_of(size):
    r = lax.broadcasted_iota(jnp.int32, (size, size), 0)
    c = lax.broadcasted_iota(jnp.int32, (size, size), 1)
    return (r == c).astype(F32).astype(BF16)


def attend_kernel(plan, len_ref, acts_ref, bias_ref, *refs):
    weights, (qkv_ref, ctx_ref, lse_ref, mask_ref) = refs[:-4], refs[-4:]
    rows, own = ctx_ref.shape
    write_mask(len_ref, mask_ref)
    for at in range(0, 3 * own, own):
        cut = slice(at, at + own)
        qkv_ref[:, cut] = (dot_nn(acts_ref[...], stacked(weights, plan, cut)) + bias_ref[:, cut]).astype(BF16)
    unit = unit_of(PAIR)
    scale = jnp.asarray(HD**-0.5, BF16)
    for pair in range(own // PAIR):
        at = pair * PAIR
        keys = qkv_ref[:, own + at : own + at + PAIR]
        values_t = dot_nt(unit, qkv_ref[:, 2 * own + at : 2 * own + at + PAIR]).astype(BF16)
        for lo, hi in row_blocks(rows):
            size = hi - lo
            both = both_heads(qkv_ref[lo:hi, at : at + PAIR] * scale)
            mask = mask_ref[:hi, lo:hi]
            scores = dot_nt(keys[:hi], both) + jnp.concatenate([mask, mask], axis=1)
            peak = jnp.max(scores, axis=0, keepdims=True)
            expo = jnp.exp(scores - peak)
            total = jnp.sum(expo, axis=0, keepdims=True)
            probs = (expo * (1.0 / total)).astype(BF16)
            lse = peak + jnp.log(total)
            lse_ref[2 * pair : 2 * pair + 1, lo:hi] = lse[:, :size]
            lse_ref[2 * pair + 1 : 2 * pair + 2, lo:hi] = lse[:, size:]
            ctx_ref[lo:hi, at : at + PAIR] = own_rows(dot_nn(values_t[:, :hi], probs)).T.astype(BF16)


def middle_kernel(lo, plan, many, rank_ref, order_ref, row_ref, bup_ref, ctx_ref, ent_ref, gbm_ref, *refs):
    weights, downs, (mid_ref, acts_ref, active_ref, ghid_ref, gn_ref, gbup_ref) = refs[:many], refs[many:-6], refs[-6:]
    plan, plan_dn = plan
    rows = slice(lo, lo + mid_ref.shape[0])
    zero = rank_ref[0, 0] == 0
    own = ctx_ref.shape[1] // 2
    last = last_of(order_ref)

    def ordered(a, b):
        return jnp.where(zero, a, b), jnp.where(zero, b, a)

    w_first, w_second = ordered(stacked(weights, plan, slice(0, own)), stacked(weights, plan, slice(own, 2 * own)))
    branch = dot_nt(ctx_ref[rows, :own], w_first) + dot_nt(ctx_ref[rows, own:], w_second) + row_ref[2:3]
    middle = ent_ref[rows, :].astype(F32) + center(branch) * (1.0 - last)
    mid_ref[...] = middle
    normed, _ = norm_of(expand(middle, last))
    acts = (normed * row_ref[1:2]).astype(BF16)
    acts_ref[...] = acts
    gbm = gbm_ref[rows, :]
    units = active_ref.shape[1]
    piece = units // 3
    total = None
    for at in range(0, units, piece):
        cut, cut_up = slice(at, at + piece), slice(2 * own + at, 2 * own + at + piece)
        up_part = stacked(weights, plan, cut_up)
        hidden = dot_nn(acts, up_part) + bup_ref[:, cut]
        gact = dot_nn(gbm, stacked(downs, plan_dn, cut))
        square = hidden * hidden
        bend = jnp.tanh(hidden * (0.7978845608028654 + 0.7978845608028654 * 0.044715 * square))
        up = 0.5 + 0.5 * bend
        active_ref[:, cut] = (hidden * up).astype(BF16)
        slope = up + (0.5 * hidden) * (1.0 - bend * bend) * (
            0.7978845608028654 + 0.7978845608028654 * 3 * 0.044715 * square
        )
        ghid = (gact * slope).astype(BF16)
        ghid_ref[:, cut] = ghid
        gbup_ref[:, cut] = jnp.sum(ghid.astype(F32), axis=0, keepdims=True)
        part = dot_nt(ghid, up_part)
        total = part if total is None else total + part
    gn_ref[...] = total.astype(BF16)


def mix_kernel(plan, parts, *refs):
    refs[-1][...] = dot_nt(joined(refs[:parts]), stacked(refs[parts:-1], plan, slice(None))).astype(BF16)


def back_kernel(lo, plan, order_ref, row_ref, own_ref, other_ref, mid_ref, top_ref, *refs):
    weights, (gmid_ref, gba_ref, gctx_ref, sum_ref) = refs[:-4], refs[-4:]
    last = last_of(order_ref)
    grad = own_ref[...].astype(F32) + other_ref[...].astype(F32)
    normed, inverse = norm_of(expand(mid_ref[...], last))
    gmid = top_ref[lo : lo + mid_ref.shape[0], :].astype(F32) + norm_backward(grad, normed, inverse, row_ref[1:2], last)
    gmid_ref[...] = gmid
    gba = center(gmid)
    low = gba.astype(BF16)
    gba_ref[...] = low
    gctx_ref[...] = dot_nn(low, stacked(weights, plan, slice(0, gctx_ref.shape[1]))).astype(BF16)
    sum_ref[0:1, :] = jnp.sum(grad * normed, axis=0, keepdims=True)
    sum_ref[1:2, :] = jnp.sum(gba, axis=0, keepdims=True)
    sum_ref[2:, :] = jnp.zeros((sum_ref.shape[0] - 2, sum_ref.shape[1]), F32)


def attend_back_kernel(
    len_ref, qkv_ref, lse_ref, *refs
):
    gctx_refs, (gq_ref, gkv_ref, mask_ref, gk_ref, gv_ref) = refs[:-5], refs[-5:]
    rows, own = gq_ref.shape
    write_mask(len_ref, mask_ref)
    unit = unit_of(PAIR)
    scale = jnp.asarray(HD**-0.5, BF16)
    for pair in range(own // PAIR):
        at = pair * PAIR
        keys = qkv_ref[:, own + at : own + at + PAIR]
        values = qkv_ref[:, 2 * own + at : 2 * own + at + PAIR]
        keys_t = dot_nt(unit, keys * scale).astype(BF16)
        gctx = joined(gctx_refs, slice(at, at + PAIR))
        for lo, hi in reversed(row_blocks(rows)):
            size = hi - lo
            both_q = both_heads(qkv_ref[lo:hi, at : at + PAIR] * scale)
            both_g = both_heads(gctx[lo:hi])
            lse = jnp.concatenate(
                [lse_ref[2 * pair : 2 * pair + 1, lo:hi], lse_ref[2 * pair + 1 : 2 * pair + 2, lo:hi]], axis=1
            )
            mask = mask_ref[:hi, lo:hi]
            probs = jnp.exp(dot_nt(keys[:hi], both_q) + jnp.concatenate([mask, mask], axis=1) - lse)
            gprobs = dot_nt(values[:hi], both_g)
            delta = jnp.sum(probs * gprobs, axis=0, keepdims=True)
            gscores = (probs * (gprobs - delta)).astype(BF16)
            gq_ref[lo:hi, at : at + PAIR] = own_rows(dot_nn(keys_t[:, :hi], gscores)).T.astype(BF16)
            gk = dot_nn(gscores, both_q)
            gv = dot_nn(probs.astype(BF16), both_g)
            if hi == rows:
                gk_ref[...] = gk
                gv_ref[...] = gv
            else:
                gk_ref[:hi, :] += gk
                gv_ref[:hi, :] += gv
        gkv_ref[:, at : at + PAIR] = gk_ref[...].astype(BF16)
        gkv_ref[:, own + at : own + at + PAIR] = gv_ref[...].astype(BF16)


def part_kernel(plan, gq_ref, gkv_ref, ent_ref, order_ref, *refs):
    weights, (part_ref, sum_ref, bias_ref) = refs[:-3], refs[-3:]
    own = gq_ref.shape[1]
    part = dot_nt(gq_ref[...], stacked(weights, plan, slice(0, own)))
    part_ref[...] = (part + dot_nt(gkv_ref[...], stacked(weights, plan, slice(own, 3 * own)))).astype(BF16)
    normed, _ = norm_of(expand(ent_ref[...].astype(F32), last_of(order_ref)))
    total = jnp.sum(part_ref[...].astype(F32) * normed, axis=0, keepdims=True)
    sum_ref[...] = total
    bias_ref[:, :own] = jnp.sum(gq_ref[...].astype(F32), axis=0, keepdims=True)
    bias_ref[:, own:] = jnp.sum(gkv_ref[:, own:].astype(F32), axis=0, keepdims=True)


def vector_kernel(parts, order_ref, row_ref, gain_ref, gain_other, bias_ref, *refs):
    sum_refs, gbup_refs, out_ref = refs[:parts], refs[parts:-1], refs[-1]
    width = order_ref.shape[1]
    chooser = chooser_of(order_ref, width)
    sums = sum(ref[0:2] for ref in sum_refs)
    gbup = sum(ref[...] for ref in gbup_refs)
    gain = gain_ref[...] + gain_other[...]
    rows = jnp.concatenate([row_ref[4:5], sums, gain, jnp.zeros((4, width), F32)], axis=0)
    plain = jnp.zeros_like(rows)
    for _ in range(3):
        low = rows.astype(BF16)
        plain = plain + dot_nt(low, chooser)
        rows = rows - low.astype(F32)
    plain = jnp.concatenate([plain[0:4], gbup[:, :width], gbup[:, width:], bias_ref[...], plain[7:8]], axis=0)
    lanes = out_ref.shape[1]
    for r in range(8):
        for j in range(width // lanes):
            at = r * (width // lanes) + j
            out_ref[at : at + 1, :] = plain[r : r + 1, j * lanes : (j + 1) * lanes]


def result_kernel(parts, order_ref, row_ref, *refs):
    mids, (own_ref, other_ref, out_ref) = refs[:parts], refs[parts:]
    last = last_of(order_ref)
    branch = own_ref[...].astype(F32) + other_ref[...].astype(F32) + row_ref[3:4]
    result = (joined(mids) + center(branch) * (1.0 - last)).astype(BF16)
    plain = dot_nt(result, chooser_of(order_ref, order_ref.shape[1]))
    out_ref[...] = plain[:, : out_ref.shape[1]].astype(BF16)


def final_kernel(order_ref, row_ref, own_ref, other_ref, ent_ref, *refs):
    gmids, out_ref = refs[:-1], refs[-1]
    last = last_of(order_ref)
    grad = own_ref[...].astype(F32) + other_ref[...].astype(F32)
    normed, inverse = norm_of(expand(ent_ref[...].astype(F32), last))
    grad = (joined(gmids) + norm_backward(grad, normed, inverse, row_ref[0:1], last)).astype(BF16)
    plain = dot_nt(grad, chooser_of(order_ref, order_ref.shape[1]))
    out_ref[...] = plain[:, : out_ref.shape[1]].astype(BF16)


def pairs_of(refs, counts):
    found, at = [], 0
    for acts, grads in counts:
        found.append((refs[at : at + acts], refs[at + acts : at + acts + grads]))
        at += acts + grads
    return found


def send_kernel(counts, pieces, *refs):
    outs, at = refs[-pieces:], 0
    rows = outs[0].shape[0]
    for acts, grads in pairs_of(refs, counts):
        half = acts[0].shape[1] // 2
        cut = slice(at, at + grads[0].shape[1])
        made = dot_tn(joined(acts, slice(half, None)), joined(grads)).astype(BF16)
        for i, out_ref in enumerate(outs):
            out_ref[:, cut] = made[i * rows : (i + 1) * rows]
        at += grads[0].shape[1]


def keep_kernel(counts, pieces, radix, each, with_far, *refs):
    many = (radix - 1) * each
    far = ()
    if with_far:
        *refs, keep_ref, sems = refs
        far = [refs[-many - 1]]
    else:
        keep_ref = refs[-many - 1]
    send_refs = refs[len(refs) - many :]
    got = joined(refs[-many - 1 - pieces : -many - 1]).astype(F32)
    rows, at = keep_ref.shape[0], 0
    size = rows // each
    found = []
    for acts, grads in pairs_of(refs, counts):
        acts, grads = joined(acts, slice(0, rows * radix)), joined(grads)
        cut = slice(at, at + grads.shape[1])
        keep_ref[:, cut] = dot_tn(acts[:, :rows], grads) + got[:rows, cut]
        at += grads.shape[1]
        found.append((cut, acts, grads))
    out = move(sems, (keep_ref, far[0])) if with_far else []
    for cut, acts, grads in found:
        half = dot_tn(acts[:, rows:], grads) + got[rows:, cut]
        for k, send_ref in enumerate(send_refs):
            send_ref[:, cut] = half[k * size : (k + 1) * size].astype(BF16)
    for copy in out:
        copy.wait()


def sum_far(given, each, refs):
    near, sems = refs[-2 - given : -1], refs[-1]
    got = move(sems, *zip(refs[: 1 + given], near))
    for copy in got:
        copy.wait()
    total = near[0][...]
    for i in range(1, 1 + given, each):
        total = total + joined(near[i : i + each]).astype(F32)
    return total, refs[: -2 - given]


def far_scratch(arrays):
    return [pltpu.VMEM(a.shape, a.dtype) for a in arrays] + [pltpu.SemaphoreType.DMA((len(arrays),))]


def add_kernel(given, each, *refs):
    total = refs[0][...]
    for i in range(1, 1 + given, each):
        total = total + joined(refs[i : i + each]).astype(F32)
    rows = refs[1 + given].shape[0]
    refs[1 + given][...] = total[:rows]
    for k, ref in enumerate(refs[2 + given :]):
        ref[...] = total[(k + 1) * rows : (k + 2) * rows].astype(BF16)


def add_vector_kernel(given, each, *refs):
    vector, refs = refs[0][...].astype(BF16), refs[1:]
    total, refs = sum_far(given, each, refs)
    rows, columns = refs[1 + given].shape
    refs[1 + given][...] = total[:rows]
    for k, ref in enumerate(refs[2 + given :]):
        ref[:, :columns] = total[(k + 1) * rows : (k + 2) * rows].astype(BF16)
        ref[:, columns:] = vector


def finish_kernel(given, vector_ref, keep_ref, *refs):
    got, (*cuts, sum_ref) = refs[:given], refs[given:]
    columns = keep_ref.shape[1]
    total = keep_ref[...]
    parts = [vector_ref[...].astype(BF16).astype(F32)]
    for ref in got:
        total = total + ref[:, :columns].astype(F32)
        parts.append(ref[:, columns:].astype(F32))
    at = 0
    for ref in cuts:
        ref[...] = total[:, at : at + ref.shape[1]]
        at += ref.shape[1]
    while len(parts) > 1:
        parts = [parts[i] + parts[i + 1] for i in range(0, len(parts), 2)]
    sum_ref[...] = parts[0]


def gather_far(shard, count):
    return jnp.concatenate(gather_far_pieces(shard, count), axis=0)


def gather_far_pieces(shard, count):
    pieces = [shard]
    for stride, radix in reversed(phases_of(count)[2:]):
        held = pieces[0] if len(pieces) == 1 else jnp.concatenate(pieces, axis=0)
        pieces = [held] + [swap(held, k * stride) for k in range(1, radix)]
    return pieces


def gather_near(held, count):
    pieces = [held]
    for stride, radix in phases_of(count)[1:2]:
        pieces += [swap(held, k * stride) for k in range(1, radix)]
    return pieces


def plan_of(pieces):
    return tuple((i, 0, piece.shape[0]) for i, piece in enumerate(pieces))


def near_first(shard, count):
    middle = shard.shape[1] // 2
    halves = [shard[:, :middle], shard[:, middle:]]
    if len(phases_of(count)) != 3:
        return halves
    return [piece for pair in zip(*(gather_near(half, count) for half in halves)) for piece in pair]


def then_far(held, count):
    phases = phases_of(count)
    if len(phases) != 3:
        pieces = gather_near(gather_far(held, count), count)
        return pieces, plan_of(pieces + pieces)
    (_, near), (stride, far) = phases[1:]
    rows = held.shape[0] // near
    pieces = [held] + [swap(held, k * stride) for k in range(1, far)]
    plan = [(core * far + z, x * rows, rows) for core in range(2) for x in range(near) for z in range(far)]
    return pieces, tuple(plan)


class Sum:
    def __init__(self, pairs, count, first=4, second=1, far=False):
        self.flat = [a for pair in pairs for parts in pair for a in parts]
        self.counts = tuple((len(acts), len(grads)) for acts, grads in pairs)
        self.phases = phases_of(count)
        self.columns = sum(grads[0].shape[1] for _, grads in pairs)
        self.rows = pairs[0][0][0].shape[1] // 2
        self.each, self.second, self.far = first, second, far
        self.sent = call(
            functools.partial(send_kernel, self.counts, first),
            [shape(self.rows // first, self.columns, BF16)] * first,
            self.flat,
        )
        self.keep = None
        self.got = []

    def go(self):
        (stride, _), self.phases = self.phases[0], self.phases[1:]
        self.got = [swap(piece, (k // self.each + 1) * stride) for k, piece in enumerate(self.sent)]
        return self

    def work(self):
        got = self.got
        if not self.phases:
            total = self.keep
            for piece in got:
                total = total + piece.astype(F32)
            self.keep = total
            return self
        radix = self.phases[0][1]
        self.rows //= radix
        outs = [shape(self.rows, self.columns, F32)]
        if self.keep is None:
            each = self.second if self.rows % (16 * self.second) == 0 else 1
            outs += [shape(self.rows // each, self.columns, BF16)] * ((radix - 1) * each)
            kernel = functools.partial(keep_kernel, self.counts, len(got), radix, each, self.far)
            scratch = [pltpu.VMEM((self.rows, self.columns), F32), pltpu.SemaphoreType.DMA((1,))]
            outs = call(
                kernel, outs, self.flat + got, far_outs=(0,) if self.far else (), scratch=scratch if self.far else ()
            )
        elif self.rows % 16 == 0:
            outs += [shape(self.rows, self.columns, BF16)] * (radix - 1)
            outs = call(functools.partial(add_kernel, len(got), self.each), outs, [self.keep] + got)
            each = 1
        else:
            total = self.keep
            for i in range(0, len(got), self.each):
                total = total + jnp.concatenate(got[i : i + self.each], axis=0).astype(F32)
            parts = [total[k * self.rows : (k + 1) * self.rows] for k in range(radix)]
            outs = [parts[0]] + [part.astype(BF16) for part in parts[1:]]
            each = 1
        self.each = each
        self.keep, *self.sent = outs
        return self

    def end(self):
        while self.phases:
            self.go().work()
        return self.keep


def tie(sums, *arrays):
    flat = list(arrays) + [piece for one in sums for piece in one.got]
    flat = lax.optimization_barrier(tuple(flat))
    at = len(arrays)
    for one in sums:
        one.got = list(flat[at : at + len(one.got)])
        at += len(one.got)
    return flat[: len(arrays)]


def flips_of(phases):
    found = [0]
    for stride, radix in phases:
        found = [k * stride + f for k in range(radix) for f in found]
    return found[1:]


def reduce_all(vector, flips):
    return total_of([vector] + [swap(vector, flip) for flip in flips])


def total_of(parts):
    while len(parts) > 1:
        parts = [parts[i] + parts[i + 1] for i in range(0, len(parts), 2)]
    return parts[0]


def body(
    stream,
    w_query,
    w_key,
    w_value,
    b_query,
    b_value,
    w_out,
    b_out,
    gain_attn,
    w_up,
    b_up,
    w_down,
    b_down,
    gain_mlp,
    cotangent,
    lengths,
):
    rows, inner_width = stream.shape
    count = lax.axis_size("dp")
    me = lax.axis_index("dp")
    rank = lax.axis_index("tensor").astype(jnp.int32).reshape(1, 1)
    shard_rows, own = w_query.shape
    width = shard_rows * count
    units = w_up.shape[1]
    blocks = jnp.array(relative_order(count), jnp.int32)
    order = ((me ^ blocks)[:, None] * shard_rows + jnp.arange(shard_rows, dtype=jnp.int32)).reshape(1, -1)

    shard_qkv = pack([w_query, w_key, w_value])
    qkv_far = gather_far_pieces(shard_qkv, count)
    w_out_t, w_up, shard_dn, order = lax.optimization_barrier((w_out.T, w_up, w_down.T, order, shard_qkv))[:4]
    shard_ou = pack([w_out_t, swap_tensor(w_out_t), w_up])
    ent, acts_a = call(first_kernel, [shape(rows, width, BF16)] * 2, [order, stream, gain_attn])
    dn_near = near_first(shard_dn, count)
    flat = lax.optimization_barrier((shard_ou, acts_a, *qkv_far, *dn_near))
    shard_ou, acts_a, qkv_far, dn_near = flat[0], flat[1], flat[2 : 2 + len(qkv_far)], flat[2 + len(qkv_far) :]
    middle_at = (len(qkv_far) + 1) // 2
    halves = [jnp.concatenate(part, axis=0) for part in (qkv_far[:middle_at], qkv_far[middle_at:]) if part]
    qkv_w = [piece for group in zip(*(gather_near(half, count) for half in halves)) for piece in group]
    ou_far = gather_far_pieces(shard_ou, count)

    qkv_w = qkv_w + [swap(piece, 1) for piece in qkv_w]
    plan = plan_of(qkv_w)
    bias_qkv = jnp.concatenate([b_query, jnp.zeros_like(b_query), b_value]).astype(F32)[None]
    qkv, context, lse = call(
        functools.partial(attend_kernel, plan),
        [shape(rows, 3 * own, BF16), shape(rows, own, BF16), shape(8, rows, F32)],
        [lengths, acts_a, bias_qkv] + qkv_w,
        scalars=1,
        scratch=[pltpu.VMEM((rows, rows), F32)],
    )
    context, *ou_far = lax.optimization_barrier((context, *ou_far))
    dn_near = jnp.concatenate([jnp.concatenate(dn_near[i::2], axis=0) for i in range(2)], axis=1)
    ou_far = jnp.concatenate(ou_far, axis=0)
    other_context = [swap_tensor(context)]
    ou_w = gather_near(ou_far, count)
    dn_w, plan_dn = then_far(dn_near, count)
    made = call(
        prepare_kernel,
        [shape(rows, width, BF16)] * 4 + [shape(8, width, F32)],
        [rank, order, cotangent, context, *other_context, ent, gain_attn, gain_mlp, b_out, b_down],
        scalars=1,
    )
    flat = lax.optimization_barrier((*made, *ou_w, *dn_w))
    (context_all, ent_mid, top, gbm, row), flat = flat[:5], flat[5:]
    ou_w, dn_w = list(flat[: len(ou_w)]), list(flat[len(ou_w) :])
    ou_w = ou_w + [swap(piece, 1) for piece in ou_w]
    plan_ou = plan_of(ou_w)
    dn_w = dn_w + [swap(piece, 1) for piece in dn_w]

    cuts = [(0, rows)]
    bias_up = b_up.astype(F32)[None]
    middle, acts_m, active, ghid, gn, gn_other, gbup = [], [], [], [], [], [], []
    for lo, size in cuts:
        made = call(
            functools.partial(middle_kernel, lo, (plan_ou, plan_dn), len(ou_w)),
            [
                shape(size, width, F32),
                shape(size, width, BF16),
                shape(size, units, BF16),
                shape(size, units, BF16),
                shape(size, width, BF16),
                shape(1, units, F32),
            ],
            [rank, order, row, bias_up, context_all, ent_mid, gbm] + ou_w + dn_w,
            scalars=1,
        )
        for held, new in zip((middle, acts_m, active, ghid, gn, gbup), made):
            held.append(new)
        gn_other.append(swap_tensor(gn[-1]))

    sum_dn = Sum([((gbm,), active)], count).go()
    sum_up = Sum([(acts_m, ghid)], count).go()
    sum_dn.work().go()
    sum_up.work().go()
    (mlp,) = call(
        functools.partial(mix_kernel, plan_dn, len(active)),
        [shape(rows, width, BF16)],
        [after(active[0], sum_up.sent)] + active[1:] + dn_w,
    )
    mlp_other = swap_tensor(mlp)
    sum_dn.work().go()

    gmid, gba, gctx, sums = [], [], [], []
    gn_other[0] = after(gn_other[0], sum_dn.sent, sum_up.sent, mlp)
    for i, (lo, size) in enumerate(cuts):
        made = call(
            functools.partial(back_kernel, lo, plan_ou),
            [shape(size, width, F32), shape(size, width, BF16), shape(size, own, BF16), shape(8, width, F32)],
            [order, row, gn[i], gn_other[i], middle[i], top] + ou_w,
        )
        for held, new in zip((gmid, gba, gctx, sums), made):
            held.append(new)
    gq, gkv = call(
        attend_back_kernel,
        [shape(rows, own, BF16), shape(rows, 2 * own, BF16)],
        [lengths, qkv, lse] + gctx,
        scalars=1,
        scratch=[pltpu.VMEM((rows, rows), F32), pltpu.VMEM((rows, PAIR), F32), pltpu.VMEM((rows, PAIR), F32)],
        cost=LONG,
    )
    gq, gkv = tie([sum_dn, sum_up], gq, gkv)
    sum_last = Sum([(gba, (context,)), ((acts_a,), (gq,)), ((acts_a,), (gkv,))], count, far=len(phases_of(count)) == 3).go()
    sum_last.work().go()
    sum_up.work().go()
    gq, gkv, mlp_other = lax.optimization_barrier((gq, gkv, mlp_other, *sum_last.sent, *sum_up.sent))[:3]
    part, gain, gbias = call(
        functools.partial(part_kernel, plan),
        [shape(rows, width, BF16), shape(1, width, F32), shape(1, 2 * own, F32)],
        [gq, gkv, ent, order] + qkv_w,
        cost=LONG,
    )
    gain_other = swap_tensor(gain)
    part_other = swap_tensor(part)
    (plain,) = call(
        functools.partial(vector_kernel, len(cuts)),
        [shape(8 * width // 128, 128, F32)],
        [order, row, gain, gain_other, gbias] + sums + gbup,
    )
    phases = phases_of(count)
    parts = [plain] + [swap(plain, flip) for flip in flips_of(phases[:2])]
    plain = total_of(list(tie([sum_last, sum_up], *parts)))
    short = len(phases) == 3
    if short:
        block = plain
        given, radix, size = len(sum_last.got), phases[2][1], sum_last.rows // phases[2][1]
        columns = sum_last.columns
        keep, *sent = call(
            functools.partial(add_vector_kernel, given, sum_last.each),
            [shape(size, columns, F32)] + [shape(size, columns + block.shape[1], BF16)] * (radix - 1),
            [block, sum_last.keep] + sum_last.got,
            far=range(1, 2 + given),
            scratch=far_scratch([sum_last.keep] + sum_last.got),
        )
        last_got = [swap(piece, (k + 1) * phases[2][0]) for k, piece in enumerate(sent)]
    else:
        sum_last.work()
        sent = sum_last.sent
        sum_last.go()
        for phase in phases[2:]:
            plain = reduce_all(plain, flips_of([phase]))
    mlp_other = after(mlp_other, sent)
    (out_rows,) = call(
        functools.partial(result_kernel, len(cuts)),
        [shape(rows, inner_width, BF16)],
        [order, row, *middle, mlp, mlp_other],
    )
    part_other, out_rows = lax.optimization_barrier((part_other, out_rows))
    (grad_stream,) = call(
        final_kernel, [shape(rows, inner_width, BF16)], [order, row, part, part_other, ent, *gmid]
    )
    shard_dn_t, shard_up = (one.work().end() for one in (sum_dn, sum_up))
    if short:
        keep, grad_stream = lax.optimization_barrier((keep, grad_stream))
        out_t, grad_q, grad_k, grad_v, block = call(
            functools.partial(finish_kernel, len(last_got)),
            [shape(shard_rows, own, F32)] * 4 + [shape(*block.shape, F32)],
            [block, keep] + last_got,
        )
        plain = block
    else:
        last = sum_last.work().end()
        out_t, grad_q, grad_k, grad_v = (last[:, i * own : (i + 1) * own] for i in range(4))
    plain = plain.reshape(8, width)
    return (
        out_rows,
        grad_stream,
        grad_q,
        grad_k,
        grad_v,
        plain[6, :own],
        plain[6, own:],
        out_t.T,
        plain[2],
        plain[3],
        shard_up,
        plain[4:6].reshape(-1),
        shard_dn_t.T,
        plain[0],
        plain[1],
    )


def solution(mesh):
    return jax.shard_map(
        body,
        mesh=mesh,
        in_specs=(
            P("dp", None),
            P("dp", "tensor"),
            P("dp", "tensor"),
            P("dp", "tensor"),
            P("tensor"),
            P("tensor"),
            P("tensor", "dp"),
            P(),
            P(),
            P("dp", "tensor"),
            P("tensor"),
            P("tensor", "dp"),
            P(),
            P(),
            P("dp", None),
            P("dp", None),
        ),
        out_specs=(
            P("dp", None),
            P("dp", None),
            P("dp", "tensor"),
            P("dp", "tensor"),
            P("dp", "tensor"),
            P("tensor"),
            P("tensor"),
            P("tensor", "dp"),
            P(),
            P(),
            P("dp", "tensor"),
            P("tensor"),
            P("tensor", "dp"),
            P(),
            P(),
        ),
        check_vma=False,
    )
```

```python
import functools

import jax
import jax.numpy as jnp
from jax import lax
from jax.experimental import pallas as pl
from jax.experimental.pallas import tpu as pltpu
from jax.sharding import PartitionSpec as P

HD = 64
PAIR = 2 * HD
STEP = 384
epsilon = 1e-05
ROOM = 12 * 1024 * 1024
LONG = 100_000_000_000
F32 = jnp.float32
BF16 = jnp.bfloat16
VMEM = pl.BlockSpec(memory_space=pltpu.VMEM)
SMEM = pl.BlockSpec(memory_space=pltpu.SMEM)
FAR = pl.BlockSpec(memory_space=pltpu.HBM)


def phases_of(count):
    found, stride = [], 1
    while stride < count:
        rest = count // stride
        radix = 2 if stride == 1 or (rest.bit_length() - 1) % 2 == 1 else 4
        found.append((stride, radix))
        stride *= radix
    return found


def relative_order(count):
    blocks = [0]
    for stride, radix in reversed(phases_of(count)):
        blocks = [b ^ (k * stride) for k in range(radix) for b in blocks]
    return blocks


def swap(array, flip):
    count = lax.axis_size("dp")
    return lax.ppermute(array, "dp", [(i, i ^ flip) for i in range(count)])


def swap_tensor(array):
    count = lax.axis_size("tensor")
    return lax.ppermute(array, "tensor", [(i, i ^ 1) for i in range(count)])


def dot_nn(left, right):
    return lax.dot_general(left, right, (((1,), (0,)), ((), ())), preferred_element_type=F32)


def dot_nt(left, right):
    return lax.dot_general(left, right, (((1,), (1,)), ((), ())), preferred_element_type=F32)


def dot_tn(left, right):
    return lax.dot_general(left, right, (((0,), (0,)), ((), ())), preferred_element_type=F32)


def shape(rows, columns, dtype):
    return jax.ShapeDtypeStruct((rows, columns), dtype)


def after(array, *others):
    return lax.optimization_barrier((array,) + others)[0]


def call(kernel, outs, args, scalars=0, scratch=(), room=ROOM, cost=0, far=(), far_outs=()):
    return pl.pallas_call(
        kernel,
        out_shape=outs,
        in_specs=[SMEM] * scalars + [FAR if i in far else VMEM for i in range(scalars, len(args))],
        out_specs=[FAR if i in far_outs else VMEM for i in range(len(outs))],
        scratch_shapes=list(scratch),
        compiler_params=pltpu.CompilerParams(vmem_limit_bytes=room),
        cost_estimate=pl.CostEstimate(flops=cost, bytes_accessed=1024, transcendentals=0),
    )(*args)


def chooser_of(order_ref, rows):
    place = lax.broadcasted_iota(jnp.int32, (rows, order_ref.shape[1]), 0)
    return (place == order_ref[...]).astype(F32).astype(BF16)


def last_of(order_ref):
    return (order_ref[...] == order_ref.shape[1] - 1).astype(F32)


def expand(rows, last):
    return rows - jnp.sum(rows, axis=1, keepdims=True) * last


def norm_of(full):
    inverse = lax.rsqrt(jnp.mean(full * full, axis=1, keepdims=True) + epsilon)
    return full * inverse, inverse


def norm_backward(grad, normed, inverse, gain, last):
    scaled = grad * gain
    full = inverse * (scaled - normed * jnp.mean(scaled * normed, axis=1, keepdims=True))
    return (full - jnp.sum(full * last, axis=1, keepdims=True)) * (1.0 - last)


def center(rows):
    return rows - jnp.mean(rows, axis=1, keepdims=True)


def pack_kernel(*refs):
    at = 0
    for ref in refs[:-1]:
        refs[-1][:, at : at + ref.shape[1]] = ref[...]
        at += ref.shape[1]


def move(sems, *pairs):
    copies = [pltpu.make_async_copy(source, target, sems.at[i]) for i, (source, target) in enumerate(pairs)]
    for copy in copies:
        copy.start()
    return copies


def pack_far_kernel(*refs):
    *parts, out_ref, sems = refs
    pairs, at = [], 0
    for ref in parts:
        pairs.append((ref, out_ref.at[:, at : at + ref.shape[1]]))
        at += ref.shape[1]
    for copy in move(sems, *pairs):
        copy.wait()


def pack(arrays):
    rows, columns = arrays[0].shape[0], sum(a.shape[1] for a in arrays)
    if rows % 16:
        return call(pack_kernel, [shape(rows, columns, BF16)], arrays)[0]
    return pl.pallas_call(
        pack_far_kernel,
        out_shape=shape(rows, columns, BF16),
        in_specs=[FAR] * len(arrays),
        out_specs=VMEM,
        scratch_shapes=[pltpu.SemaphoreType.DMA((len(arrays),))],
        compiler_params=pltpu.CompilerParams(vmem_limit_bytes=ROOM),
        cost_estimate=pl.CostEstimate(flops=0, bytes_accessed=1024, transcendentals=0),
    )(*arrays)


def joined(refs, columns=slice(None)):
    return refs[0][:, columns] if len(refs) == 1 else jnp.concatenate([ref[:, columns] for ref in refs], axis=0)


def stacked(refs, plan, columns):
    parts = [refs[i][a : a + n, columns] for i, a, n in plan]
    return parts[0] if len(parts) == 1 else jnp.concatenate(parts, axis=0)


def first_kernel(order_ref, stream_ref, gain_ref, ent_ref, acts_ref):
    chooser = chooser_of(order_ref, order_ref.shape[1])
    gain = gain_ref[...].astype(F32).reshape(1, -1)
    gain = dot_nn(jnp.concatenate([gain] * 8, axis=0).astype(BF16), chooser)[0:1]
    entering = dot_nn(stream_ref[...], chooser[: stream_ref.shape[1]])
    ent_ref[...] = entering.astype(BF16)
    normed, _ = norm_of(expand(entering, last_of(order_ref)))
    acts_ref[...] = (normed * gain).astype(BF16)


def prepare_kernel(rank_ref, order_ref, cot_ref, own_ref, other_ref, ent_in, *refs):
    vec_refs, (ctx_ref, ent_ref, top_ref, gbm_ref, row_ref) = refs[:-5], refs[-5:]
    zero = rank_ref[0, 0] == 0
    width = own_ref.shape[1]
    own, other = own_ref[...], other_ref[...]
    ctx_ref[:, :width] = jnp.where(zero, own, other)
    ctx_ref[:, width:] = jnp.where(zero, other, own)
    ent_ref[...] = ent_in[...]
    chooser = chooser_of(order_ref, order_ref.shape[1])
    plain = [ref[...].astype(F32).reshape(1, -1) for ref in vec_refs]
    rows = dot_nn(jnp.concatenate(plain + plain, axis=0).astype(BF16), chooser)
    top = dot_nn(cot_ref[...], chooser[: cot_ref.shape[1]])
    top_ref[...] = top.astype(BF16)
    gbm = center(top)
    gbm_ref[...] = gbm.astype(BF16)
    row_ref[:4, :] = rows[:4]
    row_ref[4:5, :] = jnp.sum(gbm, axis=0, keepdims=True)
    row_ref[5:, :] = jnp.zeros((row_ref.shape[0] - 5, row_ref.shape[1]), F32)


def row_blocks(rows):
    return [(i, min(rows, i + STEP)) for i in range(0, rows, STEP)]


def write_mask(len_ref, mask_ref):
    for lo, hi in row_blocks(mask_ref.shape[0]):
        place = lax.broadcasted_iota(jnp.int32, (1, hi - lo), 1) + lo
        first = jnp.zeros_like(place)
        end = jnp.int32(0)
        for j in range(len_ref.shape[1] - 1):
            end = end + len_ref[0, j]
            first = jnp.where(place >= end, end, first)
        key = lax.broadcasted_iota(jnp.int32, (hi, hi - lo), 0)
        mask_ref[:hi, lo:hi] = jnp.where((key >= first) & (key <= place), 0.0, -1e30)


def both_heads(block):
    zero = jnp.zeros_like(block)
    first = lax.broadcasted_iota(jnp.int32, block.shape, 1) < HD
    return jnp.concatenate([jnp.where(first, block, zero), jnp.where(first, zero, block)], axis=0)


def own_rows(both):
    size = both.shape[1] // 2
    row = lax.broadcasted_iota(jnp.int32, (PAIR, size), 0)
    return jnp.where(row < HD, both[:, :size], both[:, size:])


def unit_of(size):
    r = lax.broadcasted_iota(jnp.int32, (size, size), 0)
    c = lax.broadcasted_iota(jnp.int32, (size, size), 1)
    return (r == c).astype(F32).astype(BF16)


def attend_kernel(plan, len_ref, acts_ref, bias_ref, *refs):
    weights, (qkv_ref, ctx_ref, lse_ref, mask_ref) = refs[:-4], refs[-4:]
    rows, own = ctx_ref.shape
    write_mask(len_ref, mask_ref)
    for at in range(0, 3 * own, own):
        cut = slice(at, at + own)
        qkv_ref[:, cut] = (dot_nn(acts_ref[...], stacked(weights, plan, cut)) + bias_ref[:, cut]).astype(BF16)
    unit = unit_of(PAIR)
    scale = jnp.asarray(HD**-0.5, BF16)
    for pair in range(own // PAIR):
        at = pair * PAIR
        keys = qkv_ref[:, own + at : own + at + PAIR]
        values_t = dot_nt(unit, qkv_ref[:, 2 * own + at : 2 * own + at + PAIR]).astype(BF16)
        for lo, hi in row_blocks(rows):
            size = hi - lo
            both = both_heads(qkv_ref[lo:hi, at : at + PAIR] * scale)
            mask = mask_ref[:hi, lo:hi]
            scores = dot_nt(keys[:hi], both) + jnp.concatenate([mask, mask], axis=1)
            peak = jnp.max(scores, axis=0, keepdims=True)
            expo = jnp.exp(scores - peak)
            total = jnp.sum(expo, axis=0, keepdims=True)
            probs = (expo * (1.0 / total)).astype(BF16)
            lse = peak + jnp.log(total)
            lse_ref[2 * pair : 2 * pair + 1, lo:hi] = lse[:, :size]
            lse_ref[2 * pair + 1 : 2 * pair + 2, lo:hi] = lse[:, size:]
            ctx_ref[lo:hi, at : at + PAIR] = own_rows(dot_nn(values_t[:, :hi], probs)).T.astype(BF16)


def middle_kernel(lo, plan, many, rank_ref, order_ref, row_ref, bup_ref, ctx_ref, ent_ref, gbm_ref, *refs):
    weights, downs, (mid_ref, acts_ref, active_ref, ghid_ref, gn_ref, gbup_ref) = refs[:many], refs[many:-6], refs[-6:]
    plan, plan_dn = plan
    rows = slice(lo, lo + mid_ref.shape[0])
    zero = rank_ref[0, 0] == 0
    own = ctx_ref.shape[1] // 2
    last = last_of(order_ref)

    def ordered(a, b):
        return jnp.where(zero, a, b), jnp.where(zero, b, a)

    w_first, w_second = ordered(stacked(weights, plan, slice(0, own)), stacked(weights, plan, slice(own, 2 * own)))
    branch = dot_nt(ctx_ref[rows, :own], w_first) + dot_nt(ctx_ref[rows, own:], w_second) + row_ref[2:3]
    middle = ent_ref[rows, :].astype(F32) + center(branch) * (1.0 - last)
    mid_ref[...] = middle
    normed, _ = norm_of(expand(middle, last))
    acts = (normed * row_ref[1:2]).astype(BF16)
    acts_ref[...] = acts
    gbm = gbm_ref[rows, :]
    units = active_ref.shape[1]
    piece = units // 3
    total = None
    for at in range(0, units, piece):
        cut, cut_up = slice(at, at + piece), slice(2 * own + at, 2 * own + at + piece)
        up_part = stacked(weights, plan, cut_up)
        hidden = dot_nn(acts, up_part) + bup_ref[:, cut]
        gact = dot_nn(gbm, stacked(downs, plan_dn, cut))
        square = hidden * hidden
        bend = jnp.tanh(hidden * (0.7978845608028654 + 0.7978845608028654 * 0.044715 * square))
        up = 0.5 + 0.5 * bend
        active_ref[:, cut] = (hidden * up).astype(BF16)
        slope = up + (0.5 * hidden) * (1.0 - bend * bend) * (
            0.7978845608028654 + 0.7978845608028654 * 3 * 0.044715 * square
        )
        ghid = (gact * slope).astype(BF16)
        ghid_ref[:, cut] = ghid
        gbup_ref[:, cut] = jnp.sum(ghid.astype(F32), axis=0, keepdims=True)
        part = dot_nt(ghid, up_part)
        total = part if total is None else total + part
    gn_ref[...] = total.astype(BF16)


def mix_kernel(plan, parts, *refs):
    refs[-1][...] = dot_nt(joined(refs[:parts]), stacked(refs[parts:-1], plan, slice(None))).astype(BF16)


def back_kernel(lo, plan, order_ref, row_ref, own_ref, other_ref, mid_ref, top_ref, *refs):
    weights, (gmid_ref, gba_ref, gctx_ref, sum_ref) = refs[:-4], refs[-4:]
    last = last_of(order_ref)
    grad = own_ref[...].astype(F32) + other_ref[...].astype(F32)
    normed, inverse = norm_of(expand(mid_ref[...], last))
    gmid = top_ref[lo : lo + mid_ref.shape[0], :].astype(F32) + norm_backward(grad, normed, inverse, row_ref[1:2], last)
    gmid_ref[...] = gmid
    gba = center(gmid)
    low = gba.astype(BF16)
    gba_ref[...] = low
    gctx_ref[...] = dot_nn(low, stacked(weights, plan, slice(0, gctx_ref.shape[1]))).astype(BF16)
    sum_ref[0:1, :] = jnp.sum(grad * normed, axis=0, keepdims=True)
    sum_ref[1:2, :] = jnp.sum(gba, axis=0, keepdims=True)
    sum_ref[2:, :] = jnp.zeros((sum_ref.shape[0] - 2, sum_ref.shape[1]), F32)


def attend_back_kernel(
    len_ref, qkv_ref, lse_ref, *refs
):
    gctx_refs, (gq_ref, gkv_ref, mask_ref, gk_ref, gv_ref) = refs[:-5], refs[-5:]
    rows, own = gq_ref.shape
    write_mask(len_ref, mask_ref)
    unit = unit_of(PAIR)
    scale = jnp.asarray(HD**-0.5, BF16)
    for pair in range(own // PAIR):
        at = pair * PAIR
        keys = qkv_ref[:, own + at : own + at + PAIR]
        values = qkv_ref[:, 2 * own + at : 2 * own + at + PAIR]
        keys_t = dot_nt(unit, keys * scale).astype(BF16)
        gctx = joined(gctx_refs, slice(at, at + PAIR))
        for lo, hi in reversed(row_blocks(rows)):
            size = hi - lo
            both_q = both_heads(qkv_ref[lo:hi, at : at + PAIR] * scale)
            both_g = both_heads(gctx[lo:hi])
            lse = jnp.concatenate(
                [lse_ref[2 * pair : 2 * pair + 1, lo:hi], lse_ref[2 * pair + 1 : 2 * pair + 2, lo:hi]], axis=1
            )
            mask = mask_ref[:hi, lo:hi]
            probs = jnp.exp(dot_nt(keys[:hi], both_q) + jnp.concatenate([mask, mask], axis=1) - lse)
            gprobs = dot_nt(values[:hi], both_g)
            delta = jnp.sum(probs * gprobs, axis=0, keepdims=True)
            gscores = (probs * (gprobs - delta)).astype(BF16)
            gq_ref[lo:hi, at : at + PAIR] = own_rows(dot_nn(keys_t[:, :hi], gscores)).T.astype(BF16)
            gk = dot_nn(gscores, both_q)
            gv = dot_nn(probs.astype(BF16), both_g)
            if hi == rows:
                gk_ref[...] = gk
                gv_ref[...] = gv
            else:
                gk_ref[:hi, :] += gk
                gv_ref[:hi, :] += gv
        gkv_ref[:, at : at + PAIR] = gk_ref[...].astype(BF16)
        gkv_ref[:, own + at : own + at + PAIR] = gv_ref[...].astype(BF16)


def part_kernel(plan, gq_ref, gkv_ref, ent_ref, order_ref, *refs):
    weights, (part_ref, sum_ref, bias_ref) = refs[:-3], refs[-3:]
    own = gq_ref.shape[1]
    part = dot_nt(gq_ref[...], stacked(weights, plan, slice(0, own)))
    part_ref[...] = (part + dot_nt(gkv_ref[...], stacked(weights, plan, slice(own, 3 * own)))).astype(BF16)
    normed, _ = norm_of(expand(ent_ref[...].astype(F32), last_of(order_ref)))
    total = jnp.sum(part_ref[...].astype(F32) * normed, axis=0, keepdims=True)
    sum_ref[...] = total
    bias_ref[:, :own] = jnp.sum(gq_ref[...].astype(F32), axis=0, keepdims=True)
    bias_ref[:, own:] = jnp.sum(gkv_ref[:, own:].astype(F32), axis=0, keepdims=True)


def vector_kernel(parts, order_ref, row_ref, gain_ref, gain_other, bias_ref, *refs):
    sum_refs, gbup_refs, out_ref = refs[:parts], refs[parts:-1], refs[-1]
    width = order_ref.shape[1]
    chooser = chooser_of(order_ref, width)
    sums = sum(ref[0:2] for ref in sum_refs)
    gbup = sum(ref[...] for ref in gbup_refs)
    gain = gain_ref[...] + gain_other[...]
    rows = jnp.concatenate([row_ref[4:5], sums, gain, jnp.zeros((4, width), F32)], axis=0)
    plain = jnp.zeros_like(rows)
    for _ in range(3):
        low = rows.astype(BF16)
        plain = plain + dot_nt(low, chooser)
        rows = rows - low.astype(F32)
    plain = jnp.concatenate([plain[0:4], gbup[:, :width], gbup[:, width:], bias_ref[...], plain[7:8]], axis=0)
    lanes = out_ref.shape[1]
    for r in range(8):
        for j in range(width // lanes):
            at = r * (width // lanes) + j
            out_ref[at : at + 1, :] = plain[r : r + 1, j * lanes : (j + 1) * lanes]


def result_kernel(parts, order_ref, row_ref, *refs):
    mids, (own_ref, other_ref, out_ref) = refs[:parts], refs[parts:]
    last = last_of(order_ref)
    branch = own_ref[...].astype(F32) + other_ref[...].astype(F32) + row_ref[3:4]
    result = (joined(mids) + center(branch) * (1.0 - last)).astype(BF16)
    plain = dot_nt(result, chooser_of(order_ref, order_ref.shape[1]))
    out_ref[...] = plain[:, : out_ref.shape[1]].astype(BF16)


def final_kernel(order_ref, row_ref, own_ref, other_ref, ent_ref, *refs):
    gmids, out_ref = refs[:-1], refs[-1]
    last = last_of(order_ref)
    grad = own_ref[...].astype(F32) + other_ref[...].astype(F32)
    normed, inverse = norm_of(expand(ent_ref[...].astype(F32), last))
    grad = (joined(gmids) + norm_backward(grad, normed, inverse, row_ref[0:1], last)).astype(BF16)
    plain = dot_nt(grad, chooser_of(order_ref, order_ref.shape[1]))
    out_ref[...] = plain[:, : out_ref.shape[1]].astype(BF16)


def pairs_of(refs, counts):
    found, at = [], 0
    for acts, grads in counts:
        found.append((refs[at : at + acts], refs[at + acts : at + acts + grads]))
        at += acts + grads
    return found


def send_kernel(counts, pieces, *refs):
    outs, at = refs[-pieces:], 0
    rows = outs[0].shape[0]
    for acts, grads in pairs_of(refs, counts):
        half = acts[0].shape[1] // 2
        cut = slice(at, at + grads[0].shape[1])
        made = dot_tn(joined(acts, slice(half, None)), joined(grads)).astype(BF16)
        for i, out_ref in enumerate(outs):
            out_ref[:, cut] = made[i * rows : (i + 1) * rows]
        at += grads[0].shape[1]


def keep_kernel(counts, pieces, radix, each, with_far, *refs):
    many = (radix - 1) * each
    far = ()
    if with_far:
        *refs, keep_ref, sems = refs
        far = [refs[-many - 1]]
    else:
        keep_ref = refs[-many - 1]
    send_refs = refs[len(refs) - many :]
    got = joined(refs[-many - 1 - pieces : -many - 1]).astype(F32)
    rows, at = keep_ref.shape[0], 0
    size = rows // each
    found = []
    for acts, grads in pairs_of(refs, counts):
        acts, grads = joined(acts, slice(0, rows * radix)), joined(grads)
        cut = slice(at, at + grads.shape[1])
        keep_ref[:, cut] = dot_tn(acts[:, :rows], grads) + got[:rows, cut]
        at += grads.shape[1]
        found.append((cut, acts, grads))
    out = move(sems, (keep_ref, far[0])) if with_far else []
    for cut, acts, grads in found:
        half = dot_tn(acts[:, rows:], grads) + got[rows:, cut]
        for k, send_ref in enumerate(send_refs):
            send_ref[:, cut] = half[k * size : (k + 1) * size].astype(BF16)
    for copy in out:
        copy.wait()


def sum_far(given, each, refs):
    near, sems = refs[-2 - given : -1], refs[-1]
    got = move(sems, *zip(refs[: 1 + given], near))
    for copy in got:
        copy.wait()
    total = near[0][...]
    for i in range(1, 1 + given, each):
        total = total + joined(near[i : i + each]).astype(F32)
    return total, refs[: -2 - given]


def far_scratch(arrays):
    return [pltpu.VMEM(a.shape, a.dtype) for a in arrays] + [pltpu.SemaphoreType.DMA((len(arrays),))]


def add_kernel(given, each, *refs):
    total = refs[0][...]
    for i in range(1, 1 + given, each):
        total = total + joined(refs[i : i + each]).astype(F32)
    rows = refs[1 + given].shape[0]
    refs[1 + given][...] = total[:rows]
    for k, ref in enumerate(refs[2 + given :]):
        ref[...] = total[(k + 1) * rows : (k + 2) * rows].astype(BF16)


def add_vector_kernel(given, each, *refs):
    vector, refs = refs[0][...].astype(BF16), refs[1:]
    total, refs = sum_far(given, each, refs)
    rows, columns = refs[1 + given].shape
    refs[1 + given][...] = total[:rows]
    for k, ref in enumerate(refs[2 + given :]):
        ref[:, :columns] = total[(k + 1) * rows : (k + 2) * rows].astype(BF16)
        ref[:, columns:] = vector


def finish_kernel(given, vector_ref, keep_ref, *refs):
    got, (*cuts, sum_ref) = refs[:given], refs[given:]
    columns = keep_ref.shape[1]
    total = keep_ref[...]
    parts = [vector_ref[...].astype(BF16).astype(F32)]
    for ref in got:
        total = total + ref[:, :columns].astype(F32)
        parts.append(ref[:, columns:].astype(F32))
    at = 0
    for ref in cuts:
        ref[...] = total[:, at : at + ref.shape[1]]
        at += ref.shape[1]
    while len(parts) > 1:
        parts = [parts[i] + parts[i + 1] for i in range(0, len(parts), 2)]
    sum_ref[...] = parts[0]


def gather_far(shard, count):
    return jnp.concatenate(gather_far_pieces(shard, count), axis=0)


def gather_far_pieces(shard, count):
    pieces = [shard]
    for stride, radix in reversed(phases_of(count)[2:]):
        held = pieces[0] if len(pieces) == 1 else jnp.concatenate(pieces, axis=0)
        pieces = [held] + [swap(held, k * stride) for k in range(1, radix)]
    return pieces


def gather_near(held, count):
    pieces = [held]
    for stride, radix in phases_of(count)[1:2]:
        pieces += [swap(held, k * stride) for k in range(1, radix)]
    return pieces


def plan_of(pieces):
    return tuple((i, 0, piece.shape[0]) for i, piece in enumerate(pieces))


def near_first(shard, count):
    middle = shard.shape[1] // 2
    halves = [shard[:, :middle], shard[:, middle:]]
    if len(phases_of(count)) != 3:
        return halves
    return [piece for pair in zip(*(gather_near(half, count) for half in halves)) for piece in pair]


def then_far(held, count):
    phases = phases_of(count)
    if len(phases) != 3:
        pieces = gather_near(gather_far(held, count), count)
        return pieces, plan_of(pieces + pieces)
    (_, near), (stride, far) = phases[1:]
    rows = held.shape[0] // near
    pieces = [held] + [swap(held, k * stride) for k in range(1, far)]
    plan = [(core * far + z, x * rows, rows) for core in range(2) for x in range(near) for z in range(far)]
    return pieces, tuple(plan)


class Sum:
    def __init__(self, pairs, count, first=4, second=1, far=False):
        self.flat = [a for pair in pairs for parts in pair for a in parts]
        self.counts = tuple((len(acts), len(grads)) for acts, grads in pairs)
        self.phases = phases_of(count)
        self.columns = sum(grads[0].shape[1] for _, grads in pairs)
        self.rows = pairs[0][0][0].shape[1] // 2
        self.each, self.second, self.far = first, second, far
        self.sent = call(
            functools.partial(send_kernel, self.counts, first),
            [shape(self.rows // first, self.columns, BF16)] * first,
            self.flat,
        )
        self.keep = None
        self.got = []

    def go(self):
        (stride, _), self.phases = self.phases[0], self.phases[1:]
        self.got = [swap(piece, (k // self.each + 1) * stride) for k, piece in enumerate(self.sent)]
        return self

    def work(self):
        got = self.got
        if not self.phases:
            total = self.keep
            for piece in got:
                total = total + piece.astype(F32)
            self.keep = total
            return self
        radix = self.phases[0][1]
        self.rows //= radix
        outs = [shape(self.rows, self.columns, F32)]
        if self.keep is None:
            each = self.second if self.rows % (16 * self.second) == 0 else 1
            outs += [shape(self.rows // each, self.columns, BF16)] * ((radix - 1) * each)
            kernel = functools.partial(keep_kernel, self.counts, len(got), radix, each, self.far)
            scratch = [pltpu.VMEM((self.rows, self.columns), F32), pltpu.SemaphoreType.DMA((1,))]
            outs = call(
                kernel, outs, self.flat + got, far_outs=(0,) if self.far else (), scratch=scratch if self.far else ()
            )
        elif self.rows % 16 == 0:
            outs += [shape(self.rows, self.columns, BF16)] * (radix - 1)
            outs = call(functools.partial(add_kernel, len(got), self.each), outs, [self.keep] + got)
            each = 1
        else:
            total = self.keep
            for i in range(0, len(got), self.each):
                total = total + jnp.concatenate(got[i : i + self.each], axis=0).astype(F32)
            parts = [total[k * self.rows : (k + 1) * self.rows] for k in range(radix)]
            outs = [parts[0]] + [part.astype(BF16) for part in parts[1:]]
            each = 1
        self.each = each
        self.keep, *self.sent = outs
        return self

    def end(self):
        while self.phases:
            self.go().work()
        return self.keep


def tie(sums, *arrays):
    flat = list(arrays) + [piece for one in sums for piece in one.got]
    flat = lax.optimization_barrier(tuple(flat))
    at = len(arrays)
    for one in sums:
        one.got = list(flat[at : at + len(one.got)])
        at += len(one.got)
    return flat[: len(arrays)]


def flips_of(phases):
    found = [0]
    for stride, radix in phases:
        found = [k * stride + f for k in range(radix) for f in found]
    return found[1:]


def reduce_all(vector, flips):
    return total_of([vector] + [swap(vector, flip) for flip in flips])


def total_of(parts):
    while len(parts) > 1:
        parts = [parts[i] + parts[i + 1] for i in range(0, len(parts), 2)]
    return parts[0]


def body(
    stream,
    w_query,
    w_key,
    w_value,
    b_query,
    b_value,
    w_out,
    b_out,
    gain_attn,
    w_up,
    b_up,
    w_down,
    b_down,
    gain_mlp,
    cotangent,
    lengths,
):
    rows, inner_width = stream.shape
    count = lax.axis_size("dp")
    me = lax.axis_index("dp")
    rank = lax.axis_index("tensor").astype(jnp.int32).reshape(1, 1)
    shard_rows, own = w_query.shape
    width = shard_rows * count
    units = w_up.shape[1]
    blocks = jnp.array(relative_order(count), jnp.int32)
    order = ((me ^ blocks)[:, None] * shard_rows + jnp.arange(shard_rows, dtype=jnp.int32)).reshape(1, -1)

    shard_qkv = pack([w_query, w_key, w_value])
    qkv_far = gather_far_pieces(shard_qkv, count)
    w_out_t, w_up, shard_dn, order = lax.optimization_barrier((w_out.T, w_up, w_down.T, order, shard_qkv))[:4]
    shard_ou = pack([w_out_t, swap_tensor(w_out_t), w_up])
    ent, acts_a = call(first_kernel, [shape(rows, width, BF16)] * 2, [order, stream, gain_attn])
    dn_near = near_first(shard_dn, count)
    flat = lax.optimization_barrier((shard_ou, acts_a, *qkv_far, *dn_near))
    shard_ou, acts_a, qkv_far, dn_near = flat[0], flat[1], flat[2 : 2 + len(qkv_far)], flat[2 + len(qkv_far) :]
    middle_at = (len(qkv_far) + 1) // 2
    halves = [jnp.concatenate(part, axis=0) for part in (qkv_far[:middle_at], qkv_far[middle_at:]) if part]
    qkv_w = [piece for group in zip(*(gather_near(half, count) for half in halves)) for piece in group]
    ou_far = gather_far_pieces(shard_ou, count)

    qkv_w = qkv_w + [swap(piece, 1) for piece in qkv_w]
    plan = plan_of(qkv_w)
    bias_qkv = jnp.concatenate([b_query, jnp.zeros_like(b_query), b_value]).astype(F32)[None]
    qkv, context, lse = call(
        functools.partial(attend_kernel, plan),
        [shape(rows, 3 * own, BF16), shape(rows, own, BF16), shape(8, rows, F32)],
        [lengths, acts_a, bias_qkv] + qkv_w,
        scalars=1,
        scratch=[pltpu.VMEM((rows, rows), F32)],
    )
    context, *ou_far = lax.optimization_barrier((context, *ou_far))
    dn_near = jnp.concatenate([jnp.concatenate(dn_near[i::2], axis=0) for i in range(2)], axis=1)
    ou_far = jnp.concatenate(ou_far, axis=0)
    other_context = [swap_tensor(context)]
    ou_w = gather_near(ou_far, count)
    dn_w, plan_dn = then_far(dn_near, count)
    made = call(
        prepare_kernel,
        [shape(rows, width, BF16)] * 4 + [shape(8, width, F32)],
        [rank, order, cotangent, context, *other_context, ent, gain_attn, gain_mlp, b_out, b_down],
        scalars=1,
    )
    flat = lax.optimization_barrier((*made, *ou_w, *dn_w))
    (context_all, ent_mid, top, gbm, row), flat = flat[:5], flat[5:]
    ou_w, dn_w = list(flat[: len(ou_w)]), list(flat[len(ou_w) :])
    ou_w = ou_w + [swap(piece, 1) for piece in ou_w]
    plan_ou = plan_of(ou_w)
    dn_w = dn_w + [swap(piece, 1) for piece in dn_w]

    cuts = [(0, rows)]
    bias_up = b_up.astype(F32)[None]
    middle, acts_m, active, ghid, gn, gn_other, gbup = [], [], [], [], [], [], []
    for lo, size in cuts:
        made = call(
            functools.partial(middle_kernel, lo, (plan_ou, plan_dn), len(ou_w)),
            [
                shape(size, width, F32),
                shape(size, width, BF16),
                shape(size, units, BF16),
                shape(size, units, BF16),
                shape(size, width, BF16),
                shape(1, units, F32),
            ],
            [rank, order, row, bias_up, context_all, ent_mid, gbm] + ou_w + dn_w,
            scalars=1,
        )
        for held, new in zip((middle, acts_m, active, ghid, gn, gbup), made):
            held.append(new)
        gn_other.append(swap_tensor(gn[-1]))

    sum_dn = Sum([((gbm,), active)], count).go()
    sum_up = Sum([(acts_m, ghid)], count).go()
    sum_dn.work().go()
    sum_up.work().go()
    (mlp,) = call(
        functools.partial(mix_kernel, plan_dn, len(active)),
        [shape(rows, width, BF16)],
        [after(active[0], sum_up.sent)] + active[1:] + dn_w,
    )
    mlp_other = swap_tensor(mlp)
    sum_dn.work().go()

    gmid, gba, gctx, sums = [], [], [], []
    gn_other[0] = after(gn_other[0], sum_dn.sent, sum_up.sent, mlp)
    for i, (lo, size) in enumerate(cuts):
        made = call(
            functools.partial(back_kernel, lo, plan_ou),
            [shape(size, width, F32), shape(size, width, BF16), shape(size, own, BF16), shape(8, width, F32)],
            [order, row, gn[i], gn_other[i], middle[i], top] + ou_w,
        )
        for held, new in zip((gmid, gba, gctx, sums), made):
            held.append(new)
    gq, gkv = call(
        attend_back_kernel,
        [shape(rows, own, BF16), shape(rows, 2 * own, BF16)],
        [lengths, qkv, lse] + gctx,
        scalars=1,
        scratch=[pltpu.VMEM((rows, rows), F32), pltpu.VMEM((rows, PAIR), F32), pltpu.VMEM((rows, PAIR), F32)],
        cost=LONG,
    )
    gq, gkv = tie([sum_dn, sum_up], gq, gkv)
    sum_last = Sum([(gba, (context,)), ((acts_a,), (gq,)), ((acts_a,), (gkv,))], count, far=len(phases_of(count)) == 3).go()
    sum_last.work().go()
    sum_up.work().go()
    gq, gkv, mlp_other = lax.optimization_barrier((gq, gkv, mlp_other, *sum_last.sent, *sum_up.sent))[:3]
    part, gain, gbias = call(
        functools.partial(part_kernel, plan),
        [shape(rows, width, BF16), shape(1, width, F32), shape(1, 2 * own, F32)],
        [gq, gkv, ent, order] + qkv_w,
        cost=LONG,
    )
    gain_other = swap_tensor(gain)
    part_other = swap_tensor(part)
    (plain,) = call(
        functools.partial(vector_kernel, len(cuts)),
        [shape(8 * width // 128, 128, F32)],
        [order, row, gain, gain_other, gbias] + sums + gbup,
    )
    phases = phases_of(count)
    parts = [plain] + [swap(plain, flip) for flip in flips_of(phases[:2])]
    plain = total_of(list(tie([sum_last, sum_up], *parts)))
    short = len(phases) == 3
    if short:
        block = plain
        given, radix, size = len(sum_last.got), phases[2][1], sum_last.rows // phases[2][1]
        columns = sum_last.columns
        keep, *sent = call(
            functools.partial(add_vector_kernel, given, sum_last.each),
            [shape(size, columns, F32)] + [shape(size, columns + block.shape[1], BF16)] * (radix - 1),
            [block, sum_last.keep] + sum_last.got,
            far=range(1, 2 + given),
            scratch=far_scratch([sum_last.keep] + sum_last.got),
        )
        last_got = [swap(piece, (k + 1) * phases[2][0]) for k, piece in enumerate(sent)]
    else:
        sum_last.work()
        sent = sum_last.sent
        sum_last.go()
        for phase in phases[2:]:
            plain = reduce_all(plain, flips_of([phase]))
    mlp_other = after(mlp_other, sent)
    (out_rows,) = call(
        functools.partial(result_kernel, len(cuts)),
        [shape(rows, inner_width, BF16)],
        [order, row, *middle, mlp, mlp_other],
    )
    part_other, out_rows = lax.optimization_barrier((part_other, out_rows))
    (grad_stream,) = call(
        final_kernel, [shape(rows, inner_width, BF16)], [order, row, part, part_other, ent, *gmid]
    )
    shard_dn_t, shard_up = (one.work().end() for one in (sum_dn, sum_up))
    if short:
        keep, grad_stream = lax.optimization_barrier((keep, grad_stream))
        out_t, grad_q, grad_k, grad_v, block = call(
            functools.partial(finish_kernel, len(last_got)),
            [shape(shard_rows, own, F32)] * 4 + [shape(*block.shape, F32)],
            [block, keep] + last_got,
        )
        plain = block
    else:
        last = sum_last.work().end()
        out_t, grad_q, grad_k, grad_v = (last[:, i * own : (i + 1) * own] for i in range(4))
    plain = plain.reshape(8, width)
    return (
        out_rows,
        grad_stream,
        grad_q,
        grad_k,
        grad_v,
        plain[6, :own],
        plain[6, own:],
        out_t.T,
        plain[2],
        plain[3],
        shard_up,
        plain[4:6].reshape(-1),
        shard_dn_t.T,
        plain[0],
        plain[1],
    )


def solution(mesh):
    return jax.shard_map(
        body,
        mesh=mesh,
        in_specs=(
            P("dp", None),
            P("dp", "tensor"),
            P("dp", "tensor"),
            P("dp", "tensor"),
            P("tensor"),
            P("tensor"),
            P("tensor", "dp"),
            P(),
            P(),
            P("dp", "tensor"),
            P("tensor"),
            P("tensor", "dp"),
            P(),
            P(),
            P("dp", None),
            P("dp", None),
        ),
        out_specs=(
            P("dp", None),
            P("dp", None),
            P("dp", "tensor"),
            P("dp", "tensor"),
            P("dp", "tensor"),
            P("tensor"),
            P("tensor"),
            P("tensor", "dp"),
            P(),
            P(),
            P("dp", "tensor"),
            P("tensor"),
            P("tensor", "dp"),
            P(),
            P(),
        ),
        check_vma=False,
    )
```

```python
import functools

import jax
import jax.numpy as jnp
from jax import lax
from jax.experimental import pallas as pl
from jax.experimental.pallas import tpu as pltpu
from jax.sharding import PartitionSpec as P

HD = 64
PAIR = 2 * HD
STEP = 384
epsilon = 1e-05
ROOM = 10 * 1024 * 1024
LONG = 100_000_000_000
F32 = jnp.float32
BF16 = jnp.bfloat16
VMEM = pl.BlockSpec(memory_space=pltpu.VMEM)
SMEM = pl.BlockSpec(memory_space=pltpu.SMEM)
FAR = pl.BlockSpec(memory_space=pltpu.HBM)


def phases_of(count):
    found, stride = [], 1
    while stride < count:
        rest = count // stride
        radix = 2 if stride == 1 or (rest.bit_length() - 1) % 2 == 1 else 4
        found.append((stride, radix))
        stride *= radix
    return found


def relative_order(count):
    blocks = [0]
    for stride, radix in reversed(phases_of(count)):
        blocks = [b ^ (k * stride) for k in range(radix) for b in blocks]
    return blocks


def swap(array, flip):
    count = lax.axis_size("dp")
    return lax.ppermute(array, "dp", [(i, i ^ flip) for i in range(count)])


def swap_tensor(array):
    count = lax.axis_size("tensor")
    return lax.ppermute(array, "tensor", [(i, i ^ 1) for i in range(count)])


def dot_nn(left, right):
    return lax.dot_general(left, right, (((1,), (0,)), ((), ())), preferred_element_type=F32)


def dot_nt(left, right):
    return lax.dot_general(left, right, (((1,), (1,)), ((), ())), preferred_element_type=F32)


def dot_tn(left, right):
    return lax.dot_general(left, right, (((0,), (0,)), ((), ())), preferred_element_type=F32)


def shape(rows, columns, dtype):
    return jax.ShapeDtypeStruct((rows, columns), dtype)


def after(array, *others):
    return lax.optimization_barrier((array,) + others)[0]


def call(kernel, outs, args, scalars=0, scratch=(), room=ROOM, cost=0, far=(), far_outs=()):
    return pl.pallas_call(
        kernel,
        out_shape=outs,
        in_specs=[SMEM] * scalars + [FAR if i in far else VMEM for i in range(scalars, len(args))],
        out_specs=[FAR if i in far_outs else VMEM for i in range(len(outs))],
        scratch_shapes=list(scratch),
        compiler_params=pltpu.CompilerParams(vmem_limit_bytes=room),
        cost_estimate=pl.CostEstimate(flops=cost, bytes_accessed=1024, transcendentals=0),
    )(*args)


def chooser_of(order_ref, rows):
    place = lax.broadcasted_iota(jnp.int32, (rows, order_ref.shape[1]), 0)
    return (place == order_ref[...]).astype(F32).astype(BF16)


def last_of(order_ref):
    return (order_ref[...] == order_ref.shape[1] - 1).astype(F32)


def expand(rows, last):
    return rows - jnp.sum(rows, axis=1, keepdims=True) * last


def norm_of(full):
    inverse = lax.rsqrt(jnp.mean(full * full, axis=1, keepdims=True) + epsilon)
    return full * inverse, inverse


def norm_backward(grad, normed, inverse, gain, last):
    scaled = grad * gain
    full = inverse * (scaled - normed * jnp.mean(scaled * normed, axis=1, keepdims=True))
    return (full - jnp.sum(full * last, axis=1, keepdims=True)) * (1.0 - last)


def center(rows):
    return rows - jnp.mean(rows, axis=1, keepdims=True)


def pack_kernel(*refs):
    at = 0
    for ref in refs[:-1]:
        refs[-1][:, at : at + ref.shape[1]] = ref[...]
        at += ref.shape[1]


def move(sems, *pairs):
    copies = [pltpu.make_async_copy(source, target, sems.at[i]) for i, (source, target) in enumerate(pairs)]
    for copy in copies:
        copy.start()
    return copies


def pack_far_kernel(*refs):
    *parts, out_ref, sems = refs
    pairs, at = [], 0
    for ref in parts:
        pairs.append((ref, out_ref.at[:, at : at + ref.shape[1]]))
        at += ref.shape[1]
    for copy in move(sems, *pairs):
        copy.wait()


def pack(arrays):
    rows, columns = arrays[0].shape[0], sum(a.shape[1] for a in arrays)
    if rows % 16:
        return call(pack_kernel, [shape(rows, columns, BF16)], arrays)[0]
    return pl.pallas_call(
        pack_far_kernel,
        out_shape=shape(rows, columns, BF16),
        in_specs=[FAR] * len(arrays),
        out_specs=VMEM,
        scratch_shapes=[pltpu.SemaphoreType.DMA((len(arrays),))],
        compiler_params=pltpu.CompilerParams(vmem_limit_bytes=ROOM),
        cost_estimate=pl.CostEstimate(flops=0, bytes_accessed=1024, transcendentals=0),
    )(*arrays)


def joined(refs, columns=slice(None)):
    return refs[0][:, columns] if len(refs) == 1 else jnp.concatenate([ref[:, columns] for ref in refs], axis=0)


def stacked(refs, plan, columns):
    parts = [refs[i][a : a + n, columns] for i, a, n in plan]
    return parts[0] if len(parts) == 1 else jnp.concatenate(parts, axis=0)


def first_kernel(order_ref, stream_ref, gain_ref, ent_ref, acts_ref):
    chooser = chooser_of(order_ref, order_ref.shape[1])
    gain = gain_ref[...].astype(F32).reshape(1, -1)
    gain = dot_nn(jnp.concatenate([gain] * 8, axis=0).astype(BF16), chooser)[0:1]
    entering = dot_nn(stream_ref[...], chooser[: stream_ref.shape[1]])
    ent_ref[...] = entering.astype(BF16)
    normed, _ = norm_of(expand(entering, last_of(order_ref)))
    acts_ref[...] = (normed * gain).astype(BF16)


def prepare_kernel(rank_ref, order_ref, cot_ref, own_ref, other_ref, ent_in, *refs):
    vec_refs, (ctx_ref, ent_ref, top_ref, gbm_ref, row_ref) = refs[:-5], refs[-5:]
    zero = rank_ref[0, 0] == 0
    width = own_ref.shape[1]
    own, other = own_ref[...], other_ref[...]
    ctx_ref[:, :width] = jnp.where(zero, own, other)
    ctx_ref[:, width:] = jnp.where(zero, other, own)
    ent_ref[...] = ent_in[...]
    chooser = chooser_of(order_ref, order_ref.shape[1])
    plain = [ref[...].astype(F32).reshape(1, -1) for ref in vec_refs]
    rows = dot_nn(jnp.concatenate(plain + plain, axis=0).astype(BF16), chooser)
    top = dot_nn(cot_ref[...], chooser[: cot_ref.shape[1]])
    top_ref[...] = top.astype(BF16)
    gbm = center(top)
    gbm_ref[...] = gbm.astype(BF16)
    row_ref[:4, :] = rows[:4]
    row_ref[4:5, :] = jnp.sum(gbm, axis=0, keepdims=True)
    row_ref[5:, :] = jnp.zeros((row_ref.shape[0] - 5, row_ref.shape[1]), F32)


def row_blocks(rows):
    return [(i, min(rows, i + STEP)) for i in range(0, rows, STEP)]


def write_mask(len_ref, mask_ref):
    for lo, hi in row_blocks(mask_ref.shape[0]):
        place = lax.broadcasted_iota(jnp.int32, (1, hi - lo), 1) + lo
        first = jnp.zeros_like(place)
        end = jnp.int32(0)
        for j in range(len_ref.shape[1] - 1):
            end = end + len_ref[0, j]
            first = jnp.where(place >= end, end, first)
        key = lax.broadcasted_iota(jnp.int32, (hi, hi - lo), 0)
        mask_ref[:hi, lo:hi] = jnp.where((key >= first) & (key <= place), 0.0, -1e30)


def both_heads(block):
    zero = jnp.zeros_like(block)
    first = lax.broadcasted_iota(jnp.int32, block.shape, 1) < HD
    return jnp.concatenate([jnp.where(first, block, zero), jnp.where(first, zero, block)], axis=0)


def own_rows(both):
    size = both.shape[1] // 2
    row = lax.broadcasted_iota(jnp.int32, (PAIR, size), 0)
    return jnp.where(row < HD, both[:, :size], both[:, size:])


def unit_of(size):
    r = lax.broadcasted_iota(jnp.int32, (size, size), 0)
    c = lax.broadcasted_iota(jnp.int32, (size, size), 1)
    return (r == c).astype(F32).astype(BF16)


def attend_kernel(plan, len_ref, acts_ref, bias_ref, *refs):
    weights, (qkv_ref, ctx_ref, lse_ref, mask_ref) = refs[:-4], refs[-4:]
    rows, own = ctx_ref.shape
    write_mask(len_ref, mask_ref)
    for at in range(0, 3 * own, own):
        cut = slice(at, at + own)
        qkv_ref[:, cut] = (dot_nn(acts_ref[...], stacked(weights, plan, cut)) + bias_ref[:, cut]).astype(BF16)
    unit = unit_of(PAIR)
    scale = jnp.asarray(HD**-0.5, BF16)
    for pair in range(own // PAIR):
        at = pair * PAIR
        keys = qkv_ref[:, own + at : own + at + PAIR]
        values_t = dot_nt(unit, qkv_ref[:, 2 * own + at : 2 * own + at + PAIR]).astype(BF16)
        for lo, hi in row_blocks(rows):
            size = hi - lo
            both = both_heads(qkv_ref[lo:hi, at : at + PAIR] * scale)
            mask = mask_ref[:hi, lo:hi]
            scores = dot_nt(keys[:hi], both) + jnp.concatenate([mask, mask], axis=1)
            peak = jnp.max(scores, axis=0, keepdims=True)
            expo = jnp.exp(scores - peak)
            total = jnp.sum(expo, axis=0, keepdims=True)
            probs = (expo * (1.0 / total)).astype(BF16)
            lse = peak + jnp.log(total)
            lse_ref[2 * pair : 2 * pair + 1, lo:hi] = lse[:, :size]
            lse_ref[2 * pair + 1 : 2 * pair + 2, lo:hi] = lse[:, size:]
            ctx_ref[lo:hi, at : at + PAIR] = own_rows(dot_nn(values_t[:, :hi], probs)).T.astype(BF16)


def middle_kernel(lo, plan, many, rank_ref, order_ref, row_ref, bup_ref, ctx_ref, ent_ref, gbm_ref, *refs):
    weights, downs, (mid_ref, acts_ref, active_ref, ghid_ref, gn_ref, gbup_ref) = refs[:many], refs[many:-6], refs[-6:]
    plan, plan_dn = plan
    rows = slice(lo, lo + mid_ref.shape[0])
    zero = rank_ref[0, 0] == 0
    own = ctx_ref.shape[1] // 2
    last = last_of(order_ref)

    def ordered(a, b):
        return jnp.where(zero, a, b), jnp.where(zero, b, a)

    w_first, w_second = ordered(stacked(weights, plan, slice(0, own)), stacked(weights, plan, slice(own, 2 * own)))
    branch = dot_nt(ctx_ref[rows, :own], w_first) + dot_nt(ctx_ref[rows, own:], w_second) + row_ref[2:3]
    middle = ent_ref[rows, :].astype(F32) + center(branch) * (1.0 - last)
    mid_ref[...] = middle
    normed, _ = norm_of(expand(middle, last))
    acts = (normed * row_ref[1:2]).astype(BF16)
    acts_ref[...] = acts
    gbm = gbm_ref[rows, :]
    units = active_ref.shape[1]
    piece = units // 2
    total = None
    for at in range(0, units, piece):
        cut, cut_up = slice(at, at + piece), slice(2 * own + at, 2 * own + at + piece)
        up_part = stacked(weights, plan, cut_up)
        hidden = dot_nn(acts, up_part) + bup_ref[:, cut]
        gact = dot_nn(gbm, stacked(downs, plan_dn, cut))
        square = hidden * hidden
        bend = jnp.tanh(hidden * (0.7978845608028654 + 0.7978845608028654 * 0.044715 * square))
        up = 0.5 + 0.5 * bend
        active_ref[:, cut] = (hidden * up).astype(BF16)
        slope = up + (0.5 * hidden) * (1.0 - bend * bend) * (
            0.7978845608028654 + 0.7978845608028654 * 3 * 0.044715 * square
        )
        ghid = (gact * slope).astype(BF16)
        ghid_ref[:, cut] = ghid
        gbup_ref[:, cut] = jnp.sum(ghid.astype(F32), axis=0, keepdims=True)
        part = dot_nt(ghid, up_part)
        total = part if total is None else total + part
    gn_ref[...] = total.astype(BF16)


def mix_kernel(plan, parts, *refs):
    refs[-1][...] = dot_nt(joined(refs[:parts]), stacked(refs[parts:-1], plan, slice(None))).astype(BF16)


def back_kernel(lo, plan, order_ref, row_ref, own_ref, other_ref, mid_ref, top_ref, *refs):
    weights, (gmid_ref, gba_ref, gctx_ref, sum_ref) = refs[:-4], refs[-4:]
    last = last_of(order_ref)
    grad = own_ref[...].astype(F32) + other_ref[...].astype(F32)
    normed, inverse = norm_of(expand(mid_ref[...], last))
    gmid = top_ref[lo : lo + mid_ref.shape[0], :].astype(F32) + norm_backward(grad, normed, inverse, row_ref[1:2], last)
    gmid_ref[...] = gmid
    gba = center(gmid)
    low = gba.astype(BF16)
    gba_ref[...] = low
    gctx_ref[...] = dot_nn(low, stacked(weights, plan, slice(0, gctx_ref.shape[1]))).astype(BF16)
    sum_ref[0:1, :] = jnp.sum(grad * normed, axis=0, keepdims=True)
    sum_ref[1:2, :] = jnp.sum(gba, axis=0, keepdims=True)
    sum_ref[2:, :] = jnp.zeros((sum_ref.shape[0] - 2, sum_ref.shape[1]), F32)


def attend_back_kernel(
    len_ref, qkv_ref, lse_ref, *refs
):
    gctx_refs, (gq_ref, gkv_ref, mask_ref, gk_ref, gv_ref) = refs[:-5], refs[-5:]
    rows, own = gq_ref.shape
    write_mask(len_ref, mask_ref)
    unit = unit_of(PAIR)
    scale = jnp.asarray(HD**-0.5, BF16)
    for pair in range(own // PAIR):
        at = pair * PAIR
        keys = qkv_ref[:, own + at : own + at + PAIR]
        values = qkv_ref[:, 2 * own + at : 2 * own + at + PAIR]
        keys_t = dot_nt(unit, keys * scale).astype(BF16)
        gctx = joined(gctx_refs, slice(at, at + PAIR))
        for lo, hi in reversed(row_blocks(rows)):
            size = hi - lo
            both_q = both_heads(qkv_ref[lo:hi, at : at + PAIR] * scale)
            both_g = both_heads(gctx[lo:hi])
            lse = jnp.concatenate(
                [lse_ref[2 * pair : 2 * pair + 1, lo:hi], lse_ref[2 * pair + 1 : 2 * pair + 2, lo:hi]], axis=1
            )
            mask = mask_ref[:hi, lo:hi]
            probs = jnp.exp(dot_nt(keys[:hi], both_q) + jnp.concatenate([mask, mask], axis=1) - lse)
            gprobs = dot_nt(values[:hi], both_g)
            delta = jnp.sum(probs * gprobs, axis=0, keepdims=True)
            gscores = (probs * (gprobs - delta)).astype(BF16)
            gq_ref[lo:hi, at : at + PAIR] = own_rows(dot_nn(keys_t[:, :hi], gscores)).T.astype(BF16)
            gk = dot_nn(gscores, both_q)
            gv = dot_nn(probs.astype(BF16), both_g)
            if hi == rows:
                gk_ref[...] = gk
                gv_ref[...] = gv
            else:
                gk_ref[:hi, :] += gk
                gv_ref[:hi, :] += gv
        gkv_ref[:, at : at + PAIR] = gk_ref[...].astype(BF16)
        gkv_ref[:, own + at : own + at + PAIR] = gv_ref[...].astype(BF16)


def part_kernel(plan, gq_ref, gkv_ref, ent_ref, order_ref, *refs):
    weights, (part_ref, sum_ref, bias_ref) = refs[:-3], refs[-3:]
    own = gq_ref.shape[1]
    part = dot_nt(gq_ref[...], stacked(weights, plan, slice(0, own)))
    part_ref[...] = (part + dot_nt(gkv_ref[...], stacked(weights, plan, slice(own, 3 * own)))).astype(BF16)
    normed, _ = norm_of(expand(ent_ref[...].astype(F32), last_of(order_ref)))
    total = jnp.sum(part_ref[...].astype(F32) * normed, axis=0, keepdims=True)
    sum_ref[...] = total
    bias_ref[:, :own] = jnp.sum(gq_ref[...].astype(F32), axis=0, keepdims=True)
    bias_ref[:, own:] = jnp.sum(gkv_ref[:, own:].astype(F32), axis=0, keepdims=True)


def vector_kernel(parts, order_ref, row_ref, gain_ref, gain_other, bias_ref, *refs):
    sum_refs, gbup_refs, out_ref = refs[:parts], refs[parts:-1], refs[-1]
    width = order_ref.shape[1]
    chooser = chooser_of(order_ref, width)
    sums = sum(ref[0:2] for ref in sum_refs)
    gbup = sum(ref[...] for ref in gbup_refs)
    gain = gain_ref[...] + gain_other[...]
    rows = jnp.concatenate([row_ref[4:5], sums, gain, jnp.zeros((4, width), F32)], axis=0)
    plain = jnp.zeros_like(rows)
    for _ in range(3):
        low = rows.astype(BF16)
        plain = plain + dot_nt(low, chooser)
        rows = rows - low.astype(F32)
    plain = jnp.concatenate([plain[0:4], gbup[:, :width], gbup[:, width:], bias_ref[...], plain[7:8]], axis=0)
    lanes = out_ref.shape[1]
    for r in range(8):
        for j in range(width // lanes):
            at = r * (width // lanes) + j
            out_ref[at : at + 1, :] = plain[r : r + 1, j * lanes : (j + 1) * lanes]


def result_kernel(parts, order_ref, row_ref, *refs):
    mids, (own_ref, other_ref, out_ref) = refs[:parts], refs[parts:]
    last = last_of(order_ref)
    branch = own_ref[...].astype(F32) + other_ref[...].astype(F32) + row_ref[3:4]
    result = (joined(mids) + center(branch) * (1.0 - last)).astype(BF16)
    plain = dot_nt(result, chooser_of(order_ref, order_ref.shape[1]))
    out_ref[...] = plain[:, : out_ref.shape[1]].astype(BF16)


def final_kernel(order_ref, row_ref, own_ref, other_ref, ent_ref, *refs):
    gmids, out_ref = refs[:-1], refs[-1]
    last = last_of(order_ref)
    grad = own_ref[...].astype(F32) + other_ref[...].astype(F32)
    normed, inverse = norm_of(expand(ent_ref[...].astype(F32), last))
    grad = (joined(gmids) + norm_backward(grad, normed, inverse, row_ref[0:1], last)).astype(BF16)
    plain = dot_nt(grad, chooser_of(order_ref, order_ref.shape[1]))
    out_ref[...] = plain[:, : out_ref.shape[1]].astype(BF16)


def pairs_of(refs, counts):
    found, at = [], 0
    for acts, grads in counts:
        found.append((refs[at : at + acts], refs[at + acts : at + acts + grads]))
        at += acts + grads
    return found


def send_kernel(counts, pieces, *refs):
    outs, at = refs[-pieces:], 0
    rows = outs[0].shape[0]
    for acts, grads in pairs_of(refs, counts):
        half = acts[0].shape[1] // 2
        cut = slice(at, at + grads[0].shape[1])
        made = dot_tn(joined(acts, slice(half, None)), joined(grads)).astype(BF16)
        for i, out_ref in enumerate(outs):
            out_ref[:, cut] = made[i * rows : (i + 1) * rows]
        at += grads[0].shape[1]


def keep_kernel(counts, pieces, radix, each, with_far, *refs):
    many = (radix - 1) * each
    far = ()
    if with_far:
        *refs, keep_ref, sems = refs
        far = [refs[-many - 1]]
    else:
        keep_ref = refs[-many - 1]
    send_refs = refs[len(refs) - many :]
    got = joined(refs[-many - 1 - pieces : -many - 1]).astype(F32)
    rows, at = keep_ref.shape[0], 0
    size = rows // each
    found = []
    for acts, grads in pairs_of(refs, counts):
        acts, grads = joined(acts, slice(0, rows * radix)), joined(grads)
        cut = slice(at, at + grads.shape[1])
        keep_ref[:, cut] = dot_tn(acts[:, :rows], grads) + got[:rows, cut]
        at += grads.shape[1]
        found.append((cut, acts, grads))
    out = move(sems, (keep_ref, far[0])) if with_far else []
    for cut, acts, grads in found:
        half = dot_tn(acts[:, rows:], grads) + got[rows:, cut]
        for k, send_ref in enumerate(send_refs):
            send_ref[:, cut] = half[k * size : (k + 1) * size].astype(BF16)
    for copy in out:
        copy.wait()


def sum_far(given, each, refs):
    near, sems = refs[-2 - given : -1], refs[-1]
    got = move(sems, *zip(refs[: 1 + given], near))
    for copy in got:
        copy.wait()
    total = near[0][...]
    for i in range(1, 1 + given, each):
        total = total + joined(near[i : i + each]).astype(F32)
    return total, refs[: -2 - given]


def far_scratch(arrays):
    return [pltpu.VMEM(a.shape, a.dtype) for a in arrays] + [pltpu.SemaphoreType.DMA((len(arrays),))]


def add_kernel(given, each, *refs):
    total = refs[0][...]
    for i in range(1, 1 + given, each):
        total = total + joined(refs[i : i + each]).astype(F32)
    rows = refs[1 + given].shape[0]
    refs[1 + given][...] = total[:rows]
    for k, ref in enumerate(refs[2 + given :]):
        ref[...] = total[(k + 1) * rows : (k + 2) * rows].astype(BF16)


def add_vector_kernel(given, each, *refs):
    vector, refs = refs[0][...].astype(BF16), refs[1:]
    total, refs = sum_far(given, each, refs)
    rows, columns = refs[1 + given].shape
    refs[1 + given][...] = total[:rows]
    for k, ref in enumerate(refs[2 + given :]):
        ref[:, :columns] = total[(k + 1) * rows : (k + 2) * rows].astype(BF16)
        ref[:, columns:] = vector


def finish_kernel(given, vector_ref, keep_ref, *refs):
    got, (*cuts, sum_ref) = refs[:given], refs[given:]
    columns = keep_ref.shape[1]
    total = keep_ref[...]
    parts = [vector_ref[...].astype(BF16).astype(F32)]
    for ref in got:
        total = total + ref[:, :columns].astype(F32)
        parts.append(ref[:, columns:].astype(F32))
    at = 0
    for ref in cuts:
        ref[...] = total[:, at : at + ref.shape[1]]
        at += ref.shape[1]
    while len(parts) > 1:
        parts = [parts[i] + parts[i + 1] for i in range(0, len(parts), 2)]
    sum_ref[...] = parts[0]


def gather_far(shard, count):
    return jnp.concatenate(gather_far_pieces(shard, count), axis=0)


def gather_far_pieces(shard, count):
    pieces = [shard]
    for stride, radix in reversed(phases_of(count)[2:]):
        held = pieces[0] if len(pieces) == 1 else jnp.concatenate(pieces, axis=0)
        pieces = [held] + [swap(held, k * stride) for k in range(1, radix)]
    return pieces


def gather_near(held, count):
    pieces = [held]
    for stride, radix in phases_of(count)[1:2]:
        pieces += [swap(held, k * stride) for k in range(1, radix)]
    return pieces


def plan_of(pieces):
    return tuple((i, 0, piece.shape[0]) for i, piece in enumerate(pieces))


def near_first(shard, count):
    middle = shard.shape[1] // 2
    halves = [shard[:, :middle], shard[:, middle:]]
    if len(phases_of(count)) != 3:
        return halves
    return [piece for pair in zip(*(gather_near(half, count) for half in halves)) for piece in pair]


def then_far(held, count):
    phases = phases_of(count)
    if len(phases) != 3:
        pieces = gather_near(gather_far(held, count), count)
        return pieces, plan_of(pieces + pieces)
    (_, near), (stride, far) = phases[1:]
    rows = held.shape[0] // near
    pieces = [held] + [swap(held, k * stride) for k in range(1, far)]
    plan = [(core * far + z, x * rows, rows) for core in range(2) for x in range(near) for z in range(far)]
    return pieces, tuple(plan)


class Sum:
    def __init__(self, pairs, count, first=4, second=1, far=False):
        self.flat = [a for pair in pairs for parts in pair for a in parts]
        self.counts = tuple((len(acts), len(grads)) for acts, grads in pairs)
        self.phases = phases_of(count)
        self.columns = sum(grads[0].shape[1] for _, grads in pairs)
        self.rows = pairs[0][0][0].shape[1] // 2
        self.each, self.second, self.far = first, second, far
        self.sent = call(
            functools.partial(send_kernel, self.counts, first),
            [shape(self.rows // first, self.columns, BF16)] * first,
            self.flat,
        )
        self.keep = None
        self.got = []

    def go(self):
        (stride, _), self.phases = self.phases[0], self.phases[1:]
        self.got = [swap(piece, (k // self.each + 1) * stride) for k, piece in enumerate(self.sent)]
        return self

    def work(self):
        got = self.got
        if not self.phases:
            total = self.keep
            for piece in got:
                total = total + piece.astype(F32)
            self.keep = total
            return self
        radix = self.phases[0][1]
        self.rows //= radix
        outs = [shape(self.rows, self.columns, F32)]
        if self.keep is None:
            each = self.second if self.rows % (16 * self.second) == 0 else 1
            outs += [shape(self.rows // each, self.columns, BF16)] * ((radix - 1) * each)
            kernel = functools.partial(keep_kernel, self.counts, len(got), radix, each, self.far)
            scratch = [pltpu.VMEM((self.rows, self.columns), F32), pltpu.SemaphoreType.DMA((1,))]
            outs = call(
                kernel, outs, self.flat + got, far_outs=(0,) if self.far else (), scratch=scratch if self.far else ()
            )
        elif self.rows % 16 == 0:
            outs += [shape(self.rows, self.columns, BF16)] * (radix - 1)
            outs = call(functools.partial(add_kernel, len(got), self.each), outs, [self.keep] + got)
            each = 1
        else:
            total = self.keep
            for i in range(0, len(got), self.each):
                total = total + jnp.concatenate(got[i : i + self.each], axis=0).astype(F32)
            parts = [total[k * self.rows : (k + 1) * self.rows] for k in range(radix)]
            outs = [parts[0]] + [part.astype(BF16) for part in parts[1:]]
            each = 1
        self.each = each
        self.keep, *self.sent = outs
        return self

    def end(self):
        while self.phases:
            self.go().work()
        return self.keep


def tie(sums, *arrays):
    flat = list(arrays) + [piece for one in sums for piece in one.got]
    flat = lax.optimization_barrier(tuple(flat))
    at = len(arrays)
    for one in sums:
        one.got = list(flat[at : at + len(one.got)])
        at += len(one.got)
    return flat[: len(arrays)]


def flips_of(phases):
    found = [0]
    for stride, radix in phases:
        found = [k * stride + f for k in range(radix) for f in found]
    return found[1:]


def reduce_all(vector, flips):
    return total_of([vector] + [swap(vector, flip) for flip in flips])


def total_of(parts):
    while len(parts) > 1:
        parts = [parts[i] + parts[i + 1] for i in range(0, len(parts), 2)]
    return parts[0]


def body(
    stream,
    w_query,
    w_key,
    w_value,
    b_query,
    b_value,
    w_out,
    b_out,
    gain_attn,
    w_up,
    b_up,
    w_down,
    b_down,
    gain_mlp,
    cotangent,
    lengths,
):
    rows, inner_width = stream.shape
    count = lax.axis_size("dp")
    me = lax.axis_index("dp")
    rank = lax.axis_index("tensor").astype(jnp.int32).reshape(1, 1)
    shard_rows, own = w_query.shape
    width = shard_rows * count
    units = w_up.shape[1]
    blocks = jnp.array(relative_order(count), jnp.int32)
    order = ((me ^ blocks)[:, None] * shard_rows + jnp.arange(shard_rows, dtype=jnp.int32)).reshape(1, -1)

    shard_qkv = pack([w_query, w_key, w_value])
    qkv_far = gather_far_pieces(shard_qkv, count)
    w_out_t, w_up, shard_dn, order = lax.optimization_barrier((w_out.T, w_up, w_down.T, order, shard_qkv))[:4]
    shard_ou = pack([w_out_t, swap_tensor(w_out_t), w_up])
    ent, acts_a = call(first_kernel, [shape(rows, width, BF16)] * 2, [order, stream, gain_attn])
    dn_near = near_first(shard_dn, count)
    flat = lax.optimization_barrier((shard_ou, acts_a, *qkv_far, *dn_near))
    shard_ou, acts_a, qkv_far, dn_near = flat[0], flat[1], flat[2 : 2 + len(qkv_far)], flat[2 + len(qkv_far) :]
    middle_at = (len(qkv_far) + 1) // 2
    halves = [jnp.concatenate(part, axis=0) for part in (qkv_far[:middle_at], qkv_far[middle_at:]) if part]
    qkv_w = [piece for group in zip(*(gather_near(half, count) for half in halves)) for piece in group]
    ou_far = gather_far_pieces(shard_ou, count)

    qkv_w = qkv_w + [swap(piece, 1) for piece in qkv_w]
    plan = plan_of(qkv_w)
    bias_qkv = jnp.concatenate([b_query, jnp.zeros_like(b_query), b_value]).astype(F32)[None]
    qkv, context, lse = call(
        functools.partial(attend_kernel, plan),
        [shape(rows, 3 * own, BF16), shape(rows, own, BF16), shape(8, rows, F32)],
        [lengths, acts_a, bias_qkv] + qkv_w,
        scalars=1,
        scratch=[pltpu.VMEM((rows, rows), F32)],
    )
    context, *ou_far = lax.optimization_barrier((context, *ou_far))
    dn_near = jnp.concatenate([jnp.concatenate(dn_near[i::2], axis=0) for i in range(2)], axis=1)
    ou_far = jnp.concatenate(ou_far, axis=0)
    other_context = [swap_tensor(context)]
    ou_w = gather_near(ou_far, count)
    dn_w, plan_dn = then_far(dn_near, count)
    made = call(
        prepare_kernel,
        [shape(rows, width, BF16)] * 4 + [shape(8, width, F32)],
        [rank, order, cotangent, context, *other_context, ent, gain_attn, gain_mlp, b_out, b_down],
        scalars=1,
    )
    flat = lax.optimization_barrier((*made, *ou_w, *dn_w))
    (context_all, ent_mid, top, gbm, row), flat = flat[:5], flat[5:]
    ou_w, dn_w = list(flat[: len(ou_w)]), list(flat[len(ou_w) :])
    ou_w = ou_w + [swap(piece, 1) for piece in ou_w]
    plan_ou = plan_of(ou_w)
    dn_w = dn_w + [swap(piece, 1) for piece in dn_w]

    cuts = [(0, rows)]
    bias_up = b_up.astype(F32)[None]
    middle, acts_m, active, ghid, gn, gn_other, gbup = [], [], [], [], [], [], []
    for lo, size in cuts:
        made = call(
            functools.partial(middle_kernel, lo, (plan_ou, plan_dn), len(ou_w)),
            [
                shape(size, width, F32),
                shape(size, width, BF16),
                shape(size, units, BF16),
                shape(size, units, BF16),
                shape(size, width, BF16),
                shape(1, units, F32),
            ],
            [rank, order, row, bias_up, context_all, ent_mid, gbm] + ou_w + dn_w,
            scalars=1,
        )
        for held, new in zip((middle, acts_m, active, ghid, gn, gbup), made):
            held.append(new)
        gn_other.append(swap_tensor(gn[-1]))

    sum_dn = Sum([((gbm,), active)], count, first=2).go()
    sum_up = Sum([(acts_m, ghid)], count, first=2).go()
    sum_dn.work().go()
    sum_up.work().go()
    (mlp,) = call(
        functools.partial(mix_kernel, plan_dn, len(active)),
        [shape(rows, width, BF16)],
        [after(active[0], sum_up.sent)] + active[1:] + dn_w,
    )
    mlp_other = swap_tensor(mlp)
    sum_dn.work().go()

    gmid, gba, gctx, sums = [], [], [], []
    gn_other[0] = after(gn_other[0], sum_dn.sent, sum_up.sent, mlp)
    for i, (lo, size) in enumerate(cuts):
        made = call(
            functools.partial(back_kernel, lo, plan_ou),
            [shape(size, width, F32), shape(size, width, BF16), shape(size, own, BF16), shape(8, width, F32)],
            [order, row, gn[i], gn_other[i], middle[i], top] + ou_w,
        )
        for held, new in zip((gmid, gba, gctx, sums), made):
            held.append(new)
    gq, gkv = call(
        attend_back_kernel,
        [shape(rows, own, BF16), shape(rows, 2 * own, BF16)],
        [lengths, qkv, lse] + gctx,
        scalars=1,
        scratch=[pltpu.VMEM((rows, rows), F32), pltpu.VMEM((rows, PAIR), F32), pltpu.VMEM((rows, PAIR), F32)],
        cost=LONG,
    )
    gq, gkv = tie([sum_dn, sum_up], gq, gkv)
    sum_last = Sum([(gba, (context,)), ((acts_a,), (gq,)), ((acts_a,), (gkv,))], count, first=2, far=len(phases_of(count)) == 3).go()
    sum_last.work().go()
    sum_up.work().go()
    gq, gkv, mlp_other = lax.optimization_barrier((gq, gkv, mlp_other, *sum_last.sent, *sum_up.sent))[:3]
    part, gain, gbias = call(
        functools.partial(part_kernel, plan),
        [shape(rows, width, BF16), shape(1, width, F32), shape(1, 2 * own, F32)],
        [gq, gkv, ent, order] + qkv_w,
        cost=LONG,
    )
    gain_other = swap_tensor(gain)
    part_other = swap_tensor(part)
    (plain,) = call(
        functools.partial(vector_kernel, len(cuts)),
        [shape(8 * width // 128, 128, F32)],
        [order, row, gain, gain_other, gbias] + sums + gbup,
    )
    phases = phases_of(count)
    parts = [plain] + [swap(plain, flip) for flip in flips_of(phases[:2])]
    plain = total_of(list(tie([sum_last, sum_up], *parts)))
    short = len(phases) == 3
    if short:
        block = plain
        given, radix, size = len(sum_last.got), phases[2][1], sum_last.rows // phases[2][1]
        columns = sum_last.columns
        keep, *sent = call(
            functools.partial(add_vector_kernel, given, sum_last.each),
            [shape(size, columns, F32)] + [shape(size, columns + block.shape[1], BF16)] * (radix - 1),
            [block, sum_last.keep] + sum_last.got,
            far=range(1, 2 + given),
            scratch=far_scratch([sum_last.keep] + sum_last.got),
        )
        last_got = [swap(piece, (k + 1) * phases[2][0]) for k, piece in enumerate(sent)]
    else:
        sum_last.work()
        sent = sum_last.sent
        sum_last.go()
        for phase in phases[2:]:
            plain = reduce_all(plain, flips_of([phase]))
    mlp_other = after(mlp_other, sent)
    (out_rows,) = call(
        functools.partial(result_kernel, len(cuts)),
        [shape(rows, inner_width, BF16)],
        [order, row, *middle, mlp, mlp_other],
    )
    part_other, out_rows = lax.optimization_barrier((part_other, out_rows))
    (grad_stream,) = call(
        final_kernel, [shape(rows, inner_width, BF16)], [order, row, part, part_other, ent, *gmid]
    )
    shard_dn_t, shard_up = (one.work().end() for one in (sum_dn, sum_up))
    if short:
        keep, grad_stream = lax.optimization_barrier((keep, grad_stream))
        out_t, grad_q, grad_k, grad_v, block = call(
            functools.partial(finish_kernel, len(last_got)),
            [shape(shard_rows, own, F32)] * 4 + [shape(*block.shape, F32)],
            [block, keep] + last_got,
        )
        plain = block
    else:
        last = sum_last.work().end()
        out_t, grad_q, grad_k, grad_v = (last[:, i * own : (i + 1) * own] for i in range(4))
    plain = plain.reshape(8, width)
    return (
        out_rows,
        grad_stream,
        grad_q,
        grad_k,
        grad_v,
        plain[6, :own],
        plain[6, own:],
        out_t.T,
        plain[2],
        plain[3],
        shard_up,
        plain[4:6].reshape(-1),
        shard_dn_t.T,
        plain[0],
        plain[1],
    )


def solution(mesh):
    return jax.shard_map(
        body,
        mesh=mesh,
        in_specs=(
            P("dp", None),
            P("dp", "tensor"),
            P("dp", "tensor"),
            P("dp", "tensor"),
            P("tensor"),
            P("tensor"),
            P("tensor", "dp"),
            P(),
            P(),
            P("dp", "tensor"),
            P("tensor"),
            P("tensor", "dp"),
            P(),
            P(),
            P("dp", None),
            P("dp", None),
        ),
        out_specs=(
            P("dp", None),
            P("dp", None),
            P("dp", "tensor"),
            P("dp", "tensor"),
            P("dp", "tensor"),
            P("tensor"),
            P("tensor"),
            P("tensor", "dp"),
            P(),
            P(),
            P("dp", "tensor"),
            P("tensor"),
            P("tensor", "dp"),
            P(),
            P(),
        ),
        check_vma=False,
    )
```

```python
import functools

import jax
import jax.numpy as jnp
from jax import lax
from jax.experimental import pallas as pl
from jax.experimental.pallas import tpu as pltpu
from jax.sharding import PartitionSpec as P

HD = 64
PAIR = 2 * HD
STEP = 384
epsilon = 1e-05
ROOM = 10 * 1024 * 1024
LONG = 100_000_000_000
F32 = jnp.float32
BF16 = jnp.bfloat16
VMEM = pl.BlockSpec(memory_space=pltpu.VMEM)
SMEM = pl.BlockSpec(memory_space=pltpu.SMEM)
FAR = pl.BlockSpec(memory_space=pltpu.HBM)


def phases_of(count):
    found, stride = [], 1
    while stride < count:
        rest = count // stride
        radix = 2 if stride == 1 or (rest.bit_length() - 1) % 2 == 1 else 4
        found.append((stride, radix))
        stride *= radix
    return found


def relative_order(count):
    blocks = [0]
    for stride, radix in reversed(phases_of(count)):
        blocks = [b ^ (k * stride) for k in range(radix) for b in blocks]
    return blocks


def swap(array, flip):
    count = lax.axis_size("dp")
    return lax.ppermute(array, "dp", [(i, i ^ flip) for i in range(count)])


def swap_tensor(array):
    count = lax.axis_size("tensor")
    return lax.ppermute(array, "tensor", [(i, i ^ 1) for i in range(count)])


def dot_nn(left, right):
    return lax.dot_general(left, right, (((1,), (0,)), ((), ())), preferred_element_type=F32)


def dot_nt(left, right):
    return lax.dot_general(left, right, (((1,), (1,)), ((), ())), preferred_element_type=F32)


def dot_tn(left, right):
    return lax.dot_general(left, right, (((0,), (0,)), ((), ())), preferred_element_type=F32)


def shape(rows, columns, dtype):
    return jax.ShapeDtypeStruct((rows, columns), dtype)


def after(array, *others):
    return lax.optimization_barrier((array,) + others)[0]


def call(kernel, outs, args, scalars=0, scratch=(), room=ROOM, cost=0):
    return pl.pallas_call(
        kernel,
        out_shape=outs,
        in_specs=[SMEM] * scalars + [VMEM] * (len(args) - scalars),
        out_specs=[VMEM] * len(outs),
        scratch_shapes=list(scratch),
        compiler_params=pltpu.CompilerParams(vmem_limit_bytes=room),
        cost_estimate=pl.CostEstimate(flops=cost, bytes_accessed=1024, transcendentals=0),
    )(*args)


def chooser_of(order_ref, rows):
    place = lax.broadcasted_iota(jnp.int32, (rows, order_ref.shape[1]), 0)
    return (place == order_ref[...]).astype(F32).astype(BF16)


def last_of(order_ref):
    return (order_ref[...] == order_ref.shape[1] - 1).astype(F32)


def expand(rows, last):
    return rows - jnp.sum(rows, axis=1, keepdims=True) * last


def norm_of(full):
    inverse = lax.rsqrt(jnp.mean(full * full, axis=1, keepdims=True) + epsilon)
    return full * inverse, inverse


def norm_backward(grad, normed, inverse, gain, last):
    scaled = grad * gain
    full = inverse * (scaled - normed * jnp.mean(scaled * normed, axis=1, keepdims=True))
    return (full - jnp.sum(full * last, axis=1, keepdims=True)) * (1.0 - last)


def center(rows):
    return rows - jnp.mean(rows, axis=1, keepdims=True)


def pack_kernel(*refs):
    at = 0
    for ref in refs[:-1]:
        refs[-1][:, at : at + ref.shape[1]] = ref[...]
        at += ref.shape[1]


def move(sems, *pairs):
    copies = [pltpu.make_async_copy(source, target, sems.at[i]) for i, (source, target) in enumerate(pairs)]
    for copy in copies:
        copy.start()
    return copies


def pack_far_kernel(*refs):
    *parts, out_ref, sems = refs
    pairs, at = [], 0
    for ref in parts:
        pairs.append((ref, out_ref.at[:, at : at + ref.shape[1]]))
        at += ref.shape[1]
    for copy in move(sems, *pairs):
        copy.wait()


def pack(arrays, room=ROOM):
    rows, columns = arrays[0].shape[0], sum(a.shape[1] for a in arrays)
    if rows % 16:
        return call(pack_kernel, [shape(rows, columns, BF16)], arrays)[0]
    return pl.pallas_call(
        pack_far_kernel,
        out_shape=shape(rows, columns, BF16),
        in_specs=[FAR] * len(arrays),
        out_specs=VMEM,
        scratch_shapes=[pltpu.SemaphoreType.DMA((len(arrays),))],
        compiler_params=pltpu.CompilerParams(vmem_limit_bytes=room),
        cost_estimate=pl.CostEstimate(flops=0, bytes_accessed=1024, transcendentals=0),
    )(*arrays)


def joined(refs, columns=slice(None)):
    return refs[0][:, columns] if len(refs) == 1 else jnp.concatenate([ref[:, columns] for ref in refs], axis=0)


def stacked(refs, plan, columns):
    parts = [refs[i][a : a + n, columns] for i, a, n in plan]
    return parts[0] if len(parts) == 1 else jnp.concatenate(parts, axis=0)


def first_kernel(order_ref, stream_ref, gain_ref, ent_ref, acts_ref):
    chooser = chooser_of(order_ref, order_ref.shape[1])
    gain = gain_ref[...].astype(F32).reshape(1, -1)
    gain = dot_nn(jnp.concatenate([gain] * 8, axis=0).astype(BF16), chooser)[0:1]
    entering = dot_nn(stream_ref[...], chooser[: stream_ref.shape[1]])
    ent_ref[...] = entering.astype(BF16)
    normed, _ = norm_of(expand(entering, last_of(order_ref)))
    acts_ref[...] = (normed * gain).astype(BF16)


def prepare_kernel(rank_ref, order_ref, cot_ref, own_ref, other_ref, ent_in, *refs):
    vec_refs, (ctx_ref, ent_ref, top_ref, gbm_ref, row_ref) = refs[:-5], refs[-5:]
    zero = rank_ref[0, 0] == 0
    width = own_ref.shape[1]
    own, other = own_ref[...], other_ref[...]
    ctx_ref[:, :width] = jnp.where(zero, own, other)
    ctx_ref[:, width:] = jnp.where(zero, other, own)
    ent_ref[...] = ent_in[...]
    chooser = chooser_of(order_ref, order_ref.shape[1])
    plain = [ref[...].astype(F32).reshape(1, -1) for ref in vec_refs]
    rows = dot_nn(jnp.concatenate(plain + plain, axis=0).astype(BF16), chooser)
    top = dot_nn(cot_ref[...], chooser[: cot_ref.shape[1]])
    top_ref[...] = top.astype(BF16)
    gbm = center(top)
    gbm_ref[...] = gbm.astype(BF16)
    row_ref[:4, :] = rows[:4]
    row_ref[4:5, :] = jnp.sum(gbm, axis=0, keepdims=True)
    row_ref[5:, :] = jnp.zeros((row_ref.shape[0] - 5, row_ref.shape[1]), F32)


def row_blocks(rows):
    return [(i, min(rows, i + STEP)) for i in range(0, rows, STEP)]


def write_mask(len_ref, mask_ref):
    for lo, hi in row_blocks(mask_ref.shape[0]):
        place = lax.broadcasted_iota(jnp.int32, (1, hi - lo), 1) + lo
        first = jnp.zeros_like(place)
        end = jnp.int32(0)
        for j in range(len_ref.shape[1] - 1):
            end = end + len_ref[0, j]
            first = jnp.where(place >= end, end, first)
        key = lax.broadcasted_iota(jnp.int32, (hi, hi - lo), 0)
        mask_ref[:hi, lo:hi] = jnp.where((key >= first) & (key <= place), 0.0, -1e30)


def both_heads(block):
    zero = jnp.zeros_like(block)
    first = lax.broadcasted_iota(jnp.int32, block.shape, 1) < HD
    return jnp.concatenate([jnp.where(first, block, zero), jnp.where(first, zero, block)], axis=0)


def own_rows(both):
    size = both.shape[1] // 2
    row = lax.broadcasted_iota(jnp.int32, (PAIR, size), 0)
    return jnp.where(row < HD, both[:, :size], both[:, size:])


def unit_of(size):
    r = lax.broadcasted_iota(jnp.int32, (size, size), 0)
    c = lax.broadcasted_iota(jnp.int32, (size, size), 1)
    return (r == c).astype(F32).astype(BF16)


def attend_kernel(plan, len_ref, acts_ref, bias_ref, *refs):
    weights, (qkv_ref, ctx_ref, lse_ref, mask_ref) = refs[:-4], refs[-4:]
    rows, own = ctx_ref.shape
    write_mask(len_ref, mask_ref)
    for at in range(0, 3 * own, own):
        cut = slice(at, at + own)
        qkv_ref[:, cut] = (dot_nn(acts_ref[...], stacked(weights, plan, cut)) + bias_ref[:, cut]).astype(BF16)
    unit = unit_of(PAIR)
    scale = jnp.asarray(HD**-0.5, BF16)
    for pair in range(own // PAIR):
        at = pair * PAIR
        keys = qkv_ref[:, own + at : own + at + PAIR]
        values_t = dot_nt(unit, qkv_ref[:, 2 * own + at : 2 * own + at + PAIR]).astype(BF16)
        for lo, hi in row_blocks(rows):
            size = hi - lo
            both = both_heads(qkv_ref[lo:hi, at : at + PAIR] * scale)
            mask = mask_ref[:hi, lo:hi]
            scores = dot_nt(keys[:hi], both) + jnp.concatenate([mask, mask], axis=1)
            peak = jnp.max(scores, axis=0, keepdims=True)
            expo = jnp.exp(scores - peak)
            total = jnp.sum(expo, axis=0, keepdims=True)
            probs = (expo * (1.0 / total)).astype(BF16)
            lse = peak + jnp.log(total)
            lse_ref[2 * pair : 2 * pair + 1, lo:hi] = lse[:, :size]
            lse_ref[2 * pair + 1 : 2 * pair + 2, lo:hi] = lse[:, size:]
            ctx_ref[lo:hi, at : at + PAIR] = own_rows(dot_nn(values_t[:, :hi], probs)).T.astype(BF16)


def middle_kernel(lo, plan, many, rank_ref, order_ref, row_ref, bup_ref, ctx_ref, ent_ref, gbm_ref, *refs):
    weights, downs, (mid_ref, acts_ref, active_ref, ghid_ref, gn_ref, gbup_ref) = refs[:many], refs[many:-6], refs[-6:]
    plan, plan_dn = plan
    rows = slice(lo, lo + mid_ref.shape[0])
    zero = rank_ref[0, 0] == 0
    own = ctx_ref.shape[1] // 2
    last = last_of(order_ref)

    def ordered(a, b):
        return jnp.where(zero, a, b), jnp.where(zero, b, a)

    w_first, w_second = ordered(stacked(weights, plan, slice(0, own)), stacked(weights, plan, slice(own, 2 * own)))
    branch = dot_nt(ctx_ref[rows, :own], w_first) + dot_nt(ctx_ref[rows, own:], w_second) + row_ref[2:3]
    middle = ent_ref[rows, :].astype(F32) + center(branch) * (1.0 - last)
    mid_ref[...] = middle
    normed, _ = norm_of(expand(middle, last))
    acts = (normed * row_ref[1:2]).astype(BF16)
    acts_ref[...] = acts
    gbm = gbm_ref[rows, :]
    units = active_ref.shape[1]
    piece = units // 2
    total = None
    for at in range(0, units, piece):
        cut, cut_up = slice(at, at + piece), slice(2 * own + at, 2 * own + at + piece)
        up_part = stacked(weights, plan, cut_up)
        hidden = dot_nn(acts, up_part) + bup_ref[:, cut]
        gact = dot_nn(gbm, stacked(downs, plan_dn, cut))
        square = hidden * hidden
        bend = jnp.tanh(hidden * (0.7978845608028654 + 0.7978845608028654 * 0.044715 * square))
        up = 0.5 + 0.5 * bend
        active_ref[:, cut] = (hidden * up).astype(BF16)
        slope = up + (0.5 * hidden) * (1.0 - bend * bend) * (
            0.7978845608028654 + 0.7978845608028654 * 3 * 0.044715 * square
        )
        ghid = (gact * slope).astype(BF16)
        ghid_ref[:, cut] = ghid
        gbup_ref[:, cut] = jnp.sum(ghid.astype(F32), axis=0, keepdims=True)
        part = dot_nt(ghid, up_part)
        total = part if total is None else total + part
    gn_ref[...] = total.astype(BF16)


def mix_kernel(plan, parts, *refs):
    refs[-1][...] = dot_nt(joined(refs[:parts]), stacked(refs[parts:-1], plan, slice(None))).astype(BF16)


def back_kernel(lo, plan, order_ref, row_ref, own_ref, other_ref, mid_ref, top_ref, *refs):
    weights, (gmid_ref, gba_ref, gctx_ref, sum_ref) = refs[:-4], refs[-4:]
    last = last_of(order_ref)
    grad = own_ref[...].astype(F32) + other_ref[...].astype(F32)
    normed, inverse = norm_of(expand(mid_ref[...], last))
    gmid = top_ref[lo : lo + mid_ref.shape[0], :].astype(F32) + norm_backward(grad, normed, inverse, row_ref[1:2], last)
    gmid_ref[...] = gmid
    gba = center(gmid)
    low = gba.astype(BF16)
    gba_ref[...] = low
    gctx_ref[...] = dot_nn(low, stacked(weights, plan, slice(0, gctx_ref.shape[1]))).astype(BF16)
    sum_ref[0:1, :] = jnp.sum(grad * normed, axis=0, keepdims=True)
    sum_ref[1:2, :] = jnp.sum(gba, axis=0, keepdims=True)
    sum_ref[2:, :] = jnp.zeros((sum_ref.shape[0] - 2, sum_ref.shape[1]), F32)


def attend_back_kernel(
    len_ref, qkv_ref, lse_ref, *refs
):
    gctx_refs, (gq_ref, gkv_ref, mask_ref, gk_ref, gv_ref) = refs[:-5], refs[-5:]
    rows, own = gq_ref.shape
    write_mask(len_ref, mask_ref)
    unit = unit_of(PAIR)
    scale = jnp.asarray(HD**-0.5, BF16)
    for pair in range(own // PAIR):
        at = pair * PAIR
        keys = qkv_ref[:, own + at : own + at + PAIR]
        values = qkv_ref[:, 2 * own + at : 2 * own + at + PAIR]
        keys_t = dot_nt(unit, keys * scale).astype(BF16)
        gctx = joined(gctx_refs, slice(at, at + PAIR))
        for lo, hi in reversed(row_blocks(rows)):
            size = hi - lo
            both_q = both_heads(qkv_ref[lo:hi, at : at + PAIR] * scale)
            both_g = both_heads(gctx[lo:hi])
            lse = jnp.concatenate(
                [lse_ref[2 * pair : 2 * pair + 1, lo:hi], lse_ref[2 * pair + 1 : 2 * pair + 2, lo:hi]], axis=1
            )
            mask = mask_ref[:hi, lo:hi]
            probs = jnp.exp(dot_nt(keys[:hi], both_q) + jnp.concatenate([mask, mask], axis=1) - lse)
            gprobs = dot_nt(values[:hi], both_g)
            delta = jnp.sum(probs * gprobs, axis=0, keepdims=True)
            gscores = (probs * (gprobs - delta)).astype(BF16)
            gq_ref[lo:hi, at : at + PAIR] = own_rows(dot_nn(keys_t[:, :hi], gscores)).T.astype(BF16)
            gk = dot_nn(gscores, both_q)
            gv = dot_nn(probs.astype(BF16), both_g)
            if hi == rows:
                gk_ref[...] = gk
                gv_ref[...] = gv
            else:
                gk_ref[:hi, :] += gk
                gv_ref[:hi, :] += gv
        gkv_ref[:, at : at + PAIR] = gk_ref[...].astype(BF16)
        gkv_ref[:, own + at : own + at + PAIR] = gv_ref[...].astype(BF16)


def part_kernel(plan, gq_ref, gkv_ref, ent_ref, order_ref, *refs):
    weights, (part_ref, sum_ref, bias_ref) = refs[:-3], refs[-3:]
    own = gq_ref.shape[1]
    part = dot_nt(gq_ref[...], stacked(weights, plan, slice(0, own)))
    part_ref[...] = (part + dot_nt(gkv_ref[...], stacked(weights, plan, slice(own, 3 * own)))).astype(BF16)
    normed, _ = norm_of(expand(ent_ref[...].astype(F32), last_of(order_ref)))
    total = jnp.sum(part_ref[...].astype(F32) * normed, axis=0, keepdims=True)
    sum_ref[...] = total
    bias_ref[:, :own] = jnp.sum(gq_ref[...].astype(F32), axis=0, keepdims=True)
    bias_ref[:, own:] = jnp.sum(gkv_ref[:, own:].astype(F32), axis=0, keepdims=True)


def vector_kernel(parts, order_ref, row_ref, gain_ref, gain_other, bias_ref, *refs):
    sum_refs, gbup_refs, out_ref = refs[:parts], refs[parts:-1], refs[-1]
    width = order_ref.shape[1]
    chooser = chooser_of(order_ref, width)
    sums = sum(ref[0:2] for ref in sum_refs)
    gbup = sum(ref[...] for ref in gbup_refs)
    gain = gain_ref[...] + gain_other[...]
    rows = jnp.concatenate([row_ref[4:5], sums, gain, jnp.zeros((4, width), F32)], axis=0)
    plain = jnp.zeros_like(rows)
    for _ in range(3):
        low = rows.astype(BF16)
        plain = plain + dot_nt(low, chooser)
        rows = rows - low.astype(F32)
    plain = jnp.concatenate([plain[0:4], gbup[:, :width], gbup[:, width:], bias_ref[...], plain[7:8]], axis=0)
    lanes = out_ref.shape[1]
    for r in range(8):
        for j in range(width // lanes):
            at = r * (width // lanes) + j
            out_ref[at : at + 1, :] = plain[r : r + 1, j * lanes : (j + 1) * lanes]


def result_kernel(parts, order_ref, row_ref, *refs):
    mids, (own_ref, other_ref, out_ref) = refs[:parts], refs[parts:]
    last = last_of(order_ref)
    branch = own_ref[...].astype(F32) + other_ref[...].astype(F32) + row_ref[3:4]
    result = (joined(mids) + center(branch) * (1.0 - last)).astype(BF16)
    plain = dot_nt(result, chooser_of(order_ref, order_ref.shape[1]))
    out_ref[...] = plain[:, : out_ref.shape[1]].astype(BF16)


def final_kernel(order_ref, row_ref, own_ref, other_ref, ent_ref, *refs):
    gmids, out_ref = refs[:-1], refs[-1]
    last = last_of(order_ref)
    grad = own_ref[...].astype(F32) + other_ref[...].astype(F32)
    normed, inverse = norm_of(expand(ent_ref[...].astype(F32), last))
    grad = (joined(gmids) + norm_backward(grad, normed, inverse, row_ref[0:1], last)).astype(BF16)
    plain = dot_nt(grad, chooser_of(order_ref, order_ref.shape[1]))
    out_ref[...] = plain[:, : out_ref.shape[1]].astype(BF16)


def pairs_of(refs, counts):
    found, at = [], 0
    for acts, grads in counts:
        found.append((refs[at : at + acts], refs[at + acts : at + acts + grads]))
        at += acts + grads
    return found


def send_kernel(counts, pieces, *refs):
    outs, at = refs[-pieces:], 0
    rows = outs[0].shape[0]
    for acts, grads in pairs_of(refs, counts):
        half = acts[0].shape[1] // 2
        cut = slice(at, at + grads[0].shape[1])
        made = dot_tn(joined(acts, slice(half, None)), joined(grads)).astype(BF16)
        for i, out_ref in enumerate(outs):
            out_ref[:, cut] = made[i * rows : (i + 1) * rows]
        at += grads[0].shape[1]


def keep_kernel(counts, pieces, radix, each, *refs):
    many = (radix - 1) * each
    keep_ref, send_refs = refs[-many - 1], refs[len(refs) - many :]
    got = joined(refs[-many - 1 - pieces : -many - 1]).astype(F32)
    rows, at = keep_ref.shape[0], 0
    size = rows // each
    for acts, grads in pairs_of(refs, counts):
        cut = slice(at, at + grads[0].shape[1])
        half = dot_tn(joined(acts, slice(0, rows * radix)), joined(grads)) + got[:, cut]
        keep_ref[:, cut] = half[:rows]
        for k, send_ref in enumerate(send_refs):
            send_ref[:, cut] = half[rows + k * size : rows + (k + 1) * size].astype(BF16)
        at += grads[0].shape[1]


def add_kernel(given, each, *refs):
    total = refs[0][...]
    for i in range(1, 1 + given, each):
        total = total + joined(refs[i : i + each]).astype(F32)
    rows = refs[1 + given].shape[0]
    refs[1 + given][...] = total[:rows]
    for k, ref in enumerate(refs[2 + given :]):
        ref[...] = total[(k + 1) * rows : (k + 2) * rows].astype(BF16)


def add_vector_kernel(given, each, *refs):
    vector, refs = refs[0][...].astype(BF16), refs[1:]
    total = refs[0][...]
    for i in range(1, 1 + given, each):
        total = total + joined(refs[i : i + each]).astype(F32)
    rows, columns = refs[1 + given].shape
    refs[1 + given][...] = total[:rows]
    for k, ref in enumerate(refs[2 + given :]):
        ref[:, :columns] = total[(k + 1) * rows : (k + 2) * rows].astype(BF16)
        ref[:, columns:] = vector


def finish_kernel(given, vectors, vector_ref, keep_ref, *refs):
    got, cuts, vec_refs = refs[:given], refs[given:-vectors], refs[-vectors:]
    columns = keep_ref.shape[1]
    total = keep_ref[...]
    parts = [vector_ref[...].astype(BF16).astype(F32)]
    for ref in got:
        total = total + ref[:, :columns].astype(F32)
        parts.append(ref[:, columns:].astype(F32))
    at = 0
    for ref in cuts:
        ref[...] = total[:, at : at + ref.shape[1]]
        at += ref.shape[1]
    while len(parts) > 1:
        parts = [parts[i] + parts[i + 1] for i in range(0, len(parts), 2)]
    at, lanes = 0, parts[0].shape[1]
    for ref in vec_refs:
        for j in range(ref.shape[0] // lanes):
            ref[j * lanes : (j + 1) * lanes] = parts[0][at]
            at += 1


def gather_far(shard, count):
    return jnp.concatenate(gather_far_pieces(shard, count), axis=0)


def gather_far_pieces(shard, count):
    pieces = [shard]
    for stride, radix in reversed(phases_of(count)[2:]):
        held = pieces[0] if len(pieces) == 1 else jnp.concatenate(pieces, axis=0)
        pieces = [held] + [swap(held, k * stride) for k in range(1, radix)]
    return pieces


def gather_near(held, count):
    pieces = [held]
    for stride, radix in phases_of(count)[1:2]:
        pieces += [swap(held, k * stride) for k in range(1, radix)]
    return pieces


def plan_of(pieces):
    return tuple((i, 0, piece.shape[0]) for i, piece in enumerate(pieces))


def near_first(shard, count):
    middle = shard.shape[1] // 2
    halves = [shard[:, :middle], shard[:, middle:]]
    if len(phases_of(count)) != 3:
        return halves
    return [piece for pair in zip(*(gather_near(half, count) for half in halves)) for piece in pair]


def then_far(held, count):
    phases = phases_of(count)
    if len(phases) != 3:
        pieces = gather_near(gather_far(held, count), count)
        return pieces, plan_of(pieces + pieces)
    (_, near), (stride, far) = phases[1:]
    rows = held.shape[0] // near
    pieces = [held] + [swap(held, k * stride) for k in range(1, far)]
    plan = [(core * far + z, x * rows, rows) for core in range(2) for x in range(near) for z in range(far)]
    return pieces, tuple(plan)


class Sum:
    def __init__(self, pairs, count, first=4, second=1):
        self.flat = [a for pair in pairs for parts in pair for a in parts]
        self.counts = tuple((len(acts), len(grads)) for acts, grads in pairs)
        self.phases = phases_of(count)
        self.columns = sum(grads[0].shape[1] for _, grads in pairs)
        self.rows = pairs[0][0][0].shape[1] // 2
        self.each, self.second = first, second
        self.sent = call(
            functools.partial(send_kernel, self.counts, first),
            [shape(self.rows // first, self.columns, BF16)] * first,
            self.flat,
        )
        self.keep = None
        self.got = []

    def go(self):
        (stride, _), self.phases = self.phases[0], self.phases[1:]
        self.got = [swap(piece, (k // self.each + 1) * stride) for k, piece in enumerate(self.sent)]
        return self

    def work(self):
        got = self.got
        if not self.phases:
            total = self.keep
            for piece in got:
                total = total + piece.astype(F32)
            self.keep = total
            return self
        radix = self.phases[0][1]
        self.rows //= radix
        outs = [shape(self.rows, self.columns, F32)]
        if self.keep is None:
            each = self.second if self.rows % (16 * self.second) == 0 else 1
            outs += [shape(self.rows // each, self.columns, BF16)] * ((radix - 1) * each)
            kernel = functools.partial(keep_kernel, self.counts, len(got), radix, each)
            outs = call(kernel, outs, self.flat + got)
        elif self.rows % 16 == 0:
            outs += [shape(self.rows, self.columns, BF16)] * (radix - 1)
            outs = call(functools.partial(add_kernel, len(got), self.each), outs, [self.keep] + got)
            each = 1
        else:
            total = self.keep
            for i in range(0, len(got), self.each):
                total = total + jnp.concatenate(got[i : i + self.each], axis=0).astype(F32)
            parts = [total[k * self.rows : (k + 1) * self.rows] for k in range(radix)]
            outs = [parts[0]] + [part.astype(BF16) for part in parts[1:]]
            each = 1
        self.each = each
        self.keep, *self.sent = outs
        return self

    def end(self):
        while self.phases:
            self.go().work()
        return self.keep


def tie(sums, *arrays):
    flat = list(arrays) + [piece for one in sums for piece in one.got]
    flat = lax.optimization_barrier(tuple(flat))
    at = len(arrays)
    for one in sums:
        one.got = list(flat[at : at + len(one.got)])
        at += len(one.got)
    return flat[: len(arrays)]


def flips_of(phases):
    found = [0]
    for stride, radix in phases:
        found = [k * stride + f for k in range(radix) for f in found]
    return found[1:]


def reduce_all(vector, flips):
    return total_of([vector] + [swap(vector, flip) for flip in flips])


def total_of(parts):
    while len(parts) > 1:
        parts = [parts[i] + parts[i + 1] for i in range(0, len(parts), 2)]
    return parts[0]


def body(
    stream,
    w_query,
    w_key,
    w_value,
    b_query,
    b_value,
    w_out,
    b_out,
    gain_attn,
    w_up,
    b_up,
    w_down,
    b_down,
    gain_mlp,
    cotangent,
    lengths,
):
    rows, inner_width = stream.shape
    count = lax.axis_size("dp")
    me = lax.axis_index("dp")
    rank = lax.axis_index("tensor").astype(jnp.int32).reshape(1, 1)
    shard_rows, own = w_query.shape
    width = shard_rows * count
    units = w_up.shape[1]
    blocks = jnp.array(relative_order(count), jnp.int32)
    order = ((me ^ blocks)[:, None] * shard_rows + jnp.arange(shard_rows, dtype=jnp.int32)).reshape(1, -1)

    shard_qkv = pack([w_query, w_key, w_value], 56 * 1024 * 1024)
    qkv_far = gather_far_pieces(shard_qkv, count)
    w_out_t, w_up, shard_dn, order, rank = lax.optimization_barrier((w_out.T, w_up, w_down.T, order, rank, shard_qkv))[:5]
    shard_ou = pack([w_out_t, swap_tensor(w_out_t), w_up])
    ent, acts_a = call(first_kernel, [shape(rows, width, BF16)] * 2, [order, stream, gain_attn])
    dn_near = near_first(shard_dn, count)
    flat = lax.optimization_barrier((shard_ou, acts_a, *qkv_far, *dn_near))
    shard_ou, acts_a, qkv_far, dn_near = flat[0], flat[1], flat[2 : 2 + len(qkv_far)], flat[2 + len(qkv_far) :]
    middle_at = (len(qkv_far) + 1) // 2
    halves = [jnp.concatenate(part, axis=0) for part in (qkv_far[:middle_at], qkv_far[middle_at:]) if part]
    qkv_w = [piece for group in zip(*(gather_near(half, count) for half in halves)) for piece in group]
    ou_far = gather_far_pieces(shard_ou, count)

    qkv_w = qkv_w + [swap(piece, 1) for piece in qkv_w]
    plan = plan_of(qkv_w)
    bias_qkv = jnp.concatenate([b_query, jnp.zeros_like(b_query), b_value]).astype(F32)[None]
    qkv, context, lse = call(
        functools.partial(attend_kernel, plan),
        [shape(rows, 3 * own, BF16), shape(rows, own, BF16), shape(8, rows, F32)],
        [lengths, acts_a, bias_qkv] + qkv_w,
        scalars=1,
        scratch=[pltpu.VMEM((rows, rows), F32)],
    )
    context, *ou_far = lax.optimization_barrier((context, *ou_far))
    dn_near = jnp.concatenate([jnp.concatenate(dn_near[i::2], axis=0) for i in range(2)], axis=1)
    ou_far = jnp.concatenate(ou_far, axis=0)
    other_context = [swap_tensor(context)]
    ou_w = gather_near(ou_far, count)
    dn_w, plan_dn = then_far(dn_near, count)
    made = call(
        prepare_kernel,
        [shape(rows, width, BF16)] * 4 + [shape(8, width, F32)],
        [rank, order, cotangent, context, *other_context, ent, gain_attn, gain_mlp, b_out, b_down],
        scalars=1,
    )
    flat = lax.optimization_barrier((*made, *ou_w, *dn_w))
    (context_all, ent_mid, top, gbm, row), flat = flat[:5], flat[5:]
    ou_w, dn_w = list(flat[: len(ou_w)]), list(flat[len(ou_w) :])
    ou_w = ou_w + [swap(piece, 1) for piece in ou_w]
    plan_ou = plan_of(ou_w)
    dn_w = dn_w + [swap(piece, 1) for piece in dn_w]

    cuts = [(0, rows)]
    bias_up = b_up.astype(F32)[None]
    middle, acts_m, active, ghid, gn, gn_other, gbup = [], [], [], [], [], [], []
    for lo, size in cuts:
        made = call(
            functools.partial(middle_kernel, lo, (plan_ou, plan_dn), len(ou_w)),
            [
                shape(size, width, F32),
                shape(size, width, BF16),
                shape(size, units, BF16),
                shape(size, units, BF16),
                shape(size, width, BF16),
                shape(1, units, F32),
            ],
            [rank, order, row, bias_up, context_all, ent_mid, gbm] + ou_w + dn_w,
            scalars=1,
        )
        for held, new in zip((middle, acts_m, active, ghid, gn, gbup), made):
            held.append(new)
        gn_other.append(swap_tensor(gn[-1]))

    sum_dn = Sum([((gbm,), active)], count, first=2).go()
    sum_up = Sum([(acts_m, ghid)], count, first=2).go()
    sum_dn.work().go()
    sum_up.work().go()
    (mlp,) = call(
        functools.partial(mix_kernel, plan_dn, len(active)),
        [shape(rows, width, BF16)],
        [after(active[0], sum_up.sent)] + active[1:] + dn_w,
    )
    mlp_other = swap_tensor(mlp)
    sum_dn.work().go()

    gmid, gba, gctx, sums = [], [], [], []
    gn_other[0] = after(gn_other[0], sum_dn.sent, sum_up.sent, mlp)
    for i, (lo, size) in enumerate(cuts):
        made = call(
            functools.partial(back_kernel, lo, plan_ou),
            [shape(size, width, F32), shape(size, width, BF16), shape(size, own, BF16), shape(8, width, F32)],
            [order, row, gn[i], gn_other[i], middle[i], top] + ou_w,
        )
        for held, new in zip((gmid, gba, gctx, sums), made):
            held.append(new)
    gq, gkv = call(
        attend_back_kernel,
        [shape(rows, own, BF16), shape(rows, 2 * own, BF16)],
        [lengths, qkv, lse] + gctx,
        scalars=1,
        scratch=[pltpu.VMEM((rows, rows), F32), pltpu.VMEM((rows, PAIR), F32), pltpu.VMEM((rows, PAIR), F32)],
        cost=LONG,
    )
    gq, gkv = tie([sum_dn, sum_up], gq, gkv)
    sum_last = Sum([(gba, (context,)), ((acts_a,), (gq,)), ((acts_a,), (gkv,))], count, first=2).go()
    sum_last.work().go()
    sum_up.work().go()
    gq, gkv, mlp_other = lax.optimization_barrier((gq, gkv, mlp_other, *sum_last.sent, *sum_up.sent))[:3]
    part, gain, gbias = call(
        functools.partial(part_kernel, plan),
        [shape(rows, width, BF16), shape(1, width, F32), shape(1, 2 * own, F32)],
        [gq, gkv, ent, order] + qkv_w,
        cost=LONG,
    )
    gain_other = swap_tensor(gain)
    part_other = swap_tensor(part)
    (plain,) = call(
        functools.partial(vector_kernel, len(cuts)),
        [shape(8 * width // 128, 128, F32)],
        [order, row, gain, gain_other, gbias] + sums + gbup,
    )
    phases = phases_of(count)
    parts = [plain] + [swap(plain, flip) for flip in flips_of(phases[:2])]
    plain = total_of(list(tie([sum_last, sum_up], *parts)))
    short = len(phases) == 3
    if short:
        block = plain
        given, radix, size = len(sum_last.got), phases[2][1], sum_last.rows // phases[2][1]
        columns = sum_last.columns
        keep, *sent = call(
            functools.partial(add_vector_kernel, given, sum_last.each),
            [shape(size, columns, F32)] + [shape(size, columns + block.shape[1], BF16)] * (radix - 1),
            [block, sum_last.keep] + sum_last.got,
        )
        last_got = [swap(piece, (k + 1) * phases[2][0]) for k, piece in enumerate(sent)]
    else:
        sum_last.work()
        sent = sum_last.sent
        sum_last.go()
        for phase in phases[2:]:
            plain = reduce_all(plain, flips_of([phase]))
    mlp_other = after(mlp_other, sent)
    (out_rows,) = call(
        functools.partial(result_kernel, len(cuts)),
        [shape(rows, inner_width, BF16)],
        [order, row, *middle, mlp, mlp_other],
    )
    part_other, out_rows = lax.optimization_barrier((part_other, out_rows))
    (grad_stream,) = call(
        final_kernel, [shape(rows, inner_width, BF16)], [order, row, part, part_other, ent, *gmid]
    )
    shard_dn_t, shard_up = (one.work().end() for one in (sum_dn, sum_up))
    if short:
        keep, grad_stream = lax.optimization_barrier((keep, grad_stream))
        sizes = [width] * 4 + [2 * width, own, own]
        out_t, grad_q, grad_k, grad_v, *vectors = call(
            functools.partial(finish_kernel, len(last_got), len(sizes)),
            [shape(shard_rows, own, F32)] * 4 + [jax.ShapeDtypeStruct((size,), F32) for size in sizes],
            [block, keep] + last_got,
        )
    else:
        last = sum_last.work().end()
        out_t, grad_q, grad_k, grad_v = (last[:, i * own : (i + 1) * own] for i in range(4))
        plain = plain.reshape(8, width)
        vectors = [plain[0], plain[1], plain[2], plain[3], plain[4:6].reshape(-1), plain[6, :own], plain[6, own:]]
    grad_b_down, grad_gain_mlp, grad_b_out, grad_gain_attn, grad_b_up, grad_b_query, grad_b_value = vectors
    return (
        out_rows,
        grad_stream,
        grad_q,
        grad_k,
        grad_v,
        grad_b_query,
        grad_b_value,
        out_t.T,
        grad_b_out,
        grad_gain_attn,
        shard_up,
        grad_b_up,
        shard_dn_t.T,
        grad_b_down,
        grad_gain_mlp,
    )


def solution(mesh):
    return jax.shard_map(
        body,
        mesh=mesh,
        in_specs=(
            P("dp", None),
            P("dp", "tensor"),
            P("dp", "tensor"),
            P("dp", "tensor"),
            P("tensor"),
            P("tensor"),
            P("tensor", "dp"),
            P(),
            P(),
            P("dp", "tensor"),
            P("tensor"),
            P("tensor", "dp"),
            P(),
            P(),
            P("dp", None),
            P("dp", None),
        ),
        out_specs=(
            P("dp", None),
            P("dp", None),
            P("dp", "tensor"),
            P("dp", "tensor"),
            P("dp", "tensor"),
            P("tensor"),
            P("tensor"),
            P("tensor", "dp"),
            P(),
            P(),
            P("dp", "tensor"),
            P("tensor"),
            P("tensor", "dp"),
            P(),
            P(),
        ),
        check_vma=False,
    )
```

```python
import functools

import jax
import jax.numpy as jnp
from jax import lax
from jax.experimental import pallas as pl
from jax.experimental.pallas import tpu as pltpu
from jax.sharding import PartitionSpec as P

HD = 64
PAIR = 2 * HD
STEP = 384
epsilon = 1e-05
ROOM = 10 * 1024 * 1024
LONG = 100_000_000_000
F32 = jnp.float32
BF16 = jnp.bfloat16
VMEM = pl.BlockSpec(memory_space=pltpu.VMEM)
SMEM = pl.BlockSpec(memory_space=pltpu.SMEM)
FAR = pl.BlockSpec(memory_space=pltpu.HBM)


def phases_of(count):
    found, stride = [], 1
    while stride < count:
        rest = count // stride
        radix = 2 if stride == 1 or (rest.bit_length() - 1) % 2 == 1 else 4
        found.append((stride, radix))
        stride *= radix
    return found


def relative_order(count):
    blocks = [0]
    for stride, radix in reversed(phases_of(count)):
        blocks = [b ^ (k * stride) for k in range(radix) for b in blocks]
    return blocks


def swap(array, flip):
    count = lax.axis_size("dp")
    return lax.ppermute(array, "dp", [(i, i ^ flip) for i in range(count)])


def swap_tensor(array):
    count = lax.axis_size("tensor")
    return lax.ppermute(array, "tensor", [(i, i ^ 1) for i in range(count)])


def dot_nn(left, right):
    return lax.dot_general(left, right, (((1,), (0,)), ((), ())), preferred_element_type=F32)


def dot_nt(left, right):
    return lax.dot_general(left, right, (((1,), (1,)), ((), ())), preferred_element_type=F32)


def dot_tn(left, right):
    return lax.dot_general(left, right, (((0,), (0,)), ((), ())), preferred_element_type=F32)


def shape(rows, columns, dtype):
    return jax.ShapeDtypeStruct((rows, columns), dtype)


def after(array, *others):
    return lax.optimization_barrier((array,) + others)[0]


def call(kernel, outs, args, scalars=0, scratch=(), room=ROOM, cost=0):
    return pl.pallas_call(
        kernel,
        out_shape=outs,
        in_specs=[SMEM] * scalars + [VMEM] * (len(args) - scalars),
        out_specs=[VMEM] * len(outs),
        scratch_shapes=list(scratch),
        compiler_params=pltpu.CompilerParams(vmem_limit_bytes=room),
        cost_estimate=pl.CostEstimate(flops=cost, bytes_accessed=1024, transcendentals=0),
    )(*args)


def chooser_of(order_ref, rows):
    place = lax.broadcasted_iota(jnp.int32, (rows, order_ref.shape[1]), 0)
    return (place == order_ref[...]).astype(F32).astype(BF16)


def last_of(order_ref):
    return (order_ref[...] == order_ref.shape[1] - 1).astype(F32)


def expand(rows, last):
    return rows - jnp.sum(rows, axis=1, keepdims=True) * last


def norm_of(full):
    inverse = lax.rsqrt(jnp.mean(full * full, axis=1, keepdims=True) + epsilon)
    return full * inverse, inverse


def norm_backward(grad, normed, inverse, gain, last):
    scaled = grad * gain
    full = inverse * (scaled - normed * jnp.mean(scaled * normed, axis=1, keepdims=True))
    return (full - jnp.sum(full * last, axis=1, keepdims=True)) * (1.0 - last)


def center(rows):
    return rows - jnp.mean(rows, axis=1, keepdims=True)


def by_rows(rows, body, carry=0):
    step = next(size for size in (192, 144, 96, 48, rows) if rows % size == 0)
    return lax.fori_loop(0, rows // step, lambda i, c: body(pl.ds(pl.multiple_of(i * step, step), step), c), carry)


def pack_kernel(*refs):
    at = 0
    for ref in refs[:-1]:
        refs[-1][:, at : at + ref.shape[1]] = ref[...]
        at += ref.shape[1]


def move(sems, *pairs):
    copies = [pltpu.make_async_copy(source, target, sems.at[i]) for i, (source, target) in enumerate(pairs)]
    for copy in copies:
        copy.start()
    return copies


def pack_far_kernel(*refs):
    *parts, out_ref, sems = refs
    pairs, at = [], 0
    for ref in parts:
        pairs.append((ref, out_ref.at[:, at : at + ref.shape[1]]))
        at += ref.shape[1]
    for copy in move(sems, *pairs):
        copy.wait()


def pack(arrays, room=ROOM):
    rows, columns = arrays[0].shape[0], sum(a.shape[1] for a in arrays)
    if rows % 16:
        return call(pack_kernel, [shape(rows, columns, BF16)], arrays)[0]
    return pl.pallas_call(
        pack_far_kernel,
        out_shape=shape(rows, columns, BF16),
        in_specs=[FAR] * len(arrays),
        out_specs=VMEM,
        scratch_shapes=[pltpu.SemaphoreType.DMA((len(arrays),))],
        compiler_params=pltpu.CompilerParams(vmem_limit_bytes=room),
        cost_estimate=pl.CostEstimate(flops=0, bytes_accessed=1024, transcendentals=0),
    )(*arrays)


def joined(refs, columns=slice(None)):
    return refs[0][:, columns] if len(refs) == 1 else jnp.concatenate([ref[:, columns] for ref in refs], axis=0)


def stacked(refs, plan, columns):
    parts = [refs[i][a : a + n, columns] for i, a, n in plan]
    return parts[0] if len(parts) == 1 else jnp.concatenate(parts, axis=0)


def first_kernel(order_ref, stream_ref, gain_ref, ent_ref, acts_ref, chooser_ref):
    chooser_ref[...] = chooser_of(order_ref, order_ref.shape[1])
    last = last_of(order_ref)
    gain = gain_ref[...].astype(F32).reshape(1, -1)
    gain = dot_nn(jnp.concatenate([gain] * 8, axis=0).astype(BF16), chooser_ref[...])[0:1]
    inner = stream_ref.shape[1]

    def one(at, carry):
        entering = dot_nn(stream_ref[at, :], chooser_ref[:inner, :])
        ent_ref[at, :] = entering.astype(BF16)
        normed, _ = norm_of(expand(entering, last))
        acts_ref[at, :] = (normed * gain).astype(BF16)
        return carry

    by_rows(stream_ref.shape[0], one)


def prepare_kernel(rank_ref, order_ref, cot_ref, own_ref, other_ref, ent_in, *refs):
    vec_refs, (ctx_ref, ent_ref, top_ref, gbm_ref, row_ref) = refs[:-5], refs[-5:]
    zero = rank_ref[0, 0] == 0
    width = own_ref.shape[1]
    own, other = own_ref[...], other_ref[...]
    ctx_ref[:, :width] = jnp.where(zero, own, other)
    ctx_ref[:, width:] = jnp.where(zero, other, own)
    ent_ref[...] = ent_in[...]
    chooser = chooser_of(order_ref, order_ref.shape[1])
    plain = [ref[...].astype(F32).reshape(1, -1) for ref in vec_refs]
    rows = dot_nn(jnp.concatenate(plain + plain, axis=0).astype(BF16), chooser)
    top = dot_nn(cot_ref[...], chooser[: cot_ref.shape[1]])
    top_ref[...] = top.astype(BF16)
    gbm = center(top)
    gbm_ref[...] = gbm.astype(BF16)
    row_ref[:4, :] = rows[:4]
    row_ref[4:5, :] = jnp.sum(gbm, axis=0, keepdims=True)
    row_ref[5:, :] = jnp.zeros((row_ref.shape[0] - 5, row_ref.shape[1]), F32)


def row_blocks(rows):
    return [(i, min(rows, i + STEP)) for i in range(0, rows, STEP)]


def write_mask(len_ref, mask_ref):
    for lo, hi in row_blocks(mask_ref.shape[0]):
        place = lax.broadcasted_iota(jnp.int32, (1, hi - lo), 1) + lo
        first = jnp.zeros_like(place)
        end = jnp.int32(0)
        for j in range(len_ref.shape[1] - 1):
            end = end + len_ref[0, j]
            first = jnp.where(place >= end, end, first)
        key = lax.broadcasted_iota(jnp.int32, (hi, hi - lo), 0)
        mask_ref[:hi, lo:hi] = jnp.where((key >= first) & (key <= place), 0.0, -1e30)


def both_heads(block):
    zero = jnp.zeros_like(block)
    first = lax.broadcasted_iota(jnp.int32, block.shape, 1) < HD
    return jnp.concatenate([jnp.where(first, block, zero), jnp.where(first, zero, block)], axis=0)


def own_rows(both):
    size = both.shape[1] // 2
    row = lax.broadcasted_iota(jnp.int32, (PAIR, size), 0)
    return jnp.where(row < HD, both[:, :size], both[:, size:])


def unit_of(size):
    r = lax.broadcasted_iota(jnp.int32, (size, size), 0)
    c = lax.broadcasted_iota(jnp.int32, (size, size), 1)
    return (r == c).astype(F32).astype(BF16)


def attend_kernel(plan, len_ref, acts_ref, bias_ref, *refs):
    weights, (qkv_ref, ctx_ref, lse_ref, mask_ref) = refs[:-4], refs[-4:]
    rows, own = ctx_ref.shape
    write_mask(len_ref, mask_ref)
    for at in range(0, 3 * own, own):
        cut = slice(at, at + own)
        qkv_ref[:, cut] = (dot_nn(acts_ref[...], stacked(weights, plan, cut)) + bias_ref[:, cut]).astype(BF16)
    unit = unit_of(PAIR)
    scale = jnp.asarray(HD**-0.5, BF16)
    for pair in range(own // PAIR):
        at = pair * PAIR
        keys = qkv_ref[:, own + at : own + at + PAIR]
        values_t = dot_nt(unit, qkv_ref[:, 2 * own + at : 2 * own + at + PAIR]).astype(BF16)
        for lo, hi in row_blocks(rows):
            size = hi - lo
            both = both_heads(qkv_ref[lo:hi, at : at + PAIR] * scale)
            mask = mask_ref[:hi, lo:hi]
            scores = dot_nt(keys[:hi], both) + jnp.concatenate([mask, mask], axis=1)
            peak = jnp.max(scores, axis=0, keepdims=True)
            expo = jnp.exp(scores - peak)
            total = jnp.sum(expo, axis=0, keepdims=True)
            probs = (expo * (1.0 / total)).astype(BF16)
            lse = peak + jnp.log(total)
            lse_ref[2 * pair : 2 * pair + 1, lo:hi] = lse[:, :size]
            lse_ref[2 * pair + 1 : 2 * pair + 2, lo:hi] = lse[:, size:]
            ctx_ref[lo:hi, at : at + PAIR] = own_rows(dot_nn(values_t[:, :hi], probs)).T.astype(BF16)


def middle_kernel(lo, plan, many, rank_ref, order_ref, row_ref, bup_ref, ctx_ref, ent_ref, gbm_ref, *refs):
    weights, downs, (mid_ref, acts_ref, active_ref, ghid_ref, gn_ref, gbup_ref) = refs[:many], refs[many:-6], refs[-6:]
    plan, plan_dn = plan
    rows = slice(lo, lo + mid_ref.shape[0])
    zero = rank_ref[0, 0] == 0
    own = ctx_ref.shape[1] // 2
    last = last_of(order_ref)

    def ordered(a, b):
        return jnp.where(zero, a, b), jnp.where(zero, b, a)

    w_first, w_second = ordered(stacked(weights, plan, slice(0, own)), stacked(weights, plan, slice(own, 2 * own)))
    branch = dot_nt(ctx_ref[rows, :own], w_first) + dot_nt(ctx_ref[rows, own:], w_second) + row_ref[2:3]
    middle = ent_ref[rows, :].astype(F32) + center(branch) * (1.0 - last)
    mid_ref[...] = middle
    normed, _ = norm_of(expand(middle, last))
    acts = (normed * row_ref[1:2]).astype(BF16)
    acts_ref[...] = acts
    gbm = gbm_ref[rows, :]
    units = active_ref.shape[1]
    piece = units // 2
    total = None
    for at in range(0, units, piece):
        cut, cut_up = slice(at, at + piece), slice(2 * own + at, 2 * own + at + piece)
        up_part = stacked(weights, plan, cut_up)
        hidden = dot_nn(acts, up_part) + bup_ref[:, cut]
        gact = dot_nn(gbm, stacked(downs, plan_dn, cut))
        square = hidden * hidden
        bend = jnp.tanh(hidden * (0.7978845608028654 + 0.7978845608028654 * 0.044715 * square))
        up = 0.5 + 0.5 * bend
        active_ref[:, cut] = (hidden * up).astype(BF16)
        slope = up + (0.5 * hidden) * (1.0 - bend * bend) * (
            0.7978845608028654 + 0.7978845608028654 * 3 * 0.044715 * square
        )
        ghid = (gact * slope).astype(BF16)
        ghid_ref[:, cut] = ghid
        gbup_ref[:, cut] = jnp.sum(ghid.astype(F32), axis=0, keepdims=True)
        part = dot_nt(ghid, up_part)
        total = part if total is None else total + part
    gn_ref[...] = total.astype(BF16)


def mix_kernel(plan, parts, *refs):
    refs[-1][...] = dot_nt(joined(refs[:parts]), stacked(refs[parts:-1], plan, slice(None))).astype(BF16)


def back_kernel(lo, plan, order_ref, row_ref, own_ref, other_ref, mid_ref, top_ref, *refs):
    weights, (gmid_ref, gba_ref, gctx_ref, sum_ref) = refs[:-4], refs[-4:]
    last = last_of(order_ref)
    gain = row_ref[1:2]
    weights = stacked(weights, plan, slice(0, gctx_ref.shape[1]))

    def one(at, carry):
        grad = own_ref[at, :].astype(F32) + other_ref[at, :].astype(F32)
        normed, inverse = norm_of(expand(mid_ref[at, :], last))
        gmid = top_ref[at, :].astype(F32) + norm_backward(grad, normed, inverse, gain, last)
        gmid_ref[at, :] = gmid
        gba = center(gmid)
        low = gba.astype(BF16)
        gba_ref[at, :] = low
        gctx_ref[at, :] = dot_nn(low, weights).astype(BF16)
        gain_sum, ba_sum = carry
        return (
            gain_sum + jnp.sum(grad * normed, axis=0, keepdims=True),
            ba_sum + jnp.sum(gba, axis=0, keepdims=True),
        )

    zero = jnp.zeros((1, sum_ref.shape[1]), F32)
    sum_ref[0:1, :], sum_ref[1:2, :] = by_rows(own_ref.shape[0], one, (zero, zero))
    sum_ref[2:, :] = jnp.zeros((sum_ref.shape[0] - 2, sum_ref.shape[1]), F32)


def attend_back_kernel(
    len_ref, qkv_ref, lse_ref, *refs
):
    gctx_refs, (gq_ref, gkv_ref, mask_ref, gk_ref, gv_ref) = refs[:-5], refs[-5:]
    rows, own = gq_ref.shape
    write_mask(len_ref, mask_ref)
    unit = unit_of(PAIR)
    scale = jnp.asarray(HD**-0.5, BF16)
    for pair in range(own // PAIR):
        at = pair * PAIR
        keys = qkv_ref[:, own + at : own + at + PAIR]
        values = qkv_ref[:, 2 * own + at : 2 * own + at + PAIR]
        keys_t = dot_nt(unit, keys * scale).astype(BF16)
        gctx = joined(gctx_refs, slice(at, at + PAIR))
        for lo, hi in reversed(row_blocks(rows)):
            size = hi - lo
            both_q = both_heads(qkv_ref[lo:hi, at : at + PAIR] * scale)
            both_g = both_heads(gctx[lo:hi])
            lse = jnp.concatenate(
                [lse_ref[2 * pair : 2 * pair + 1, lo:hi], lse_ref[2 * pair + 1 : 2 * pair + 2, lo:hi]], axis=1
            )
            mask = mask_ref[:hi, lo:hi]
            probs = jnp.exp(dot_nt(keys[:hi], both_q) + jnp.concatenate([mask, mask], axis=1) - lse)
            gprobs = dot_nt(values[:hi], both_g)
            delta = jnp.sum(probs * gprobs, axis=0, keepdims=True)
            gscores = (probs * (gprobs - delta)).astype(BF16)
            gq_ref[lo:hi, at : at + PAIR] = own_rows(dot_nn(keys_t[:, :hi], gscores)).T.astype(BF16)
            gk = dot_nn(gscores, both_q)
            gv = dot_nn(probs.astype(BF16), both_g)
            if hi == rows:
                gk_ref[...] = gk
                gv_ref[...] = gv
            else:
                gk_ref[:hi, :] += gk
                gv_ref[:hi, :] += gv
        gkv_ref[:, at : at + PAIR] = gk_ref[...].astype(BF16)
        gkv_ref[:, own + at : own + at + PAIR] = gv_ref[...].astype(BF16)


def part_kernel(plan, gq_ref, gkv_ref, ent_ref, order_ref, *refs):
    weights, (part_ref, sum_ref, bias_ref) = refs[:-3], refs[-3:]
    own = gq_ref.shape[1]
    last = last_of(order_ref)
    w_q, w_kv = stacked(weights, plan, slice(0, own)), stacked(weights, plan, slice(own, 3 * own))

    def one(at, carry):
        gq, gkv = gq_ref[at, :], gkv_ref[at, :]
        part = (dot_nt(gq, w_q) + dot_nt(gkv, w_kv)).astype(BF16)
        part_ref[at, :] = part
        normed, _ = norm_of(expand(ent_ref[at, :].astype(F32), last))
        gain_sum, q_sum, v_sum = carry
        return (
            gain_sum + jnp.sum(part.astype(F32) * normed, axis=0, keepdims=True),
            q_sum + jnp.sum(gq.astype(F32), axis=0, keepdims=True),
            v_sum + jnp.sum(gkv[:, own:].astype(F32), axis=0, keepdims=True),
        )

    zeros = jnp.zeros((1, 2 * own), F32), jnp.zeros((1, own), F32), jnp.zeros((1, own), F32)
    sum_ref[...], bias_ref[:, :own], bias_ref[:, own:] = by_rows(gq_ref.shape[0], one, zeros)


def vector_kernel(parts, order_ref, row_ref, gain_ref, gain_other, bias_ref, *refs):
    sum_refs, gbup_refs, out_ref = refs[:parts], refs[parts:-1], refs[-1]
    width = order_ref.shape[1]
    chooser = chooser_of(order_ref, width)
    sums = sum(ref[0:2] for ref in sum_refs)
    gbup = sum(ref[...] for ref in gbup_refs)
    gain = gain_ref[...] + gain_other[...]
    rows = jnp.concatenate([row_ref[4:5], sums, gain, jnp.zeros((4, width), F32)], axis=0)
    plain = jnp.zeros_like(rows)
    for _ in range(3):
        low = rows.astype(BF16)
        plain = plain + dot_nt(low, chooser)
        rows = rows - low.astype(F32)
    plain = jnp.concatenate([plain[0:4], gbup[:, :width], gbup[:, width:], bias_ref[...], plain[7:8]], axis=0)
    lanes = out_ref.shape[1]
    for r in range(8):
        for j in range(width // lanes):
            at = r * (width // lanes) + j
            out_ref[at : at + 1, :] = plain[r : r + 1, j * lanes : (j + 1) * lanes]


def result_kernel(order_ref, row_ref, mid_ref, own_ref, other_ref, out_ref, chooser_ref):
    last = last_of(order_ref)
    chooser_ref[...] = chooser_of(order_ref, order_ref.shape[1])

    def one(at, carry):
        branch = own_ref[at, :].astype(F32) + other_ref[at, :].astype(F32) + row_ref[3:4]
        result = (mid_ref[at, :] + center(branch) * (1.0 - last)).astype(BF16)
        out_ref[at, :] = dot_nt(result, chooser_ref[...])[:, : out_ref.shape[1]].astype(BF16)
        return carry

    by_rows(mid_ref.shape[0], one)


def final_kernel(order_ref, row_ref, own_ref, other_ref, ent_ref, gmid_ref, out_ref, chooser_ref):
    last = last_of(order_ref)
    chooser_ref[...] = chooser_of(order_ref, order_ref.shape[1])

    def one(at, carry):
        grad = own_ref[at, :].astype(F32) + other_ref[at, :].astype(F32)
        normed, inverse = norm_of(expand(ent_ref[at, :].astype(F32), last))
        grad = (gmid_ref[at, :] + norm_backward(grad, normed, inverse, row_ref[0:1], last)).astype(BF16)
        out_ref[at, :] = dot_nt(grad, chooser_ref[...])[:, : out_ref.shape[1]].astype(BF16)
        return carry

    by_rows(ent_ref.shape[0], one)


def pairs_of(refs, counts):
    found, at = [], 0
    for acts, grads in counts:
        found.append((refs[at : at + acts], refs[at + acts : at + acts + grads]))
        at += acts + grads
    return found


def send_kernel(counts, pieces, *refs):
    outs, at = refs[-pieces:], 0
    rows = outs[0].shape[0]
    for acts, grads in pairs_of(refs, counts):
        half = acts[0].shape[1] // 2
        cut = slice(at, at + grads[0].shape[1])
        made = dot_tn(joined(acts, slice(half, None)), joined(grads)).astype(BF16)
        for i, out_ref in enumerate(outs):
            out_ref[:, cut] = made[i * rows : (i + 1) * rows]
        at += grads[0].shape[1]


def keep_kernel(counts, pieces, radix, each, *refs):
    many = (radix - 1) * each
    keep_ref, send_refs = refs[-many - 1], refs[len(refs) - many :]
    got = joined(refs[-many - 1 - pieces : -many - 1]).astype(F32)
    rows, at = keep_ref.shape[0], 0
    size = rows // each
    for acts, grads in pairs_of(refs, counts):
        cut = slice(at, at + grads[0].shape[1])
        half = dot_tn(joined(acts, slice(0, rows * radix)), joined(grads)) + got[:, cut]
        keep_ref[:, cut] = half[:rows]
        for k, send_ref in enumerate(send_refs):
            send_ref[:, cut] = half[rows + k * size : rows + (k + 1) * size].astype(BF16)
        at += grads[0].shape[1]


def add_kernel(given, each, *refs):
    total = refs[0][...]
    for i in range(1, 1 + given, each):
        total = total + joined(refs[i : i + each]).astype(F32)
    rows = refs[1 + given].shape[0]
    refs[1 + given][...] = total[:rows]
    for k, ref in enumerate(refs[2 + given :]):
        ref[...] = total[(k + 1) * rows : (k + 2) * rows].astype(BF16)


def add_vector_kernel(given, each, *refs):
    vector, refs = refs[0][...].astype(BF16), refs[1:]
    total = refs[0][...]
    for i in range(1, 1 + given, each):
        total = total + joined(refs[i : i + each]).astype(F32)
    rows, columns = refs[1 + given].shape
    refs[1 + given][...] = total[:rows]
    for k, ref in enumerate(refs[2 + given :]):
        ref[:, :columns] = total[(k + 1) * rows : (k + 2) * rows].astype(BF16)
        ref[:, columns:] = vector


def finish_kernel(given, vectors, vector_ref, keep_ref, *refs):
    got, cuts, vec_refs = refs[:given], refs[given:-vectors], refs[-vectors:]
    columns = keep_ref.shape[1]
    total = keep_ref[...]
    parts = [vector_ref[...].astype(BF16).astype(F32)]
    for ref in got:
        total = total + ref[:, :columns].astype(F32)
        parts.append(ref[:, columns:].astype(F32))
    at = 0
    for ref in cuts:
        ref[...] = total[:, at : at + ref.shape[1]]
        at += ref.shape[1]
    while len(parts) > 1:
        parts = [parts[i] + parts[i + 1] for i in range(0, len(parts), 2)]
    at, lanes = 0, parts[0].shape[1]
    for ref in vec_refs:
        for j in range(ref.shape[0] // lanes):
            ref[j * lanes : (j + 1) * lanes] = parts[0][at]
            at += 1


def gather_far(shard, count):
    return jnp.concatenate(gather_far_pieces(shard, count), axis=0)


def gather_far_pieces(shard, count):
    pieces = [shard]
    for stride, radix in reversed(phases_of(count)[2:]):
        held = pieces[0] if len(pieces) == 1 else jnp.concatenate(pieces, axis=0)
        pieces = [held] + [swap(held, k * stride) for k in range(1, radix)]
    return pieces


def gather_near(held, count):
    pieces = [held]
    for stride, radix in phases_of(count)[1:2]:
        pieces += [swap(held, k * stride) for k in range(1, radix)]
    return pieces


def plan_of(pieces):
    return tuple((i, 0, piece.shape[0]) for i, piece in enumerate(pieces))


def near_first(shard, count):
    middle = shard.shape[1] // 2
    halves = [shard[:, :middle], shard[:, middle:]]
    if len(phases_of(count)) != 3:
        return halves
    return [piece for pair in zip(*(gather_near(half, count) for half in halves)) for piece in pair]


def then_far(held, count):
    phases = phases_of(count)
    if len(phases) != 3:
        pieces = gather_near(gather_far(held, count), count)
        return pieces, plan_of(pieces + pieces)
    (_, near), (stride, far) = phases[1:]
    rows = held.shape[0] // near
    pieces = [held] + [swap(held, k * stride) for k in range(1, far)]
    plan = [(core * far + z, x * rows, rows) for core in range(2) for x in range(near) for z in range(far)]
    return pieces, tuple(plan)


class Sum:
    def __init__(self, pairs, count, first=4, second=1):
        self.flat = [a for pair in pairs for parts in pair for a in parts]
        self.counts = tuple((len(acts), len(grads)) for acts, grads in pairs)
        self.phases = phases_of(count)
        self.columns = sum(grads[0].shape[1] for _, grads in pairs)
        self.rows = pairs[0][0][0].shape[1] // 2
        self.each, self.second = first, second
        self.sent = call(
            functools.partial(send_kernel, self.counts, first),
            [shape(self.rows // first, self.columns, BF16)] * first,
            self.flat,
        )
        self.keep = None
        self.got = []

    def go(self):
        (stride, _), self.phases = self.phases[0], self.phases[1:]
        self.got = [swap(piece, (k // self.each + 1) * stride) for k, piece in enumerate(self.sent)]
        return self

    def work(self):
        got = self.got
        if not self.phases:
            total = self.keep
            for piece in got:
                total = total + piece.astype(F32)
            self.keep = total
            return self
        radix = self.phases[0][1]
        self.rows //= radix
        outs = [shape(self.rows, self.columns, F32)]
        if self.keep is None:
            each = self.second if self.rows % (16 * self.second) == 0 else 1
            outs += [shape(self.rows // each, self.columns, BF16)] * ((radix - 1) * each)
            kernel = functools.partial(keep_kernel, self.counts, len(got), radix, each)
            outs = call(kernel, outs, self.flat + got)
        elif self.rows % 16 == 0:
            outs += [shape(self.rows, self.columns, BF16)] * (radix - 1)
            outs = call(functools.partial(add_kernel, len(got), self.each), outs, [self.keep] + got)
            each = 1
        else:
            total = self.keep
            for i in range(0, len(got), self.each):
                total = total + jnp.concatenate(got[i : i + self.each], axis=0).astype(F32)
            parts = [total[k * self.rows : (k + 1) * self.rows] for k in range(radix)]
            outs = [parts[0]] + [part.astype(BF16) for part in parts[1:]]
            each = 1
        self.each = each
        self.keep, *self.sent = outs
        return self

    def end(self):
        while self.phases:
            self.go().work()
        return self.keep


def tie(sums, *arrays):
    flat = list(arrays) + [piece for one in sums for piece in one.got]
    flat = lax.optimization_barrier(tuple(flat))
    at = len(arrays)
    for one in sums:
        one.got = list(flat[at : at + len(one.got)])
        at += len(one.got)
    return flat[: len(arrays)]


def flips_of(phases):
    found = [0]
    for stride, radix in phases:
        found = [k * stride + f for k in range(radix) for f in found]
    return found[1:]


def reduce_all(vector, flips):
    return total_of([vector] + [swap(vector, flip) for flip in flips])


def total_of(parts):
    while len(parts) > 1:
        parts = [parts[i] + parts[i + 1] for i in range(0, len(parts), 2)]
    return parts[0]


def body(
    stream,
    w_query,
    w_key,
    w_value,
    b_query,
    b_value,
    w_out,
    b_out,
    gain_attn,
    w_up,
    b_up,
    w_down,
    b_down,
    gain_mlp,
    cotangent,
    lengths,
):
    rows, inner_width = stream.shape
    count = lax.axis_size("dp")
    me = lax.axis_index("dp")
    rank = lax.axis_index("tensor").astype(jnp.int32).reshape(1, 1)
    shard_rows, own = w_query.shape
    width = shard_rows * count
    units = w_up.shape[1]
    blocks = jnp.array(relative_order(count), jnp.int32)
    order = ((me ^ blocks)[:, None] * shard_rows + jnp.arange(shard_rows, dtype=jnp.int32)).reshape(1, -1)

    shard_qkv = pack([w_query, w_key, w_value], 56 * 1024 * 1024)
    qkv_far = gather_far_pieces(shard_qkv, count)
    w_out_t, w_up, shard_dn, order, rank = lax.optimization_barrier((w_out.T, w_up, w_down.T, order, rank, shard_qkv))[:5]
    shard_ou = pack([w_out_t, swap_tensor(w_out_t), w_up])
    ent, acts_a = call(
        first_kernel,
        [shape(rows, width, BF16)] * 2,
        [order, stream, gain_attn],
        scratch=[pltpu.VMEM((width, width), BF16)],
    )
    dn_near = near_first(shard_dn, count)
    flat = lax.optimization_barrier((shard_ou, acts_a, *qkv_far, *dn_near))
    shard_ou, acts_a, qkv_far, dn_near = flat[0], flat[1], flat[2 : 2 + len(qkv_far)], flat[2 + len(qkv_far) :]
    middle_at = (len(qkv_far) + 1) // 2
    halves = [jnp.concatenate(part, axis=0) for part in (qkv_far[:middle_at], qkv_far[middle_at:]) if part]
    qkv_w = [piece for group in zip(*(gather_near(half, count) for half in halves)) for piece in group]
    ou_far = gather_far_pieces(shard_ou, count)

    qkv_w = qkv_w + [swap(piece, 1) for piece in qkv_w]
    plan = plan_of(qkv_w)
    bias_qkv = jnp.concatenate([b_query, jnp.zeros_like(b_query), b_value]).astype(F32)[None]
    qkv, context, lse = call(
        functools.partial(attend_kernel, plan),
        [shape(rows, 3 * own, BF16), shape(rows, own, BF16), shape(8, rows, F32)],
        [lengths, acts_a, bias_qkv] + qkv_w,
        scalars=1,
        scratch=[pltpu.VMEM((rows, rows), F32)],
    )
    context, *ou_far = lax.optimization_barrier((context, *ou_far))
    dn_near = jnp.concatenate([jnp.concatenate(dn_near[i::2], axis=0) for i in range(2)], axis=1)
    ou_far = jnp.concatenate(ou_far, axis=0)
    other_context = [swap_tensor(context)]
    ou_w = gather_near(ou_far, count)
    dn_w, plan_dn = then_far(dn_near, count)
    made = call(
        prepare_kernel,
        [shape(rows, width, BF16)] * 4 + [shape(8, width, F32)],
        [rank, order, cotangent, context, *other_context, ent, gain_attn, gain_mlp, b_out, b_down],
        scalars=1,
    )
    flat = lax.optimization_barrier((*made, *ou_w, *dn_w))
    (context_all, ent_mid, top, gbm, row), flat = flat[:5], flat[5:]
    ou_w, dn_w = list(flat[: len(ou_w)]), list(flat[len(ou_w) :])
    ou_w = ou_w + [swap(piece, 1) for piece in ou_w]
    plan_ou = plan_of(ou_w)
    dn_w = dn_w + [swap(piece, 1) for piece in dn_w]

    cuts = [(0, rows)]
    bias_up = b_up.astype(F32)[None]
    middle, acts_m, active, ghid, gn, gn_other, gbup = [], [], [], [], [], [], []
    for lo, size in cuts:
        made = call(
            functools.partial(middle_kernel, lo, (plan_ou, plan_dn), len(ou_w)),
            [
                shape(size, width, F32),
                shape(size, width, BF16),
                shape(size, units, BF16),
                shape(size, units, BF16),
                shape(size, width, BF16),
                shape(1, units, F32),
            ],
            [rank, order, row, bias_up, context_all, ent_mid, gbm] + ou_w + dn_w,
            scalars=1,
        )
        for held, new in zip((middle, acts_m, active, ghid, gn, gbup), made):
            held.append(new)
        gn_other.append(swap_tensor(gn[-1]))

    sum_dn = Sum([((gbm,), active)], count, first=2).go()
    sum_up = Sum([(acts_m, ghid)], count, first=2).go()
    sum_dn.work().go()
    sum_up.work().go()
    (mlp,) = call(
        functools.partial(mix_kernel, plan_dn, len(active)),
        [shape(rows, width, BF16)],
        [after(active[0], sum_up.sent)] + active[1:] + dn_w,
    )
    mlp_other = swap_tensor(mlp)
    sum_dn.work().go()

    gmid, gba, gctx, sums = [], [], [], []
    gn_other[0] = after(gn_other[0], sum_dn.sent, sum_up.sent, mlp)
    for i, (lo, size) in enumerate(cuts):
        made = call(
            functools.partial(back_kernel, lo, plan_ou),
            [shape(size, width, F32), shape(size, width, BF16), shape(size, own, BF16), shape(8, width, F32)],
            [order, row, gn[i], gn_other[i], middle[i], top] + ou_w,
        )
        for held, new in zip((gmid, gba, gctx, sums), made):
            held.append(new)
    gq, gkv = call(
        attend_back_kernel,
        [shape(rows, own, BF16), shape(rows, 2 * own, BF16)],
        [lengths, qkv, lse] + gctx,
        scalars=1,
        scratch=[pltpu.VMEM((rows, rows), F32), pltpu.VMEM((rows, PAIR), F32), pltpu.VMEM((rows, PAIR), F32)],
        cost=LONG,
    )
    gq, gkv = tie([sum_dn, sum_up], gq, gkv)
    sum_last = Sum([(gba, (context,)), ((acts_a,), (gq,)), ((acts_a,), (gkv,))], count, first=2).go()
    sum_last.work().go()
    sum_up.work().go()
    gq, gkv, mlp_other = lax.optimization_barrier((gq, gkv, mlp_other, *sum_last.sent, *sum_up.sent))[:3]
    part, gain, gbias = call(
        functools.partial(part_kernel, plan),
        [shape(rows, width, BF16), shape(1, width, F32), shape(1, 2 * own, F32)],
        [gq, gkv, ent, order] + qkv_w,
        cost=LONG,
    )
    gain_other = swap_tensor(gain)
    part_other = swap_tensor(part)
    (plain,) = call(
        functools.partial(vector_kernel, len(cuts)),
        [shape(8 * width // 128, 128, F32)],
        [order, row, gain, gain_other, gbias] + sums + gbup,
    )
    phases = phases_of(count)
    parts = [plain] + [swap(plain, flip) for flip in flips_of(phases[:2])]
    plain = total_of(list(tie([sum_last, sum_up], *parts)))
    short = len(phases) == 3
    if short:
        block = plain
        given, radix, size = len(sum_last.got), phases[2][1], sum_last.rows // phases[2][1]
        columns = sum_last.columns
        keep, *sent = call(
            functools.partial(add_vector_kernel, given, sum_last.each),
            [shape(size, columns, F32)] + [shape(size, columns + block.shape[1], BF16)] * (radix - 1),
            [block, sum_last.keep] + sum_last.got,
        )
        last_got = [swap(piece, (k + 1) * phases[2][0]) for k, piece in enumerate(sent)]
    else:
        sum_last.work()
        sent = sum_last.sent
        sum_last.go()
        for phase in phases[2:]:
            plain = reduce_all(plain, flips_of([phase]))
    mlp_other = after(mlp_other, sent)
    (out_rows,) = call(
        result_kernel,
        [shape(rows, inner_width, BF16)],
        [order, row, *middle, mlp, mlp_other],
        scratch=[pltpu.VMEM((width, width), BF16)],
    )
    part_other, out_rows = lax.optimization_barrier((part_other, out_rows))
    (grad_stream,) = call(
        final_kernel,
        [shape(rows, inner_width, BF16)],
        [order, row, part, part_other, ent, *gmid],
        scratch=[pltpu.VMEM((width, width), BF16)],
    )
    shard_dn_t, shard_up = (one.work().end() for one in (sum_dn, sum_up))
    if short:
        keep, grad_stream = lax.optimization_barrier((keep, grad_stream))
        sizes = [width] * 4 + [2 * width, own, own]
        out_t, grad_q, grad_k, grad_v, *vectors = call(
            functools.partial(finish_kernel, len(last_got), len(sizes)),
            [shape(shard_rows, own, F32)] * 4 + [jax.ShapeDtypeStruct((size,), F32) for size in sizes],
            [block, keep] + last_got,
        )
    else:
        last = sum_last.work().end()
        out_t, grad_q, grad_k, grad_v = (last[:, i * own : (i + 1) * own] for i in range(4))
        plain = plain.reshape(8, width)
        vectors = [plain[0], plain[1], plain[2], plain[3], plain[4:6].reshape(-1), plain[6, :own], plain[6, own:]]
    grad_b_down, grad_gain_mlp, grad_b_out, grad_gain_attn, grad_b_up, grad_b_query, grad_b_value = vectors
    return (
        out_rows,
        grad_stream,
        grad_q,
        grad_k,
        grad_v,
        grad_b_query,
        grad_b_value,
        out_t.T,
        grad_b_out,
        grad_gain_attn,
        shard_up,
        grad_b_up,
        shard_dn_t.T,
        grad_b_down,
        grad_gain_mlp,
    )


def solution(mesh):
    return jax.shard_map(
        body,
        mesh=mesh,
        in_specs=(
            P("dp", None),
            P("dp", "tensor"),
            P("dp", "tensor"),
            P("dp", "tensor"),
            P("tensor"),
            P("tensor"),
            P("tensor", "dp"),
            P(),
            P(),
            P("dp", "tensor"),
            P("tensor"),
            P("tensor", "dp"),
            P(),
            P(),
            P("dp", None),
            P("dp", None),
        ),
        out_specs=(
            P("dp", None),
            P("dp", None),
            P("dp", "tensor"),
            P("dp", "tensor"),
            P("dp", "tensor"),
            P("tensor"),
            P("tensor"),
            P("tensor", "dp"),
            P(),
            P(),
            P("dp", "tensor"),
            P("tensor"),
            P("tensor", "dp"),
            P(),
            P(),
        ),
        check_vma=False,
    )
```

```python
import functools

import jax
import jax.numpy as jnp
from jax import lax
from jax.experimental import pallas as pl
from jax.experimental.pallas import tpu as pltpu
from jax.sharding import PartitionSpec as P

HD = 64
PAIR = 2 * HD
STEP = 384
epsilon = 1e-05
ROOM = 10 * 1024 * 1024
LONG = 100_000_000_000
F32 = jnp.float32
BF16 = jnp.bfloat16
VMEM = pl.BlockSpec(memory_space=pltpu.VMEM)
SMEM = pl.BlockSpec(memory_space=pltpu.SMEM)
FAR = pl.BlockSpec(memory_space=pltpu.HBM)


def phases_of(count):
    found, stride = [], 1
    while stride < count:
        rest = count // stride
        radix = 2 if stride == 1 or (rest.bit_length() - 1) % 2 == 1 else 4
        found.append((stride, radix))
        stride *= radix
    return found


def relative_order(count):
    blocks = [0]
    for stride, radix in reversed(phases_of(count)):
        blocks = [b ^ (k * stride) for k in range(radix) for b in blocks]
    return blocks


def swap(array, flip):
    count = lax.axis_size("dp")
    return lax.ppermute(array, "dp", [(i, i ^ flip) for i in range(count)])


def swap_tensor(array):
    count = lax.axis_size("tensor")
    return lax.ppermute(array, "tensor", [(i, i ^ 1) for i in range(count)])


def dot_nn(left, right):
    return lax.dot_general(left, right, (((1,), (0,)), ((), ())), preferred_element_type=F32)


def dot_nt(left, right):
    return lax.dot_general(left, right, (((1,), (1,)), ((), ())), preferred_element_type=F32)


def dot_tn(left, right):
    return lax.dot_general(left, right, (((0,), (0,)), ((), ())), preferred_element_type=F32)


def shape(rows, columns, dtype):
    return jax.ShapeDtypeStruct((rows, columns), dtype)


def after(array, *others):
    return lax.optimization_barrier((array,) + others)[0]


def call(kernel, outs, args, scalars=0, scratch=(), room=ROOM, cost=0):
    return pl.pallas_call(
        kernel,
        out_shape=outs,
        in_specs=[SMEM] * scalars + [VMEM] * (len(args) - scalars),
        out_specs=[VMEM] * len(outs),
        scratch_shapes=list(scratch),
        compiler_params=pltpu.CompilerParams(vmem_limit_bytes=room),
        cost_estimate=pl.CostEstimate(flops=cost, bytes_accessed=1024, transcendentals=0),
    )(*args)


def chooser_of(order_ref, rows):
    place = lax.broadcasted_iota(jnp.int32, (rows, order_ref.shape[1]), 0)
    return (place == order_ref[...]).astype(F32).astype(BF16)


def last_of(order_ref):
    return (order_ref[...] == order_ref.shape[1] - 1).astype(F32)


def expand(rows, last):
    return rows - jnp.sum(rows, axis=1, keepdims=True) * last


def norm_of(full):
    inverse = lax.rsqrt(jnp.mean(full * full, axis=1, keepdims=True) + epsilon)
    return full * inverse, inverse


def norm_backward(grad, normed, inverse, gain, last):
    scaled = grad * gain
    full = inverse * (scaled - normed * jnp.mean(scaled * normed, axis=1, keepdims=True))
    return (full - jnp.sum(full * last, axis=1, keepdims=True)) * (1.0 - last)


def center(rows):
    return rows - jnp.mean(rows, axis=1, keepdims=True)


def by_rows(rows, body, carry=0):
    step = next(size for size in (288, 192, 144, 96, 48, rows) if rows % size == 0)
    return lax.fori_loop(0, rows // step, lambda i, c: body(pl.ds(pl.multiple_of(i * step, step), step), c), carry)


def pack_kernel(*refs):
    at = 0
    for ref in refs[:-1]:
        refs[-1][:, at : at + ref.shape[1]] = ref[...]
        at += ref.shape[1]


def move(sems, *pairs):
    copies = [pltpu.make_async_copy(source, target, sems.at[i]) for i, (source, target) in enumerate(pairs)]
    for copy in copies:
        copy.start()
    return copies


def pack_far_kernel(*refs):
    *parts, out_ref, sems = refs
    pairs, at = [], 0
    for ref in parts:
        pairs.append((ref, out_ref.at[:, at : at + ref.shape[1]]))
        at += ref.shape[1]
    for copy in move(sems, *pairs):
        copy.wait()


def pack(arrays, room=ROOM):
    rows, columns = arrays[0].shape[0], sum(a.shape[1] for a in arrays)
    if rows % 16:
        return call(pack_kernel, [shape(rows, columns, BF16)], arrays)[0]
    return pl.pallas_call(
        pack_far_kernel,
        out_shape=shape(rows, columns, BF16),
        in_specs=[FAR] * len(arrays),
        out_specs=VMEM,
        scratch_shapes=[pltpu.SemaphoreType.DMA((len(arrays),))],
        compiler_params=pltpu.CompilerParams(vmem_limit_bytes=room),
        cost_estimate=pl.CostEstimate(flops=0, bytes_accessed=1024, transcendentals=0),
    )(*arrays)


def joined(refs, columns=slice(None)):
    return refs[0][:, columns] if len(refs) == 1 else jnp.concatenate([ref[:, columns] for ref in refs], axis=0)


def stacked(refs, plan, columns):
    parts = [refs[i][a : a + n, columns] for i, a, n in plan]
    return parts[0] if len(parts) == 1 else jnp.concatenate(parts, axis=0)


def first_kernel(order_ref, stream_ref, gain_ref, ent_ref, acts_ref, chooser_ref):
    chooser_ref[...] = chooser_of(order_ref, order_ref.shape[1])
    last = last_of(order_ref)
    gain = gain_ref[...].astype(F32).reshape(1, -1)
    gain = dot_nn(jnp.concatenate([gain] * 8, axis=0).astype(BF16), chooser_ref[...])[0:1]
    inner = stream_ref.shape[1]

    def one(at, carry):
        entering = dot_nn(stream_ref[at, :], chooser_ref[:inner, :])
        ent_ref[at, :] = entering.astype(BF16)
        normed, _ = norm_of(expand(entering, last))
        acts_ref[at, :] = (normed * gain).astype(BF16)
        return carry

    by_rows(stream_ref.shape[0], one)


def prepare_kernel(rank_ref, order_ref, cot_ref, own_ref, other_ref, ent_in, *refs):
    vec_refs, (ctx_ref, ent_ref, top_ref, gbm_ref, row_ref) = refs[:-5], refs[-5:]
    zero = rank_ref[0, 0] == 0
    width = own_ref.shape[1]
    own, other = own_ref[...], other_ref[...]
    ctx_ref[:, :width] = jnp.where(zero, own, other)
    ctx_ref[:, width:] = jnp.where(zero, other, own)
    ent_ref[...] = ent_in[...]
    chooser = chooser_of(order_ref, order_ref.shape[1])
    plain = [ref[...].astype(F32).reshape(1, -1) for ref in vec_refs]
    rows = dot_nn(jnp.concatenate(plain + plain, axis=0).astype(BF16), chooser)
    top = dot_nn(cot_ref[...], chooser[: cot_ref.shape[1]])
    top_ref[...] = top.astype(BF16)
    gbm = center(top)
    gbm_ref[...] = gbm.astype(BF16)
    row_ref[:4, :] = rows[:4]
    row_ref[4:5, :] = jnp.sum(gbm, axis=0, keepdims=True)
    row_ref[5:, :] = jnp.zeros((row_ref.shape[0] - 5, row_ref.shape[1]), F32)


def row_blocks(rows):
    return [(i, min(rows, i + STEP)) for i in range(0, rows, STEP)]


def write_mask(len_ref, mask_ref):
    for lo, hi in row_blocks(mask_ref.shape[0]):
        place = lax.broadcasted_iota(jnp.int32, (1, hi - lo), 1) + lo
        first = jnp.zeros_like(place)
        end = jnp.int32(0)
        for j in range(len_ref.shape[1] - 1):
            end = end + len_ref[0, j]
            first = jnp.where(place >= end, end, first)
        key = lax.broadcasted_iota(jnp.int32, (hi, hi - lo), 0)
        mask_ref[:hi, lo:hi] = jnp.where((key >= first) & (key <= place), 0.0, -1e30)


def both_heads(block):
    zero = jnp.zeros_like(block)
    first = lax.broadcasted_iota(jnp.int32, block.shape, 1) < HD
    return jnp.concatenate([jnp.where(first, block, zero), jnp.where(first, zero, block)], axis=0)


def own_rows(both):
    size = both.shape[1] // 2
    row = lax.broadcasted_iota(jnp.int32, (PAIR, size), 0)
    return jnp.where(row < HD, both[:, :size], both[:, size:])


def unit_of(size):
    r = lax.broadcasted_iota(jnp.int32, (size, size), 0)
    c = lax.broadcasted_iota(jnp.int32, (size, size), 1)
    return (r == c).astype(F32).astype(BF16)


def attend_kernel(plan, len_ref, acts_ref, bias_ref, *refs):
    weights, (qkv_ref, ctx_ref, lse_ref, mask_ref) = refs[:-4], refs[-4:]
    rows, own = ctx_ref.shape
    write_mask(len_ref, mask_ref)
    for at in range(0, 3 * own, own):
        cut = slice(at, at + own)
        qkv_ref[:, cut] = (dot_nn(acts_ref[...], stacked(weights, plan, cut)) + bias_ref[:, cut]).astype(BF16)
    unit = unit_of(PAIR)
    scale = jnp.asarray(HD**-0.5, BF16)
    for pair in range(own // PAIR):
        at = pair * PAIR
        keys = qkv_ref[:, own + at : own + at + PAIR]
        values_t = dot_nt(unit, qkv_ref[:, 2 * own + at : 2 * own + at + PAIR]).astype(BF16)
        for lo, hi in row_blocks(rows):
            size = hi - lo
            both = both_heads(qkv_ref[lo:hi, at : at + PAIR] * scale)
            mask = mask_ref[:hi, lo:hi]
            scores = dot_nt(keys[:hi], both) + jnp.concatenate([mask, mask], axis=1)
            peak = jnp.max(scores, axis=0, keepdims=True)
            expo = jnp.exp(scores - peak)
            total = jnp.sum(expo, axis=0, keepdims=True)
            probs = (expo * (1.0 / total)).astype(BF16)
            lse = peak + jnp.log(total)
            lse_ref[2 * pair : 2 * pair + 1, lo:hi] = lse[:, :size]
            lse_ref[2 * pair + 1 : 2 * pair + 2, lo:hi] = lse[:, size:]
            ctx_ref[lo:hi, at : at + PAIR] = own_rows(dot_nn(values_t[:, :hi], probs)).T.astype(BF16)


def middle_kernel(lo, plan, many, rank_ref, order_ref, row_ref, bup_ref, ctx_ref, ent_ref, gbm_ref, *refs):
    weights, downs, (mid_ref, acts_ref, active_ref, ghid_ref, gn_ref, gbup_ref) = refs[:many], refs[many:-6], refs[-6:]
    plan, plan_dn = plan
    rows = slice(lo, lo + mid_ref.shape[0])
    zero = rank_ref[0, 0] == 0
    own = ctx_ref.shape[1] // 2
    last = last_of(order_ref)

    def ordered(a, b):
        return jnp.where(zero, a, b), jnp.where(zero, b, a)

    w_first, w_second = ordered(stacked(weights, plan, slice(0, own)), stacked(weights, plan, slice(own, 2 * own)))
    branch = dot_nt(ctx_ref[rows, :own], w_first) + dot_nt(ctx_ref[rows, own:], w_second) + row_ref[2:3]
    middle = ent_ref[rows, :].astype(F32) + center(branch) * (1.0 - last)
    mid_ref[...] = middle
    normed, _ = norm_of(expand(middle, last))
    acts = (normed * row_ref[1:2]).astype(BF16)
    acts_ref[...] = acts
    gbm = gbm_ref[rows, :]
    units = active_ref.shape[1]
    piece = units // 2
    total = None
    for at in range(0, units, piece):
        cut, cut_up = slice(at, at + piece), slice(2 * own + at, 2 * own + at + piece)
        up_part = stacked(weights, plan, cut_up)
        hidden = dot_nn(acts, up_part) + bup_ref[:, cut]
        gact = dot_nn(gbm, stacked(downs, plan_dn, cut))
        square = hidden * hidden
        bend = jnp.tanh(hidden * (0.7978845608028654 + 0.7978845608028654 * 0.044715 * square))
        up = 0.5 + 0.5 * bend
        active_ref[:, cut] = (hidden * up).astype(BF16)
        slope = up + (0.5 * hidden) * (1.0 - bend * bend) * (
            0.7978845608028654 + 0.7978845608028654 * 3 * 0.044715 * square
        )
        ghid = (gact * slope).astype(BF16)
        ghid_ref[:, cut] = ghid
        gbup_ref[:, cut] = jnp.sum(ghid.astype(F32), axis=0, keepdims=True)
        part = dot_nt(ghid, up_part)
        total = part if total is None else total + part
    gn_ref[...] = total.astype(BF16)


def mix_kernel(plan, parts, *refs):
    refs[-1][...] = dot_nt(joined(refs[:parts]), stacked(refs[parts:-1], plan, slice(None))).astype(BF16)


def back_kernel(lo, plan, order_ref, row_ref, own_ref, other_ref, mid_ref, top_ref, *refs):
    weights, (gmid_ref, gba_ref, gctx_ref, sum_ref) = refs[:-4], refs[-4:]
    last = last_of(order_ref)
    gain = row_ref[1:2]
    weights = stacked(weights, plan, slice(0, gctx_ref.shape[1]))

    def one(at, carry):
        grad = own_ref[at, :].astype(F32) + other_ref[at, :].astype(F32)
        normed, inverse = norm_of(expand(mid_ref[at, :], last))
        gmid = top_ref[at, :].astype(F32) + norm_backward(grad, normed, inverse, gain, last)
        gmid_ref[at, :] = gmid
        gba = center(gmid)
        low = gba.astype(BF16)
        gba_ref[at, :] = low
        gctx_ref[at, :] = dot_nn(low, weights).astype(BF16)
        gain_sum, ba_sum = carry
        return (
            gain_sum + jnp.sum(grad * normed, axis=0, keepdims=True),
            ba_sum + jnp.sum(gba, axis=0, keepdims=True),
        )

    zero = jnp.zeros((1, sum_ref.shape[1]), F32)
    sum_ref[0:1, :], sum_ref[1:2, :] = by_rows(own_ref.shape[0], one, (zero, zero))
    sum_ref[2:, :] = jnp.zeros((sum_ref.shape[0] - 2, sum_ref.shape[1]), F32)


def attend_back_kernel(
    len_ref, qkv_ref, lse_ref, *refs
):
    gctx_refs, (gq_ref, gkv_ref, mask_ref, gk_ref, gv_ref) = refs[:-5], refs[-5:]
    rows, own = gq_ref.shape
    write_mask(len_ref, mask_ref)
    unit = unit_of(PAIR)
    scale = jnp.asarray(HD**-0.5, BF16)
    for pair in range(own // PAIR):
        at = pair * PAIR
        keys = qkv_ref[:, own + at : own + at + PAIR]
        values = qkv_ref[:, 2 * own + at : 2 * own + at + PAIR]
        keys_t = dot_nt(unit, keys * scale).astype(BF16)
        gctx = joined(gctx_refs, slice(at, at + PAIR))
        for lo, hi in reversed(row_blocks(rows)):
            size = hi - lo
            both_q = both_heads(qkv_ref[lo:hi, at : at + PAIR] * scale)
            both_g = both_heads(gctx[lo:hi])
            lse = jnp.concatenate(
                [lse_ref[2 * pair : 2 * pair + 1, lo:hi], lse_ref[2 * pair + 1 : 2 * pair + 2, lo:hi]], axis=1
            )
            mask = mask_ref[:hi, lo:hi]
            probs = jnp.exp(dot_nt(keys[:hi], both_q) + jnp.concatenate([mask, mask], axis=1) - lse)
            gprobs = dot_nt(values[:hi], both_g)
            delta = jnp.sum(probs * gprobs, axis=0, keepdims=True)
            gscores = (probs * (gprobs - delta)).astype(BF16)
            gq_ref[lo:hi, at : at + PAIR] = own_rows(dot_nn(keys_t[:, :hi], gscores)).T.astype(BF16)
            gk = dot_nn(gscores, both_q)
            gv = dot_nn(probs.astype(BF16), both_g)
            if hi == rows:
                gk_ref[...] = gk
                gv_ref[...] = gv
            else:
                gk_ref[:hi, :] += gk
                gv_ref[:hi, :] += gv
        gkv_ref[:, at : at + PAIR] = gk_ref[...].astype(BF16)
        gkv_ref[:, own + at : own + at + PAIR] = gv_ref[...].astype(BF16)


def part_kernel(plan, gq_ref, gkv_ref, ent_ref, order_ref, *refs):
    weights, (part_ref, sum_ref, bias_ref) = refs[:-3], refs[-3:]
    own = gq_ref.shape[1]
    last = last_of(order_ref)
    w_q, w_kv = stacked(weights, plan, slice(0, own)), stacked(weights, plan, slice(own, 3 * own))

    def one(at, carry):
        gq, gkv = gq_ref[at, :], gkv_ref[at, :]
        part = (dot_nt(gq, w_q) + dot_nt(gkv, w_kv)).astype(BF16)
        part_ref[at, :] = part
        normed, _ = norm_of(expand(ent_ref[at, :].astype(F32), last))
        gain_sum, q_sum, v_sum = carry
        return (
            gain_sum + jnp.sum(part.astype(F32) * normed, axis=0, keepdims=True),
            q_sum + jnp.sum(gq.astype(F32), axis=0, keepdims=True),
            v_sum + jnp.sum(gkv[:, own:].astype(F32), axis=0, keepdims=True),
        )

    zeros = jnp.zeros((1, 2 * own), F32), jnp.zeros((1, own), F32), jnp.zeros((1, own), F32)
    sum_ref[...], bias_ref[:, :own], bias_ref[:, own:] = by_rows(gq_ref.shape[0], one, zeros)


def vector_kernel(parts, order_ref, row_ref, gain_ref, gain_other, bias_ref, *refs):
    sum_refs, gbup_refs, out_ref = refs[:parts], refs[parts:-1], refs[-1]
    width = order_ref.shape[1]
    chooser = chooser_of(order_ref, width)
    sums = sum(ref[0:2] for ref in sum_refs)
    gbup = sum(ref[...] for ref in gbup_refs)
    gain = gain_ref[...] + gain_other[...]
    rows = jnp.concatenate([row_ref[4:5], sums, gain, jnp.zeros((4, width), F32)], axis=0)
    plain = jnp.zeros_like(rows)
    for _ in range(3):
        low = rows.astype(BF16)
        plain = plain + dot_nt(low, chooser)
        rows = rows - low.astype(F32)
    plain = jnp.concatenate([plain[0:4], gbup[:, :width], gbup[:, width:], bias_ref[...], plain[7:8]], axis=0)
    lanes = out_ref.shape[1]
    for r in range(8):
        for j in range(width // lanes):
            at = r * (width // lanes) + j
            out_ref[at : at + 1, :] = plain[r : r + 1, j * lanes : (j + 1) * lanes]


def result_kernel(order_ref, row_ref, mid_ref, own_ref, other_ref, out_ref, chooser_ref):
    last = last_of(order_ref)
    chooser_ref[...] = chooser_of(order_ref, order_ref.shape[1])

    def one(at, carry):
        branch = own_ref[at, :].astype(F32) + other_ref[at, :].astype(F32) + row_ref[3:4]
        result = (mid_ref[at, :] + center(branch) * (1.0 - last)).astype(BF16)
        out_ref[at, :] = dot_nt(result, chooser_ref[...])[:, : out_ref.shape[1]].astype(BF16)
        return carry

    by_rows(mid_ref.shape[0], one)


def final_kernel(order_ref, row_ref, own_ref, other_ref, ent_ref, gmid_ref, out_ref, chooser_ref):
    last = last_of(order_ref)
    chooser_ref[...] = chooser_of(order_ref, order_ref.shape[1])

    def one(at, carry):
        grad = own_ref[at, :].astype(F32) + other_ref[at, :].astype(F32)
        normed, inverse = norm_of(expand(ent_ref[at, :].astype(F32), last))
        grad = (gmid_ref[at, :] + norm_backward(grad, normed, inverse, row_ref[0:1], last)).astype(BF16)
        out_ref[at, :] = dot_nt(grad, chooser_ref[...])[:, : out_ref.shape[1]].astype(BF16)
        return carry

    by_rows(ent_ref.shape[0], one)


def pairs_of(refs, counts):
    found, at = [], 0
    for acts, grads in counts:
        found.append((refs[at : at + acts], refs[at + acts : at + acts + grads]))
        at += acts + grads
    return found


def send_kernel(counts, pieces, *refs):
    outs, at = refs[-pieces:], 0
    rows = outs[0].shape[0]
    for acts, grads in pairs_of(refs, counts):
        half = acts[0].shape[1] // 2
        cut = slice(at, at + grads[0].shape[1])
        made = dot_tn(joined(acts, slice(half, None)), joined(grads)).astype(BF16)
        for i, out_ref in enumerate(outs):
            out_ref[:, cut] = made[i * rows : (i + 1) * rows]
        at += grads[0].shape[1]


def keep_kernel(counts, pieces, radix, each, *refs):
    many = (radix - 1) * each
    keep_ref, send_refs = refs[-many - 1], refs[len(refs) - many :]
    got = joined(refs[-many - 1 - pieces : -many - 1]).astype(F32)
    rows, at = keep_ref.shape[0], 0
    size = rows // each
    for acts, grads in pairs_of(refs, counts):
        cut = slice(at, at + grads[0].shape[1])
        half = dot_tn(joined(acts, slice(0, rows * radix)), joined(grads)) + got[:, cut]
        keep_ref[:, cut] = half[:rows]
        for k, send_ref in enumerate(send_refs):
            send_ref[:, cut] = half[rows + k * size : rows + (k + 1) * size].astype(BF16)
        at += grads[0].shape[1]


def add_kernel(given, each, *refs):
    total = refs[0][...]
    for i in range(1, 1 + given, each):
        total = total + joined(refs[i : i + each]).astype(F32)
    rows = refs[1 + given].shape[0]
    refs[1 + given][...] = total[:rows]
    for k, ref in enumerate(refs[2 + given :]):
        ref[...] = total[(k + 1) * rows : (k + 2) * rows].astype(BF16)


def add_vector_kernel(given, each, *refs):
    vector, refs = refs[0][...].astype(BF16), refs[1:]
    total = refs[0][...]
    for i in range(1, 1 + given, each):
        total = total + joined(refs[i : i + each]).astype(F32)
    rows, columns = refs[1 + given].shape
    refs[1 + given][...] = total[:rows]
    for k, ref in enumerate(refs[2 + given :]):
        ref[:, :columns] = total[(k + 1) * rows : (k + 2) * rows].astype(BF16)
        ref[:, columns:] = vector


def finish_kernel(given, vectors, vector_ref, keep_ref, *refs):
    got, cuts, vec_refs = refs[:given], refs[given:-vectors], refs[-vectors:]
    columns = keep_ref.shape[1]
    total = keep_ref[...]
    parts = [vector_ref[...].astype(BF16).astype(F32)]
    for ref in got:
        total = total + ref[:, :columns].astype(F32)
        parts.append(ref[:, columns:].astype(F32))
    at = 0
    for ref in cuts:
        ref[...] = total[:, at : at + ref.shape[1]]
        at += ref.shape[1]
    while len(parts) > 1:
        parts = [parts[i] + parts[i + 1] for i in range(0, len(parts), 2)]
    at, lanes = 0, parts[0].shape[1]
    for ref in vec_refs:
        for j in range(ref.shape[0] // lanes):
            ref[j * lanes : (j + 1) * lanes] = parts[0][at]
            at += 1


def gather_far(shard, count):
    return jnp.concatenate(gather_far_pieces(shard, count), axis=0)


def gather_far_pieces(shard, count):
    pieces = [shard]
    for stride, radix in reversed(phases_of(count)[2:]):
        held = pieces[0] if len(pieces) == 1 else jnp.concatenate(pieces, axis=0)
        pieces = [held] + [swap(held, k * stride) for k in range(1, radix)]
    return pieces


def gather_near(held, count):
    pieces = [held]
    for stride, radix in phases_of(count)[1:2]:
        pieces += [swap(held, k * stride) for k in range(1, radix)]
    return pieces


def plan_of(pieces):
    return tuple((i, 0, piece.shape[0]) for i, piece in enumerate(pieces))


def near_first(shard, count):
    middle = shard.shape[1] // 2
    halves = [shard[:, :middle], shard[:, middle:]]
    if len(phases_of(count)) != 3:
        return halves
    return [piece for pair in zip(*(gather_near(half, count) for half in halves)) for piece in pair]


def then_far(held, count):
    phases = phases_of(count)
    if len(phases) != 3:
        pieces = gather_near(gather_far(held, count), count)
        return pieces, plan_of(pieces + pieces)
    (_, near), (stride, far) = phases[1:]
    rows = held.shape[0] // near
    pieces = [held] + [swap(held, k * stride) for k in range(1, far)]
    plan = [(core * far + z, x * rows, rows) for core in range(2) for x in range(near) for z in range(far)]
    return pieces, tuple(plan)


class Sum:
    def __init__(self, pairs, count, first=4, second=1):
        self.flat = [a for pair in pairs for parts in pair for a in parts]
        self.counts = tuple((len(acts), len(grads)) for acts, grads in pairs)
        self.phases = phases_of(count)
        self.columns = sum(grads[0].shape[1] for _, grads in pairs)
        self.rows = pairs[0][0][0].shape[1] // 2
        self.each, self.second = first, second
        self.sent = call(
            functools.partial(send_kernel, self.counts, first),
            [shape(self.rows // first, self.columns, BF16)] * first,
            self.flat,
        )
        self.keep = None
        self.got = []

    def go(self):
        (stride, _), self.phases = self.phases[0], self.phases[1:]
        self.got = [swap(piece, (k // self.each + 1) * stride) for k, piece in enumerate(self.sent)]
        return self

    def work(self):
        got = self.got
        if not self.phases:
            total = self.keep
            for piece in got:
                total = total + piece.astype(F32)
            self.keep = total
            return self
        radix = self.phases[0][1]
        self.rows //= radix
        outs = [shape(self.rows, self.columns, F32)]
        if self.keep is None:
            each = self.second if self.rows % (16 * self.second) == 0 else 1
            outs += [shape(self.rows // each, self.columns, BF16)] * ((radix - 1) * each)
            kernel = functools.partial(keep_kernel, self.counts, len(got), radix, each)
            outs = call(kernel, outs, self.flat + got)
        elif self.rows % 16 == 0:
            outs += [shape(self.rows, self.columns, BF16)] * (radix - 1)
            outs = call(functools.partial(add_kernel, len(got), self.each), outs, [self.keep] + got)
            each = 1
        else:
            total = self.keep
            for i in range(0, len(got), self.each):
                total = total + jnp.concatenate(got[i : i + self.each], axis=0).astype(F32)
            parts = [total[k * self.rows : (k + 1) * self.rows] for k in range(radix)]
            outs = [parts[0]] + [part.astype(BF16) for part in parts[1:]]
            each = 1
        self.each = each
        self.keep, *self.sent = outs
        return self

    def end(self):
        while self.phases:
            self.go().work()
        return self.keep


def tie(sums, *arrays):
    flat = list(arrays) + [piece for one in sums for piece in one.got]
    flat = lax.optimization_barrier(tuple(flat))
    at = len(arrays)
    for one in sums:
        one.got = list(flat[at : at + len(one.got)])
        at += len(one.got)
    return flat[: len(arrays)]


def flips_of(phases):
    found = [0]
    for stride, radix in phases:
        found = [k * stride + f for k in range(radix) for f in found]
    return found[1:]


def reduce_all(vector, flips):
    return total_of([vector] + [swap(vector, flip) for flip in flips])


def total_of(parts):
    while len(parts) > 1:
        parts = [parts[i] + parts[i + 1] for i in range(0, len(parts), 2)]
    return parts[0]


def body(
    stream,
    w_query,
    w_key,
    w_value,
    b_query,
    b_value,
    w_out,
    b_out,
    gain_attn,
    w_up,
    b_up,
    w_down,
    b_down,
    gain_mlp,
    cotangent,
    lengths,
):
    rows, inner_width = stream.shape
    count = lax.axis_size("dp")
    me = lax.axis_index("dp")
    rank = lax.axis_index("tensor").astype(jnp.int32).reshape(1, 1)
    shard_rows, own = w_query.shape
    width = shard_rows * count
    units = w_up.shape[1]
    blocks = jnp.array(relative_order(count), jnp.int32)
    order = ((me ^ blocks)[:, None] * shard_rows + jnp.arange(shard_rows, dtype=jnp.int32)).reshape(1, -1)

    shard_qkv = pack([w_query, w_key, w_value], 56 * 1024 * 1024)
    qkv_far = gather_far_pieces(shard_qkv, count)
    w_out_t, w_up, shard_dn, order, rank = lax.optimization_barrier((w_out.T, w_up, w_down.T, order, rank, shard_qkv))[:5]
    shard_ou = pack([w_out_t, swap_tensor(w_out_t), w_up])
    ent, acts_a = call(
        first_kernel,
        [shape(rows, width, BF16)] * 2,
        [order, stream, gain_attn],
        scratch=[pltpu.VMEM((width, width), BF16)],
    )
    dn_near = near_first(shard_dn, count)
    flat = lax.optimization_barrier((shard_ou, acts_a, *qkv_far, *dn_near))
    shard_ou, acts_a, qkv_far, dn_near = flat[0], flat[1], flat[2 : 2 + len(qkv_far)], flat[2 + len(qkv_far) :]
    middle_at = (len(qkv_far) + 1) // 2
    halves = [jnp.concatenate(part, axis=0) for part in (qkv_far[:middle_at], qkv_far[middle_at:]) if part]
    qkv_w = [piece for group in zip(*(gather_near(half, count) for half in halves)) for piece in group]
    ou_far = gather_far_pieces(shard_ou, count)

    qkv_w = qkv_w + [swap(piece, 1) for piece in qkv_w]
    plan = plan_of(qkv_w)
    bias_qkv = jnp.concatenate([b_query, jnp.zeros_like(b_query), b_value]).astype(F32)[None]
    qkv, context, lse = call(
        functools.partial(attend_kernel, plan),
        [shape(rows, 3 * own, BF16), shape(rows, own, BF16), shape(8, rows, F32)],
        [lengths, acts_a, bias_qkv] + qkv_w,
        scalars=1,
        scratch=[pltpu.VMEM((rows, rows), F32)],
    )
    context, *ou_far = lax.optimization_barrier((context, *ou_far))
    dn_near = jnp.concatenate([jnp.concatenate(dn_near[i::2], axis=0) for i in range(2)], axis=1)
    ou_far = jnp.concatenate(ou_far, axis=0)
    other_context = [swap_tensor(context)]
    ou_w = gather_near(ou_far, count)
    dn_w, plan_dn = then_far(dn_near, count)
    made = call(
        prepare_kernel,
        [shape(rows, width, BF16)] * 4 + [shape(8, width, F32)],
        [rank, order, cotangent, context, *other_context, ent, gain_attn, gain_mlp, b_out, b_down],
        scalars=1,
    )
    flat = lax.optimization_barrier((*made, *ou_w, *dn_w))
    (context_all, ent_mid, top, gbm, row), flat = flat[:5], flat[5:]
    ou_w, dn_w = list(flat[: len(ou_w)]), list(flat[len(ou_w) :])
    ou_w = ou_w + [swap(piece, 1) for piece in ou_w]
    plan_ou = plan_of(ou_w)
    dn_w = dn_w + [swap(piece, 1) for piece in dn_w]

    cuts = [(0, rows)]
    bias_up = b_up.astype(F32)[None]
    middle, acts_m, active, ghid, gn, gn_other, gbup = [], [], [], [], [], [], []
    for lo, size in cuts:
        made = call(
            functools.partial(middle_kernel, lo, (plan_ou, plan_dn), len(ou_w)),
            [
                shape(size, width, F32),
                shape(size, width, BF16),
                shape(size, units, BF16),
                shape(size, units, BF16),
                shape(size, width, BF16),
                shape(1, units, F32),
            ],
            [rank, order, row, bias_up, context_all, ent_mid, gbm] + ou_w + dn_w,
            scalars=1,
        )
        for held, new in zip((middle, acts_m, active, ghid, gn, gbup), made):
            held.append(new)
        gn_other.append(swap_tensor(gn[-1]))

    sum_dn = Sum([((gbm,), active)], count, first=2).go()
    sum_up = Sum([(acts_m, ghid)], count, first=2).go()
    sum_dn.work().go()
    sum_up.work().go()
    (mlp,) = call(
        functools.partial(mix_kernel, plan_dn, len(active)),
        [shape(rows, width, BF16)],
        [after(active[0], sum_up.sent)] + active[1:] + dn_w,
    )
    mlp_other = swap_tensor(mlp)
    sum_dn.work().go()

    gmid, gba, gctx, sums = [], [], [], []
    gn_other[0] = after(gn_other[0], sum_dn.sent, sum_up.sent, mlp)
    for i, (lo, size) in enumerate(cuts):
        made = call(
            functools.partial(back_kernel, lo, plan_ou),
            [shape(size, width, F32), shape(size, width, BF16), shape(size, own, BF16), shape(8, width, F32)],
            [order, row, gn[i], gn_other[i], middle[i], top] + ou_w,
        )
        for held, new in zip((gmid, gba, gctx, sums), made):
            held.append(new)
    gq, gkv = call(
        attend_back_kernel,
        [shape(rows, own, BF16), shape(rows, 2 * own, BF16)],
        [lengths, qkv, lse] + gctx,
        scalars=1,
        scratch=[pltpu.VMEM((rows, rows), F32), pltpu.VMEM((rows, PAIR), F32), pltpu.VMEM((rows, PAIR), F32)],
        cost=LONG,
    )
    gq, gkv = tie([sum_dn, sum_up], gq, gkv)
    sum_last = Sum([(gba, (context,)), ((acts_a,), (gq,)), ((acts_a,), (gkv,))], count, first=2).go()
    sum_last.work().go()
    sum_up.work().go()
    gq, gkv, mlp_other = lax.optimization_barrier((gq, gkv, mlp_other, *sum_last.sent, *sum_up.sent))[:3]
    part, gain, gbias = call(
        functools.partial(part_kernel, plan),
        [shape(rows, width, BF16), shape(1, width, F32), shape(1, 2 * own, F32)],
        [gq, gkv, ent, order] + qkv_w,
        cost=LONG,
    )
    gain_other = swap_tensor(gain)
    part_other = swap_tensor(part)
    (plain,) = call(
        functools.partial(vector_kernel, len(cuts)),
        [shape(8 * width // 128, 128, F32)],
        [order, row, gain, gain_other, gbias] + sums + gbup,
    )
    phases = phases_of(count)
    parts = [plain] + [swap(plain, flip) for flip in flips_of(phases[:2])]
    plain = total_of(list(tie([sum_last, sum_up], *parts)))
    short = len(phases) == 3
    if short:
        block = plain
        given, radix, size = len(sum_last.got), phases[2][1], sum_last.rows // phases[2][1]
        columns = sum_last.columns
        keep, *sent = call(
            functools.partial(add_vector_kernel, given, sum_last.each),
            [shape(size, columns, F32)] + [shape(size, columns + block.shape[1], BF16)] * (radix - 1),
            [block, sum_last.keep] + sum_last.got,
        )
        last_got = [swap(piece, (k + 1) * phases[2][0]) for k, piece in enumerate(sent)]
    else:
        sum_last.work()
        sent = sum_last.sent
        sum_last.go()
        for phase in phases[2:]:
            plain = reduce_all(plain, flips_of([phase]))
    mlp_other = after(mlp_other, sent)
    (out_rows,) = call(
        result_kernel,
        [shape(rows, inner_width, BF16)],
        [order, row, *middle, mlp, mlp_other],
        scratch=[pltpu.VMEM((width, width), BF16)],
    )
    part_other, out_rows = lax.optimization_barrier((part_other, out_rows))
    (grad_stream,) = call(
        final_kernel,
        [shape(rows, inner_width, BF16)],
        [order, row, part, part_other, ent, *gmid],
        scratch=[pltpu.VMEM((width, width), BF16)],
    )
    shard_dn_t, shard_up = (one.work().end() for one in (sum_dn, sum_up))
    if short:
        keep, grad_stream = lax.optimization_barrier((keep, grad_stream))
        sizes = [width] * 4 + [2 * width, own, own]
        out_t, grad_q, grad_k, grad_v, *vectors = call(
            functools.partial(finish_kernel, len(last_got), len(sizes)),
            [shape(shard_rows, own, F32)] * 4 + [jax.ShapeDtypeStruct((size,), F32) for size in sizes],
            [block, keep] + last_got,
        )
    else:
        last = sum_last.work().end()
        out_t, grad_q, grad_k, grad_v = (last[:, i * own : (i + 1) * own] for i in range(4))
        plain = plain.reshape(8, width)
        vectors = [plain[0], plain[1], plain[2], plain[3], plain[4:6].reshape(-1), plain[6, :own], plain[6, own:]]
    grad_b_down, grad_gain_mlp, grad_b_out, grad_gain_attn, grad_b_up, grad_b_query, grad_b_value = vectors
    return (
        out_rows,
        grad_stream,
        grad_q,
        grad_k,
        grad_v,
        grad_b_query,
        grad_b_value,
        out_t.T,
        grad_b_out,
        grad_gain_attn,
        shard_up,
        grad_b_up,
        shard_dn_t.T,
        grad_b_down,
        grad_gain_mlp,
    )


def solution(mesh):
    return jax.shard_map(
        body,
        mesh=mesh,
        in_specs=(
            P("dp", None),
            P("dp", "tensor"),
            P("dp", "tensor"),
            P("dp", "tensor"),
            P("tensor"),
            P("tensor"),
            P("tensor", "dp"),
            P(),
            P(),
            P("dp", "tensor"),
            P("tensor"),
            P("tensor", "dp"),
            P(),
            P(),
            P("dp", None),
            P("dp", None),
        ),
        out_specs=(
            P("dp", None),
            P("dp", None),
            P("dp", "tensor"),
            P("dp", "tensor"),
            P("dp", "tensor"),
            P("tensor"),
            P("tensor"),
            P("tensor", "dp"),
            P(),
            P(),
            P("dp", "tensor"),
            P("tensor"),
            P("tensor", "dp"),
            P(),
            P(),
        ),
        check_vma=False,
    )
```

```python
import functools

import jax
import jax.numpy as jnp
from jax import lax
from jax.experimental import pallas as pl
from jax.experimental.pallas import tpu as pltpu
from jax.sharding import PartitionSpec as P

HD = 64
PAIR = 2 * HD
STEP = 384
epsilon = 1e-05
ROOM = 10 * 1024 * 1024
LONG = 100_000_000_000
F32 = jnp.float32
BF16 = jnp.bfloat16
VMEM = pl.BlockSpec(memory_space=pltpu.VMEM)
SMEM = pl.BlockSpec(memory_space=pltpu.SMEM)
FAR = pl.BlockSpec(memory_space=pltpu.HBM)


def phases_of(count):
    found, stride = [], 1
    while stride < count:
        rest = count // stride
        radix = 2 if stride == 1 or (rest.bit_length() - 1) % 2 == 1 else 4
        found.append((stride, radix))
        stride *= radix
    return found


def relative_order(count):
    blocks = [0]
    for stride, radix in reversed(phases_of(count)):
        blocks = [b ^ (k * stride) for k in range(radix) for b in blocks]
    return blocks


def swap(array, flip):
    count = lax.axis_size("dp")
    return lax.ppermute(array, "dp", [(i, i ^ flip) for i in range(count)])


def swap_tensor(array):
    count = lax.axis_size("tensor")
    return lax.ppermute(array, "tensor", [(i, i ^ 1) for i in range(count)])


def dot_nn(left, right):
    return lax.dot_general(left, right, (((1,), (0,)), ((), ())), preferred_element_type=F32)


def dot_nt(left, right):
    return lax.dot_general(left, right, (((1,), (1,)), ((), ())), preferred_element_type=F32)


def dot_tn(left, right):
    return lax.dot_general(left, right, (((0,), (0,)), ((), ())), preferred_element_type=F32)


def shape(rows, columns, dtype):
    return jax.ShapeDtypeStruct((rows, columns), dtype)


def after(array, *others):
    return lax.optimization_barrier((array,) + others)[0]


def call(kernel, outs, args, scalars=0, scratch=(), room=ROOM, cost=0):
    return pl.pallas_call(
        kernel,
        out_shape=outs,
        in_specs=[SMEM] * scalars + [VMEM] * (len(args) - scalars),
        out_specs=[VMEM] * len(outs),
        scratch_shapes=list(scratch),
        compiler_params=pltpu.CompilerParams(vmem_limit_bytes=room),
        cost_estimate=pl.CostEstimate(flops=cost, bytes_accessed=1024, transcendentals=0),
    )(*args)


def chooser_of(order_ref, rows):
    place = lax.broadcasted_iota(jnp.int32, (rows, order_ref.shape[1]), 0)
    return (place == order_ref[...]).astype(F32).astype(BF16)


def last_of(order_ref):
    return (order_ref[...] == order_ref.shape[1] - 1).astype(F32)


def expand(rows, last):
    return rows - jnp.sum(rows, axis=1, keepdims=True) * last


def norm_of(full):
    inverse = lax.rsqrt(jnp.mean(full * full, axis=1, keepdims=True) + epsilon)
    return full * inverse, inverse


def norm_backward(grad, normed, inverse, gain, last):
    scaled = grad * gain
    full = inverse * (scaled - normed * jnp.mean(scaled * normed, axis=1, keepdims=True))
    return (full - jnp.sum(full * last, axis=1, keepdims=True)) * (1.0 - last)


def center(rows):
    return rows - jnp.mean(rows, axis=1, keepdims=True)


def by_rows_one(rows, body, carry=0):
    return body(slice(0, rows), carry)


def by_rows(rows, body, carry=0):
    step = next(size for size in (288, 192, 144, 96, 48, rows) if rows % size == 0)
    return lax.fori_loop(0, rows // step, lambda i, c: body(pl.ds(pl.multiple_of(i * step, step), step), c), carry)


def pack_kernel(*refs):
    at = 0
    for ref in refs[:-1]:
        refs[-1][:, at : at + ref.shape[1]] = ref[...]
        at += ref.shape[1]


def move(sems, *pairs):
    copies = [pltpu.make_async_copy(source, target, sems.at[i]) for i, (source, target) in enumerate(pairs)]
    for copy in copies:
        copy.start()
    return copies


def pack_far_kernel(*refs):
    *parts, out_ref, sems = refs
    pairs, at = [], 0
    for ref in parts:
        pairs.append((ref, out_ref.at[:, at : at + ref.shape[1]]))
        at += ref.shape[1]
    for copy in move(sems, *pairs):
        copy.wait()


def pack(arrays, room=ROOM):
    rows, columns = arrays[0].shape[0], sum(a.shape[1] for a in arrays)
    if rows % 16:
        return call(pack_kernel, [shape(rows, columns, BF16)], arrays)[0]
    return pl.pallas_call(
        pack_far_kernel,
        out_shape=shape(rows, columns, BF16),
        in_specs=[FAR] * len(arrays),
        out_specs=VMEM,
        scratch_shapes=[pltpu.SemaphoreType.DMA((len(arrays),))],
        compiler_params=pltpu.CompilerParams(vmem_limit_bytes=room),
        cost_estimate=pl.CostEstimate(flops=0, bytes_accessed=1024, transcendentals=0),
    )(*arrays)


def joined(refs, columns=slice(None)):
    return refs[0][:, columns] if len(refs) == 1 else jnp.concatenate([ref[:, columns] for ref in refs], axis=0)


def stacked(refs, plan, columns):
    parts = [refs[i][a : a + n, columns] for i, a, n in plan]
    return parts[0] if len(parts) == 1 else jnp.concatenate(parts, axis=0)


def first_kernel(order_ref, stream_ref, gain_ref, ent_ref, acts_ref, chooser_ref):
    chooser_ref[...] = chooser_of(order_ref, order_ref.shape[1])
    last = last_of(order_ref)
    gain = gain_ref[...].astype(F32).reshape(1, -1)
    gain = dot_nn(jnp.concatenate([gain] * 8, axis=0).astype(BF16), chooser_ref[...])[0:1]
    inner = stream_ref.shape[1]

    def one(at, carry):
        entering = dot_nn(stream_ref[at, :], chooser_ref[:inner, :])
        ent_ref[at, :] = entering.astype(BF16)
        normed, _ = norm_of(expand(entering, last))
        acts_ref[at, :] = (normed * gain).astype(BF16)
        return carry

    by_rows_one(stream_ref.shape[0], one)


def prepare_kernel(rank_ref, order_ref, cot_ref, own_ref, other_ref, ent_in, *refs):
    vec_refs, (ctx_ref, ent_ref, top_ref, gbm_ref, row_ref) = refs[:-5], refs[-5:]
    zero = rank_ref[0, 0] == 0
    width = own_ref.shape[1]
    own, other = own_ref[...], other_ref[...]
    ctx_ref[:, :width] = jnp.where(zero, own, other)
    ctx_ref[:, width:] = jnp.where(zero, other, own)
    ent_ref[...] = ent_in[...]
    chooser = chooser_of(order_ref, order_ref.shape[1])
    plain = [ref[...].astype(F32).reshape(1, -1) for ref in vec_refs]
    rows = dot_nn(jnp.concatenate(plain + plain, axis=0).astype(BF16), chooser)
    top = dot_nn(cot_ref[...], chooser[: cot_ref.shape[1]])
    top_ref[...] = top.astype(BF16)
    gbm = center(top)
    gbm_ref[...] = gbm.astype(BF16)
    row_ref[:4, :] = rows[:4]
    row_ref[4:5, :] = jnp.sum(gbm, axis=0, keepdims=True)
    row_ref[5:, :] = jnp.zeros((row_ref.shape[0] - 5, row_ref.shape[1]), F32)


def row_blocks(rows):
    return [(i, min(rows, i + STEP)) for i in range(0, rows, STEP)]


def write_mask(len_ref, mask_ref):
    for lo, hi in row_blocks(mask_ref.shape[0]):
        place = lax.broadcasted_iota(jnp.int32, (1, hi - lo), 1) + lo
        first = jnp.zeros_like(place)
        end = jnp.int32(0)
        for j in range(len_ref.shape[1] - 1):
            end = end + len_ref[0, j]
            first = jnp.where(place >= end, end, first)
        key = lax.broadcasted_iota(jnp.int32, (hi, hi - lo), 0)
        mask_ref[:hi, lo:hi] = jnp.where((key >= first) & (key <= place), 0.0, -1e30)


def both_heads(block):
    zero = jnp.zeros_like(block)
    first = lax.broadcasted_iota(jnp.int32, block.shape, 1) < HD
    return jnp.concatenate([jnp.where(first, block, zero), jnp.where(first, zero, block)], axis=0)


def own_rows(both):
    size = both.shape[1] // 2
    row = lax.broadcasted_iota(jnp.int32, (PAIR, size), 0)
    return jnp.where(row < HD, both[:, :size], both[:, size:])


def unit_of(size):
    r = lax.broadcasted_iota(jnp.int32, (size, size), 0)
    c = lax.broadcasted_iota(jnp.int32, (size, size), 1)
    return (r == c).astype(F32).astype(BF16)


def attend_kernel(plan, len_ref, acts_ref, bias_ref, *refs):
    weights, (qkv_ref, ctx_ref, lse_ref, mask_ref) = refs[:-4], refs[-4:]
    rows, own = ctx_ref.shape
    write_mask(len_ref, mask_ref)
    for at in range(0, 3 * own, own):
        cut = slice(at, at + own)
        qkv_ref[:, cut] = (dot_nn(acts_ref[...], stacked(weights, plan, cut)) + bias_ref[:, cut]).astype(BF16)
    unit = unit_of(PAIR)
    scale = jnp.asarray(HD**-0.5, BF16)
    for pair in range(own // PAIR):
        at = pair * PAIR
        keys = qkv_ref[:, own + at : own + at + PAIR]
        values_t = dot_nt(unit, qkv_ref[:, 2 * own + at : 2 * own + at + PAIR]).astype(BF16)
        for lo, hi in row_blocks(rows):
            size = hi - lo
            both = both_heads(qkv_ref[lo:hi, at : at + PAIR] * scale)
            mask = mask_ref[:hi, lo:hi]
            scores = dot_nt(keys[:hi], both) + jnp.concatenate([mask, mask], axis=1)
            peak = jnp.max(scores, axis=0, keepdims=True)
            expo = jnp.exp(scores - peak)
            total = jnp.sum(expo, axis=0, keepdims=True)
            probs = (expo * (1.0 / total)).astype(BF16)
            lse = peak + jnp.log(total)
            lse_ref[2 * pair : 2 * pair + 1, lo:hi] = lse[:, :size]
            lse_ref[2 * pair + 1 : 2 * pair + 2, lo:hi] = lse[:, size:]
            ctx_ref[lo:hi, at : at + PAIR] = own_rows(dot_nn(values_t[:, :hi], probs)).T.astype(BF16)


def middle_kernel(lo, plan, many, rank_ref, order_ref, row_ref, bup_ref, ctx_ref, ent_ref, gbm_ref, *refs):
    weights, downs, (mid_ref, acts_ref, active_ref, ghid_ref, gn_ref, gbup_ref) = refs[:many], refs[many:-6], refs[-6:]
    plan, plan_dn = plan
    rows = slice(lo, lo + mid_ref.shape[0])
    zero = rank_ref[0, 0] == 0
    own = ctx_ref.shape[1] // 2
    last = last_of(order_ref)

    def ordered(a, b):
        return jnp.where(zero, a, b), jnp.where(zero, b, a)

    w_first, w_second = ordered(stacked(weights, plan, slice(0, own)), stacked(weights, plan, slice(own, 2 * own)))
    branch = dot_nt(ctx_ref[rows, :own], w_first) + dot_nt(ctx_ref[rows, own:], w_second) + row_ref[2:3]
    middle = ent_ref[rows, :].astype(F32) + center(branch) * (1.0 - last)
    mid_ref[...] = middle
    normed, _ = norm_of(expand(middle, last))
    acts = (normed * row_ref[1:2]).astype(BF16)
    acts_ref[...] = acts
    gbm = gbm_ref[rows, :]
    units = active_ref.shape[1]
    piece = units // 2
    total = None
    for at in range(0, units, piece):
        cut, cut_up = slice(at, at + piece), slice(2 * own + at, 2 * own + at + piece)
        up_part = stacked(weights, plan, cut_up)
        hidden = dot_nn(acts, up_part) + bup_ref[:, cut]
        gact = dot_nn(gbm, stacked(downs, plan_dn, cut))
        square = hidden * hidden
        bend = jnp.tanh(hidden * (0.7978845608028654 + 0.7978845608028654 * 0.044715 * square))
        up = 0.5 + 0.5 * bend
        active_ref[:, cut] = (hidden * up).astype(BF16)
        slope = up + (0.5 * hidden) * (1.0 - bend * bend) * (
            0.7978845608028654 + 0.7978845608028654 * 3 * 0.044715 * square
        )
        ghid = (gact * slope).astype(BF16)
        ghid_ref[:, cut] = ghid
        gbup_ref[:, cut] = jnp.sum(ghid.astype(F32), axis=0, keepdims=True)
        part = dot_nt(ghid, up_part)
        total = part if total is None else total + part
    gn_ref[...] = total.astype(BF16)


def mix_kernel(plan, parts, *refs):
    refs[-1][...] = dot_nt(joined(refs[:parts]), stacked(refs[parts:-1], plan, slice(None))).astype(BF16)


def back_kernel(lo, plan, order_ref, row_ref, own_ref, other_ref, mid_ref, top_ref, *refs):
    weights, (gmid_ref, gba_ref, gctx_ref, sum_ref) = refs[:-4], refs[-4:]
    last = last_of(order_ref)
    gain = row_ref[1:2]
    weights = stacked(weights, plan, slice(0, gctx_ref.shape[1]))

    def one(at, carry):
        grad = own_ref[at, :].astype(F32) + other_ref[at, :].astype(F32)
        normed, inverse = norm_of(expand(mid_ref[at, :], last))
        gmid = top_ref[at, :].astype(F32) + norm_backward(grad, normed, inverse, gain, last)
        gmid_ref[at, :] = gmid
        gba = center(gmid)
        low = gba.astype(BF16)
        gba_ref[at, :] = low
        gctx_ref[at, :] = dot_nn(low, weights).astype(BF16)
        gain_sum, ba_sum = carry
        return (
            gain_sum + jnp.sum(grad * normed, axis=0, keepdims=True),
            ba_sum + jnp.sum(gba, axis=0, keepdims=True),
        )

    zero = jnp.zeros((1, sum_ref.shape[1]), F32)
    sum_ref[0:1, :], sum_ref[1:2, :] = by_rows_one(own_ref.shape[0], one, (zero, zero))
    sum_ref[2:, :] = jnp.zeros((sum_ref.shape[0] - 2, sum_ref.shape[1]), F32)


def attend_back_kernel(
    len_ref, qkv_ref, lse_ref, *refs
):
    gctx_refs, (gq_ref, gkv_ref, mask_ref, gk_ref, gv_ref) = refs[:-5], refs[-5:]
    rows, own = gq_ref.shape
    write_mask(len_ref, mask_ref)
    unit = unit_of(PAIR)
    scale = jnp.asarray(HD**-0.5, BF16)
    for pair in range(own // PAIR):
        at = pair * PAIR
        keys = qkv_ref[:, own + at : own + at + PAIR]
        values = qkv_ref[:, 2 * own + at : 2 * own + at + PAIR]
        keys_t = dot_nt(unit, keys * scale).astype(BF16)
        gctx = joined(gctx_refs, slice(at, at + PAIR))
        for lo, hi in reversed(row_blocks(rows)):
            size = hi - lo
            both_q = both_heads(qkv_ref[lo:hi, at : at + PAIR] * scale)
            both_g = both_heads(gctx[lo:hi])
            lse = jnp.concatenate(
                [lse_ref[2 * pair : 2 * pair + 1, lo:hi], lse_ref[2 * pair + 1 : 2 * pair + 2, lo:hi]], axis=1
            )
            mask = mask_ref[:hi, lo:hi]
            probs = jnp.exp(dot_nt(keys[:hi], both_q) + jnp.concatenate([mask, mask], axis=1) - lse)
            gprobs = dot_nt(values[:hi], both_g)
            delta = jnp.sum(probs * gprobs, axis=0, keepdims=True)
            gscores = (probs * (gprobs - delta)).astype(BF16)
            gq_ref[lo:hi, at : at + PAIR] = own_rows(dot_nn(keys_t[:, :hi], gscores)).T.astype(BF16)
            gk = dot_nn(gscores, both_q)
            gv = dot_nn(probs.astype(BF16), both_g)
            if hi == rows:
                gk_ref[...] = gk
                gv_ref[...] = gv
            else:
                gk_ref[:hi, :] += gk
                gv_ref[:hi, :] += gv
        gkv_ref[:, at : at + PAIR] = gk_ref[...].astype(BF16)
        gkv_ref[:, own + at : own + at + PAIR] = gv_ref[...].astype(BF16)


def part_kernel(plan, gq_ref, gkv_ref, ent_ref, order_ref, *refs):
    weights, (part_ref, sum_ref, bias_ref) = refs[:-3], refs[-3:]
    own = gq_ref.shape[1]
    last = last_of(order_ref)
    w_q, w_kv = stacked(weights, plan, slice(0, own)), stacked(weights, plan, slice(own, 3 * own))

    def one(at, carry):
        gq, gkv = gq_ref[at, :], gkv_ref[at, :]
        part = (dot_nt(gq, w_q) + dot_nt(gkv, w_kv)).astype(BF16)
        part_ref[at, :] = part
        normed, _ = norm_of(expand(ent_ref[at, :].astype(F32), last))
        gain_sum, q_sum, v_sum = carry
        return (
            gain_sum + jnp.sum(part.astype(F32) * normed, axis=0, keepdims=True),
            q_sum + jnp.sum(gq.astype(F32), axis=0, keepdims=True),
            v_sum + jnp.sum(gkv[:, own:].astype(F32), axis=0, keepdims=True),
        )

    zeros = jnp.zeros((1, 2 * own), F32), jnp.zeros((1, own), F32), jnp.zeros((1, own), F32)
    sum_ref[...], bias_ref[:, :own], bias_ref[:, own:] = by_rows(gq_ref.shape[0], one, zeros)


def vector_kernel(parts, order_ref, row_ref, gain_ref, gain_other, bias_ref, *refs):
    sum_refs, gbup_refs, out_ref = refs[:parts], refs[parts:-1], refs[-1]
    width = order_ref.shape[1]
    chooser = chooser_of(order_ref, width)
    sums = sum(ref[0:2] for ref in sum_refs)
    gbup = sum(ref[...] for ref in gbup_refs)
    gain = gain_ref[...] + gain_other[...]
    rows = jnp.concatenate([row_ref[4:5], sums, gain, jnp.zeros((4, width), F32)], axis=0)
    plain = jnp.zeros_like(rows)
    for _ in range(3):
        low = rows.astype(BF16)
        plain = plain + dot_nt(low, chooser)
        rows = rows - low.astype(F32)
    plain = jnp.concatenate([plain[0:4], gbup[:, :width], gbup[:, width:], bias_ref[...], plain[7:8]], axis=0)
    lanes = out_ref.shape[1]
    for r in range(8):
        for j in range(width // lanes):
            at = r * (width // lanes) + j
            out_ref[at : at + 1, :] = plain[r : r + 1, j * lanes : (j + 1) * lanes]


def result_kernel(order_ref, row_ref, mid_ref, own_ref, other_ref, out_ref, chooser_ref):
    last = last_of(order_ref)
    chooser_ref[...] = chooser_of(order_ref, order_ref.shape[1])

    def one(at, carry):
        branch = own_ref[at, :].astype(F32) + other_ref[at, :].astype(F32) + row_ref[3:4]
        result = (mid_ref[at, :] + center(branch) * (1.0 - last)).astype(BF16)
        out_ref[at, :] = dot_nt(result, chooser_ref[...])[:, : out_ref.shape[1]].astype(BF16)
        return carry

    by_rows(mid_ref.shape[0], one)


def final_kernel(order_ref, row_ref, own_ref, other_ref, ent_ref, gmid_ref, out_ref, chooser_ref):
    last = last_of(order_ref)
    chooser_ref[...] = chooser_of(order_ref, order_ref.shape[1])

    def one(at, carry):
        grad = own_ref[at, :].astype(F32) + other_ref[at, :].astype(F32)
        normed, inverse = norm_of(expand(ent_ref[at, :].astype(F32), last))
        grad = (gmid_ref[at, :] + norm_backward(grad, normed, inverse, row_ref[0:1], last)).astype(BF16)
        out_ref[at, :] = dot_nt(grad, chooser_ref[...])[:, : out_ref.shape[1]].astype(BF16)
        return carry

    by_rows(ent_ref.shape[0], one)


def pairs_of(refs, counts):
    found, at = [], 0
    for acts, grads in counts:
        found.append((refs[at : at + acts], refs[at + acts : at + acts + grads]))
        at += acts + grads
    return found


def send_kernel(counts, pieces, *refs):
    outs, at = refs[-pieces:], 0
    rows = outs[0].shape[0]
    for acts, grads in pairs_of(refs, counts):
        half = acts[0].shape[1] // 2
        cut = slice(at, at + grads[0].shape[1])
        made = dot_tn(joined(acts, slice(half, None)), joined(grads)).astype(BF16)
        for i, out_ref in enumerate(outs):
            out_ref[:, cut] = made[i * rows : (i + 1) * rows]
        at += grads[0].shape[1]


def keep_kernel(counts, pieces, radix, each, *refs):
    many = (radix - 1) * each
    keep_ref, send_refs = refs[-many - 1], refs[len(refs) - many :]
    got = joined(refs[-many - 1 - pieces : -many - 1]).astype(F32)
    rows, at = keep_ref.shape[0], 0
    size = rows // each
    for acts, grads in pairs_of(refs, counts):
        cut = slice(at, at + grads[0].shape[1])
        half = dot_tn(joined(acts, slice(0, rows * radix)), joined(grads)) + got[:, cut]
        keep_ref[:, cut] = half[:rows]
        for k, send_ref in enumerate(send_refs):
            send_ref[:, cut] = half[rows + k * size : rows + (k + 1) * size].astype(BF16)
        at += grads[0].shape[1]


def add_kernel(given, each, *refs):
    total = refs[0][...]
    for i in range(1, 1 + given, each):
        total = total + joined(refs[i : i + each]).astype(F32)
    rows = refs[1 + given].shape[0]
    refs[1 + given][...] = total[:rows]
    for k, ref in enumerate(refs[2 + given :]):
        ref[...] = total[(k + 1) * rows : (k + 2) * rows].astype(BF16)


def add_vector_kernel(given, each, *refs):
    vector, refs = refs[0][...].astype(BF16), refs[1:]
    total = refs[0][...]
    for i in range(1, 1 + given, each):
        total = total + joined(refs[i : i + each]).astype(F32)
    rows, columns = refs[1 + given].shape
    refs[1 + given][...] = total[:rows]
    for k, ref in enumerate(refs[2 + given :]):
        ref[:, :columns] = total[(k + 1) * rows : (k + 2) * rows].astype(BF16)
        ref[:, columns:] = vector


def finish_kernel(given, vectors, vector_ref, keep_ref, *refs):
    got, cuts, vec_refs = refs[:given], refs[given:-vectors], refs[-vectors:]
    columns = keep_ref.shape[1]
    total = keep_ref[...]
    parts = [vector_ref[...].astype(BF16).astype(F32)]
    for ref in got:
        total = total + ref[:, :columns].astype(F32)
        parts.append(ref[:, columns:].astype(F32))
    at = 0
    for ref in cuts:
        ref[...] = total[:, at : at + ref.shape[1]]
        at += ref.shape[1]
    while len(parts) > 1:
        parts = [parts[i] + parts[i + 1] for i in range(0, len(parts), 2)]
    at, lanes = 0, parts[0].shape[1]
    for ref in vec_refs:
        for j in range(ref.shape[0] // lanes):
            ref[j * lanes : (j + 1) * lanes] = parts[0][at]
            at += 1


def gather_far(shard, count):
    return jnp.concatenate(gather_far_pieces(shard, count), axis=0)


def gather_far_pieces(shard, count):
    pieces = [shard]
    for stride, radix in reversed(phases_of(count)[2:]):
        held = pieces[0] if len(pieces) == 1 else jnp.concatenate(pieces, axis=0)
        pieces = [held] + [swap(held, k * stride) for k in range(1, radix)]
    return pieces


def gather_near(held, count):
    pieces = [held]
    for stride, radix in phases_of(count)[1:2]:
        pieces += [swap(held, k * stride) for k in range(1, radix)]
    return pieces


def plan_of(pieces):
    return tuple((i, 0, piece.shape[0]) for i, piece in enumerate(pieces))


def near_first(shard, count):
    middle = shard.shape[1] // 2
    halves = [shard[:, :middle], shard[:, middle:]]
    if len(phases_of(count)) != 3:
        return halves
    return [piece for pair in zip(*(gather_near(half, count) for half in halves)) for piece in pair]


def then_far(held, count):
    phases = phases_of(count)
    if len(phases) != 3:
        pieces = gather_near(gather_far(held, count), count)
        return pieces, plan_of(pieces + pieces)
    (_, near), (stride, far) = phases[1:]
    rows = held.shape[0] // near
    pieces = [held] + [swap(held, k * stride) for k in range(1, far)]
    plan = [(core * far + z, x * rows, rows) for core in range(2) for x in range(near) for z in range(far)]
    return pieces, tuple(plan)


class Sum:
    def __init__(self, pairs, count, first=4, second=1):
        self.flat = [a for pair in pairs for parts in pair for a in parts]
        self.counts = tuple((len(acts), len(grads)) for acts, grads in pairs)
        self.phases = phases_of(count)
        self.columns = sum(grads[0].shape[1] for _, grads in pairs)
        self.rows = pairs[0][0][0].shape[1] // 2
        self.each, self.second = first, second
        self.sent = call(
            functools.partial(send_kernel, self.counts, first),
            [shape(self.rows // first, self.columns, BF16)] * first,
            self.flat,
        )
        self.keep = None
        self.got = []

    def go(self):
        (stride, _), self.phases = self.phases[0], self.phases[1:]
        self.got = [swap(piece, (k // self.each + 1) * stride) for k, piece in enumerate(self.sent)]
        return self

    def work(self):
        got = self.got
        if not self.phases:
            total = self.keep
            for piece in got:
                total = total + piece.astype(F32)
            self.keep = total
            return self
        radix = self.phases[0][1]
        self.rows //= radix
        outs = [shape(self.rows, self.columns, F32)]
        if self.keep is None:
            each = self.second if self.rows % (16 * self.second) == 0 else 1
            outs += [shape(self.rows // each, self.columns, BF16)] * ((radix - 1) * each)
            kernel = functools.partial(keep_kernel, self.counts, len(got), radix, each)
            outs = call(kernel, outs, self.flat + got)
        elif self.rows % 16 == 0:
            outs += [shape(self.rows, self.columns, BF16)] * (radix - 1)
            outs = call(functools.partial(add_kernel, len(got), self.each), outs, [self.keep] + got)
            each = 1
        else:
            total = self.keep
            for i in range(0, len(got), self.each):
                total = total + jnp.concatenate(got[i : i + self.each], axis=0).astype(F32)
            parts = [total[k * self.rows : (k + 1) * self.rows] for k in range(radix)]
            outs = [parts[0]] + [part.astype(BF16) for part in parts[1:]]
            each = 1
        self.each = each
        self.keep, *self.sent = outs
        return self

    def end(self):
        while self.phases:
            self.go().work()
        return self.keep


def tie(sums, *arrays):
    flat = list(arrays) + [piece for one in sums for piece in one.got]
    flat = lax.optimization_barrier(tuple(flat))
    at = len(arrays)
    for one in sums:
        one.got = list(flat[at : at + len(one.got)])
        at += len(one.got)
    return flat[: len(arrays)]


def flips_of(phases):
    found = [0]
    for stride, radix in phases:
        found = [k * stride + f for k in range(radix) for f in found]
    return found[1:]


def reduce_all(vector, flips):
    return total_of([vector] + [swap(vector, flip) for flip in flips])


def total_of(parts):
    while len(parts) > 1:
        parts = [parts[i] + parts[i + 1] for i in range(0, len(parts), 2)]
    return parts[0]


def body(
    stream,
    w_query,
    w_key,
    w_value,
    b_query,
    b_value,
    w_out,
    b_out,
    gain_attn,
    w_up,
    b_up,
    w_down,
    b_down,
    gain_mlp,
    cotangent,
    lengths,
):
    rows, inner_width = stream.shape
    count = lax.axis_size("dp")
    me = lax.axis_index("dp")
    rank = lax.axis_index("tensor").astype(jnp.int32).reshape(1, 1)
    shard_rows, own = w_query.shape
    width = shard_rows * count
    units = w_up.shape[1]
    blocks = jnp.array(relative_order(count), jnp.int32)
    order = ((me ^ blocks)[:, None] * shard_rows + jnp.arange(shard_rows, dtype=jnp.int32)).reshape(1, -1)

    shard_qkv = pack([w_query, w_key, w_value], 56 * 1024 * 1024)
    qkv_far = gather_far_pieces(shard_qkv, count)
    w_out_t, w_up, shard_dn, order, rank = lax.optimization_barrier((w_out.T, w_up, w_down.T, order, rank, shard_qkv))[:5]
    shard_ou = pack([w_out_t, swap_tensor(w_out_t), w_up])
    ent, acts_a = call(
        first_kernel,
        [shape(rows, width, BF16)] * 2,
        [order, stream, gain_attn],
        scratch=[pltpu.VMEM((width, width), BF16)],
    )
    dn_near = near_first(shard_dn, count)
    flat = lax.optimization_barrier((shard_ou, acts_a, *qkv_far, *dn_near))
    shard_ou, acts_a, qkv_far, dn_near = flat[0], flat[1], flat[2 : 2 + len(qkv_far)], flat[2 + len(qkv_far) :]
    middle_at = (len(qkv_far) + 1) // 2
    halves = [jnp.concatenate(part, axis=0) for part in (qkv_far[:middle_at], qkv_far[middle_at:]) if part]
    qkv_w = [piece for group in zip(*(gather_near(half, count) for half in halves)) for piece in group]
    ou_far = gather_far_pieces(shard_ou, count)

    qkv_w = qkv_w + [swap(piece, 1) for piece in qkv_w]
    plan = plan_of(qkv_w)
    bias_qkv = jnp.concatenate([b_query, jnp.zeros_like(b_query), b_value]).astype(F32)[None]
    qkv, context, lse = call(
        functools.partial(attend_kernel, plan),
        [shape(rows, 3 * own, BF16), shape(rows, own, BF16), shape(8, rows, F32)],
        [lengths, acts_a, bias_qkv] + qkv_w,
        scalars=1,
        scratch=[pltpu.VMEM((rows, rows), F32)],
    )
    context, *ou_far = lax.optimization_barrier((context, *ou_far))
    dn_near = jnp.concatenate([jnp.concatenate(dn_near[i::2], axis=0) for i in range(2)], axis=1)
    ou_far = jnp.concatenate(ou_far, axis=0)
    other_context = [swap_tensor(context)]
    ou_w = gather_near(ou_far, count)
    dn_w, plan_dn = then_far(dn_near, count)
    made = call(
        prepare_kernel,
        [shape(rows, width, BF16)] * 4 + [shape(8, width, F32)],
        [rank, order, cotangent, context, *other_context, ent, gain_attn, gain_mlp, b_out, b_down],
        scalars=1,
    )
    flat = lax.optimization_barrier((*made, *ou_w, *dn_w))
    (context_all, ent_mid, top, gbm, row), flat = flat[:5], flat[5:]
    ou_w, dn_w = list(flat[: len(ou_w)]), list(flat[len(ou_w) :])
    ou_w = ou_w + [swap(piece, 1) for piece in ou_w]
    plan_ou = plan_of(ou_w)
    dn_w = dn_w + [swap(piece, 1) for piece in dn_w]

    cuts = [(0, rows)]
    bias_up = b_up.astype(F32)[None]
    middle, acts_m, active, ghid, gn, gn_other, gbup = [], [], [], [], [], [], []
    for lo, size in cuts:
        made = call(
            functools.partial(middle_kernel, lo, (plan_ou, plan_dn), len(ou_w)),
            [
                shape(size, width, F32),
                shape(size, width, BF16),
                shape(size, units, BF16),
                shape(size, units, BF16),
                shape(size, width, BF16),
                shape(1, units, F32),
            ],
            [rank, order, row, bias_up, context_all, ent_mid, gbm] + ou_w + dn_w,
            scalars=1,
        )
        for held, new in zip((middle, acts_m, active, ghid, gn, gbup), made):
            held.append(new)
        gn_other.append(swap_tensor(gn[-1]))

    sum_dn = Sum([((gbm,), active)], count, first=2).go()
    sum_up = Sum([(acts_m, ghid)], count, first=2).go()
    sum_dn.work().go()
    sum_up.work().go()
    (mlp,) = call(
        functools.partial(mix_kernel, plan_dn, len(active)),
        [shape(rows, width, BF16)],
        [after(active[0], sum_up.sent)] + active[1:] + dn_w,
    )
    mlp_other = swap_tensor(mlp)
    sum_dn.work().go()

    gmid, gba, gctx, sums = [], [], [], []
    gn_other[0] = after(gn_other[0], sum_dn.sent, sum_up.sent, mlp)
    for i, (lo, size) in enumerate(cuts):
        made = call(
            functools.partial(back_kernel, lo, plan_ou),
            [shape(size, width, F32), shape(size, width, BF16), shape(size, own, BF16), shape(8, width, F32)],
            [order, row, gn[i], gn_other[i], middle[i], top] + ou_w,
        )
        for held, new in zip((gmid, gba, gctx, sums), made):
            held.append(new)
    gq, gkv = call(
        attend_back_kernel,
        [shape(rows, own, BF16), shape(rows, 2 * own, BF16)],
        [lengths, qkv, lse] + gctx,
        scalars=1,
        scratch=[pltpu.VMEM((rows, rows), F32), pltpu.VMEM((rows, PAIR), F32), pltpu.VMEM((rows, PAIR), F32)],
        cost=LONG,
    )
    gq, gkv = tie([sum_dn, sum_up], gq, gkv)
    sum_last = Sum([(gba, (context,)), ((acts_a,), (gq,)), ((acts_a,), (gkv,))], count, first=2).go()
    sum_last.work().go()
    sum_up.work().go()
    gq, gkv, mlp_other = lax.optimization_barrier((gq, gkv, mlp_other, *sum_last.sent, *sum_up.sent))[:3]
    part, gain, gbias = call(
        functools.partial(part_kernel, plan),
        [shape(rows, width, BF16), shape(1, width, F32), shape(1, 2 * own, F32)],
        [gq, gkv, ent, order] + qkv_w,
        cost=LONG,
    )
    gain_other = swap_tensor(gain)
    part_other = swap_tensor(part)
    (plain,) = call(
        functools.partial(vector_kernel, len(cuts)),
        [shape(8 * width // 128, 128, F32)],
        [order, row, gain, gain_other, gbias] + sums + gbup,
    )
    phases = phases_of(count)
    parts = [plain] + [swap(plain, flip) for flip in flips_of(phases[:2])]
    plain = total_of(list(tie([sum_last, sum_up], *parts)))
    short = len(phases) == 3
    if short:
        block = plain
        given, radix, size = len(sum_last.got), phases[2][1], sum_last.rows // phases[2][1]
        columns = sum_last.columns
        keep, *sent = call(
            functools.partial(add_vector_kernel, given, sum_last.each),
            [shape(size, columns, F32)] + [shape(size, columns + block.shape[1], BF16)] * (radix - 1),
            [block, sum_last.keep] + sum_last.got,
        )
        last_got = [swap(piece, (k + 1) * phases[2][0]) for k, piece in enumerate(sent)]
    else:
        sum_last.work()
        sent = sum_last.sent
        sum_last.go()
        for phase in phases[2:]:
            plain = reduce_all(plain, flips_of([phase]))
    mlp_other = after(mlp_other, sent)
    (out_rows,) = call(
        result_kernel,
        [shape(rows, inner_width, BF16)],
        [order, row, *middle, mlp, mlp_other],
        scratch=[pltpu.VMEM((width, width), BF16)],
    )
    part_other, out_rows = lax.optimization_barrier((part_other, out_rows))
    (grad_stream,) = call(
        final_kernel,
        [shape(rows, inner_width, BF16)],
        [order, row, part, part_other, ent, *gmid],
        scratch=[pltpu.VMEM((width, width), BF16)],
    )
    shard_dn_t, shard_up = (one.work().end() for one in (sum_dn, sum_up))
    if short:
        keep, grad_stream = lax.optimization_barrier((keep, grad_stream))
        sizes = [width] * 4 + [2 * width, own, own]
        out_t, grad_q, grad_k, grad_v, *vectors = call(
            functools.partial(finish_kernel, len(last_got), len(sizes)),
            [shape(shard_rows, own, F32)] * 4 + [jax.ShapeDtypeStruct((size,), F32) for size in sizes],
            [block, keep] + last_got,
        )
    else:
        last = sum_last.work().end()
        out_t, grad_q, grad_k, grad_v = (last[:, i * own : (i + 1) * own] for i in range(4))
        plain = plain.reshape(8, width)
        vectors = [plain[0], plain[1], plain[2], plain[3], plain[4:6].reshape(-1), plain[6, :own], plain[6, own:]]
    grad_b_down, grad_gain_mlp, grad_b_out, grad_gain_attn, grad_b_up, grad_b_query, grad_b_value = vectors
    return (
        out_rows,
        grad_stream,
        grad_q,
        grad_k,
        grad_v,
        grad_b_query,
        grad_b_value,
        out_t.T,
        grad_b_out,
        grad_gain_attn,
        shard_up,
        grad_b_up,
        shard_dn_t.T,
        grad_b_down,
        grad_gain_mlp,
    )


def solution(mesh):
    return jax.shard_map(
        body,
        mesh=mesh,
        in_specs=(
            P("dp", None),
            P("dp", "tensor"),
            P("dp", "tensor"),
            P("dp", "tensor"),
            P("tensor"),
            P("tensor"),
            P("tensor", "dp"),
            P(),
            P(),
            P("dp", "tensor"),
            P("tensor"),
            P("tensor", "dp"),
            P(),
            P(),
            P("dp", None),
            P("dp", None),
        ),
        out_specs=(
            P("dp", None),
            P("dp", None),
            P("dp", "tensor"),
            P("dp", "tensor"),
            P("dp", "tensor"),
            P("tensor"),
            P("tensor"),
            P("tensor", "dp"),
            P(),
            P(),
            P("dp", "tensor"),
            P("tensor"),
            P("tensor", "dp"),
            P(),
            P(),
        ),
        check_vma=False,
    )
```

```python
import functools

import jax
import jax.numpy as jnp
from jax import lax
from jax.experimental import pallas as pl
from jax.experimental.pallas import tpu as pltpu
from jax.sharding import PartitionSpec as P

HD = 64
PAIR = 2 * HD
STEP = 384
epsilon = 1e-05
ROOM = 10 * 1024 * 1024
LONG = 100_000_000_000
F32 = jnp.float32
BF16 = jnp.bfloat16
VMEM = pl.BlockSpec(memory_space=pltpu.VMEM)
SMEM = pl.BlockSpec(memory_space=pltpu.SMEM)
FAR = pl.BlockSpec(memory_space=pltpu.HBM)


def phases_of(count):
    found, stride = [], 1
    while stride < count:
        rest = count // stride
        radix = 2 if stride == 1 or (rest.bit_length() - 1) % 2 == 1 else 4
        found.append((stride, radix))
        stride *= radix
    return found


def relative_order(count):
    blocks = [0]
    for stride, radix in reversed(phases_of(count)):
        blocks = [b ^ (k * stride) for k in range(radix) for b in blocks]
    return blocks


def swap(array, flip):
    count = lax.axis_size("dp")
    return lax.ppermute(array, "dp", [(i, i ^ flip) for i in range(count)])


def swap_tensor(array):
    count = lax.axis_size("tensor")
    return lax.ppermute(array, "tensor", [(i, i ^ 1) for i in range(count)])


def dot_nn(left, right):
    return lax.dot_general(left, right, (((1,), (0,)), ((), ())), preferred_element_type=F32)


def dot_nt(left, right):
    return lax.dot_general(left, right, (((1,), (1,)), ((), ())), preferred_element_type=F32)


def dot_tn(left, right):
    return lax.dot_general(left, right, (((0,), (0,)), ((), ())), preferred_element_type=F32)


def shape(rows, columns, dtype):
    return jax.ShapeDtypeStruct((rows, columns), dtype)


def after(array, *others):
    return lax.optimization_barrier((array,) + others)[0]


def call(kernel, outs, args, scalars=0, scratch=(), room=ROOM, cost=0):
    return pl.pallas_call(
        kernel,
        out_shape=outs,
        in_specs=[SMEM] * scalars + [VMEM] * (len(args) - scalars),
        out_specs=[VMEM] * len(outs),
        scratch_shapes=list(scratch),
        compiler_params=pltpu.CompilerParams(vmem_limit_bytes=room),
        cost_estimate=pl.CostEstimate(flops=cost, bytes_accessed=1024, transcendentals=0),
    )(*args)


def chooser_of(order_ref, rows):
    place = lax.broadcasted_iota(jnp.int32, (rows, order_ref.shape[1]), 0)
    return (place == order_ref[...]).astype(F32).astype(BF16)


def last_of(order_ref):
    return (order_ref[...] == order_ref.shape[1] - 1).astype(F32)


def expand(rows, last):
    return rows - jnp.sum(rows, axis=1, keepdims=True) * last


def norm_of(full):
    inverse = lax.rsqrt(jnp.mean(full * full, axis=1, keepdims=True) + epsilon)
    return full * inverse, inverse


def norm_backward(grad, normed, inverse, gain, last):
    scaled = grad * gain
    full = inverse * (scaled - normed * jnp.mean(scaled * normed, axis=1, keepdims=True))
    return (full - jnp.sum(full * last, axis=1, keepdims=True)) * (1.0 - last)


def center(rows):
    return rows - jnp.mean(rows, axis=1, keepdims=True)


def by_rows(rows, body, carry=0):
    step = next(size for size in (288, 192, 144, 96, 48, rows) if rows % size == 0)
    return lax.fori_loop(0, rows // step, lambda i, c: body(pl.ds(pl.multiple_of(i * step, step), step), c), carry)


def pack_kernel(*refs):
    at = 0
    for ref in refs[:-1]:
        refs[-1][:, at : at + ref.shape[1]] = ref[...]
        at += ref.shape[1]


def move(sems, *pairs):
    copies = [pltpu.make_async_copy(source, target, sems.at[i]) for i, (source, target) in enumerate(pairs)]
    for copy in copies:
        copy.start()
    return copies


def pack_far_kernel(*refs):
    *parts, out_ref, sems = refs
    pairs, at = [], 0
    for ref in parts:
        pairs.append((ref, out_ref.at[:, at : at + ref.shape[1]]))
        at += ref.shape[1]
    for copy in move(sems, *pairs):
        copy.wait()


def pack(arrays, room=ROOM):
    rows, columns = arrays[0].shape[0], sum(a.shape[1] for a in arrays)
    if rows % 16:
        return call(pack_kernel, [shape(rows, columns, BF16)], arrays)[0]
    return pl.pallas_call(
        pack_far_kernel,
        out_shape=shape(rows, columns, BF16),
        in_specs=[FAR] * len(arrays),
        out_specs=VMEM,
        scratch_shapes=[pltpu.SemaphoreType.DMA((len(arrays),))],
        compiler_params=pltpu.CompilerParams(vmem_limit_bytes=room),
        cost_estimate=pl.CostEstimate(flops=0, bytes_accessed=1024, transcendentals=0),
    )(*arrays)


def joined(refs, columns=slice(None)):
    return refs[0][:, columns] if len(refs) == 1 else jnp.concatenate([ref[:, columns] for ref in refs], axis=0)


def stacked(refs, plan, columns):
    parts = [refs[i][a : a + n, columns] for i, a, n in plan]
    return parts[0] if len(parts) == 1 else jnp.concatenate(parts, axis=0)


def first_kernel(order_ref, stream_ref, gain_ref, ent_ref, acts_ref, chooser_ref):
    chooser_ref[...] = chooser_of(order_ref, order_ref.shape[1])
    last = last_of(order_ref)
    gain = gain_ref[...].astype(F32).reshape(1, -1)
    gain = dot_nn(jnp.concatenate([gain] * 8, axis=0).astype(BF16), chooser_ref[...])[0:1]
    inner = stream_ref.shape[1]

    def one(at, carry):
        entering = dot_nn(stream_ref[at, :], chooser_ref[:inner, :])
        ent_ref[at, :] = entering.astype(BF16)
        normed, _ = norm_of(expand(entering, last))
        acts_ref[at, :] = (normed * gain).astype(BF16)
        return carry

    by_rows(stream_ref.shape[0], one)


def prepare_kernel(rank_ref, order_ref, cot_ref, own_ref, other_ref, ent_in, *refs):
    vec_refs, (ctx_ref, ent_ref, top_ref, gbm_ref, row_ref) = refs[:-5], refs[-5:]
    zero = rank_ref[0, 0] == 0
    width = own_ref.shape[1]
    own, other = own_ref[...], other_ref[...]
    ctx_ref[:, :width] = jnp.where(zero, own, other)
    ctx_ref[:, width:] = jnp.where(zero, other, own)
    ent_ref[...] = ent_in[...]
    chooser = chooser_of(order_ref, order_ref.shape[1])
    plain = [ref[...].astype(F32).reshape(1, -1) for ref in vec_refs]
    rows = dot_nn(jnp.concatenate(plain + plain, axis=0).astype(BF16), chooser)
    top = dot_nn(cot_ref[...], chooser[: cot_ref.shape[1]])
    top_ref[...] = top.astype(BF16)
    gbm = center(top)
    gbm_ref[...] = gbm.astype(BF16)
    row_ref[:4, :] = rows[:4]
    row_ref[4:5, :] = jnp.sum(gbm, axis=0, keepdims=True)
    row_ref[5:, :] = jnp.zeros((row_ref.shape[0] - 5, row_ref.shape[1]), F32)


def row_blocks(rows):
    return [(i, min(rows, i + STEP)) for i in range(0, rows, STEP)]


def write_mask(len_ref, mask_ref):
    for lo, hi in row_blocks(mask_ref.shape[0]):
        place = lax.broadcasted_iota(jnp.int32, (1, hi - lo), 1) + lo
        first = jnp.zeros_like(place)
        end = jnp.int32(0)
        for j in range(len_ref.shape[1] - 1):
            end = end + len_ref[0, j]
            first = jnp.where(place >= end, end, first)
        key = lax.broadcasted_iota(jnp.int32, (hi, hi - lo), 0)
        mask_ref[:hi, lo:hi] = jnp.where((key >= first) & (key <= place), 0.0, -1e30)


def both_heads(block):
    zero = jnp.zeros_like(block)
    first = lax.broadcasted_iota(jnp.int32, block.shape, 1) < HD
    return jnp.concatenate([jnp.where(first, block, zero), jnp.where(first, zero, block)], axis=0)


def own_rows(both):
    size = both.shape[1] // 2
    row = lax.broadcasted_iota(jnp.int32, (PAIR, size), 0)
    return jnp.where(row < HD, both[:, :size], both[:, size:])


def unit_of(size):
    r = lax.broadcasted_iota(jnp.int32, (size, size), 0)
    c = lax.broadcasted_iota(jnp.int32, (size, size), 1)
    return (r == c).astype(F32).astype(BF16)


def attend_kernel(plan, len_ref, acts_ref, bias_ref, *refs):
    weights, (qkv_ref, ctx_ref, lse_ref, mask_ref) = refs[:-4], refs[-4:]
    rows, own = ctx_ref.shape
    write_mask(len_ref, mask_ref)
    for at in range(0, 3 * own, own):
        cut = slice(at, at + own)
        qkv_ref[:, cut] = (dot_nn(acts_ref[...], stacked(weights, plan, cut)) + bias_ref[:, cut]).astype(BF16)
    unit = unit_of(PAIR)
    scale = jnp.asarray(HD**-0.5, BF16)
    for pair in range(own // PAIR):
        at = pair * PAIR
        keys = qkv_ref[:, own + at : own + at + PAIR]
        values_t = dot_nt(unit, qkv_ref[:, 2 * own + at : 2 * own + at + PAIR]).astype(BF16)
        for lo, hi in row_blocks(rows):
            size = hi - lo
            both = both_heads(qkv_ref[lo:hi, at : at + PAIR] * scale)
            mask = mask_ref[:hi, lo:hi]
            scores = dot_nt(keys[:hi], both) + jnp.concatenate([mask, mask], axis=1)
            peak = jnp.max(scores, axis=0, keepdims=True)
            expo = jnp.exp(scores - peak)
            total = jnp.sum(expo, axis=0, keepdims=True)
            probs = (expo * (1.0 / total)).astype(BF16)
            lse = peak + jnp.log(total)
            lse_ref[2 * pair : 2 * pair + 1, lo:hi] = lse[:, :size]
            lse_ref[2 * pair + 1 : 2 * pair + 2, lo:hi] = lse[:, size:]
            ctx_ref[lo:hi, at : at + PAIR] = own_rows(dot_nn(values_t[:, :hi], probs)).T.astype(BF16)


def middle_kernel(lo, plan, many, rank_ref, order_ref, row_ref, bup_ref, ctx_ref, ent_ref, gbm_ref, *refs):
    weights, downs, (mid_ref, acts_ref, active_ref, ghid_ref, gn_ref, gbup_ref) = refs[:many], refs[many:-6], refs[-6:]
    plan, plan_dn = plan
    rows = slice(lo, lo + mid_ref.shape[0])
    zero = rank_ref[0, 0] == 0
    own = ctx_ref.shape[1] // 2
    last = last_of(order_ref)

    def ordered(a, b):
        return jnp.where(zero, a, b), jnp.where(zero, b, a)

    w_first, w_second = ordered(stacked(weights, plan, slice(0, own)), stacked(weights, plan, slice(own, 2 * own)))
    branch = dot_nt(ctx_ref[rows, :own], w_first) + dot_nt(ctx_ref[rows, own:], w_second) + row_ref[2:3]
    middle = ent_ref[rows, :].astype(F32) + center(branch) * (1.0 - last)
    mid_ref[...] = middle
    normed, _ = norm_of(expand(middle, last))
    acts = (normed * row_ref[1:2]).astype(BF16)
    acts_ref[...] = acts
    gbm = gbm_ref[rows, :]
    units = active_ref.shape[1]
    piece = units // 2
    total = None
    for at in range(0, units, piece):
        cut, cut_up = slice(at, at + piece), slice(2 * own + at, 2 * own + at + piece)
        up_part = stacked(weights, plan, cut_up)
        hidden = dot_nn(acts, up_part) + bup_ref[:, cut]
        gact = dot_nn(gbm, stacked(downs, plan_dn, cut))
        square = hidden * hidden
        bend = jnp.tanh(hidden * (0.7978845608028654 + 0.7978845608028654 * 0.044715 * square))
        up = 0.5 + 0.5 * bend
        active_ref[:, cut] = (hidden * up).astype(BF16)
        slope = up + (0.5 * hidden) * (1.0 - bend * bend) * (
            0.7978845608028654 + 0.7978845608028654 * 3 * 0.044715 * square
        )
        ghid = (gact * slope).astype(BF16)
        ghid_ref[:, cut] = ghid
        gbup_ref[:, cut] = jnp.sum(ghid.astype(F32), axis=0, keepdims=True)
        part = dot_nt(ghid, up_part)
        total = part if total is None else total + part
    gn_ref[...] = total.astype(BF16)


def mix_kernel(plan, parts, *refs):
    refs[-1][...] = dot_nt(joined(refs[:parts]), stacked(refs[parts:-1], plan, slice(None))).astype(BF16)


def back_kernel(lo, plan, order_ref, row_ref, own_ref, other_ref, mid_ref, top_ref, *refs):
    weights, (gmid_ref, gba_ref, gctx_ref, sum_ref) = refs[:-4], refs[-4:]
    last = last_of(order_ref)
    gain = row_ref[1:2]
    weights = stacked(weights, plan, slice(0, gctx_ref.shape[1]))

    def one(at, carry):
        grad = own_ref[at, :].astype(F32) + other_ref[at, :].astype(F32)
        normed, inverse = norm_of(expand(mid_ref[at, :], last))
        gmid = top_ref[at, :].astype(F32) + norm_backward(grad, normed, inverse, gain, last)
        gmid_ref[at, :] = gmid
        gba = center(gmid)
        low = gba.astype(BF16)
        gba_ref[at, :] = low
        gctx_ref[at, :] = dot_nn(low, weights).astype(BF16)
        gain_sum, ba_sum = carry
        return (
            gain_sum + jnp.sum(grad * normed, axis=0, keepdims=True),
            ba_sum + jnp.sum(gba, axis=0, keepdims=True),
        )

    zero = jnp.zeros((1, sum_ref.shape[1]), F32)
    sum_ref[0:1, :], sum_ref[1:2, :] = by_rows(own_ref.shape[0], one, (zero, zero))
    sum_ref[2:, :] = jnp.zeros((sum_ref.shape[0] - 2, sum_ref.shape[1]), F32)


def attend_back_kernel(
    len_ref, qkv_ref, lse_ref, *refs
):
    gctx_refs, (gq_ref, gkv_ref, mask_ref, gk_ref, gv_ref) = refs[:-5], refs[-5:]
    rows, own = gq_ref.shape
    write_mask(len_ref, mask_ref)
    unit = unit_of(PAIR)
    scale = jnp.asarray(HD**-0.5, BF16)
    for pair in range(own // PAIR):
        at = pair * PAIR
        keys = qkv_ref[:, own + at : own + at + PAIR]
        values = qkv_ref[:, 2 * own + at : 2 * own + at + PAIR]
        keys_t = dot_nt(unit, keys * scale).astype(BF16)
        gctx = joined(gctx_refs, slice(at, at + PAIR))
        for lo, hi in reversed(row_blocks(rows)):
            size = hi - lo
            both_q = both_heads(qkv_ref[lo:hi, at : at + PAIR] * scale)
            both_g = both_heads(gctx[lo:hi])
            lse = jnp.concatenate(
                [lse_ref[2 * pair : 2 * pair + 1, lo:hi], lse_ref[2 * pair + 1 : 2 * pair + 2, lo:hi]], axis=1
            )
            mask = mask_ref[:hi, lo:hi]
            probs = jnp.exp(dot_nt(keys[:hi], both_q) + jnp.concatenate([mask, mask], axis=1) - lse)
            gprobs = dot_nt(values[:hi], both_g)
            delta = jnp.sum(probs * gprobs, axis=0, keepdims=True)
            gscores = (probs * (gprobs - delta)).astype(BF16)
            gq_ref[lo:hi, at : at + PAIR] = own_rows(dot_nn(keys_t[:, :hi], gscores)).T.astype(BF16)
            gk = dot_nn(gscores, both_q)
            gv = dot_nn(probs.astype(BF16), both_g)
            if hi == rows:
                gk_ref[...] = gk
                gv_ref[...] = gv
            else:
                gk_ref[:hi, :] += gk
                gv_ref[:hi, :] += gv
        gkv_ref[:, at : at + PAIR] = gk_ref[...].astype(BF16)
        gkv_ref[:, own + at : own + at + PAIR] = gv_ref[...].astype(BF16)


def part_kernel(plan, gq_ref, gkv_ref, ent_ref, order_ref, *refs):
    weights, (part_ref, sum_ref, bias_ref) = refs[:-3], refs[-3:]
    own = gq_ref.shape[1]
    last = last_of(order_ref)
    w_q, w_kv = stacked(weights, plan, slice(0, own)), stacked(weights, plan, slice(own, 3 * own))

    def one(at, carry):
        gq, gkv = gq_ref[at, :], gkv_ref[at, :]
        part = (dot_nt(gq, w_q) + dot_nt(gkv, w_kv)).astype(BF16)
        part_ref[at, :] = part
        normed, _ = norm_of(expand(ent_ref[at, :].astype(F32), last))
        gain_sum, q_sum, v_sum = carry
        return (
            gain_sum + jnp.sum(part.astype(F32) * normed, axis=0, keepdims=True),
            q_sum + jnp.sum(gq.astype(F32), axis=0, keepdims=True),
            v_sum + jnp.sum(gkv[:, own:].astype(F32), axis=0, keepdims=True),
        )

    zeros = jnp.zeros((1, 2 * own), F32), jnp.zeros((1, own), F32), jnp.zeros((1, own), F32)
    sum_ref[...], bias_ref[:, :own], bias_ref[:, own:] = by_rows(gq_ref.shape[0], one, zeros)


def vector_kernel(parts, order_ref, row_ref, gain_ref, gain_other, bias_ref, *refs):
    sum_refs, gbup_refs, out_ref = refs[:parts], refs[parts:-1], refs[-1]
    width = order_ref.shape[1]
    chooser = chooser_of(order_ref, width)
    sums = sum(ref[0:2] for ref in sum_refs)
    gbup = sum(ref[...] for ref in gbup_refs)
    gain = gain_ref[...] + gain_other[...]
    rows = jnp.concatenate([row_ref[4:5], sums, gain, jnp.zeros((4, width), F32)], axis=0)
    plain = jnp.zeros_like(rows)
    for _ in range(3):
        low = rows.astype(BF16)
        plain = plain + dot_nt(low, chooser)
        rows = rows - low.astype(F32)
    plain = jnp.concatenate([plain[0:4], gbup[:, :width], gbup[:, width:], bias_ref[...], plain[7:8]], axis=0)
    lanes = out_ref.shape[1]
    for r in range(8):
        for j in range(width // lanes):
            at = r * (width // lanes) + j
            out_ref[at : at + 1, :] = plain[r : r + 1, j * lanes : (j + 1) * lanes]


def result_kernel(order_ref, row_ref, mid_ref, own_ref, other_ref, out_ref, chooser_ref):
    last = last_of(order_ref)
    chooser_ref[...] = chooser_of(order_ref, order_ref.shape[1])

    def one(at, carry):
        branch = own_ref[at, :].astype(F32) + other_ref[at, :].astype(F32) + row_ref[3:4]
        result = (mid_ref[at, :] + center(branch) * (1.0 - last)).astype(BF16)
        out_ref[at, :] = dot_nt(result, chooser_ref[...])[:, : out_ref.shape[1]].astype(BF16)
        return carry

    by_rows(mid_ref.shape[0], one)


def final_kernel(order_ref, row_ref, own_ref, other_ref, ent_ref, gmid_ref, out_ref, chooser_ref):
    last = last_of(order_ref)
    chooser_ref[...] = chooser_of(order_ref, order_ref.shape[1])

    def one(at, carry):
        grad = own_ref[at, :].astype(F32) + other_ref[at, :].astype(F32)
        normed, inverse = norm_of(expand(ent_ref[at, :].astype(F32), last))
        grad = (gmid_ref[at, :] + norm_backward(grad, normed, inverse, row_ref[0:1], last)).astype(BF16)
        out_ref[at, :] = dot_nt(grad, chooser_ref[...])[:, : out_ref.shape[1]].astype(BF16)
        return carry

    by_rows(ent_ref.shape[0], one)


def pairs_of(refs, counts):
    found, at = [], 0
    for acts, grads in counts:
        found.append((refs[at : at + acts], refs[at + acts : at + acts + grads]))
        at += acts + grads
    return found


def send_kernel(counts, pieces, *refs):
    outs, at = refs[-pieces:], 0
    rows = outs[0].shape[0]
    for acts, grads in pairs_of(refs, counts):
        half = acts[0].shape[1] // 2
        cut = slice(at, at + grads[0].shape[1])
        made = dot_tn(joined(acts, slice(half, None)), joined(grads)).astype(BF16)
        for i, out_ref in enumerate(outs):
            out_ref[:, cut] = made[i * rows : (i + 1) * rows]
        at += grads[0].shape[1]


def keep_kernel(counts, pieces, radix, each, *refs):
    many = (radix - 1) * each
    keep_ref, send_refs = refs[-many - 1], refs[len(refs) - many :]
    got = joined(refs[-many - 1 - pieces : -many - 1]).astype(F32)
    rows, at = keep_ref.shape[0], 0
    size = rows // each
    for acts, grads in pairs_of(refs, counts):
        cut = slice(at, at + grads[0].shape[1])
        half = dot_tn(joined(acts, slice(0, rows * radix)), joined(grads)) + got[:, cut]
        keep_ref[:, cut] = half[:rows]
        for k, send_ref in enumerate(send_refs):
            send_ref[:, cut] = half[rows + k * size : rows + (k + 1) * size].astype(BF16)
        at += grads[0].shape[1]


def add_kernel(given, each, *refs):
    total = refs[0][...]
    for i in range(1, 1 + given, each):
        total = total + joined(refs[i : i + each]).astype(F32)
    rows = refs[1 + given].shape[0]
    refs[1 + given][...] = total[:rows]
    for k, ref in enumerate(refs[2 + given :]):
        ref[...] = total[(k + 1) * rows : (k + 2) * rows].astype(BF16)


def add_vector_kernel(given, each, *refs):
    vector, refs = refs[0][...].astype(BF16), refs[1:]
    total = refs[0][...]
    for i in range(1, 1 + given, each):
        total = total + joined(refs[i : i + each]).astype(F32)
    rows, columns = refs[1 + given].shape
    refs[1 + given][...] = total[:rows]
    for k, ref in enumerate(refs[2 + given :]):
        ref[:, :columns] = total[(k + 1) * rows : (k + 2) * rows].astype(BF16)
        ref[:, columns:] = vector


def finish_kernel(given, vectors, vector_ref, keep_ref, *refs):
    got, cuts, vec_refs = refs[:given], refs[given:-vectors], refs[-vectors:]
    columns = keep_ref.shape[1]
    total = keep_ref[...]
    parts = [vector_ref[...].astype(BF16).astype(F32)]
    for ref in got:
        total = total + ref[:, :columns].astype(F32)
        parts.append(ref[:, columns:].astype(F32))
    at = 0
    for ref in cuts:
        ref[...] = total[:, at : at + ref.shape[1]]
        at += ref.shape[1]
    while len(parts) > 1:
        parts = [parts[i] + parts[i + 1] for i in range(0, len(parts), 2)]
    at, lanes = 0, parts[0].shape[1]
    for ref in vec_refs:
        for j in range(ref.shape[0] // lanes):
            ref[j * lanes : (j + 1) * lanes] = parts[0][at]
            at += 1


def gather_far(shard, count):
    return jnp.concatenate(gather_far_pieces(shard, count), axis=0)


def gather_far_pieces(shard, count):
    pieces = [shard]
    for stride, radix in reversed(phases_of(count)[2:]):
        held = pieces[0] if len(pieces) == 1 else jnp.concatenate(pieces, axis=0)
        pieces = [held] + [swap(held, k * stride) for k in range(1, radix)]
    return pieces


def gather_near(held, count):
    pieces = [held]
    for stride, radix in phases_of(count)[1:2]:
        pieces += [swap(held, k * stride) for k in range(1, radix)]
    return pieces


def plan_of(pieces):
    return tuple((i, 0, piece.shape[0]) for i, piece in enumerate(pieces))


def near_first(shard, count):
    middle = shard.shape[1] // 2
    halves = [shard[:, :middle], shard[:, middle:]]
    if len(phases_of(count)) != 3:
        return halves
    return [piece for pair in zip(*(gather_near(half, count) for half in halves)) for piece in pair]


def then_far(held, count):
    phases = phases_of(count)
    if len(phases) != 3:
        pieces = gather_near(gather_far(held, count), count)
        return pieces, plan_of(pieces + pieces)
    (_, near), (stride, far) = phases[1:]
    rows = held.shape[0] // near
    pieces = [held] + [swap(held, k * stride) for k in range(1, far)]
    plan = [(core * far + z, x * rows, rows) for core in range(2) for x in range(near) for z in range(far)]
    return pieces, tuple(plan)


class Sum:
    def __init__(self, pairs, count, first=4, second=1):
        self.flat = [a for pair in pairs for parts in pair for a in parts]
        self.counts = tuple((len(acts), len(grads)) for acts, grads in pairs)
        self.phases = phases_of(count)
        self.columns = sum(grads[0].shape[1] for _, grads in pairs)
        self.rows = pairs[0][0][0].shape[1] // 2
        self.each, self.second = first, second
        self.sent = call(
            functools.partial(send_kernel, self.counts, first),
            [shape(self.rows // first, self.columns, BF16)] * first,
            self.flat,
        )
        self.keep = None
        self.got = []

    def go(self):
        (stride, _), self.phases = self.phases[0], self.phases[1:]
        self.got = [swap(piece, (k // self.each + 1) * stride) for k, piece in enumerate(self.sent)]
        return self

    def work(self):
        got = self.got
        if not self.phases:
            total = self.keep
            for piece in got:
                total = total + piece.astype(F32)
            self.keep = total
            return self
        radix = self.phases[0][1]
        self.rows //= radix
        outs = [shape(self.rows, self.columns, F32)]
        if self.keep is None:
            each = self.second if self.rows % (16 * self.second) == 0 else 1
            outs += [shape(self.rows // each, self.columns, BF16)] * ((radix - 1) * each)
            kernel = functools.partial(keep_kernel, self.counts, len(got), radix, each)
            outs = call(kernel, outs, self.flat + got)
        elif self.rows % 16 == 0:
            outs += [shape(self.rows, self.columns, BF16)] * (radix - 1)
            outs = call(functools.partial(add_kernel, len(got), self.each), outs, [self.keep] + got)
            each = 1
        else:
            total = self.keep
            for i in range(0, len(got), self.each):
                total = total + jnp.concatenate(got[i : i + self.each], axis=0).astype(F32)
            parts = [total[k * self.rows : (k + 1) * self.rows] for k in range(radix)]
            outs = [parts[0]] + [part.astype(BF16) for part in parts[1:]]
            each = 1
        self.each = each
        self.keep, *self.sent = outs
        return self

    def end(self):
        while self.phases:
            self.go().work()
        return self.keep


def tie(sums, *arrays):
    flat = list(arrays) + [piece for one in sums for piece in one.got]
    flat = lax.optimization_barrier(tuple(flat))
    at = len(arrays)
    for one in sums:
        one.got = list(flat[at : at + len(one.got)])
        at += len(one.got)
    return flat[: len(arrays)]


def flips_of(phases):
    found = [0]
    for stride, radix in phases:
        found = [k * stride + f for k in range(radix) for f in found]
    return found[1:]


def reduce_all(vector, flips):
    return total_of([vector] + [swap(vector, flip) for flip in flips])


def total_of(parts):
    while len(parts) > 1:
        parts = [parts[i] + parts[i + 1] for i in range(0, len(parts), 2)]
    return parts[0]


def body(
    stream,
    w_query,
    w_key,
    w_value,
    b_query,
    b_value,
    w_out,
    b_out,
    gain_attn,
    w_up,
    b_up,
    w_down,
    b_down,
    gain_mlp,
    cotangent,
    lengths,
):
    rows, inner_width = stream.shape
    count = lax.axis_size("dp")
    me = lax.axis_index("dp")
    rank = lax.axis_index("tensor").astype(jnp.int32).reshape(1, 1)
    shard_rows, own = w_query.shape
    width = shard_rows * count
    units = w_up.shape[1]
    blocks = jnp.array(relative_order(count), jnp.int32)
    order = ((me ^ blocks)[:, None] * shard_rows + jnp.arange(shard_rows, dtype=jnp.int32)).reshape(1, -1)

    shard_qkv = pack([w_query, w_key, w_value], 56 * 1024 * 1024)
    qkv_far = gather_far_pieces(shard_qkv, count)
    w_out_t, w_up, shard_dn, order, rank = lax.optimization_barrier((w_out.T, w_up, w_down.T, order, rank, shard_qkv))[:5]
    shard_ou = pack([w_out_t, swap_tensor(w_out_t), w_up])
    ent, acts_a = call(
        first_kernel,
        [shape(rows, width, BF16)] * 2,
        [order, stream, gain_attn],
        scratch=[pltpu.VMEM((width, width), BF16)],
    )
    dn_near = near_first(shard_dn, count)
    flat = lax.optimization_barrier((shard_ou, acts_a, *qkv_far, *dn_near))
    shard_ou, acts_a, qkv_far, dn_near = flat[0], flat[1], flat[2 : 2 + len(qkv_far)], flat[2 + len(qkv_far) :]
    middle_at = (len(qkv_far) + 1) // 2
    halves = [jnp.concatenate(part, axis=0) for part in (qkv_far[:middle_at], qkv_far[middle_at:]) if part]
    qkv_w = [piece for group in zip(*(gather_near(half, count) for half in halves)) for piece in group]
    ou_far = gather_far_pieces(shard_ou, count)

    qkv_w = qkv_w + [swap(piece, 1) for piece in qkv_w]
    plan = plan_of(qkv_w)
    bias_qkv = jnp.concatenate([b_query, jnp.zeros_like(b_query), b_value]).astype(F32)[None]
    qkv, context, lse = call(
        functools.partial(attend_kernel, plan),
        [shape(rows, 3 * own, BF16), shape(rows, own, BF16), shape(8, rows, F32)],
        [lengths, acts_a, bias_qkv] + qkv_w,
        scalars=1,
        scratch=[pltpu.VMEM((rows, rows), F32)],
    )
    context, *ou_far = lax.optimization_barrier((context, *ou_far))
    dn_near = jnp.concatenate([jnp.concatenate(dn_near[i::2], axis=0) for i in range(2)], axis=1)
    ou_far = jnp.concatenate(ou_far, axis=0)
    other_context = [swap_tensor(context)]
    ou_w = gather_near(ou_far, count)
    dn_w, plan_dn = then_far(dn_near, count)
    made = call(
        prepare_kernel,
        [shape(rows, width, BF16)] * 4 + [shape(8, width, F32)],
        [rank, order, cotangent, context, *other_context, ent, gain_attn, gain_mlp, b_out, b_down],
        scalars=1,
    )
    flat = lax.optimization_barrier((*made, *ou_w, *dn_w))
    (context_all, ent_mid, top, gbm, row), flat = flat[:5], flat[5:]
    ou_w, dn_w = list(flat[: len(ou_w)]), list(flat[len(ou_w) :])
    ou_w = ou_w + [swap(piece, 1) for piece in ou_w]
    plan_ou = plan_of(ou_w)
    dn_w = dn_w + [swap(piece, 1) for piece in dn_w]

    cuts = [(0, rows)]
    bias_up = b_up.astype(F32)[None]
    middle, acts_m, active, ghid, gn, gn_other, gbup = [], [], [], [], [], [], []
    for lo, size in cuts:
        made = call(
            functools.partial(middle_kernel, lo, (plan_ou, plan_dn), len(ou_w)),
            [
                shape(size, width, F32),
                shape(size, width, BF16),
                shape(size, units, BF16),
                shape(size, units, BF16),
                shape(size, width, BF16),
                shape(1, units, F32),
            ],
            [rank, order, row, bias_up, context_all, ent_mid, gbm] + ou_w + dn_w,
            scalars=1,
        )
        for held, new in zip((middle, acts_m, active, ghid, gn, gbup), made):
            held.append(new)
        gn_other.append(swap_tensor(gn[-1]))

    sum_dn = Sum([((gbm,), active)], count, first=2).go()
    sum_up = Sum([(acts_m, ghid)], count, first=2).go()
    sum_dn.work().go()
    sum_up.work().go()
    (mlp,) = call(
        functools.partial(mix_kernel, plan_dn, len(active)),
        [shape(rows, width, BF16)],
        [after(active[0], sum_up.sent)] + active[1:] + dn_w,
    )
    mlp_other = swap_tensor(mlp)
    sum_dn.work().go()

    gmid, gba, gctx, sums = [], [], [], []
    gn_other[0] = after(gn_other[0], sum_dn.sent, sum_up.sent, mlp)
    for i, (lo, size) in enumerate(cuts):
        made = call(
            functools.partial(back_kernel, lo, plan_ou),
            [shape(size, width, F32), shape(size, width, BF16), shape(size, own, BF16), shape(8, width, F32)],
            [order, row, gn[i], gn_other[i], middle[i], top] + ou_w,
        )
        for held, new in zip((gmid, gba, gctx, sums), made):
            held.append(new)
    gq, gkv = call(
        attend_back_kernel,
        [shape(rows, own, BF16), shape(rows, 2 * own, BF16)],
        [lengths, qkv, lse] + gctx,
        scalars=1,
        scratch=[pltpu.VMEM((rows, rows), F32), pltpu.VMEM((rows, PAIR), F32), pltpu.VMEM((rows, PAIR), F32)],
    )
    gq, gkv = tie([sum_dn, sum_up], gq, gkv)
    sum_last = Sum([(gba, (context,)), ((acts_a,), (gq,)), ((acts_a,), (gkv,))], count, first=2).go()
    sum_last.work().go()
    sum_up.work().go()
    gq, gkv, mlp_other = lax.optimization_barrier((gq, gkv, mlp_other, *sum_last.sent, *sum_up.sent))[:3]
    part, gain, gbias = call(
        functools.partial(part_kernel, plan),
        [shape(rows, width, BF16), shape(1, width, F32), shape(1, 2 * own, F32)],
        [gq, gkv, ent, order] + qkv_w,
        cost=LONG,
    )
    gain_other = swap_tensor(gain)
    part_other = swap_tensor(part)
    (plain,) = call(
        functools.partial(vector_kernel, len(cuts)),
        [shape(8 * width // 128, 128, F32)],
        [order, row, gain, gain_other, gbias] + sums + gbup,
    )
    phases = phases_of(count)
    parts = [plain] + [swap(plain, flip) for flip in flips_of(phases[:2])]
    plain = total_of(list(tie([sum_last, sum_up], *parts)))
    short = len(phases) == 3
    if short:
        block = plain
        given, radix, size = len(sum_last.got), phases[2][1], sum_last.rows // phases[2][1]
        columns = sum_last.columns
        keep, *sent = call(
            functools.partial(add_vector_kernel, given, sum_last.each),
            [shape(size, columns, F32)] + [shape(size, columns + block.shape[1], BF16)] * (radix - 1),
            [block, sum_last.keep] + sum_last.got,
        )
        last_got = [swap(piece, (k + 1) * phases[2][0]) for k, piece in enumerate(sent)]
    else:
        sum_last.work()
        sent = sum_last.sent
        sum_last.go()
        for phase in phases[2:]:
            plain = reduce_all(plain, flips_of([phase]))
    mlp_other = after(mlp_other, sent)
    (out_rows,) = call(
        result_kernel,
        [shape(rows, inner_width, BF16)],
        [order, row, *middle, mlp, mlp_other],
        scratch=[pltpu.VMEM((width, width), BF16)],
    )
    part_other, out_rows = lax.optimization_barrier((part_other, out_rows))
    (grad_stream,) = call(
        final_kernel,
        [shape(rows, inner_width, BF16)],
        [order, row, part, part_other, ent, *gmid],
        scratch=[pltpu.VMEM((width, width), BF16)],
    )
    shard_dn_t, shard_up = (one.work().end() for one in (sum_dn, sum_up))
    if short:
        keep, grad_stream = lax.optimization_barrier((keep, grad_stream))
        sizes = [width] * 4 + [2 * width, own, own]
        out_t, grad_q, grad_k, grad_v, *vectors = call(
            functools.partial(finish_kernel, len(last_got), len(sizes)),
            [shape(shard_rows, own, F32)] * 4 + [jax.ShapeDtypeStruct((size,), F32) for size in sizes],
            [block, keep] + last_got,
        )
    else:
        last = sum_last.work().end()
        out_t, grad_q, grad_k, grad_v = (last[:, i * own : (i + 1) * own] for i in range(4))
        plain = plain.reshape(8, width)
        vectors = [plain[0], plain[1], plain[2], plain[3], plain[4:6].reshape(-1), plain[6, :own], plain[6, own:]]
    grad_b_down, grad_gain_mlp, grad_b_out, grad_gain_attn, grad_b_up, grad_b_query, grad_b_value = vectors
    return (
        out_rows,
        grad_stream,
        grad_q,
        grad_k,
        grad_v,
        grad_b_query,
        grad_b_value,
        out_t.T,
        grad_b_out,
        grad_gain_attn,
        shard_up,
        grad_b_up,
        shard_dn_t.T,
        grad_b_down,
        grad_gain_mlp,
    )


def solution(mesh):
    return jax.shard_map(
        body,
        mesh=mesh,
        in_specs=(
            P("dp", None),
            P("dp", "tensor"),
            P("dp", "tensor"),
            P("dp", "tensor"),
            P("tensor"),
            P("tensor"),
            P("tensor", "dp"),
            P(),
            P(),
            P("dp", "tensor"),
            P("tensor"),
            P("tensor", "dp"),
            P(),
            P(),
            P("dp", None),
            P("dp", None),
        ),
        out_specs=(
            P("dp", None),
            P("dp", None),
            P("dp", "tensor"),
            P("dp", "tensor"),
            P("dp", "tensor"),
            P("tensor"),
            P("tensor"),
            P("tensor", "dp"),
            P(),
            P(),
            P("dp", "tensor"),
            P("tensor"),
            P("tensor", "dp"),
            P(),
            P(),
        ),
        check_vma=False,
    )
```
